32 devices in a mesh: section: 2 (over x), dp: 16 (over z, y, core).
Axes of the slice: x: 2, y: 2, z: 4, core: 2. Of those that a mesh axis runs over, the one named last changes fastest.
Arguments:
- pixels: bfloat16 [64, 196, 768], P('dp')
- visible: int32 [64, 49], P('dp'), may hold values from 0 to 195, as said below
- restore: int32 [64, 196], P('dp'), may hold values from 0 to 195, as said below
- mat_master: float32 [2, 7667712], P('section', 'dp')
- mat_first: float32 [2, 7667712], P('section', 'dp')
- mat_second: float32 [2, 7667712], P('section', 'dp')
- vec_master: float32 [2, 162816], P('section', 'dp')
- vec_first: float32 [2, 162816], P('section', 'dp')
- vec_second: float32 [2, 162816], P('section', 'dp')
Outputs:
- loss_sum: float32 [], replicated
- grad_norm: float32 [], replicated
- mat_new: float32 [2, 7667712], P('section', 'dp')
- mat_first_new: float32 [2, 7667712], P('section', 'dp')
- mat_second_new: float32 [2, 7667712], P('section', 'dp')
- mat_copy: bfloat16 [2, 7667712], P('section', 'dp')
- vec_new: float32 [2, 162816], P('section', 'dp')
- vec_first_new: float32 [2, 162816], P('section', 'dp')
- vec_second_new: float32 [2, 162816], P('section', 'dp')
- vec_copy: bfloat16 [2, 162816], P('section', 'dp')
The draws below stay inside these ranges and needn't reach their ends.
Inputs may be any that keep to these rules, and one draw needn't show every extreme that they name: restore[i] is the inverse of a permutation of the 196 patches whose first 49 entries are visible[i], in order. `visible`: each row holds 49 different patches.
All inputs are finite; a program needn't handle non-finite values.
Results may differ from the reference program's by a relative error of at most 0.011.
Values may be sent and summed in bfloat16 or wider, within the bound.
A program may use at most 576 MiB of HBM per device.

```python
import math
import jax
import jax.numpy as jnp
from jax import lax

PIX = 768
DE = 768
HE = 12
FE = 3072
DD = 512
HD = 16
FD = 2048
PATCHES = 196
VIS = 49
STEP = 10
IMG_MB = 2
IMAGES = 64
PM = 7667712
PV = 162816


CLIP = 0.001


def shuffle_orders(key):
    keys = jax.random.split(key, IMAGES)
    return jax.vmap(lambda item: jax.random.permutation(item, PATCHES))(keys).astype(jnp.int32)


def draw_visible(key, part):
    orders = shuffle_orders(key)
    return orders[:, :VIS]


def draw_restore(key, part):
    orders = shuffle_orders(key)
    return jnp.argsort(orders, axis=1, stable=True).astype(jnp.int32)


def draw_pixels(key, part):
    key = jax.random.fold_in(key, 11)
    ramp = jnp.arange(IMAGES, dtype=jnp.float32) / max(IMAGES - 1, 1)
    base = jnp.clip(jax.random.normal(key, (IMAGES, PATCHES, PIX), jnp.float32), -6.0, 6.0)
    scale = 1.0 + 2.0 * ramp
    return (base * scale[:, None, None]).astype(jnp.bfloat16)


def matrix_plans():
    encoder_plan = [(PIX * DE, PIX ** (-0.5)), (3 * DE * DE, DE ** (-0.5)), (DE * DE, 0.5 * (VIS / DE) ** 0.5), (DE * FE, DE ** (-0.5)), (FE * DE, FE ** (-0.5))]
    decoder_plan = [(DE * DD, DE ** (-0.5)), (3 * DD * DD, DD ** (-0.5)), (DD * DD, 0.5 * (PATCHES / DD) ** 0.5), (DD * FD, DD ** (-0.5)), (FD * DD, FD ** (-0.5)), (DD * PIX, DD ** (-0.5))]
    return [encoder_plan, decoder_plan]


def vector_plans():
    encoder_plan = [(DE, 0.1), (PATCHES * DE, 0.5), (DE, -1.0), (DE, 0.1), (2 * DE, 0.1), (DE, 0.1), (DE, -1.0), (DE, 0.1), (FE, 0.1), (DE, 0.1), (DE, -1.0), (DE, 0.1)]
    decoder_plan = [(DD, 0.1), (DD, 1.0), (PATCHES * DD, 0.5), (DD, -1.0), (DD, 0.1), (2 * DD, 0.1), (DD, 0.1), (DD, -1.0), (DD, 0.1), (FD, 0.1), (DD, 0.1), (DD, -1.0), (DD, 0.1), (PIX, 0.1)]
    return [encoder_plan, decoder_plan]


def draw_piece(key, count, spread, stretch):
    if spread < 0.0:
        ramp = jnp.arange(count, dtype=jnp.float32) / max(count - 1, 1)
        lift = jax.random.uniform(key, (count,), jnp.float32, 0.7, 1.3)
        return lift * (0.6 + stretch * ramp)
    return jnp.clip(jax.random.normal(key, (count,), jnp.float32), -6.0, 6.0) * spread


def draw_packed(key, plans, total):
    stretch = 1.2
    rows = []
    for section in range(2):
        pieces = []
        used = 0
        for index, (count, spread) in enumerate(plans[section]):
            pieces.append(draw_piece(jax.random.fold_in(key, 100 * section + index), count, spread, stretch))
            used = used + count
        if used < total:
            pieces.append(draw_piece(jax.random.fold_in(key, 100 * section + 99), total - used, 0.02, stretch))
        rows.append(jnp.concatenate(pieces))
    return jnp.stack(rows)


def grad_size():
    return CLIP / math.sqrt(2.0 * (PM + PV))


def draw_mat_master(key, part):
    key = jax.random.fold_in(key, 21)
    return draw_packed(key, matrix_plans(), PM)


def draw_vec_master(key, part):
    key = jax.random.fold_in(key, 22)
    return draw_packed(key, vector_plans(), PV)


def draw_first(key, count, size):
    return jnp.clip(jax.random.normal(key, (2, count), jnp.float32), -4.0, 4.0) * (size / 9.0)


def draw_second(key, count, size):
    return jax.random.uniform(key, (2, count), jnp.float32, 1.0, 4.0) * (size * size * 0.05 / 0.95)


def draw_mat_first(key, part):
    key = jax.random.fold_in(key, 31)
    return draw_first(key, PM, grad_size())


def draw_mat_second(key, part):
    key = jax.random.fold_in(key, 32)
    return draw_second(key, PM, grad_size())


def draw_vec_first(key, part):
    key = jax.random.fold_in(key, 33)
    return draw_first(key, PV, 3.0 * grad_size())


def draw_vec_second(key, part):
    key = jax.random.fold_in(key, 34)
    return draw_second(key, PV, 3.0 * grad_size())


def setup_inputs(seed: int = 0) -> dict:
    arg_keys = jax.random.split(jax.random.key(seed), 10)
    return {
        "pixels": draw_pixels(jax.random.fold_in(arg_keys[9], 71), 0),
        "visible": draw_visible(jax.random.fold_in(arg_keys[9], 71), 0),
        "restore": draw_restore(jax.random.fold_in(arg_keys[9], 71), 0),
        "mat_master": draw_mat_master(jax.random.fold_in(arg_keys[9], 71), 0),
        "mat_first": draw_mat_first(jax.random.fold_in(arg_keys[9], 71), 0),
        "mat_second": draw_mat_second(jax.random.fold_in(arg_keys[9], 71), 0),
        "vec_master": draw_vec_master(jax.random.fold_in(arg_keys[9], 71), 0),
        "vec_first": draw_vec_first(jax.random.fold_in(arg_keys[9], 71), 0),
        "vec_second": draw_vec_second(jax.random.fold_in(arg_keys[9], 71), 0),
    }


@jax.custom_vjp
def low(v):
    return lax.optimization_barrier(v.astype(jnp.bfloat16)).astype(jnp.float32)

@jax.custom_vjp
def low_back(v):
    return v

def low_keep(v):
    return (low(v), None)

def low_pass(kept, grad):
    return (grad,)

def back_keep(v):
    return (v, None)

def back_low(kept, grad):
    return (low(grad),)
low.defvjp(low_keep, low_pass)
low_back.defvjp(back_keep, back_low)

def product(left, right):
    return jnp.matmul(left, right, precision=lax.Precision.HIGHEST)

def carve(flat, shapes):
    pieces = []
    offset = 0
    for shape in shapes:
        count = math.prod(shape)
        pieces.append(flat[offset:offset + count].reshape(shape))
        offset = offset + count
    return pieces

def encoder_shapes():
    mats = [(PIX, DE), (DE, 3 * DE), (DE, DE), (DE, FE), (FE, DE)]
    vecs = [(DE,), (PATCHES, DE), (DE,), (DE,), (2 * DE,), (DE,), (DE,), (DE,), (FE,), (DE,), (DE,), (DE,)]
    return (mats, vecs)

def decoder_shapes():
    mats = [(DE, DD), (DD, 3 * DD), (DD, DD), (DD, FD), (FD, DD), (DD, PIX)]
    vecs = [(DD,), (DD,), (PATCHES, DD), (DD,), (DD,), (2 * DD,), (DD,), (DD,), (DD,), (FD,), (DD,), (DD,), (DD,), (PIX,)]
    return (mats, vecs)

def layer_norm(values, gain, shift):
    centred = values - lax.optimization_barrier(jnp.mean(values, -1, keepdims=True))
    spread = lax.optimization_barrier(jnp.mean(centred * centred, -1, keepdims=True))
    return centred * lax.rsqrt(spread + 1e-06) * gain + shift

def linear(values, weight):
    shape = values.shape
    result = low_back(product(values.reshape(-1, shape[-1]), weight))
    return result.reshape(shape[:-1] + (weight.shape[1],))

def block(state, mats, vecs, heads):
    w_qkv, w_proj, w_up, w_down = mats
    gain_one, shift_one, qv_bias, proj_bias, gain_two, shift_two, up_bias, down_bias = vecs
    batch, count, width = state.shape
    size = width // heads
    normed = low(layer_norm(state, gain_one, shift_one))
    bias = jnp.concatenate([qv_bias[:width], jnp.zeros((width,), qv_bias.dtype), qv_bias[width:]])
    mixed = (linear(normed, w_qkv) + bias).reshape(batch, count, 3, heads, size).transpose(2, 0, 3, 1, 4)
    query = low(mixed[0] * size ** (-0.5))
    keys = low(mixed[1])
    values = low(mixed[2])
    scores = low_back(product(query, jnp.swapaxes(keys, -1, -2)))
    weights = low(jax.nn.softmax(scores, axis=-1))
    attended = low_back(product(weights, values))
    attended = low(attended.transpose(0, 2, 1, 3).reshape(batch, count, width))
    state = state + linear(attended, w_proj) + proj_bias
    normed = low(layer_norm(state, gain_two, shift_two))
    hidden = low(jax.nn.gelu(linear(normed, w_up) + up_bias))
    return state + linear(hidden, w_down) + down_bias

def encoder(mats, vecs, pixels, visible):
    shapes_mat, shapes_vec = encoder_shapes()
    w_embed, w_qkv, w_proj, w_up, w_down = carve(mats, shapes_mat)
    pieces = carve(vecs, shapes_vec)
    chosen = jnp.take_along_axis(pixels, visible[:, :, None], axis=1)
    state = linear(chosen, w_embed) + pieces[0] + pieces[1][visible]
    state = block(state, (w_qkv, w_proj, w_up, w_down), pieces[2:10], HE)
    return low(layer_norm(state, pieces[10], pieces[11]))

def decoder(mats, vecs, latent, pixels, restore):
    latent = low_back(latent)
    shapes_mat, shapes_vec = decoder_shapes()
    w_embed, w_qkv, w_proj, w_up, w_down, w_head = carve(mats, shapes_mat)
    pieces = carve(vecs, shapes_vec)
    batch = latent.shape[0]
    embedded = linear(latent, w_embed) + pieces[0]
    filler = jnp.broadcast_to(pieces[1], (batch, PATCHES - VIS, DD))
    joined = jnp.concatenate([embedded, filler], 1)
    state = jnp.take_along_axis(joined, restore[:, :, None], axis=1) + pieces[2]
    state = block(state, (w_qkv, w_proj, w_up, w_down), pieces[3:11], HD)
    guess = linear(low(layer_norm(state, pieces[11], pieces[12])), w_head) + pieces[13]
    masked = (restore >= VIS).astype(guess.dtype)
    error = guess - pixels
    return jnp.sum(lax.optimization_barrier(jnp.mean(error * error, -1)) * masked)

def adam_update(master, first, second, grad, rate, decay):
    first = 0.9 * first + 0.1 * grad
    second = 0.95 * second + 0.05 * grad * grad
    step_first = first / (1.0 - 0.9 ** STEP)
    step_second = second / (1.0 - 0.95 ** STEP)
    master = master - rate * (step_first / (jnp.sqrt(step_second) + 1e-08) + decay * master)
    return (master, first, second)

def reference(pixels, visible, restore, mat_master, mat_first, mat_second, vec_master, vec_first, vec_second):
    groups = IMAGES // IMG_MB
    masked_total = (PATCHES - VIS) * IMAGES
    pix = pixels.astype(jnp.float32).reshape(groups, IMG_MB, PATCHES, PIX)
    vis = visible.reshape(groups, IMG_MB, VIS)
    order = restore.reshape(groups, IMG_MB, PATCHES)

    def group_loss(mats, vecs, images, seen, places):
        mats = low(mats)
        vecs = low(vecs)
        latent = encoder(mats[0], vecs[0], images, seen)
        return decoder(mats[1], vecs[1], latent, images, places)

    def advance(carry, inputs):
        total, grad_mats, grad_vecs = carry
        value, pull = jax.vjp(lambda a, b: group_loss(a, b, *inputs), mat_master, vec_master)
        delta_mats, delta_vecs = pull(jnp.ones_like(value) / masked_total)
        return ((total + value, grad_mats + delta_mats, grad_vecs + delta_vecs), None)
    start = (jnp.zeros((), jnp.float32), jnp.zeros_like(mat_master), jnp.zeros_like(vec_master))
    (loss_sum, grad_mats, grad_vecs), _ = lax.scan(advance, start, (pix, vis, order))
    grad_norm = jnp.sqrt(jnp.sum(grad_mats * grad_mats) + jnp.sum(grad_vecs * grad_vecs))
    factor = jnp.minimum(1.0, 0.001 / (grad_norm + 1e-06))
    mat_new, mat_first_new, mat_second_new = adam_update(mat_master, mat_first, mat_second, factor * grad_mats, 0.05, 0.05)
    vec_new, vec_first_new, vec_second_new = adam_update(vec_master, vec_first, vec_second, factor * grad_vecs, 0.3, 0.0)
    return (loss_sum, grad_norm, mat_new, mat_first_new, mat_second_new, mat_new.astype(jnp.bfloat16), vec_new, vec_first_new, vec_second_new, vec_new.astype(jnp.bfloat16))
```

```python
import functools
import math

import jax
import jax.numpy as jnp
from jax import lax
from jax.experimental import pallas as pl
from jax.experimental.pallas import tpu as pltpu
from jax.sharding import PartitionSpec as P

PIX = 768
DE = 768
HE = 12
FE = 3072
DD = 512
HD = 16
FD = 2048
PATCHES = 196
VIS = 49
STEP = 10
ROWS_E = 64
ROWS_D = 208
EPS = 1e-6
BF = jnp.bfloat16
F32 = jnp.float32
VMEM_LIMIT = 63 * 1024 * 1024

ENC_MATS = [(PIX, DE), (DE, 3 * DE), (DE, DE), (DE, FE), (FE, DE)]
DEC_MATS = [(DE, DD), (DD, 3 * DD), (DD, DD), (DD, FD), (FD, DD), (DD, PIX)]
ENC_VECS = [DE, PATCHES * DE, DE, DE, 2 * DE, DE, DE, DE, FE, DE, DE, DE]
DEC_VECS = [DD, DD, PATCHES * DD, DD, DD, 2 * DD, DD, DD, DD, FD, DD, DD, DD, PIX]


def starts(sizes):
    total, found = 0, []
    for size in sizes:
        found.append(total)
        total += size
    return found, total


ENC_TILES = [k * n // 2048 for k, n in ENC_MATS]
DEC_TILES = [k * n // 2048 for k, n in DEC_MATS]
ENC_BASE, ENC_TOTAL = starts(ENC_TILES)
DEC_BASE, DEC_TOTAL = starts(DEC_TILES)
EV, _ = starts([size // 128 for size in ENC_VECS])
DV, _ = starts([size // 128 for size in DEC_VECS])


class Mat:
    def __init__(self, ref, base, shape):
        self.rows, self.columns = shape
        self.blocks = self.columns // 128
        count = self.rows * self.columns // 2048
        self.ref = ref.at[pl.ds(base, count)].reshape(self.rows // 16, self.blocks, 16, 128)

    def cols(self, block):
        parts = [self.ref[:, 2 * block + half].reshape(self.rows, 128) for half in range(2)]
        return jnp.concatenate(parts, 1)

    def band(self, block):
        part = self.ref.at[pl.ds(block * 16, 16)]
        return jnp.concatenate([part[:, j].reshape(256, 128) for j in range(self.blocks)], 1)

    def put_cols(self, block, value):
        for half in range(2):
            piece = value[:, half * 128 : (half + 1) * 128].astype(BF)
            self.ref[:, 2 * block + half] = piece.reshape(self.rows // 16, 16, 128)

    def put_band(self, block, value):
        part = self.ref.at[pl.ds(block * 16, 16)]
        for j in range(self.blocks):
            part[:, j] = value[:, j * 128 : (j + 1) * 128].astype(BF).reshape(16, 16, 128)


def dot(a, b):
    return jnp.dot(a, b, preferred_element_type=F32)


def dot_t(a, b):
    return lax.dot_general(a, b, (((1,), (1,)), ((), ())), preferred_element_type=F32)


def t_dot(a, b):
    return lax.dot_general(a, b, (((0,), (0,)), ((), ())), preferred_element_type=F32)


def loop(count, body, init=0):
    return lax.fori_loop(0, count, body, init)


def lanes(block, width=256):
    return pl.ds(pl.multiple_of(block * width, width), width)


def row_of(vec, start, width):
    return jnp.concatenate([vec[start + j : start + j + 1, :] for j in range(width // 128)], 1)


def row_at(vec, start, block):
    return jnp.concatenate([vec[pl.ds(start + 2 * block + h, 1), :] for h in range(2)], 1)


def put_row(dvec, start, value):
    for j in range(value.shape[1] // 128):
        dvec[start + j : start + j + 1, :] = value[:, j * 128 : (j + 1) * 128]


def put_row_at(dvec, start, block, value):
    for h in range(2):
        dvec[pl.ds(start + 2 * block + h, 1), :] = value[:, h * 128 : (h + 1) * 128]


def fold(value):
    return value.reshape(value.shape[0] // 8, 8, value.shape[1]).sum(0)


def total_row(value):
    return jnp.sum(value, 0, keepdims=True)


def norm_parts(x):
    mean = jnp.mean(x, -1, keepdims=True)
    centred = x - mean
    scale = lax.rsqrt(jnp.mean(centred * centred, -1, keepdims=True) + EPS)
    return centred * scale, scale


CHUNK = 32


def chunk_rows(i):
    return pl.ds(pl.multiple_of(i * CHUNK, CHUNK), CHUNK)


def norm_rows(x_ref, out_ref, vec, gain_at, shift_at, width, add_ref=None, bias_at=None):
    gain, shift = row_of(vec, gain_at, width), row_of(vec, shift_at, width)
    bias = None if bias_at is None else row_of(vec, bias_at, width)

    def step(i, carry):
        rows = chunk_rows(i)
        x = x_ref[rows, :]
        if add_ref is not None:
            x = x + add_ref[rows, :] + bias
            add_ref[rows, :] = x
        unit, _ = norm_parts(x)
        out_ref[rows, :] = (unit * gain + shift).astype(BF)
        return carry

    loop(x_ref.shape[0] // CHUNK, step)


def norm_back_rows(x_ref, dy_ref, dx_ref, dxb_ref, vec, dvec, gain_at, shift_at, width, bias_at, add):
    gain = row_of(vec, gain_at, width)
    zero = jnp.zeros((8, width), F32)

    def step(i, carry):
        dgain, dshift, dbias = carry
        rows = chunk_rows(i)
        unit, scale = norm_parts(x_ref[rows, :])
        dy = dy_ref[rows, :].astype(F32)
        dunit = dy * gain
        dx = scale * (
            dunit
            - jnp.mean(dunit, -1, keepdims=True)
            - unit * jnp.mean(dunit * unit, -1, keepdims=True)
        )
        if add:
            dx = dx + dx_ref[rows, :]
        dx_ref[rows, :] = dx
        dxb_ref[rows, :] = dx.astype(BF)
        return dgain + fold(dy * unit), dshift + fold(dy), dbias + fold(dx)

    dgain, dshift, dbias = loop(x_ref.shape[0] // CHUNK, step, (zero, zero, zero))
    put_row(dvec, gain_at, total_row(dgain))
    put_row(dvec, shift_at, total_row(dshift))
    if bias_at is not None:
        put_row(dvec, bias_at, total_row(dbias))
    return dbias


GELU_C = math.sqrt(2.0 / math.pi)


def gelu_parts(x):
    square = x * x
    t = jnp.tanh(x * (GELU_C + (GELU_C * 0.044715) * square))
    half = 0.5 * (1.0 + t)
    return x * half, half + (0.5 * x) * (1.0 - t * t) * (
        GELU_C + (3.0 * 0.044715 * GELU_C) * square
    )


def head_mask(size):
    lane = lax.broadcasted_iota(jnp.int32, (1, 128), 1)
    return [(lane >= h * size) & (lane < (h + 1) * size) for h in range(128 // size)]


def attention(qkv, probs, att, bias, group, groups, width, size):
    blocks = width // 128
    masks = head_mask(size)

    def step(i, carry):
        g, b = i // blocks, i % blocks
        rows = pl.ds(pl.multiple_of(g * group, 16), group)
        q = qkv[rows, lanes(b, 128)]
        k = qkv[rows, lanes(blocks + b, 128)]
        v = qkv[rows, lanes(2 * blocks + b, 128)]
        out = jnp.zeros((group, 128), F32)
        for h, mask in enumerate(masks):
            s = dot_t(jnp.where(mask, q, jnp.zeros_like(q)), k) + bias
            e = jnp.exp(s - jnp.max(s, -1, keepdims=True))
            p = (e * (1.0 / jnp.sum(e, -1, keepdims=True))).astype(BF)
            probs[i * len(masks) + h] = p
            out = jnp.where(mask, dot(p, v), out)
        att[rows, lanes(b, 128)] = out.astype(BF)
        return carry

    loop(groups * blocks, step)


def attention_back(qkv, probs, datt, dqkv, dvec, qv_at, group, groups, width, size):
    blocks = width // 128
    masks = head_mask(size)
    scale = size ** (-0.5)
    for j in range(2 * blocks):
        dvec[qv_at + j : qv_at + j + 1, :] = jnp.zeros((1, 128), F32)

    def step(i, carry):
        g, b = i // blocks, i % blocks
        rows = pl.ds(pl.multiple_of(g * group, 16), group)
        q = qkv[rows, lanes(b, 128)]
        k = qkv[rows, lanes(blocks + b, 128)]
        v = qkv[rows, lanes(2 * blocks + b, 128)]
        da = datt[rows, lanes(b, 128)]
        zero = jnp.zeros((group, 128), F32)
        dq, dk, dv = zero, zero, zero
        for h, mask in enumerate(masks):
            p = probs[i * len(masks) + h]
            dp = dot_t(jnp.where(mask, da, jnp.zeros_like(da)), v)
            wide = p.astype(F32)
            prod = wide * dp
            ds = (prod - wide * jnp.sum(prod, -1, keepdims=True)).astype(BF)
            dq = jnp.where(mask, dot(ds, k), dq)
            dk = jnp.where(mask, t_dot(ds, q), dk)
            dv = jnp.where(mask, t_dot(p, da), dv)
        dq = dq * scale
        dqkv[rows, lanes(b, 128)] = dq.astype(BF)
        dqkv[rows, lanes(blocks + b, 128)] = dk.astype(BF)
        dqkv[rows, lanes(2 * blocks + b, 128)] = dv.astype(BF)
        dvec[pl.ds(qv_at + b, 1), :] += total_row(dq)
        dvec[pl.ds(qv_at + blocks + b, 1), :] += total_row(dv)
        return carry

    loop(groups * blocks, step)


def block_forward(s, mats, vec, at, width, hidden, size, bias, group, groups):
    w_qkv, w_proj, w_up, w_down = mats
    pairs = width // 256
    scale = size ** (-0.5)
    norm_rows(s.x0, s.n1, vec, at["g1"], at["s1"], width)

    def qkv_step(j, carry):
        part = j // pairs
        row = row_at(vec, at["qv"], jnp.where(part == 0, j, jnp.maximum(j - pairs, 0)))
        value = dot(s.n1[...], w_qkv.cols(j)) + jnp.where(part == 1, 0.0, row)
        s.qkv[:, lanes(j)] = (value * jnp.where(part == 0, scale, 1.0)).astype(BF)
        return carry

    loop(3 * pairs, qkv_step)
    attention(s.qkv, s.probs, s.att, bias, group, groups, width, size)

    def proj_step(j, carry):
        s.x1[:, lanes(j)] = dot(s.att[...], w_proj.cols(j))
        return carry

    loop(pairs, proj_step)
    norm_rows(s.x0, s.n2, vec, at["g2"], at["s2"], width, s.x1, at["bo"])

    def mlp_step(j, carry):
        h = dot(s.n2[...], w_up.cols(j)) + row_at(vec, at["bu"], j)
        s.h[:, lanes(j)] = h
        u = gelu_parts(h)[0].astype(BF)
        update = dot(u, w_down.band(j))

        @pl.when(j == 0)
        def _():
            s.x2[...] = update

        @pl.when(j > 0)
        def _():
            s.x2[...] += update

        return carry

    loop(hidden // 256, mlp_step)


def block_backward(s, mats, grads, vec, dvec, at, width, hidden, size, group, groups):
    w_qkv, w_proj, w_up, w_down = mats
    d_qkv, d_proj, d_up, d_down = grads
    pairs = width // 256
    s.flip[...] = s.n2[...].T

    def mlp_step(j, carry):
        dxb = s.dxb[...]
        u, slope = gelu_parts(s.h[:, lanes(j)])
        dh = dot_t(dxb, w_down.band(j)) * slope
        put_row_at(dvec, at["bu"], j, total_row(fold(dh)))
        dh = dh.astype(BF)
        d_down.put_band(j, t_dot(u.astype(BF), dxb))
        d_up.put_cols(j, dot(s.flip[...], dh))
        update = dot_t(dh, w_up.cols(j))

        @pl.when(j == 0)
        def _():
            s.dn[...] = update

        @pl.when(j > 0)
        def _():
            s.dn[...] += update

        return carry

    loop(hidden // 256, mlp_step)
    norm_back_rows(s.x1, s.dn, s.dx, s.dxb, vec, dvec, at["g2"], at["s2"], width, at["bo"], True)

    def proj_step(j, carry):
        dxb = s.dxb[...]
        s.datt[:, lanes(j)] = dot_t(dxb, w_proj.band(j)).astype(BF)
        d_proj.put_band(j, t_dot(s.att[:, lanes(j)], dxb))
        return carry

    loop(pairs, proj_step)
    attention_back(s.qkv, s.probs, s.datt, s.dqkv, dvec, at["qv"], group, groups, width, size)
    s.flip[...] = s.n1[...].T

    def weight_step(j, carry):
        d_qkv.put_cols(j, dot(s.flip[...], s.dqkv[:, lanes(j)]))
        return carry

    loop(3 * pairs, weight_step)

    def input_step(j, carry):
        s.dn[:, lanes(j)] = dot_t(s.dqkv[...], w_qkv.band(j))
        return carry

    loop(pairs, input_step)
    norm_back_rows(s.x0, s.dn, s.dx, s.dxb, vec, dvec, at["g1"], at["s1"], width, None, True)


ENC_AT = dict(g1=EV[2], s1=EV[3], qv=EV[4], bo=EV[5], g2=EV[6], s2=EV[7], bu=EV[8])
DEC_AT = dict(g1=DV[3], s1=DV[4], qv=DV[5], bo=DV[6], g2=DV[7], s2=DV[8], bu=DV[9])


class Bag:
    def __init__(self, names, refs):
        for name, ref in zip(names, refs):
            setattr(self, name, ref)


def load_mats(source, kept, sem, copies):
    started = []
    for index, (pick, start, count) in enumerate(copies):
        copy = pltpu.make_async_copy(pick(source), kept.at[pl.ds(start, count)], sem.at[index])
        copy.start()
        started.append(copy)
    return started


def plain_copies(base, tiles):
    return [
        ((lambda ref, a=a, c=c: ref.at[pl.ds(a, c)]), a, c) for a, c in zip(base, tiles)
    ]


def visible_rows(column, count):
    lane = lax.broadcasted_iota(jnp.int32, (1, count), 1)
    return jnp.where(column == lane, 1.0, 0.0).astype(BF)


def encoder_bias(rows):
    r = lax.broadcasted_iota(jnp.int32, (rows, rows), 0)
    c = lax.broadcasted_iota(jnp.int32, (rows, rows), 1)
    same = (r // ROWS_E == c // ROWS_E) & (c % ROWS_E < VIS)
    return jnp.where(same, 0.0, -1e30)


ENC_KEEP = ["pick", "x0", "n1", "qkv", "probs", "att", "x1", "n2", "h", "x2"]


def enc_shapes(images):
    rows = images * ROWS_E
    return dict(
        pick=((rows, PIX), BF),
        x0=((rows, DE), F32),
        n1=((rows, DE), BF),
        qkv=((rows, 3 * DE), BF),
        probs=((HE, rows, rows), BF),
        att=((rows, DE), BF),
        x1=((rows, DE), F32),
        n2=((rows, DE), BF),
        h=((rows, FE), F32),
        x2=((rows, DE), F32),
    )


def position_column(vec, start, blocks, j):
    return vec[pl.ds(start + j, PATCHES, stride=blocks), :]


def encoder_forward_kernel(images, copies, vis, pix, vec, weights, *refs):
    latent = refs[0]
    s = Bag(ENC_KEEP, refs[1 : 1 + len(ENC_KEEP)])
    kept, posit, sem = refs[1 + len(ENC_KEEP) :]
    started = load_mats(weights, kept, sem, copies)
    rows = images * ROWS_E
    mats = [Mat(kept, b, shape) for b, shape in zip(ENC_BASE, ENC_MATS)]
    posit[...] = jnp.zeros_like(posit)
    for j in range(DE // 128):
        posit[0:PATCHES, j * 128 : (j + 1) * 128] = position_column(vec, EV[1], DE // 128, j)
    for i in range(images):
        where = pl.ds(i * ROWS_E, ROWS_E)
        hot = visible_rows(vis[where, :], ROWS_D)
        s.pick[where, :] = dot(hot, pix[i]).astype(BF)
        s.x0[where, :] = dot(hot, posit[...].astype(BF)) + row_of(vec, EV[0], DE)
    for copy in started:
        copy.wait()

    def embed_step(j, carry):
        s.x0[:, lanes(j)] += dot(s.pick[...], mats[0].cols(j))
        return carry

    loop(DE // 256, embed_step)
    block_forward(
        s, mats[1:5], vec, ENC_AT, DE, FE, DE // HE, encoder_bias(rows), rows, 1
    )
    norm_rows(s.x1, latent, vec, EV[10], EV[11], DE, s.x2, EV[9])


def encoder_forward(images, copies, vis, pix, vec, weights):
    shapes = enc_shapes(images)
    rows = images * ROWS_E
    vm = pl.BlockSpec(memory_space=pltpu.VMEM)
    return pl.pallas_call(
        functools.partial(encoder_forward_kernel, images, copies),
        out_shape=[jax.ShapeDtypeStruct((rows, DE), BF)]
        + [jax.ShapeDtypeStruct(*shapes[name]) for name in ENC_KEEP],
        in_specs=[vm, vm, vm, pl.BlockSpec(memory_space=pl.ANY)],
        out_specs=[vm] * (1 + len(ENC_KEEP)),
        scratch_shapes=[
            pltpu.VMEM((ENC_TOTAL, 16, 128), BF),
            pltpu.VMEM((ROWS_D, DE), F32),
            pltpu.SemaphoreType.DMA((len(copies),)),
        ],
        name="encoder_forward",
        compiler_params=pltpu.CompilerParams(vmem_limit_bytes=VMEM_LIMIT),
    )(vis, pix, vec, weights)


def store_mats(kept, out, sem, index, base, count):
    copy = pltpu.make_async_copy(
        kept.at[pl.ds(base, count)], out.at[pl.ds(base, count)], sem.at[index]
    )
    copy.start()
    return copy


def encoder_backward_kernel(images, copies, vis, vec, dlatent, *refs):
    s = Bag(ENC_KEEP, refs[: len(ENC_KEEP)])
    weights, dmats, dvec = refs[len(ENC_KEEP) : len(ENC_KEEP) + 3]
    kept, dkept, s.dx, s.dxb, s.dn, s.datt, s.dqkv, s.flip, sem, out_sem = refs[
        len(ENC_KEEP) + 3 :
    ]
    started = load_mats(weights, kept, sem, copies)
    rows = images * ROWS_E
    mats = [Mat(kept, b, shape) for b, shape in zip(ENC_BASE, ENC_MATS)]
    grads = [Mat(dkept, b, shape) for b, shape in zip(ENC_BASE, ENC_MATS)]
    dvec[EV[11] + DE // 128 :, :] = jnp.zeros_like(dvec[EV[11] + DE // 128 :, :])
    norm_back_rows(
        s.x2, dlatent, s.dx, s.dxb, vec, dvec, EV[10], EV[11], DE, EV[9], False
    )
    for copy in started:
        copy.wait()
    block_backward(
        s, mats[1:5], grads[1:5], vec, dvec, ENC_AT, DE, FE, DE // HE, rows, 1
    )
    put_row(dvec, EV[0], jnp.sum(s.dx[...], 0, keepdims=True))

    def embed_step(j, carry):
        grads[0].put_band(j, t_dot(s.pick[:, lanes(j)], s.dxb[...]))
        return carry

    loop(DE // 256, embed_step)
    out = store_mats(dkept, dmats, out_sem, 0, 0, ENC_TOTAL)
    hot = visible_rows(vis[...], ROWS_D)
    for j in range(DE // 128):
        value = t_dot(hot, s.dxb[:, j * 128 : (j + 1) * 128])
        dvec[pl.ds(EV[1] + j, PATCHES, stride=DE // 128), :] = value[0:PATCHES]
    out.wait()


def encoder_backward(images, copies, vis, vec, dlatent, saved, weights):
    rows = images * ROWS_E
    vm = pl.BlockSpec(memory_space=pltpu.VMEM)
    hbm = pl.BlockSpec(memory_space=pl.ANY)
    return pl.pallas_call(
        functools.partial(encoder_backward_kernel, images, copies),
        out_shape=[
            jax.ShapeDtypeStruct((ENC_TOTAL, 16, 128), BF),
            jax.ShapeDtypeStruct(vec.shape, F32),
        ],
        in_specs=[vm] * (3 + len(ENC_KEEP)) + [hbm],
        out_specs=[hbm, vm],
        scratch_shapes=[
            pltpu.VMEM((ENC_TOTAL, 16, 128), BF),
            pltpu.VMEM((ENC_TOTAL, 16, 128), BF),
            pltpu.VMEM((rows, DE), F32),
            pltpu.VMEM((rows, DE), BF),
            pltpu.VMEM((rows, DE), F32),
            pltpu.VMEM((rows, DE), BF),
            pltpu.VMEM((rows, 3 * DE), BF),
            pltpu.VMEM((DE, rows), BF),
            pltpu.SemaphoreType.DMA((len(copies),)),
            pltpu.SemaphoreType.DMA((1,)),
        ],
        name="encoder_backward",
        compiler_params=pltpu.CompilerParams(vmem_limit_bytes=VMEM_LIMIT),
    )(vis, vec, dlatent, *saved, weights)


def decoder_kernel(images, copies, masked_total, latent, places, pix, vec, weights, *refs):
    dlatent, loss, dmats, dvec = refs[:4]
    s = Bag(
        ["x0", "x1", "x2", "n1", "n2", "qkv", "probs", "att", "h", "dx", "dxb", "dn", "dqkv", "flip"],
        refs[4:18],
    )
    kept, dkept, posit, dguess, sem, out_sem = refs[18:]
    s.datt = s.n2
    rows = images * ROWS_D
    mats = [Mat(kept, b, shape) for b, shape in zip(DEC_BASE, DEC_MATS)]
    grads = [Mat(dkept, b, shape) for b, shape in zip(DEC_BASE, DEC_MATS)]
    started = load_mats(weights, kept, sem, copies)
    posit[...] = jnp.zeros_like(posit)
    for j in range(DD // 128):
        posit[0:PATCHES, j * 128 : (j + 1) * 128] = position_column(vec, DV[2], DD // 128, j)
    dvec[DV[13] + PIX // 128 :, :] = jnp.zeros_like(dvec[DV[13] + PIX // 128 :, :])
    for copy in started:
        copy.wait()
    for i in range(images):
        part = pl.ds(i * ROWS_E, ROWS_E)
        where = pl.ds(i * ROWS_D, ROWS_D)
        for j in range(DD // 256):
            cut = slice(j * 256, (j + 1) * 256)
            z = dot(latent[part, :], mats[0].cols(j)) + row_of(vec, DV[0] + 2 * j, 256)
            place = places[where, :]
            hot = visible_rows(jnp.where(place < VIS, place, -1), ROWS_E)
            high = z.astype(BF)
            low = (z - high.astype(F32)).astype(BF)
            token = jnp.where(place >= VIS, 1.0, 0.0) * row_of(vec, DV[1] + 2 * j, 256)
            s.x0[where, cut] = dot(hot, high) + dot(hot, low) + token + posit[:, cut]
    lane = lax.broadcasted_iota(jnp.int32, (1, ROWS_D), 1)
    bias = jnp.where(lane < PATCHES, 0.0, -1e30)
    block_forward(
        s, mats[1:5], vec, DEC_AT, DD, FD, DD // HD, bias, ROWS_D, images
    )
    norm_rows(s.x1, s.dxb, vec, DV[11], DV[12], DD, s.x2, DV[10])
    factor = 2.0 / (PIX * masked_total)

    def head_step(j, total):
        value = dot(s.dxb[...], mats[5].cols(j)) + row_at(vec, DV[13], j)
        count = jnp.zeros((8, 256), F32)
        column = jnp.zeros((8, 256), F32)
        for i in range(images):
            where = slice(i * ROWS_D, (i + 1) * ROWS_D)
            error = value[where] - pix[i, :, lanes(j)].astype(F32)
            error = jnp.where(places[where, :] >= VIS, error, 0.0)
            count = count + fold(error * error)
            error = error * factor
            column = column + fold(error)
            dguess[where, lanes(j)] = error.astype(BF)
        put_row_at(dvec, DV[13], j, total_row(column))
        return total + count

    total = loop(PIX // 256, head_step, jnp.zeros((8, 256), F32))
    loss[...] = jnp.broadcast_to(jnp.sum(total) * (1.0 / PIX), (8, 128))
    s.flip[...] = s.dxb[...].T

    def head_weight_step(j, carry):
        grads[5].put_cols(j, dot(s.flip[...], dguess[:, lanes(j)]))
        return carry

    loop(PIX // 256, head_weight_step)

    def head_input_step(j, carry):
        s.dn[:, lanes(j)] = dot_t(dguess[...], mats[5].band(j))
        return carry

    loop(DD // 256, head_input_step)
    norm_back_rows(s.x2, s.dn, s.dx, s.dxb, vec, dvec, DV[11], DV[12], DD, DV[10], False)
    block_backward(
        s, mats[1:5], grads[1:5], vec, dvec, DEC_AT, DD, FD, DD // HD, ROWS_D, images
    )
    token = jnp.zeros((8, DD), F32)
    spot = jnp.zeros((ROWS_D, DD), F32)
    back = []
    for i in range(images):
        where = pl.ds(i * ROWS_D, ROWS_D)
        place = places[where, :]
        dx = s.dx[where, :]
        spot = spot + dx
        token = token + fold(jnp.where(place >= VIS, dx, 0.0))
        hot = visible_rows(jnp.where(place < VIS, place, -1), ROWS_E)
        back.append(t_dot(hot, s.dxb[where, :]))
    posit[...] = spot
    for j in range(DD // 128):
        dvec[pl.ds(DV[2] + j, PATCHES, stride=DD // 128), :] = posit[
            0:PATCHES, j * 128 : (j + 1) * 128
        ]
    put_row(dvec, DV[1], total_row(token))
    back = jnp.concatenate(back, 0)
    put_row(dvec, DV[0], jnp.sum(back, 0, keepdims=True))
    back = back.astype(BF)
    for j in range(DE // 256):
        grads[0].put_band(j, t_dot(latent[:, j * 256 : (j + 1) * 256], back))
        dlatent[:, j * 256 : (j + 1) * 256] = dot_t(back, mats[0].band(j)).astype(BF)
    out = store_mats(dkept, dmats, out_sem, 0, 0, DEC_TOTAL)
    out.wait()


def decoder_step(images, copies, masked_total, latent, places, pix, vec, weights):
    rows = images * ROWS_D
    vm = pl.BlockSpec(memory_space=pltpu.VMEM)
    hbm = pl.BlockSpec(memory_space=pl.ANY)
    probs = images * HD
    return pl.pallas_call(
        functools.partial(decoder_kernel, images, copies, masked_total),
        out_shape=[
            jax.ShapeDtypeStruct((images * ROWS_E, DE), BF),
            jax.ShapeDtypeStruct((8, 128), F32),
            jax.ShapeDtypeStruct((DEC_TOTAL, 16, 128), BF),
            jax.ShapeDtypeStruct(vec.shape, F32),
        ],
        in_specs=[vm, vm, vm, vm, hbm],
        out_specs=[vm, vm, hbm, vm],
        scratch_shapes=[
            pltpu.VMEM((rows, DD), F32),
            pltpu.VMEM((rows, DD), F32),
            pltpu.VMEM((rows, DD), F32),
            pltpu.VMEM((rows, DD), BF),
            pltpu.VMEM((rows, DD), BF),
            pltpu.VMEM((rows, 3 * DD), BF),
            pltpu.VMEM((probs, ROWS_D, ROWS_D), BF),
            pltpu.VMEM((rows, DD), BF),
            pltpu.VMEM((rows, FD), F32),
            pltpu.VMEM((rows, DD), F32),
            pltpu.VMEM((rows, DD), BF),
            pltpu.VMEM((rows, DD), F32),
            pltpu.VMEM((rows, 3 * DD), BF),
            pltpu.VMEM((DD, rows), BF),
            pltpu.VMEM((DEC_TOTAL, 16, 128), BF),
            pltpu.VMEM((DEC_TOTAL, 16, 128), BF),
            pltpu.VMEM((ROWS_D, DD), F32),
            pltpu.VMEM((rows, PIX), BF),
            pltpu.SemaphoreType.DMA((len(copies),)),
            pltpu.SemaphoreType.DMA((1,)),
        ],
        name="decoder_step",
        compiler_params=pltpu.CompilerParams(vmem_limit_bytes=VMEM_LIMIT),
    )(latent, places, pix, vec, weights)


def natural(flat, shapes):
    pieces, offset = [], 0
    for rows, columns in shapes:
        piece = flat[offset : offset + rows * columns].reshape(rows // 16, 16, columns // 128, 128)
        pieces.append(piece.transpose(0, 2, 1, 3).reshape(-1, 16, 128))
        offset += rows * columns
    return jnp.concatenate(pieces, 0)


def flat_from_natural(tiles, shapes, total):
    pieces, offset = [], 0
    for rows, columns in shapes:
        count = rows * columns // 2048
        piece = tiles[offset : offset + count].reshape(rows // 16, columns // 128, 16, 128)
        pieces.append(piece.transpose(0, 2, 1, 3).reshape(-1))
        offset += count
    flat = jnp.concatenate(pieces)
    return jnp.pad(flat, (0, total - flat.shape[0]))


def shifted(value, axis, steps):
    count = lax.axis_size(axis)
    initial, last = (max(0, -steps), min(count, count - steps))
    return lax.ppermute(value, axis, [(source, source + steps) for source in range(initial, last)])


def adam_update(master, first, second, grad, rate, decay):
    first = 0.9 * first + 0.1 * grad
    second = 0.95 * second + 0.05 * grad * grad
    step_first = first / (1.0 - 0.9**STEP)
    step_second = second / (1.0 - 0.95**STEP)
    master = master - rate * (step_first / (jnp.sqrt(step_second) + 1e-08) + decay * master)
    return (master, first, second)


def body(
    pixels, visible, restore, mat_master, mat_first, mat_second, vec_master, vec_first, vec_second
):
    images = pixels.shape[0]
    total = mat_master.shape[1] * lax.axis_size("dp")
    masked_total = (PATCHES - VIS) * images * lax.axis_size("dp")
    encoding = lax.axis_index("section") == 0
    enc_copies = plain_copies(ENC_BASE, ENC_TILES)
    dec_copies = plain_copies(DEC_BASE, DEC_TILES)
    mats = lax.all_gather(mat_master.astype(BF), "dp", axis=1, tiled=True)[0]
    vecs = lax.all_gather(vec_master.astype(BF), "dp", axis=1, tiled=True)[0]
    vecs = vecs.astype(F32).reshape(-1, 128)
    pix = jnp.pad(pixels, ((0, 0), (0, ROWS_D - PATCHES), (0, 0)))
    vis = jnp.pad(visible, ((0, 0), (0, ROWS_E - VIS)), constant_values=-1).reshape(-1, 1)
    places = jnp.pad(restore, ((0, 0), (0, ROWS_D - PATCHES)), constant_values=-1).reshape(-1, 1)
    weights = lax.cond(
        encoding,
        lambda m: natural(m, ENC_MATS),
        lambda m: jnp.pad(natural(m, DEC_MATS), ((0, ENC_TOTAL - DEC_TOTAL), (0, 0), (0, 0))),
        mats,
    )
    blank_saved = [jnp.zeros(*item) for item in enc_shapes(images).values()]
    blank_latent = jnp.zeros((images * ROWS_E, DE), BF)
    latent, saved = lax.cond(
        encoding,
        lambda: (lambda out: (out[0], list(out[1:])))(
            encoder_forward(images, enc_copies, vis, pix, vecs, weights)
        ),
        lambda: (blank_latent, blank_saved),
    )
    arrived = shifted(latent, "section", 1)
    dlatent, loss, dmat_dec, dvec_dec = lax.cond(
        encoding,
        lambda: [
            blank_latent,
            jnp.zeros((8, 128), F32),
            jnp.zeros((DEC_TOTAL, 16, 128), BF),
            jnp.zeros(vecs.shape, F32),
        ],
        lambda: list(
            decoder_step(images, dec_copies, masked_total, arrived, places, pix, vecs, weights)
        ),
    )
    returned = shifted(dlatent, "section", -1)

    def encoder_side():
        dmats, dvec = encoder_backward(images, enc_copies, vis, vecs, returned, saved, weights)
        return flat_from_natural(dmats.astype(F32), ENC_MATS, total), dvec

    grad_mats, grad_vecs = lax.cond(
        encoding,
        encoder_side,
        lambda: (flat_from_natural(dmat_dec.astype(F32), DEC_MATS, total), dvec_dec),
    )
    summed_mats = lax.psum_scatter(grad_mats[None], "dp", scatter_dimension=1, tiled=True)
    summed_vecs = lax.psum_scatter(
        grad_vecs.reshape(1, -1), "dp", scatter_dimension=1, tiled=True
    )
    square = jnp.sum(summed_mats * summed_mats) + jnp.sum(summed_vecs * summed_vecs)
    square_all, loss_sum = lax.psum((square, loss[0, 0]), ("section", "dp"))
    grad_norm = jnp.sqrt(square_all)
    factor = jnp.minimum(1.0, 0.001 / (grad_norm + 1e-06))
    mat_new, mat_first_new, mat_second_new = adam_update(
        mat_master, mat_first, mat_second, factor * summed_mats, 0.05, 0.05
    )
    vec_new, vec_first_new, vec_second_new = adam_update(
        vec_master, vec_first, vec_second, factor * summed_vecs, 0.3, 0.0
    )
    return (
        loss_sum,
        grad_norm,
        mat_new,
        mat_first_new,
        mat_second_new,
        mat_new.astype(BF),
        vec_new,
        vec_first_new,
        vec_second_new,
        vec_new.astype(BF),
    )


def solution(mesh):
    split = P("section", "dp")
    return jax.shard_map(
        body,
        mesh=mesh,
        in_specs=(P("dp", None, None), P("dp", None), P("dp", None)) + (split,) * 6,
        out_specs=(P(), P()) + (split,) * 8,
        check_vma=False,
    )
```

```python
import functools
import math

import jax
import jax.numpy as jnp
from jax import lax
from jax.experimental import pallas as pl
from jax.experimental.pallas import tpu as pltpu
from jax.sharding import PartitionSpec as P

PIX = 768
DE = 768
HE = 12
FE = 3072
DD = 512
HD = 16
FD = 2048
PATCHES = 196
VIS = 49
STEP = 10
ROWS_E = 64
ROWS_D = 208
EPS = 1e-6
BF = jnp.bfloat16
F32 = jnp.float32
VMEM_LIMIT = 63 * 1024 * 1024

ENC_MATS = [(PIX, DE), (DE, 3 * DE), (DE, DE), (DE, FE), (FE, DE)]
DEC_MATS = [(DE, DD), (DD, 3 * DD), (DD, DD), (DD, FD), (FD, DD), (DD, PIX)]
ENC_VECS = [DE, PATCHES * DE, DE, DE, 2 * DE, DE, DE, DE, FE, DE, DE, DE]
DEC_VECS = [DD, DD, PATCHES * DD, DD, DD, 2 * DD, DD, DD, DD, FD, DD, DD, DD, PIX]


def starts(sizes):
    total, found = 0, []
    for size in sizes:
        found.append(total)
        total += size
    return found, total


ENC_TILES = [k * n // 2048 for k, n in ENC_MATS]
DEC_TILES = [k * n // 2048 for k, n in DEC_MATS]
ENC_BASE, ENC_TOTAL = starts(ENC_TILES)
DEC_BASE, DEC_TOTAL = starts(DEC_TILES)
EV, _ = starts([size // 128 for size in ENC_VECS])
DV, _ = starts([size // 128 for size in DEC_VECS])


class Mat:
    def __init__(self, ref, base, shape):
        self.rows, self.columns = shape
        self.blocks = self.columns // 128
        count = self.rows * self.columns // 2048
        self.ref = ref.at[pl.ds(base, count)].reshape(self.rows // 16, self.blocks, 16, 128)

    def cols(self, block):
        parts = [self.ref[:, 2 * block + half].reshape(self.rows, 128) for half in range(2)]
        return jnp.concatenate(parts, 1)

    def band(self, block):
        part = self.ref.at[pl.ds(block * 16, 16)]
        return jnp.concatenate([part[:, j].reshape(256, 128) for j in range(self.blocks)], 1)

    def put_cols(self, block, value):
        for half in range(2):
            piece = value[:, half * 128 : (half + 1) * 128].astype(BF)
            self.ref[:, 2 * block + half] = piece.reshape(self.rows // 16, 16, 128)

    def put_band(self, block, value):
        part = self.ref.at[pl.ds(block * 16, 16)]
        for j in range(self.blocks):
            part[:, j] = value[:, j * 128 : (j + 1) * 128].astype(BF).reshape(16, 16, 128)


def dot(a, b):
    return jnp.dot(a, b, preferred_element_type=F32)


def dot_t(a, b):
    return lax.dot_general(a, b, (((1,), (1,)), ((), ())), preferred_element_type=F32)


def t_dot(a, b):
    return lax.dot_general(a, b, (((0,), (0,)), ((), ())), preferred_element_type=F32)


def loop(count, body, init=0):
    return lax.fori_loop(0, count, body, init)


def lanes(block, width=256):
    return pl.ds(pl.multiple_of(block * width, width), width)


def row_of(vec, start, width):
    return jnp.concatenate([vec[start + j : start + j + 1, :] for j in range(width // 128)], 1)


def row_at(vec, start, block):
    return jnp.concatenate([vec[pl.ds(start + 2 * block + h, 1), :] for h in range(2)], 1)


def put_row(dvec, start, value):
    for j in range(value.shape[1] // 128):
        dvec[start + j : start + j + 1, :] = value[:, j * 128 : (j + 1) * 128]


def put_row_at(dvec, start, block, value):
    for h in range(2):
        dvec[pl.ds(start + 2 * block + h, 1), :] = value[:, h * 128 : (h + 1) * 128]


def fold(value):
    return value.reshape(value.shape[0] // 8, 8, value.shape[1]).sum(0)


def total_row(value):
    return jnp.sum(value, 0, keepdims=True)


def norm_parts(x):
    mean = jnp.mean(x, -1, keepdims=True)
    centred = x - mean
    scale = lax.rsqrt(jnp.mean(centred * centred, -1, keepdims=True) + EPS)
    return centred * scale, scale


CHUNK = 32


def chunk_rows(i):
    return pl.ds(pl.multiple_of(i * CHUNK, CHUNK), CHUNK)


def norm_rows(x_ref, out_ref, vec, gain_at, shift_at, width, add_ref=None, bias_at=None):
    gain, shift = row_of(vec, gain_at, width), row_of(vec, shift_at, width)
    bias = None if bias_at is None else row_of(vec, bias_at, width)

    def step(i, carry):
        rows = chunk_rows(i)
        x = x_ref[rows, :]
        if add_ref is not None:
            x = x + add_ref[rows, :] + bias
            add_ref[rows, :] = x
        unit, _ = norm_parts(x)
        out_ref[rows, :] = (unit * gain + shift).astype(BF)
        return carry

    loop(x_ref.shape[0] // CHUNK, step)


def norm_back_rows(x_ref, dy_ref, dx_ref, dxb_ref, vec, dvec, gain_at, shift_at, width, bias_at, add):
    gain = row_of(vec, gain_at, width)
    zero = jnp.zeros((8, width), F32)

    def step(i, carry):
        dgain, dshift, dbias = carry
        rows = chunk_rows(i)
        unit, scale = norm_parts(x_ref[rows, :])
        dy = dy_ref[rows, :].astype(F32)
        dunit = dy * gain
        dx = scale * (
            dunit
            - jnp.mean(dunit, -1, keepdims=True)
            - unit * jnp.mean(dunit * unit, -1, keepdims=True)
        )
        if add:
            dx = dx + dx_ref[rows, :]
        dx_ref[rows, :] = dx
        dxb_ref[rows, :] = dx.astype(BF)
        return dgain + fold(dy * unit), dshift + fold(dy), dbias + fold(dx)

    dgain, dshift, dbias = loop(x_ref.shape[0] // CHUNK, step, (zero, zero, zero))
    put_row(dvec, gain_at, total_row(dgain))
    put_row(dvec, shift_at, total_row(dshift))
    if bias_at is not None:
        put_row(dvec, bias_at, total_row(dbias))
    return dbias


GELU_C = math.sqrt(2.0 / math.pi)


def gelu_parts(x):
    square = x * x
    t = jnp.tanh(x * (GELU_C + (GELU_C * 0.044715) * square))
    half = 0.5 * (1.0 + t)
    return x * half, half + (0.5 * x) * (1.0 - t * t) * (
        GELU_C + (3.0 * 0.044715 * GELU_C) * square
    )


def head_mask(size):
    lane = lax.broadcasted_iota(jnp.int32, (1, 128), 1)
    return [(lane >= h * size) & (lane < (h + 1) * size) for h in range(128 // size)]


def attention(qkv, probs, att, bias, group, groups, width, size):
    blocks = width // 128
    masks = head_mask(size)

    def step(i, carry):
        g, b = i // blocks, i % blocks
        rows = pl.ds(pl.multiple_of(g * group, 16), group)
        q = qkv[rows, lanes(b, 128)]
        k = qkv[rows, lanes(blocks + b, 128)]
        v = qkv[rows, lanes(2 * blocks + b, 128)]
        out = jnp.zeros((group, 128), F32)
        for h, mask in enumerate(masks):
            s = dot_t(jnp.where(mask, q, jnp.zeros_like(q)), k) + bias
            e = jnp.exp(s - jnp.max(s, -1, keepdims=True))
            p = (e * (1.0 / jnp.sum(e, -1, keepdims=True))).astype(BF)
            probs[i * len(masks) + h] = p
            out = jnp.where(mask, dot(p, v), out)
        att[rows, lanes(b, 128)] = out.astype(BF)
        return carry

    loop(groups * blocks, step)


def attention_back(qkv, probs, datt, dqkv, dvec, qv_at, group, groups, width, size):
    blocks = width // 128
    masks = head_mask(size)
    scale = size ** (-0.5)
    for j in range(2 * blocks):
        dvec[qv_at + j : qv_at + j + 1, :] = jnp.zeros((1, 128), F32)

    def step(i, carry):
        g, b = i // blocks, i % blocks
        rows = pl.ds(pl.multiple_of(g * group, 16), group)
        q = qkv[rows, lanes(b, 128)]
        k = qkv[rows, lanes(blocks + b, 128)]
        v = qkv[rows, lanes(2 * blocks + b, 128)]
        da = datt[rows, lanes(b, 128)]
        zero = jnp.zeros((group, 128), F32)
        dq, dk, dv = zero, zero, zero
        for h, mask in enumerate(masks):
            p = probs[i * len(masks) + h]
            dp = dot_t(jnp.where(mask, da, jnp.zeros_like(da)), v)
            wide = p.astype(F32)
            prod = wide * dp
            ds = (prod - wide * jnp.sum(prod, -1, keepdims=True)).astype(BF)
            dq = jnp.where(mask, dot(ds, k), dq)
            dk = jnp.where(mask, t_dot(ds, q), dk)
            dv = jnp.where(mask, t_dot(p, da), dv)
        dq = dq * scale
        dqkv[rows, lanes(b, 128)] = dq.astype(BF)
        dqkv[rows, lanes(blocks + b, 128)] = dk.astype(BF)
        dqkv[rows, lanes(2 * blocks + b, 128)] = dv.astype(BF)
        dvec[pl.ds(qv_at + b, 1), :] += total_row(dq)
        dvec[pl.ds(qv_at + blocks + b, 1), :] += total_row(dv)
        return carry

    loop(groups * blocks, step)


def block_forward(s, mats, vec, at, width, hidden, size, bias, group, groups):
    w_qkv, w_proj, w_up, w_down = mats
    pairs = width // 256
    scale = size ** (-0.5)
    norm_rows(s.x0, s.n1, vec, at["g1"], at["s1"], width)

    def qkv_step(j, carry):
        part = j // pairs
        row = row_at(vec, at["qv"], jnp.where(part == 0, j, jnp.maximum(j - pairs, 0)))
        value = dot(s.n1[...], w_qkv.cols(j)) + jnp.where(part == 1, 0.0, row)
        s.qkv[:, lanes(j)] = (value * jnp.where(part == 0, scale, 1.0)).astype(BF)
        return carry

    loop(3 * pairs, qkv_step)
    attention(s.qkv, s.probs, s.att, bias, group, groups, width, size)

    def proj_step(j, carry):
        s.x1[:, lanes(j)] = dot(s.att[...], w_proj.cols(j))
        return carry

    loop(pairs, proj_step)
    norm_rows(s.x0, s.n2, vec, at["g2"], at["s2"], width, s.x1, at["bo"])

    def mlp_step(j, carry):
        h = dot(s.n2[...], w_up.cols(j)) + row_at(vec, at["bu"], j)
        s.h[:, lanes(j)] = h
        u = gelu_parts(h)[0].astype(BF)
        update = dot(u, w_down.band(j))

        @pl.when(j == 0)
        def _():
            s.x2[...] = update

        @pl.when(j > 0)
        def _():
            s.x2[...] += update

        return carry

    loop(hidden // 256, mlp_step)


def block_backward(s, mats, grads, vec, dvec, at, width, hidden, size, group, groups):
    w_qkv, w_proj, w_up, w_down = mats
    d_qkv, d_proj, d_up, d_down = grads
    pairs = width // 256
    s.flip[...] = s.n2[...].T

    def mlp_step(j, carry):
        dxb = s.dxb[...]
        u, slope = gelu_parts(s.h[:, lanes(j)])
        dh = dot_t(dxb, w_down.band(j)) * slope
        put_row_at(dvec, at["bu"], j, total_row(fold(dh)))
        dh = dh.astype(BF)
        d_down.put_band(j, t_dot(u.astype(BF), dxb))
        d_up.put_cols(j, dot(s.flip[...], dh))
        update = dot_t(dh, w_up.cols(j))

        @pl.when(j == 0)
        def _():
            s.dn[...] = update

        @pl.when(j > 0)
        def _():
            s.dn[...] += update

        return carry

    loop(hidden // 256, mlp_step)
    norm_back_rows(s.x1, s.dn, s.dx, s.dxb, vec, dvec, at["g2"], at["s2"], width, at["bo"], True)

    def proj_step(j, carry):
        dxb = s.dxb[...]
        s.datt[:, lanes(j)] = dot_t(dxb, w_proj.band(j)).astype(BF)
        d_proj.put_band(j, t_dot(s.att[:, lanes(j)], dxb))
        return carry

    loop(pairs, proj_step)
    attention_back(s.qkv, s.probs, s.datt, s.dqkv, dvec, at["qv"], group, groups, width, size)
    s.flip[...] = s.n1[...].T

    def weight_step(j, carry):
        d_qkv.put_cols(j, dot(s.flip[...], s.dqkv[:, lanes(j)]))
        return carry

    loop(3 * pairs, weight_step)

    def input_step(j, carry):
        s.dn[:, lanes(j)] = dot_t(s.dqkv[...], w_qkv.band(j))
        return carry

    loop(pairs, input_step)
    norm_back_rows(s.x0, s.dn, s.dx, s.dxb, vec, dvec, at["g1"], at["s1"], width, None, True)


ENC_AT = dict(g1=EV[2], s1=EV[3], qv=EV[4], bo=EV[5], g2=EV[6], s2=EV[7], bu=EV[8])
DEC_AT = dict(g1=DV[3], s1=DV[4], qv=DV[5], bo=DV[6], g2=DV[7], s2=DV[8], bu=DV[9])


class Bag:
    def __init__(self, names, refs):
        for name, ref in zip(names, refs):
            setattr(self, name, ref)


class Layout:
    def __init__(self, shape, moves, shared):
        self.shape, self.moves, self.shared = shape, moves, shared


def plain_layout(total):
    return Layout((total, 16, 128), [(lambda ref: ref, 0, total)], [])


def slot_layout(plan, shape):
    moves, shared, done = [], [], 0
    for device, (first, count, _) in enumerate(plan):
        skip = max(0, done - first)
        if skip and count:
            shared.append((lambda ref, d=device, n=skip: ref.at[d, pl.ds(0, n)], first, skip))
        if count:
            moves.append(
                (
                    lambda ref, d=device, a=skip, n=count - skip: ref.at[d, pl.ds(a, n)],
                    first + skip,
                    count - skip,
                )
            )
        done = first + count
    return Layout(shape, moves, shared)


def whole_slots(plan, shape):
    moves = [
        (lambda ref, d=device, n=count: ref.at[d, pl.ds(0, n)], first, count)
        for device, (first, count, _) in enumerate(plan)
        if count
    ]
    return Layout(shape, moves, [])


SHARED = 24


def load_mats(source, kept, side, sem, layout):
    started = []
    for index, (pick, start, count) in enumerate(layout.moves):
        copy = pltpu.make_async_copy(pick(source), kept.at[pl.ds(start, count)], sem.at[index])
        copy.start()
        started.append(copy)
    for index, (pick, start, count) in enumerate(layout.shared):
        copy = pltpu.make_async_copy(
            pick(source),
            side.at[index, pl.ds(0, count)],
            sem.at[len(layout.moves) + index],
        )
        copy.start()
        started.append(copy)
    return started


def finish_mats(started, kept, side, layout):
    for copy in started:
        copy.wait()
    for index, (_, start, count) in enumerate(layout.shared):
        there = pl.ds(start, count)
        both = kept[there].astype(F32) + side[index, 0:count].astype(F32)
        kept[there] = both.astype(BF)


def load_scratch(layout):
    return [
        pltpu.VMEM((max(1, len(layout.shared)), SHARED, 16, 128), BF),
        pltpu.SemaphoreType.DMA((len(layout.moves) + len(layout.shared),)),
    ]


def visible_rows(column, count):
    lane = lax.broadcasted_iota(jnp.int32, (1, count), 1)
    return jnp.where(column == lane, 1.0, 0.0).astype(BF)


def encoder_bias(rows):
    r = lax.broadcasted_iota(jnp.int32, (rows, rows), 0)
    c = lax.broadcasted_iota(jnp.int32, (rows, rows), 1)
    same = (r // ROWS_E == c // ROWS_E) & (c % ROWS_E < VIS)
    return jnp.where(same, 0.0, -1e30)


ENC_KEEP = ["pick", "x0", "n1", "qkv", "probs", "att", "x1", "n2", "h", "x2"]


def enc_shapes(images):
    rows = images * ROWS_E
    return dict(
        pick=((rows, PIX), BF),
        x0=((rows, DE), F32),
        n1=((rows, DE), BF),
        qkv=((rows, 3 * DE), BF),
        probs=((HE, rows, rows), BF),
        att=((rows, DE), BF),
        x1=((rows, DE), F32),
        n2=((rows, DE), BF),
        h=((rows, FE), F32),
        x2=((rows, DE), F32),
    )


def position_column(vec, start, blocks, j):
    return vec[pl.ds(start + j, PATCHES, stride=blocks), :]


def encoder_forward_kernel(images, layout, vis, pix, vec, weights, *refs):
    latent = refs[0]
    s = Bag(ENC_KEEP, refs[1 : 1 + len(ENC_KEEP)])
    kept, posit, side, sem = refs[1 + len(ENC_KEEP) :]
    started = load_mats(weights, kept, side, sem, layout)
    rows = images * ROWS_E
    mats = [Mat(kept, b, shape) for b, shape in zip(ENC_BASE, ENC_MATS)]
    posit[...] = jnp.zeros_like(posit)
    for j in range(DE // 128):
        posit[0:PATCHES, j * 128 : (j + 1) * 128] = position_column(vec, EV[1], DE // 128, j)
    for i in range(images):
        where = pl.ds(i * ROWS_E, ROWS_E)
        hot = visible_rows(vis[where, :], ROWS_D)
        s.pick[where, :] = dot(hot, pix[i]).astype(BF)
        s.x0[where, :] = dot(hot, posit[...].astype(BF)) + row_of(vec, EV[0], DE)
    finish_mats(started, kept, side, layout)

    def embed_step(j, carry):
        s.x0[:, lanes(j)] += dot(s.pick[...], mats[0].cols(j))
        return carry

    loop(DE // 256, embed_step)
    block_forward(
        s, mats[1:5], vec, ENC_AT, DE, FE, DE // HE, encoder_bias(rows), rows, 1
    )
    norm_rows(s.x1, latent, vec, EV[10], EV[11], DE, s.x2, EV[9])


def encoder_forward(images, layout, vis, pix, vec, weights):
    shapes = enc_shapes(images)
    rows = images * ROWS_E
    vm = pl.BlockSpec(memory_space=pltpu.VMEM)
    return pl.pallas_call(
        functools.partial(encoder_forward_kernel, images, layout),
        out_shape=[jax.ShapeDtypeStruct((rows, DE), BF)]
        + [jax.ShapeDtypeStruct(*shapes[name]) for name in ENC_KEEP],
        in_specs=[vm, vm, vm, pl.BlockSpec(memory_space=pl.ANY)],
        out_specs=[vm] * (1 + len(ENC_KEEP)),
        scratch_shapes=[
            pltpu.VMEM((ENC_TOTAL, 16, 128), BF),
            pltpu.VMEM((ROWS_D, DE), F32),
        ]
        + load_scratch(layout),
        name="encoder_forward",
        compiler_params=pltpu.CompilerParams(vmem_limit_bytes=VMEM_LIMIT),
    )(vis, pix, vec, weights)


def store_mats(kept, out, sem, layout):
    started = []
    for index, (pick, start, count) in enumerate(layout.moves):
        copy = pltpu.make_async_copy(kept.at[pl.ds(start, count)], pick(out), sem.at[index])
        copy.start()
        started.append(copy)
    return started


def encoder_backward_kernel(images, layout, out_layout, vis, vec, dlatent, *refs):
    s = Bag(ENC_KEEP, refs[: len(ENC_KEEP)])
    weights, dmats, dvec = refs[len(ENC_KEEP) : len(ENC_KEEP) + 3]
    kept, dkept, s.dx, s.dxb, s.dn, s.datt, s.dqkv, s.flip, out_sem, side, sem = refs[
        len(ENC_KEEP) + 3 :
    ]
    started = load_mats(weights, kept, side, sem, layout)
    rows = images * ROWS_E
    mats = [Mat(kept, b, shape) for b, shape in zip(ENC_BASE, ENC_MATS)]
    grads = [Mat(dkept, b, shape) for b, shape in zip(ENC_BASE, ENC_MATS)]
    dvec[EV[11] + DE // 128 :, :] = jnp.zeros_like(dvec[EV[11] + DE // 128 :, :])
    norm_back_rows(
        s.x2, dlatent, s.dx, s.dxb, vec, dvec, EV[10], EV[11], DE, EV[9], False
    )
    finish_mats(started, kept, side, layout)
    block_backward(
        s, mats[1:5], grads[1:5], vec, dvec, ENC_AT, DE, FE, DE // HE, rows, 1
    )
    put_row(dvec, EV[0], jnp.sum(s.dx[...], 0, keepdims=True))

    def embed_step(j, carry):
        grads[0].put_band(j, t_dot(s.pick[:, lanes(j)], s.dxb[...]))
        return carry

    loop(DE // 256, embed_step)
    stores = store_mats(dkept, dmats, out_sem, out_layout)
    hot = visible_rows(vis[...], ROWS_D)
    for j in range(DE // 128):
        value = t_dot(hot, s.dxb[:, j * 128 : (j + 1) * 128])
        dvec[pl.ds(EV[1] + j, PATCHES, stride=DE // 128), :] = value[0:PATCHES]
    for copy in stores:
        copy.wait()


def encoder_backward(images, layout, out_layout, vis, vec, dlatent, saved, weights):
    rows = images * ROWS_E
    vm = pl.BlockSpec(memory_space=pltpu.VMEM)
    hbm = pl.BlockSpec(memory_space=pl.ANY)
    return pl.pallas_call(
        functools.partial(encoder_backward_kernel, images, layout, out_layout),
        out_shape=[
            jax.ShapeDtypeStruct(out_layout.shape, BF),
            jax.ShapeDtypeStruct(vec.shape, F32),
        ],
        in_specs=[vm] * (3 + len(ENC_KEEP)) + [hbm],
        out_specs=[hbm, vm],
        scratch_shapes=[
            pltpu.VMEM((ENC_TOTAL, 16, 128), BF),
            pltpu.VMEM((ENC_TOTAL, 16, 128), BF),
            pltpu.VMEM((rows, DE), F32),
            pltpu.VMEM((rows, DE), BF),
            pltpu.VMEM((rows, DE), F32),
            pltpu.VMEM((rows, DE), BF),
            pltpu.VMEM((rows, 3 * DE), BF),
            pltpu.VMEM((DE, rows), BF),
            pltpu.SemaphoreType.DMA((len(out_layout.moves),)),
        ]
        + load_scratch(layout),
        name="encoder_backward",
        compiler_params=pltpu.CompilerParams(vmem_limit_bytes=VMEM_LIMIT),
    )(vis, vec, dlatent, *saved, weights)


def decoder_kernel(images, layout, out_layout, masked_total, latent, places, pix, vec, weights, *refs):
    dlatent, loss, dmats, dvec = refs[:4]
    s = Bag(
        ["x0", "x1", "x2", "n1", "n2", "qkv", "probs", "att", "h", "dx", "dxb", "dn", "dqkv", "flip"],
        refs[4:18],
    )
    kept, dkept, posit, dguess, out_sem, side, sem = refs[18:]
    s.datt = s.n2
    rows = images * ROWS_D
    mats = [Mat(kept, b, shape) for b, shape in zip(DEC_BASE, DEC_MATS)]
    grads = [Mat(dkept, b, shape) for b, shape in zip(DEC_BASE, DEC_MATS)]
    started = load_mats(weights, kept, side, sem, layout)
    posit[...] = jnp.zeros_like(posit)
    for j in range(DD // 128):
        posit[0:PATCHES, j * 128 : (j + 1) * 128] = position_column(vec, DV[2], DD // 128, j)
    dvec[DV[13] + PIX // 128 :, :] = jnp.zeros_like(dvec[DV[13] + PIX // 128 :, :])
    finish_mats(started, kept, side, layout)
    for i in range(images):
        part = pl.ds(i * ROWS_E, ROWS_E)
        where = pl.ds(i * ROWS_D, ROWS_D)
        for j in range(DD // 256):
            cut = slice(j * 256, (j + 1) * 256)
            z = dot(latent[part, :], mats[0].cols(j)) + row_of(vec, DV[0] + 2 * j, 256)
            place = places[where, :]
            hot = visible_rows(jnp.where(place < VIS, place, -1), ROWS_E)
            high = z.astype(BF)
            low = (z - high.astype(F32)).astype(BF)
            token = jnp.where(place >= VIS, 1.0, 0.0) * row_of(vec, DV[1] + 2 * j, 256)
            s.x0[where, cut] = dot(hot, high) + dot(hot, low) + token + posit[:, cut]
    lane = lax.broadcasted_iota(jnp.int32, (1, ROWS_D), 1)
    bias = jnp.where(lane < PATCHES, 0.0, -1e30)
    block_forward(
        s, mats[1:5], vec, DEC_AT, DD, FD, DD // HD, bias, ROWS_D, images
    )
    norm_rows(s.x1, s.dxb, vec, DV[11], DV[12], DD, s.x2, DV[10])
    factor = 2.0 / (PIX * masked_total)

    def head_step(j, total):
        value = dot(s.dxb[...], mats[5].cols(j)) + row_at(vec, DV[13], j)
        count = jnp.zeros((8, 256), F32)
        column = jnp.zeros((8, 256), F32)
        for i in range(images):
            where = slice(i * ROWS_D, (i + 1) * ROWS_D)
            error = value[where] - pix[i, :, lanes(j)].astype(F32)
            error = jnp.where(places[where, :] >= VIS, error, 0.0)
            count = count + fold(error * error)
            error = error * factor
            column = column + fold(error)
            dguess[where, lanes(j)] = error.astype(BF)
        put_row_at(dvec, DV[13], j, total_row(column))
        return total + count

    total = loop(PIX // 256, head_step, jnp.zeros((8, 256), F32))
    loss[...] = jnp.broadcast_to(jnp.sum(total) * (1.0 / PIX), (8, 128))
    s.flip[...] = s.dxb[...].T

    def head_weight_step(j, carry):
        grads[5].put_cols(j, dot(s.flip[...], dguess[:, lanes(j)]))
        return carry

    loop(PIX // 256, head_weight_step)

    def head_input_step(j, carry):
        s.dn[:, lanes(j)] = dot_t(dguess[...], mats[5].band(j))
        return carry

    loop(DD // 256, head_input_step)
    norm_back_rows(s.x2, s.dn, s.dx, s.dxb, vec, dvec, DV[11], DV[12], DD, DV[10], False)
    block_backward(
        s, mats[1:5], grads[1:5], vec, dvec, DEC_AT, DD, FD, DD // HD, ROWS_D, images
    )
    token = jnp.zeros((8, DD), F32)
    spot = jnp.zeros((ROWS_D, DD), F32)
    back = []
    for i in range(images):
        where = pl.ds(i * ROWS_D, ROWS_D)
        place = places[where, :]
        dx = s.dx[where, :]
        spot = spot + dx
        token = token + fold(jnp.where(place >= VIS, dx, 0.0))
        hot = visible_rows(jnp.where(place < VIS, place, -1), ROWS_E)
        back.append(t_dot(hot, s.dxb[where, :]))
    posit[...] = spot
    for j in range(DD // 128):
        dvec[pl.ds(DV[2] + j, PATCHES, stride=DD // 128), :] = posit[
            0:PATCHES, j * 128 : (j + 1) * 128
        ]
    put_row(dvec, DV[1], total_row(token))
    back = jnp.concatenate(back, 0)
    put_row(dvec, DV[0], jnp.sum(back, 0, keepdims=True))
    back = back.astype(BF)
    for j in range(DE // 256):
        grads[0].put_band(j, t_dot(latent[:, j * 256 : (j + 1) * 256], back))
        dlatent[:, j * 256 : (j + 1) * 256] = dot_t(back, mats[0].band(j)).astype(BF)
    for copy in store_mats(dkept, dmats, out_sem, out_layout):
        copy.wait()


def decoder_step(images, layout, out_layout, masked_total, latent, places, pix, vec, weights):
    rows = images * ROWS_D
    vm = pl.BlockSpec(memory_space=pltpu.VMEM)
    hbm = pl.BlockSpec(memory_space=pl.ANY)
    probs = images * HD
    return pl.pallas_call(
        functools.partial(decoder_kernel, images, layout, out_layout, masked_total),
        out_shape=[
            jax.ShapeDtypeStruct((images * ROWS_E, DE), BF),
            jax.ShapeDtypeStruct((8, 128), F32),
            jax.ShapeDtypeStruct(out_layout.shape, BF),
            jax.ShapeDtypeStruct(vec.shape, F32),
        ],
        in_specs=[vm, vm, vm, vm, hbm],
        out_specs=[vm, vm, hbm, vm],
        scratch_shapes=[
            pltpu.VMEM((rows, DD), F32),
            pltpu.VMEM((rows, DD), F32),
            pltpu.VMEM((rows, DD), F32),
            pltpu.VMEM((rows, DD), BF),
            pltpu.VMEM((rows, DD), BF),
            pltpu.VMEM((rows, 3 * DD), BF),
            pltpu.VMEM((probs, ROWS_D, ROWS_D), BF),
            pltpu.VMEM((rows, DD), BF),
            pltpu.VMEM((rows, FD), F32),
            pltpu.VMEM((rows, DD), F32),
            pltpu.VMEM((rows, DD), BF),
            pltpu.VMEM((rows, DD), F32),
            pltpu.VMEM((rows, 3 * DD), BF),
            pltpu.VMEM((DD, rows), BF),
            pltpu.VMEM((DEC_TOTAL, 16, 128), BF),
            pltpu.VMEM((DEC_TOTAL, 16, 128), BF),
            pltpu.VMEM((ROWS_D, DD), F32),
            pltpu.VMEM((rows, PIX), BF),
            pltpu.SemaphoreType.DMA((len(out_layout.moves),)),
        ]
        + load_scratch(layout),
        name="decoder_step",
        compiler_params=pltpu.CompilerParams(vmem_limit_bytes=VMEM_LIMIT),
    )(latent, places, pix, vec, weights)


def natural(flat, shapes):
    pieces, offset = [], 0
    for rows, columns in shapes:
        piece = flat[offset : offset + rows * columns].reshape(rows // 16, 16, columns // 128, 128)
        pieces.append(piece.transpose(0, 2, 1, 3).reshape(-1, 16, 128))
        offset += rows * columns
    return jnp.concatenate(pieces, 0)


def flat_from_natural(tiles, shapes, total):
    pieces, offset = [], 0
    for rows, columns in shapes:
        count = rows * columns // 2048
        piece = tiles[offset : offset + count].reshape(rows // 16, columns // 128, 16, 128)
        pieces.append(piece.transpose(0, 2, 1, 3).reshape(-1))
        offset += count
    flat = jnp.concatenate(pieces)
    return jnp.pad(flat, (0, total - flat.shape[0]))


MESH = pl.DeviceIdType.MESH
DEPTH, WIDTH = 4, 2
SLOT_M, SLOT_V = 264, 5
SLOT = SLOT_M + SLOT_V
PART = ((0, 224), (224, SLOT - 224))
MARGIN = 384


def shard_plan(shapes, total, devices):
    lines = total // devices // 128
    plans = []
    for device in range(devices):
        low, high = device * lines, (device + 1) * lines
        first, count, pieces = 0, 0, []
        line, tile = 0, 0
        for rows, columns in shapes:
            blocks = columns // 128
            begin, end = max(low, line), min(high, line + rows * blocks)
            if begin < end:
                top, bottom = (begin - line) // blocks, (end - line) // blocks
                assert top * blocks == begin - line and bottom * blocks == end - line
                up, down = top // 16, -(-bottom // 16)
                if not pieces:
                    first = tile + up * blocks
                pieces.append((blocks, line + up * 16 * blocks - low, down - up, count))
                count += (down - up) * blocks
            line += rows * blocks
            tile += rows * blocks // 16
        plans.append((first, count, pieces))
    return plans


def devices_around(z, y, c, s):
    at = lambda zz, yy, cc: (s, zz * 4 + yy * 2 + cc)
    around = {"side": at(z, 1 - y, c), "core": at(z, y, 1 - c)}
    if z + 1 < DEPTH:
        around["up"] = at(z + 1, y, c)
    if z > 0:
        around["down"] = at(z - 1, y, c)
    return around


def greet(around):
    barrier = pltpu.get_barrier_semaphore()
    for target in around.values():
        pl.semaphore_signal(barrier, inc=1, device_id=target, device_id_type=MESH)
    pl.semaphore_wait(barrier, len(around))


def place():
    d = lax.axis_index("dp")
    return lax.axis_index("section"), d // 4, (d // 2) % 2, d % 2


def for_each_depth(run):
    s, z_now, y, c = place()
    for z in range(DEPTH):
        pl.when(z_now == z)(functools.partial(run, s, z, y, c))


def gather_kernel(own, out, send, recv, local):
    def run(s, z, y, c):
        around = devices_around(z, y, c, s)
        greet(around)
        slot = lambda zz, yy, cc: zz * 4 + yy * 2 + cc
        sent = []

        def at(ref, index, part):
            start, count = PART[part]
            return ref.at[index, pl.ds(start, count)]

        def push(index, part, targets, mine=False):
            start, count = PART[part]
            for name in targets:
                if name not in around:
                    continue
                copy = pltpu.make_async_remote_copy(
                    own.at[pl.ds(start, count)] if mine else at(out, index, part),
                    at(out, index, part),
                    send.at[len(sent)],
                    recv.at[index, part],
                    device_id=around[name],
                    device_id_type=MESH,
                )
                copy.start()
                sent.append(copy)

        def arrive(index, part):
            pltpu.make_async_remote_copy(
                at(out, index, part),
                at(out, index, part),
                send.at[0],
                recv.at[index, part],
                device_id=around["core"],
                device_id_type=MESH,
            ).wait_recv()

        me = slot(z, y, c)
        push(me, 1, ["side"], True)
        push(me, 0, ["up", "down", "side"], True)
        push(me, 1, ["up", "down"], True)
        push(me, 0, ["core"], True)
        push(me, 1, ["core"], True)
        keep = pltpu.make_async_copy(own, out.at[me], local)
        keep.start()
        arrive(slot(z, 1 - y, c), 1)
        push(slot(z, 1 - y, c), 1, ["up", "down", "core"])
        for k in range(1, DEPTH):
            for zz in (z - k, z + k):
                if 0 <= zz < DEPTH:
                    onward = "up" if zz < z else "down"
                    arrive(slot(zz, y, c), 0)
                    push(slot(zz, y, c), 0, [onward, "side", "core"])
                    for yy in (y, 1 - y):
                        arrive(slot(zz, yy, c), 1)
                        push(slot(zz, yy, c), 1, [onward, "core"])
            for zz in sorted({z - k + 1, z + k - 1}):
                if 0 <= zz < DEPTH:
                    arrive(slot(zz, 1 - y, c), 0)
                    push(slot(zz, 1 - y, c), 0, ["core"])
        for zz in (z - DEPTH + 1, z + DEPTH - 1):
            if 0 <= zz < DEPTH:
                arrive(slot(zz, 1 - y, c), 0)
                push(slot(zz, 1 - y, c), 0, ["core"])
        for zz in range(DEPTH):
            for yy in range(WIDTH):
                for part in range(2):
                    arrive(slot(zz, yy, 1 - c), part)
        keep.wait()
        for copy in sent:
            copy.wait_send()

    for_each_depth(run)


def gather_slots(own):
    hbm = pl.BlockSpec(memory_space=pl.ANY)
    return pl.pallas_call(
        gather_kernel,
        out_shape=jax.ShapeDtypeStruct((16, SLOT, 16, 128), BF),
        in_specs=[hbm],
        out_specs=hbm,
        scratch_shapes=[
            pltpu.SemaphoreType.DMA((48,)),
            pltpu.SemaphoreType.DMA((16, 2)),
            pltpu.SemaphoreType.DMA,
        ],
        name="gather_slots",
        compiler_params=pltpu.CompilerParams(collective_id=0, has_side_effects=True),
    )(own)


def send_order(z):
    order = []
    for k in range(DEPTH - 1, -1, -1):
        for zz in (z + k, z - k):
            if 0 <= zz < DEPTH and zz not in order:
                order.append(zz)
    return order


def add_tiles(target, sources, start, count):
    step = 8

    def some(base, size):
        value = sources[0][pl.ds(base, size)].astype(F32)
        for source in sources[1:]:
            value = value + source[pl.ds(base, size)].astype(F32)
        target[pl.ds(base, size)] = value.astype(target.dtype)

    def body(i, carry):
        some(start + i * step, step)
        return carry

    lax.fori_loop(0, count // step, body, 0)
    if count % step:
        some(start + count // step * step, count % step)


class Shifted:
    def __init__(self, ref, start):
        self.ref, self.start = ref, start

    def __getitem__(self, index):
        return self.ref[pl.ds(index.start - self.start, index.size)]


def scatter_kernel(mats, vecs, out, held, core_in, side_a, side_b, z_a, z_b, load, send, r_core, r_side, r_z):
    def run(s, z, y, c):
        around = devices_around(z, y, c, s)
        loads = {}
        order = send_order(z)
        slot = lambda zz, yy, cc: zz * 4 + yy * 2 + cc
        n = 0
        for cc in (1 - c, c):
            for zz in order:
                for yy in (1 - y, y):
                    index = slot(zz, yy, cc)
                    pair = (
                        pltpu.make_async_copy(
                            mats.at[index], held.at[index, pl.ds(0, SLOT_M)], load.at[n]
                        ),
                        pltpu.make_async_copy(
                            vecs.at[index], held.at[index, pl.ds(SLOT_M, SLOT_V)], load.at[16 + n]
                        ),
                    )
                    for copy in pair:
                        copy.start()
                    loads[n] = pair
                    n += 1
        greet(around)
        sent = []

        def remote(source, target, sem, name):
            return pltpu.make_async_remote_copy(
                source,
                target,
                send.at[len(sent)],
                sem,
                device_id=around[name],
                device_id_type=MESH,
            )

        def push(source, target, sem, name):
            copy = remote(source, target, sem, name)
            copy.start()
            sent.append(copy)

        def cut(index, part):
            start, count = PART[part]
            return held.at[index, pl.ds(start, count)]

        def arrive(target, sem):
            pltpu.make_async_remote_copy(
                target, target, send.at[0], sem, device_id=around["core"], device_id_type=MESH
            ).wait_recv()

        n = 0
        for zz in order:
            for yy in (1 - y, y):
                for copy in loads[n]:
                    copy.wait()
                push(
                    held.at[slot(zz, yy, 1 - c)],
                    core_in.at[zz * 2 + yy],
                    r_core.at[zz * 2 + yy],
                    "core",
                )
                n += 1
        ready = set()

        def prepare(zz, flip):
            if (zz, flip) in ready:
                return
            ready.add((zz, flip))
            yy = 1 - y if flip else y
            for copy in loads[8 + order.index(zz) * 2 + (0 if flip else 1)]:
                copy.wait()
            arrive(core_in.at[zz * 2 + yy], r_core.at[zz * 2 + yy])

        def z_in(part, way, zz, yy):
            if part == 0:
                return z_a.at[way, zz], r_z.at[way, zz, 2]
            return z_b.at[way, zz, yy], r_z.at[way, zz, yy]

        def side_sources(zz, yy):
            return [held.at[slot(zz, yy, c)], core_in.at[zz * 2 + yy]]

        for zz in order:
            prepare(zz, True)
            index = slot(zz, 1 - y, c)
            add_tiles(held.at[index], side_sources(zz, 1 - y), *PART[0])
            push(cut(index, 0), side_a.at[zz], r_side.at[zz], "side")

        def along(part, zz, flip):
            yy = 1 - y if flip else y
            prepare(zz, flip)
            index = slot(zz, yy, c)
            way, name, first = (0, "up", 0) if zz > z else (1, "down", DEPTH - 1)
            sources = side_sources(zz, yy)
            if part == 0:
                arrive(side_a.at[zz], r_side.at[zz])
                sources.append(side_a.at[zz])
            if z != first:
                ref, sem = z_in(part, way, zz, yy)
                arrive(ref, sem)
                sources.append(ref if part == 0 else Shifted(ref, PART[1][0]))
            add_tiles(held.at[index], sources, *PART[part])
            ref, sem = z_in(part, way, zz, yy)
            push(cut(index, part), ref, sem, name)

        def gathered(part, yy):
            found = []
            for way, here in ((0, z > 0), (1, z < DEPTH - 1)):
                if here:
                    ref, sem = z_in(part, way, z, yy)
                    arrive(ref, sem)
                    found.append(ref if part == 0 else Shifted(ref, PART[1][0]))
            return found

        for zz in order[:-1]:
            along(1, zz, True)
            along(1, zz, False)
        prepare(z, False)
        index = slot(z, 1 - y, c)
        add_tiles(held.at[index], side_sources(z, 1 - y) + gathered(1, 1 - y), *PART[1])
        push(cut(index, 1), side_b, r_side.at[DEPTH], "side")
        for zz in order[:-1]:
            along(0, zz, False)
        arrive(side_b, r_side.at[DEPTH])
        add_tiles(
            out,
            side_sources(z, y) + gathered(1, y) + [Shifted(side_b, PART[1][0])],
            *PART[1],
        )
        arrive(side_a.at[z], r_side.at[z])
        add_tiles(out, side_sources(z, y) + [side_a.at[z]] + gathered(0, y), *PART[0])
        for copy in sent:
            copy.wait_send()

    for_each_depth(run)


def scatter_slots(mats, vecs):
    hbm = pl.BlockSpec(memory_space=pl.ANY)
    tail = PART[1][1]
    return pl.pallas_call(
        scatter_kernel,
        out_shape=jax.ShapeDtypeStruct((SLOT, 16, 128), F32),
        in_specs=[hbm, hbm],
        out_specs=pl.BlockSpec(memory_space=pltpu.VMEM),
        scratch_shapes=[
            pltpu.VMEM((16, SLOT, 16, 128), BF),
            pltpu.VMEM((8, SLOT, 16, 128), BF),
            pltpu.VMEM((DEPTH, PART[0][1], 16, 128), BF),
            pltpu.VMEM((tail, 16, 128), BF),
            pltpu.VMEM((2, DEPTH, PART[0][1], 16, 128), BF),
            pltpu.VMEM((2, DEPTH, 2, tail, 16, 128), BF),
            pltpu.SemaphoreType.DMA((32,)),
            pltpu.SemaphoreType.DMA((24,)),
            pltpu.SemaphoreType.DMA((8,)),
            pltpu.SemaphoreType.DMA((DEPTH + 1,)),
            pltpu.SemaphoreType.DMA((2, DEPTH, 3)),
        ],
        name="scatter_slots",
        compiler_params=pltpu.CompilerParams(
            collective_id=1, has_side_effects=True, vmem_limit_bytes=VMEM_LIMIT
        ),
    )(mats, vecs)


def piece_table(lines):
    plans = [shard_plan(m, lines * 128 * 16, 16) for m in (ENC_MATS, DEC_MATS)]
    most = max(len(pieces) for plan in plans for _, _, pieces in plan)
    table = [
        [[list(p) for p in pieces] + [[0] * 4] * (most - len(pieces)) for _, _, pieces in plan]
        for plan in plans
    ]
    widths = sorted({p[0] for plan in plans for _, _, pieces in plan for p in pieces})
    return plans, table, widths


def each_tile(table, widths, run):
    for piece in range(table.shape[0]):
        for width in widths:

            @pl.when(table[piece, 0] == width)
            def _(piece=piece, width=width):
                def step(i, carry):
                    for j in range(width):
                        line = MARGIN + table[piece, 1] + i * (16 * width) + j
                        run(line, width, table[piece, 3] + i * width + j)
                    return carry

                lax.fori_loop(0, table[piece, 2], step, 0)


def pack_kernel(widths, table, mat, vec, out, lines, sem):
    count = mat.shape[0]
    copy = pltpu.make_async_copy(mat, lines.at[pl.ds(MARGIN, count)], sem)
    copy.start()
    lines[0:MARGIN, :] = jnp.zeros((MARGIN, 128), F32)
    lines[MARGIN + count :, :] = jnp.zeros((MARGIN, 128), F32)
    out[SLOT_M:] = vec[...].astype(BF).reshape(SLOT_V, 16, 128)
    copy.wait()

    def run(line, width, tile):
        out[tile] = lines[pl.ds(line, 16, stride=width), :].astype(BF)

    each_tile(table, widths, run)


def pack(table, widths, mat, vec):
    vm = pl.BlockSpec(memory_space=pltpu.VMEM)
    return pl.pallas_call(
        functools.partial(pack_kernel, widths),
        out_shape=jax.ShapeDtypeStruct((SLOT, 16, 128), BF),
        in_specs=[
            pl.BlockSpec(memory_space=pltpu.SMEM),
            pl.BlockSpec(memory_space=pl.ANY),
            vm,
        ],
        out_specs=vm,
        scratch_shapes=[
            pltpu.VMEM((mat.shape[0] + 2 * MARGIN, 128), F32),
            pltpu.SemaphoreType.DMA,
        ],
        name="pack",
        compiler_params=pltpu.CompilerParams(vmem_limit_bytes=VMEM_LIMIT),
    )(table, mat, vec)


def unpack_kernel(widths, table, total, loss, grad, vec, part, lines):
    count = grad.shape[0]
    lines[...] = jnp.zeros_like(lines)

    def run(line, width, tile):
        lines[pl.ds(line, 16, stride=width), :] = total[tile]

    each_tile(table, widths, run)
    vec[...] = total[SLOT_M:].reshape(SLOT_V * 16, 128)

    def square(i, carry):
        rows = pl.ds(pl.multiple_of(i * 96, 96), 96)
        value = lines[pl.ds(pl.multiple_of(MARGIN + i * 96, 96), 96), :]
        grad[rows, :] = value
        return carry + fold(value * value)

    carry = fold(vec[...] * vec[...])
    carry = lax.fori_loop(0, count // 96, square, carry)
    row = lax.broadcasted_iota(jnp.int32, (8, 128), 0)
    part[...] = jnp.where(row == 0, jnp.sum(carry), loss[...])


def unpack(table, widths, count, total, loss):
    vm = pl.BlockSpec(memory_space=pltpu.VMEM)
    return pl.pallas_call(
        functools.partial(unpack_kernel, widths),
        out_shape=[
            jax.ShapeDtypeStruct((count, 128), F32),
            jax.ShapeDtypeStruct((SLOT_V * 16, 128), F32),
            jax.ShapeDtypeStruct((8, 128), F32),
        ],
        in_specs=[pl.BlockSpec(memory_space=pltpu.SMEM), vm, vm],
        out_specs=[vm, vm, vm],
        scratch_shapes=[pltpu.VMEM((count + 2 * MARGIN, 128), F32)],
        name="unpack",
        compiler_params=pltpu.CompilerParams(vmem_limit_bytes=VMEM_LIMIT),
    )(table, total, loss)


def total_kernel(part, out, parts, send, recv):
    s, d = lax.axis_index("section"), lax.axis_index("dp")
    count = parts.shape[0]
    me = s * 16 + d
    barrier = pltpu.get_barrier_semaphore()

    def target(k):
        other = lax.rem(me + k, count)
        return other, (other // 16, lax.rem(other, 16))

    for k in range(1, count):
        pl.semaphore_signal(barrier, inc=1, device_id=target(k)[1], device_id_type=MESH)
    pl.semaphore_wait(barrier, count - 1)
    sent = []
    for k in range(1, count):
        copy = pltpu.make_async_remote_copy(
            part,
            parts.at[me],
            send.at[k],
            recv.at[me],
            device_id=target(k)[1],
            device_id_type=MESH,
        )
        copy.start()
        sent.append(copy)
    parts[me] = part[...]
    for k in range(1, count):
        other = target(k)[0]
        pltpu.make_async_remote_copy(
            part,
            parts.at[other],
            send.at[k],
            recv.at[other],
            device_id=target(k)[1],
            device_id_type=MESH,
        ).wait_recv()
    out[...] = jnp.sum(parts[...], 0)
    for copy in sent:
        copy.wait_send()


def total_over_all(part):
    vm = pl.BlockSpec(memory_space=pltpu.VMEM)
    return pl.pallas_call(
        total_kernel,
        out_shape=jax.ShapeDtypeStruct((8, 128), F32),
        in_specs=[vm],
        out_specs=vm,
        scratch_shapes=[
            pltpu.VMEM((32, 8, 128), F32),
            pltpu.SemaphoreType.DMA((32,)),
            pltpu.SemaphoreType.DMA((32,)),
        ],
        name="total",
        compiler_params=pltpu.CompilerParams(collective_id=2, has_side_effects=True),
    )(part)


def clip_factor(square):
    return jnp.minimum(1.0, 0.001 / (jnp.sqrt(square) + 1e-06))


def adam_update(master, first, second, grad, rate, decay):
    first = 0.9 * first + 0.1 * grad
    second = 0.95 * second + 0.05 * grad * grad
    step_first = first / (1.0 - 0.9**STEP)
    step_second = second / (1.0 - 0.95**STEP)
    master = master - rate * (step_first / (jnp.sqrt(step_second) + 1e-08) + decay * master)
    return (master, first, second)


def adam_kernel(total, grad, master, first, second, new, new_first, new_second, copy):
    factor = clip_factor(total[0:1, :])
    step = 104

    def run(i, carry):
        rows = pl.ds(pl.multiple_of(i * step, 8), step)
        a, b, c = adam_update(
            master[rows, :], first[rows, :], second[rows, :], factor * grad[rows, :], 0.05, 0.05
        )
        new[rows, :] = a
        new_first[rows, :] = b
        new_second[rows, :] = c
        return carry

    lax.fori_loop(0, grad.shape[0] // step, run, 0)
    copy[...] = new[...].astype(BF)


def adam(total, grad, master, first, second):
    count = grad.shape[0]
    size = 624
    block = pl.BlockSpec((size, 128), lambda i: (i, 0))
    shape = jax.ShapeDtypeStruct((count, 128), F32)
    return pl.pallas_call(
        adam_kernel,
        grid=(count // size,),
        out_shape=[shape] * 3 + [jax.ShapeDtypeStruct((count, 128), BF)],
        in_specs=[pl.BlockSpec((8, 128), lambda i: (0, 0))] + [block] * 4,
        out_specs=[block] * 4,
        name="adam",
        compiler_params=pltpu.CompilerParams(vmem_limit_bytes=VMEM_LIMIT),
    )(total, grad, master, first, second)


def shifted(value, axis, steps):
    count = lax.axis_size(axis)
    initial, last = (max(0, -steps), min(count, count - steps))
    return lax.ppermute(value, axis, [(source, source + steps) for source in range(initial, last)])


def train(images, masked_total, enc, dec, enc_out, dec_out, pixels, visible, restore, vecs, weights):
    encoding = lax.axis_index("section") == 0
    pix = jnp.pad(pixels, ((0, 0), (0, ROWS_D - PATCHES), (0, 0)))
    vis = jnp.pad(visible, ((0, 0), (0, ROWS_E - VIS)), constant_values=-1).reshape(-1, 1)
    places = jnp.pad(restore, ((0, 0), (0, ROWS_D - PATCHES)), constant_values=-1).reshape(-1, 1)
    blank_saved = [jnp.zeros(*item) for item in enc_shapes(images).values()]
    blank_latent = jnp.zeros((images * ROWS_E, DE), BF)
    latent, *saved = lax.cond(
        encoding,
        lambda: list(encoder_forward(images, enc, vis, pix, vecs, weights)),
        lambda: [blank_latent] + blank_saved,
    )
    arrived = shifted(latent, "section", 1)
    dlatent, loss, dmats, dvec = lax.cond(
        encoding,
        lambda: [
            blank_latent,
            jnp.zeros((8, 128), F32),
            jnp.zeros(dec_out.shape, BF),
            jnp.zeros(vecs.shape, F32),
        ],
        lambda: list(
            decoder_step(
                images, dec, dec_out, masked_total, arrived, places, pix, vecs, weights
            )
        ),
    )
    returned = shifted(dlatent, "section", -1)
    if dec_out.shape == enc_out.shape:
        other = lambda: [dmats, dvec]
    else:
        more = enc_out.shape[0] - dec_out.shape[0]
        other = lambda: [jnp.pad(dmats, ((0, more), (0, 0), (0, 0))), dvec]
    dmats, dvec = lax.cond(
        encoding,
        lambda: list(
            encoder_backward(images, enc, enc_out, vis, vecs, returned, saved, weights)
        ),
        other,
    )
    return dmats, dvec, loss


def body_block(
    pixels, visible, restore, mat_master, mat_first, mat_second, vec_master, vec_first, vec_second
):
    images = pixels.shape[0]
    masked_total = (PATCHES - VIS) * images * 16
    count, size = mat_master.shape[1] // 128, vec_master.shape[1]
    plans, table, widths = piece_table(count)
    table = jnp.asarray(table, jnp.int32)[lax.axis_index("section"), lax.axis_index("dp")]
    lines = [value.reshape(count, 128) for value in (mat_master, mat_first, mat_second)]
    room = SLOT_V * 2048
    own = pack(
        table, widths, lines[0], jnp.pad(vec_master[0], (0, room - size)).reshape(-1, 128)
    )
    slots = gather_slots(own)
    vecs = slots[:, SLOT_M:].reshape(16, room)[:, :size].reshape(-1, 128).astype(F32)
    inward = [slot_layout(plan, slots.shape) for plan in plans]
    outward = [whole_slots(plan, (16, SLOT_M, 16, 128)) for plan in plans]
    dmats, dvec, loss = train(
        images, masked_total, *inward, *outward, pixels, visible, restore, vecs, slots
    )
    dvec = jnp.pad(dvec.reshape(16, size), ((0, 0), (0, room - size))).astype(BF)
    total = scatter_slots(dmats, dvec.reshape(16, SLOT_V, 16, 128))
    grad, grad_vec, part = unpack(table, widths, count, total, loss)
    total = total_over_all(part)
    square, loss_sum = total[0, 0], total[1, 0]
    news = adam(total, grad, *lines)
    vec_news = adam_update(
        vec_master,
        vec_first,
        vec_second,
        clip_factor(square) * grad_vec.reshape(1, room)[:, :size],
        0.3,
        0.0,
    )
    return (
        (loss_sum, jnp.sqrt(square))
        + tuple(value.reshape(mat_master.shape) for value in news)
        + tuple(vec_news)
        + (vec_news[0].astype(BF),)
    )


def body(
    pixels, visible, restore, mat_master, mat_first, mat_second, vec_master, vec_first, vec_second
):
    images = pixels.shape[0]
    total = mat_master.shape[1] * lax.axis_size("dp")
    masked_total = (PATCHES - VIS) * images * lax.axis_size("dp")
    encoding = lax.axis_index("section") == 0
    enc, dec = plain_layout(ENC_TOTAL), plain_layout(DEC_TOTAL)
    mats = lax.all_gather(mat_master.astype(BF), "dp", axis=1, tiled=True)[0]
    vecs = lax.all_gather(vec_master.astype(BF), "dp", axis=1, tiled=True)[0]
    vecs = vecs.astype(F32).reshape(-1, 128)
    weights = lax.cond(
        encoding,
        lambda m: natural(m, ENC_MATS),
        lambda m: jnp.pad(natural(m, DEC_MATS), ((0, ENC_TOTAL - DEC_TOTAL), (0, 0), (0, 0))),
        mats,
    )
    dec_in = Layout((ENC_TOTAL, 16, 128), [(lambda ref: ref.at[pl.ds(0, DEC_TOTAL)], 0, DEC_TOTAL)], [])
    dmats, grad_vecs, loss = train(
        images, masked_total, enc, dec_in, enc, dec, pixels, visible, restore, vecs, weights
    )
    grad_mats = lax.cond(
        encoding,
        lambda m: flat_from_natural(m.astype(F32), ENC_MATS, total),
        lambda m: flat_from_natural(m[0:DEC_TOTAL].astype(F32), DEC_MATS, total),
        dmats,
    )
    summed_mats = lax.psum_scatter(grad_mats[None], "dp", scatter_dimension=1, tiled=True)
    summed_vecs = lax.psum_scatter(
        grad_vecs.reshape(1, -1), "dp", scatter_dimension=1, tiled=True
    )
    square = jnp.sum(summed_mats * summed_mats) + jnp.sum(summed_vecs * summed_vecs)
    square, loss_sum = lax.psum((square, loss[0, 0]), ("section", "dp"))
    factor = clip_factor(square)
    mat_news = adam_update(mat_master, mat_first, mat_second, factor * summed_mats, 0.05, 0.05)
    vec_news = adam_update(vec_master, vec_first, vec_second, factor * summed_vecs, 0.3, 0.0)
    return (
        (loss_sum, jnp.sqrt(square))
        + tuple(mat_news)
        + (mat_news[0].astype(BF),)
        + tuple(vec_news)
        + (vec_news[0].astype(BF),)
    )


def solution(mesh):
    split = P("section", "dp")
    fits = mesh.shape["section"] == 2 and mesh.shape["dp"] == 16
    return jax.shard_map(
        body_block if fits else body,
        mesh=mesh,
        in_specs=(P("dp", None, None), P("dp", None), P("dp", None)) + (split,) * 6,
        out_specs=(P(), P()) + (split,) * 8,
        check_vma=False,
    )
```

```python
import functools
import math

import jax
import jax.numpy as jnp
from jax import lax
from jax.experimental import pallas as pl
from jax.experimental.pallas import tpu as pltpu
from jax.sharding import PartitionSpec as P

PIX = 768
DE = 768
HE = 12
FE = 3072
DD = 512
HD = 16
FD = 2048
PATCHES = 196
VIS = 49
STEP = 10
ROWS_E = 64
ROWS_D = 208
EPS = 1e-6
BF = jnp.bfloat16
F32 = jnp.float32
VMEM_LIMIT = 63 * 1024 * 1024

ENC_MATS = [(PIX, DE), (DE, 3 * DE), (DE, DE), (DE, FE), (FE, DE)]
DEC_MATS = [(DE, DD), (DD, 3 * DD), (DD, DD), (DD, FD), (FD, DD), (DD, PIX)]
ENC_VECS = [DE, PATCHES * DE, DE, DE, 2 * DE, DE, DE, DE, FE, DE, DE, DE]
DEC_VECS = [DD, DD, PATCHES * DD, DD, DD, 2 * DD, DD, DD, DD, FD, DD, DD, DD, PIX]


def starts(sizes):
    total, found = 0, []
    for size in sizes:
        found.append(total)
        total += size
    return found, total


ENC_TILES = [k * n // 2048 for k, n in ENC_MATS]
DEC_TILES = [k * n // 2048 for k, n in DEC_MATS]
ENC_BASE, ENC_TOTAL = starts(ENC_TILES)
DEC_BASE, DEC_TOTAL = starts(DEC_TILES)
EV, _ = starts([size // 128 for size in ENC_VECS])
DV, _ = starts([size // 128 for size in DEC_VECS])


class Mat:
    def __init__(self, ref, base, shape, loads=None, stores=None):
        self.base, self.loads, self.stores = base, loads, stores
        self.rows, self.columns = shape
        self.blocks = self.columns // 128
        count = self.rows * self.columns // 2048
        self.ref = ref.at[pl.ds(base, count)].reshape(self.rows // 16, self.blocks, 16, 128)

    def need(self):
        self.loads.need(self.base, self.rows * self.columns // 2048)

    def done(self):
        self.stores.done(self.base, self.rows * self.columns // 2048)

    def cols(self, block):
        parts = [self.ref[:, 2 * block + half].reshape(self.rows, 128) for half in range(2)]
        return jnp.concatenate(parts, 1)

    def band(self, block):
        part = self.ref.at[pl.ds(block * 16, 16)]
        return jnp.concatenate([part[:, j].reshape(256, 128) for j in range(self.blocks)], 1)

    def put_cols(self, block, value):
        for half in range(2):
            piece = value[:, half * 128 : (half + 1) * 128].astype(BF)
            self.ref[:, 2 * block + half] = piece.reshape(self.rows // 16, 16, 128)

    def put_band(self, block, value):
        part = self.ref.at[pl.ds(block * 16, 16)]
        for j in range(self.blocks):
            part[:, j] = value[:, j * 128 : (j + 1) * 128].astype(BF).reshape(16, 16, 128)


def dot(a, b):
    return jnp.dot(a, b, preferred_element_type=F32)


def dot_t(a, b):
    return lax.dot_general(a, b, (((1,), (1,)), ((), ())), preferred_element_type=F32)


def t_dot(a, b):
    return lax.dot_general(a, b, (((0,), (0,)), ((), ())), preferred_element_type=F32)


def loop(count, body, init=0):
    return lax.fori_loop(0, count, body, init)


def lanes(block, width=256):
    return pl.ds(pl.multiple_of(block * width, width), width)


def row_of(vec, start, width):
    return jnp.concatenate([vec[start + j : start + j + 1, :] for j in range(width // 128)], 1)


def row_at(vec, start, block):
    return jnp.concatenate([vec[pl.ds(start + 2 * block + h, 1), :] for h in range(2)], 1)


def put_row(dvec, start, value):
    for j in range(value.shape[1] // 128):
        dvec[start + j : start + j + 1, :] = value[:, j * 128 : (j + 1) * 128]


def put_row_at(dvec, start, block, value):
    for h in range(2):
        dvec[pl.ds(start + 2 * block + h, 1), :] = value[:, h * 128 : (h + 1) * 128]


def fold(value):
    return value.reshape(value.shape[0] // 8, 8, value.shape[1]).sum(0)


def total_row(value):
    return jnp.sum(value, 0, keepdims=True)


def norm_parts(x):
    mean = jnp.mean(x, -1, keepdims=True)
    centred = x - mean
    scale = lax.rsqrt(jnp.mean(centred * centred, -1, keepdims=True) + EPS)
    return centred * scale, scale


CHUNKS = (208, 128, 64, 32)


def chunk_loop(ref, step, init=0):
    count = ref.shape[0]
    size = next(c for c in CHUNKS if count % c == 0)

    def run(i, carry):
        return step(pl.ds(pl.multiple_of(i * size, size), size), carry)

    return lax.fori_loop(0, count // size, run, init)


def norm_rows(x_ref, out_ref, vec, gain_at, shift_at, width, add_ref=None, bias_at=None):
    gain, shift = row_of(vec, gain_at, width), row_of(vec, shift_at, width)
    bias = None if bias_at is None else row_of(vec, bias_at, width)

    def step(rows, carry):
        x = x_ref[rows, :]
        if add_ref is not None:
            x = x + add_ref[rows, :] + bias
            add_ref[rows, :] = x
        unit, _ = norm_parts(x)
        out_ref[rows, :] = (unit * gain + shift).astype(BF)
        return carry

    chunk_loop(x_ref, step)


def norm_back_rows(x_ref, dy_ref, dx_ref, dxb_ref, vec, dvec, gain_at, shift_at, width, bias_at, add):
    gain = row_of(vec, gain_at, width)
    zero = jnp.zeros((8, width), F32)

    def step(rows, carry):
        dgain, dshift, dbias = carry
        unit, scale = norm_parts(x_ref[rows, :])
        dy = dy_ref[rows, :].astype(F32)
        dunit = dy * gain
        dx = scale * (
            dunit
            - jnp.mean(dunit, -1, keepdims=True)
            - unit * jnp.mean(dunit * unit, -1, keepdims=True)
        )
        if add:
            dx = dx + dx_ref[rows, :]
        dx_ref[rows, :] = dx
        dxb_ref[rows, :] = dx.astype(BF)
        return dgain + fold(dy * unit), dshift + fold(dy), dbias + fold(dx)

    dgain, dshift, dbias = chunk_loop(x_ref, step, (zero, zero, zero))
    put_row(dvec, gain_at, total_row(dgain))
    put_row(dvec, shift_at, total_row(dshift))
    if bias_at is not None:
        put_row(dvec, bias_at, total_row(dbias))
    return dbias


GELU_C = math.sqrt(2.0 / math.pi)


def gelu_parts(x):
    square = x * x
    t = jnp.tanh(x * (GELU_C + (GELU_C * 0.044715) * square))
    half = 0.5 * (1.0 + t)
    return x * half, half + (0.5 * x) * (1.0 - t * t) * (
        GELU_C + (3.0 * 0.044715 * GELU_C) * square
    )


def head_mask(size):
    lane = lax.broadcasted_iota(jnp.int32, (1, 128), 1)
    return [(lane >= h * size) & (lane < (h + 1) * size) for h in range(128 // size)]


def attention(qkv, probs, att, bias, group, groups, width, size):
    blocks = width // 128
    masks = head_mask(size)

    def step(i, carry):
        g, b = i // blocks, i % blocks
        rows = pl.ds(pl.multiple_of(g * group, 16), group)
        q = qkv[rows, lanes(b, 128)]
        k = qkv[rows, lanes(blocks + b, 128)]
        v = qkv[rows, lanes(2 * blocks + b, 128)]
        out = jnp.zeros((group, 128), F32)
        for h, mask in enumerate(masks):
            s = dot_t(jnp.where(mask, q, jnp.zeros_like(q)), k) + bias
            e = jnp.exp(s - jnp.max(s, -1, keepdims=True))
            p = (e * (1.0 / jnp.sum(e, -1, keepdims=True))).astype(BF)
            probs[i * len(masks) + h] = p
            out = jnp.where(mask, dot(p, v), out)
        att[rows, lanes(b, 128)] = out.astype(BF)
        return carry

    lax.fori_loop(0, groups * blocks, step, 0, unroll=4 if groups * blocks % 4 == 0 else 2)


def attention_back(qkv, probs, datt, dqkv, dvec, qv_at, group, groups, width, size):
    blocks = width // 128
    masks = head_mask(size)
    scale = size ** (-0.5)
    for j in range(2 * blocks):
        dvec[qv_at + j : qv_at + j + 1, :] = jnp.zeros((1, 128), F32)

    def step(i, carry):
        g, b = i // blocks, i % blocks
        rows = pl.ds(pl.multiple_of(g * group, 16), group)
        q = qkv[rows, lanes(b, 128)]
        k = qkv[rows, lanes(blocks + b, 128)]
        v = qkv[rows, lanes(2 * blocks + b, 128)]
        da = datt[rows, lanes(b, 128)]
        zero = jnp.zeros((group, 128), F32)
        dq, dk, dv = zero, zero, zero
        for h, mask in enumerate(masks):
            p = probs[i * len(masks) + h]
            dp = dot_t(jnp.where(mask, da, jnp.zeros_like(da)), v)
            wide = p.astype(F32)
            prod = wide * dp
            ds = (prod - wide * jnp.sum(prod, -1, keepdims=True)).astype(BF)
            dq = jnp.where(mask, dot(ds, k), dq)
            dk = jnp.where(mask, t_dot(ds, q), dk)
            dv = jnp.where(mask, t_dot(p, da), dv)
        dq = dq * scale
        dqkv[rows, lanes(b, 128)] = dq.astype(BF)
        dqkv[rows, lanes(blocks + b, 128)] = dk.astype(BF)
        dqkv[rows, lanes(2 * blocks + b, 128)] = dv.astype(BF)
        dvec[pl.ds(qv_at + b, 1), :] += total_row(dq)
        dvec[pl.ds(qv_at + blocks + b, 1), :] += total_row(dv)
        return carry

    lax.fori_loop(0, groups * blocks, step, 0, unroll=2)


def block_forward(s, mats, vec, at, width, hidden, size, bias, group, groups):
    w_qkv, w_proj, w_up, w_down = mats
    pairs = width // 256
    scale = size ** (-0.5)
    norm_rows(s.x0, s.n1, vec, at["g1"], at["s1"], width)

    def qkv_step(j, carry):
        part = j // pairs
        row = row_at(vec, at["qv"], jnp.where(part == 0, j, jnp.maximum(j - pairs, 0)))
        value = dot(s.n1[...], w_qkv.cols(j)) + jnp.where(part == 1, 0.0, row)
        s.qkv[:, lanes(j)] = (value * jnp.where(part == 0, scale, 1.0)).astype(BF)
        return carry

    w_qkv.need()
    loop(3 * pairs, qkv_step)
    attention(s.qkv, s.probs, s.att, bias, group, groups, width, size)

    def proj_step(j, carry):
        s.x1[:, lanes(j)] = dot(s.att[...], w_proj.cols(j))
        return carry

    w_proj.need()
    loop(pairs, proj_step)
    norm_rows(s.x0, s.n2, vec, at["g2"], at["s2"], width, s.x1, at["bo"])

    def mlp_step(j, carry):
        h = dot(s.n2[...], w_up.cols(j)) + row_at(vec, at["bu"], j)
        s.h[:, lanes(j)] = h
        u = gelu_parts(h)[0].astype(BF)
        update = dot(u, w_down.band(j))

        @pl.when(j == 0)
        def _():
            s.x2[...] = update

        @pl.when(j > 0)
        def _():
            s.x2[...] += update

        return carry

    w_up.need()
    w_down.need()
    loop(hidden // 256, mlp_step)


def block_backward(s, mats, grads, vec, dvec, at, width, hidden, size, group, groups):
    w_qkv, w_proj, w_up, w_down = mats
    d_qkv, d_proj, d_up, d_down = grads
    pairs = width // 256
    s.flip[...] = s.n2[...].T

    def mlp_step(j, carry):
        dxb = s.dxb[...]
        u, slope = gelu_parts(s.h[:, lanes(j)])
        dh = dot_t(dxb, w_down.band(j)) * slope
        put_row_at(dvec, at["bu"], j, total_row(fold(dh)))
        dh = dh.astype(BF)
        d_down.put_band(j, t_dot(u.astype(BF), dxb))
        d_up.put_cols(j, dot(s.flip[...], dh))
        update = dot_t(dh, w_up.cols(j))

        @pl.when(j == 0)
        def _():
            s.dn[...] = update

        @pl.when(j > 0)
        def _():
            s.dn[...] += update

        return carry

    w_down.need()
    w_up.need()
    loop(hidden // 256, mlp_step)
    d_down.done()
    d_up.done()
    norm_back_rows(s.x1, s.dn, s.dx, s.dxb, vec, dvec, at["g2"], at["s2"], width, at["bo"], True)

    def proj_step(j, carry):
        dxb = s.dxb[...]
        s.datt[:, lanes(j)] = dot_t(dxb, w_proj.band(j)).astype(BF)
        d_proj.put_band(j, t_dot(s.att[:, lanes(j)], dxb))
        return carry

    w_proj.need()
    loop(pairs, proj_step)
    d_proj.done()
    attention_back(s.qkv, s.probs, s.datt, s.dqkv, dvec, at["qv"], group, groups, width, size)
    s.flip[...] = s.n1[...].T

    def weight_step(j, carry):
        d_qkv.put_cols(j, dot(s.flip[...], s.dqkv[:, lanes(j)]))
        return carry

    loop(3 * pairs, weight_step)
    d_qkv.done()

    def input_step(j, carry):
        s.dn[:, lanes(j)] = dot_t(s.dqkv[...], w_qkv.band(j))
        return carry

    w_qkv.need()
    loop(pairs, input_step)
    norm_back_rows(s.x0, s.dn, s.dx, s.dxb, vec, dvec, at["g1"], at["s1"], width, None, True)


ENC_AT = dict(g1=EV[2], s1=EV[3], qv=EV[4], bo=EV[5], g2=EV[6], s2=EV[7], bu=EV[8])
DEC_AT = dict(g1=DV[3], s1=DV[4], qv=DV[5], bo=DV[6], g2=DV[7], s2=DV[8], bu=DV[9])


class Bag:
    def __init__(self, names, refs):
        for name, ref in zip(names, refs):
            setattr(self, name, ref)


class Layout:
    def __init__(self, shape, moves, shared):
        self.shape, self.moves, self.shared = shape, moves, shared


def plain_layout(total):
    return Layout((total, 16, 128), [(lambda ref: ref, 0, total)], [])


def slot_layout(plan, shape, lead):
    moves, shared, done = [], [], 0
    for device, (first, count, _) in enumerate(plan):
        skip = max(0, done - first)
        if skip and count:
            shared.append((lambda ref, d=device, n=skip: ref.at[d, pl.ds(lead, n)], first, skip))
        if count:
            moves.append(
                (
                    lambda ref, d=device, a=skip, n=count - skip: ref.at[d, pl.ds(lead + a, n)],
                    first + skip,
                    count - skip,
                )
            )
        done = first + count
    return Layout(shape, moves, shared)


def whole_slots(plan, shape):
    moves = [
        (lambda ref, d=device, n=count: ref.at[d, pl.ds(0, n)], first, count)
        for device, (first, count, _) in enumerate(plan)
        if count
    ]
    return Layout(shape, moves, [])


SHARED = 24


class Loads:
    def __init__(self, source, kept, side, sem, layout, backward=False):
        self.kept, self.side, self.flying = kept, side, []
        moves = list(enumerate(layout.moves))
        for index, (pick, start, count) in moves[::-1] if backward else moves:
            copy = pltpu.make_async_copy(pick(source), kept.at[pl.ds(start, count)], sem.at[index])
            copy.start()
            self.flying.append((start, count, None, copy))
        for index, (pick, start, count) in enumerate(layout.shared):
            copy = pltpu.make_async_copy(
                pick(source),
                side.at[index, pl.ds(0, count)],
                sem.at[len(layout.moves) + index],
            )
            copy.start()
            self.flying.append((start, count, index, copy))

    def need(self, base, tiles):
        here = [f for f in self.flying if f[0] < base + tiles and f[0] + f[1] > base]
        self.flying = [f for f in self.flying if f not in here]
        for item in here:
            item[3].wait()
        for start, count, index, _ in here:
            if index is not None:
                there = pl.ds(start, count)
                both = self.kept[there].astype(F32) + self.side[index, 0:count].astype(F32)
                self.kept[there] = both.astype(BF)


class Stores:
    def __init__(self, kept, out, sem, layout):
        self.kept, self.out, self.sem = kept, out, sem
        self.left, self.ready, self.flying = list(enumerate(layout.moves)), set(), []

    def done(self, base, tiles):
        self.ready.update(range(base, base + tiles))
        for item in list(self.left):
            index, (pick, start, count) = item
            if self.ready.issuperset(range(start, start + count)):
                copy = pltpu.make_async_copy(
                    self.kept.at[pl.ds(start, count)], pick(self.out), self.sem.at[index]
                )
                copy.start()
                self.flying.append(copy)
                self.left.remove(item)

    def finish(self):
        for copy in self.flying:
            copy.wait()


def load_scratch(layout):
    return [
        pltpu.VMEM((max(1, len(layout.shared)), SHARED, 16, 128), BF),
        pltpu.SemaphoreType.DMA((len(layout.moves) + len(layout.shared),)),
    ]


def visible_rows(column, count):
    lane = lax.broadcasted_iota(jnp.int32, (1, count), 1)
    return jnp.where(column == lane, 1.0, 0.0).astype(BF)


def encoder_bias(rows):
    r = lax.broadcasted_iota(jnp.int32, (rows, rows), 0)
    c = lax.broadcasted_iota(jnp.int32, (rows, rows), 1)
    same = (r // ROWS_E == c // ROWS_E) & (c % ROWS_E < VIS)
    return jnp.where(same, 0.0, -1e30)


ENC_KEEP = ["pick", "x0", "n1", "qkv", "probs", "att", "x1", "n2", "h", "x2"]


def enc_shapes(images):
    rows = images * ROWS_E
    return dict(
        pick=((rows, PIX), BF),
        x0=((rows, DE), F32),
        n1=((rows, DE), BF),
        qkv=((rows, 3 * DE), BF),
        probs=((HE, rows, rows), BF),
        att=((rows, DE), BF),
        x1=((rows, DE), F32),
        n2=((rows, DE), BF),
        h=((rows, FE), F32),
        x2=((rows, DE), F32),
    )


def position_column(vec, start, blocks, j):
    return vec[pl.ds(start + j, PATCHES, stride=blocks), :]


def encoder_forward_kernel(images, layout, vis, pix, vec, weights, *refs):
    latent = refs[0]
    s = Bag(ENC_KEEP, refs[1 : 1 + len(ENC_KEEP)])
    kept, posit, side, sem = refs[1 + len(ENC_KEEP) :]
    loads = Loads(weights, kept, side, sem, layout)
    rows = images * ROWS_E
    mats = [Mat(kept, b, shape, loads) for b, shape in zip(ENC_BASE, ENC_MATS)]
    posit[...] = jnp.zeros_like(posit)
    for j in range(DE // 128):
        posit[0:PATCHES, j * 128 : (j + 1) * 128] = position_column(vec, EV[1], DE // 128, j)
    for i in range(images):
        where = pl.ds(i * ROWS_E, ROWS_E)
        hot = visible_rows(vis[where, :], ROWS_D)
        s.pick[where, :] = dot(hot, pix[i]).astype(BF)
        s.x0[where, :] = dot(hot, posit[...].astype(BF)) + row_of(vec, EV[0], DE)
    mats[0].need()

    def embed_step(j, carry):
        s.x0[:, lanes(j)] += dot(s.pick[...], mats[0].cols(j))
        return carry

    loop(DE // 256, embed_step)
    block_forward(
        s, mats[1:5], vec, ENC_AT, DE, FE, DE // HE, encoder_bias(rows), rows, 1
    )
    norm_rows(s.x1, latent, vec, EV[10], EV[11], DE, s.x2, EV[9])


def encoder_forward(images, layout, vis, pix, vec, weights):
    shapes = enc_shapes(images)
    rows = images * ROWS_E
    vm = pl.BlockSpec(memory_space=pltpu.VMEM)
    return pl.pallas_call(
        functools.partial(encoder_forward_kernel, images, layout),
        out_shape=[jax.ShapeDtypeStruct((rows, DE), BF)]
        + [jax.ShapeDtypeStruct(*shapes[name]) for name in ENC_KEEP],
        in_specs=[vm, vm, vm, pl.BlockSpec(memory_space=pl.ANY)],
        out_specs=[vm] * (1 + len(ENC_KEEP)),
        scratch_shapes=[
            pltpu.VMEM((ENC_TOTAL, 16, 128), BF),
            pltpu.VMEM((ROWS_D, DE), F32),
        ]
        + load_scratch(layout),
        name="encoder_forward",
        compiler_params=pltpu.CompilerParams(vmem_limit_bytes=VMEM_LIMIT),
    )(vis, pix, vec, weights)


def encoder_backward_kernel(images, layout, out_layout, vis, vec, dlatent, *refs):
    s = Bag(ENC_KEEP, refs[: len(ENC_KEEP)])
    weights, dmats, dvec = refs[len(ENC_KEEP) : len(ENC_KEEP) + 3]
    kept, dkept, s.dx, s.dxb, s.dn, s.datt, s.dqkv, s.flip, out_sem, side, sem = refs[
        len(ENC_KEEP) + 3 :
    ]
    loads = Loads(weights, kept, side, sem, layout, True)
    stores = Stores(dkept, dmats, out_sem, out_layout)
    rows = images * ROWS_E
    mats = [Mat(kept, b, shape, loads) for b, shape in zip(ENC_BASE, ENC_MATS)]
    grads = [Mat(dkept, b, shape, None, stores) for b, shape in zip(ENC_BASE, ENC_MATS)]
    dvec[EV[11] + DE // 128 :, :] = jnp.zeros_like(dvec[EV[11] + DE // 128 :, :])
    norm_back_rows(
        s.x2, dlatent, s.dx, s.dxb, vec, dvec, EV[10], EV[11], DE, EV[9], False
    )
    block_backward(
        s, mats[1:5], grads[1:5], vec, dvec, ENC_AT, DE, FE, DE // HE, rows, 1
    )
    put_row(dvec, EV[0], jnp.sum(s.dx[...], 0, keepdims=True))

    def embed_step(j, carry):
        grads[0].put_band(j, t_dot(s.pick[:, lanes(j)], s.dxb[...]))
        return carry

    loop(DE // 256, embed_step)
    grads[0].done()
    mats[0].need()
    hot = visible_rows(vis[...], ROWS_D)
    for j in range(DE // 128):
        value = t_dot(hot, s.dxb[:, j * 128 : (j + 1) * 128])
        dvec[pl.ds(EV[1] + j, PATCHES, stride=DE // 128), :] = value[0:PATCHES]
    stores.finish()


def encoder_backward(images, layout, out_layout, vis, vec, dlatent, saved, weights):
    rows = images * ROWS_E
    vm = pl.BlockSpec(memory_space=pltpu.VMEM)
    hbm = pl.BlockSpec(memory_space=pl.ANY)
    return pl.pallas_call(
        functools.partial(encoder_backward_kernel, images, layout, out_layout),
        out_shape=[
            jax.ShapeDtypeStruct(out_layout.shape, BF),
            jax.ShapeDtypeStruct(vec.shape, F32),
        ],
        in_specs=[vm] * (3 + len(ENC_KEEP)) + [hbm],
        out_specs=[hbm, vm],
        scratch_shapes=[
            pltpu.VMEM((ENC_TOTAL, 16, 128), BF),
            pltpu.VMEM((ENC_TOTAL, 16, 128), BF),
            pltpu.VMEM((rows, DE), F32),
            pltpu.VMEM((rows, DE), BF),
            pltpu.VMEM((rows, DE), F32),
            pltpu.VMEM((rows, DE), BF),
            pltpu.VMEM((rows, 3 * DE), BF),
            pltpu.VMEM((DE, rows), BF),
            pltpu.SemaphoreType.DMA((len(out_layout.moves),)),
        ]
        + load_scratch(layout),
        name="encoder_backward",
        compiler_params=pltpu.CompilerParams(vmem_limit_bytes=VMEM_LIMIT),
    )(vis, vec, dlatent, *saved, weights)


def decoder_kernel(images, layout, out_layout, masked_total, latent, places, pix, vec, weights, *refs):
    dlatent, loss, dmats, dvec = refs[:4]
    s = Bag(
        ["x0", "x1", "x2", "n1", "n2", "qkv", "probs", "att", "h", "dx", "dxb", "dn", "dqkv", "flip"],
        refs[4:18],
    )
    kept, dkept, posit, dguess, out_sem, side, sem = refs[18:]
    s.datt = s.n2
    rows = images * ROWS_D
    loads = Loads(weights, kept, side, sem, layout)
    stores = Stores(dkept, dmats, out_sem, out_layout)
    mats = [Mat(kept, b, shape, loads) for b, shape in zip(DEC_BASE, DEC_MATS)]
    grads = [Mat(dkept, b, shape, None, stores) for b, shape in zip(DEC_BASE, DEC_MATS)]
    posit[...] = jnp.zeros_like(posit)
    for j in range(DD // 128):
        posit[0:PATCHES, j * 128 : (j + 1) * 128] = position_column(vec, DV[2], DD // 128, j)
    dvec[DV[13] + PIX // 128 :, :] = jnp.zeros_like(dvec[DV[13] + PIX // 128 :, :])
    mats[0].need()
    for i in range(images):
        part = pl.ds(i * ROWS_E, ROWS_E)
        where = pl.ds(i * ROWS_D, ROWS_D)
        for j in range(DD // 256):
            cut = slice(j * 256, (j + 1) * 256)
            z = dot(latent[part, :], mats[0].cols(j)) + row_of(vec, DV[0] + 2 * j, 256)
            place = places[where, :]
            hot = visible_rows(jnp.where(place < VIS, place, -1), ROWS_E)
            high = z.astype(BF)
            low = (z - high.astype(F32)).astype(BF)
            token = jnp.where(place >= VIS, 1.0, 0.0) * row_of(vec, DV[1] + 2 * j, 256)
            s.x0[where, cut] = dot(hot, high) + dot(hot, low) + token + posit[:, cut]
    lane = lax.broadcasted_iota(jnp.int32, (1, ROWS_D), 1)
    bias = jnp.where(lane < PATCHES, 0.0, -1e30)
    block_forward(
        s, mats[1:5], vec, DEC_AT, DD, FD, DD // HD, bias, ROWS_D, images
    )
    norm_rows(s.x1, s.dxb, vec, DV[11], DV[12], DD, s.x2, DV[10])
    factor = 2.0 / (PIX * masked_total)

    def head_step(j, total):
        value = dot(s.dxb[...], mats[5].cols(j)) + row_at(vec, DV[13], j)
        count = jnp.zeros((8, 256), F32)
        column = jnp.zeros((8, 256), F32)
        for i in range(images):
            where = slice(i * ROWS_D, (i + 1) * ROWS_D)
            error = value[where] - pix[i, :, lanes(j)].astype(F32)
            error = jnp.where(places[where, :] >= VIS, error, 0.0)
            count = count + fold(error * error)
            error = error * factor
            column = column + fold(error)
            dguess[where, lanes(j)] = error.astype(BF)
        put_row_at(dvec, DV[13], j, total_row(column))
        return total + count

    mats[5].need()
    total = loop(PIX // 256, head_step, jnp.zeros((8, 256), F32))
    loss[...] = jnp.broadcast_to(jnp.sum(total) * (1.0 / PIX), (8, 128))
    s.flip[...] = s.dxb[...].T

    def head_weight_step(j, carry):
        grads[5].put_cols(j, dot(s.flip[...], dguess[:, lanes(j)]))
        return carry

    loop(PIX // 256, head_weight_step)
    grads[5].done()

    def head_input_step(j, carry):
        s.dn[:, lanes(j)] = dot_t(dguess[...], mats[5].band(j))
        return carry

    loop(DD // 256, head_input_step)
    norm_back_rows(s.x2, s.dn, s.dx, s.dxb, vec, dvec, DV[11], DV[12], DD, DV[10], False)
    block_backward(
        s, mats[1:5], grads[1:5], vec, dvec, DEC_AT, DD, FD, DD // HD, ROWS_D, images
    )
    token = jnp.zeros((8, DD), F32)
    spot = jnp.zeros((ROWS_D, DD), F32)
    back = []
    for i in range(images):
        where = pl.ds(i * ROWS_D, ROWS_D)
        place = places[where, :]
        dx = s.dx[where, :]
        spot = spot + dx
        token = token + fold(jnp.where(place >= VIS, dx, 0.0))
        hot = visible_rows(jnp.where(place < VIS, place, -1), ROWS_E)
        back.append(t_dot(hot, s.dxb[where, :]))
    posit[...] = spot
    for j in range(DD // 128):
        dvec[pl.ds(DV[2] + j, PATCHES, stride=DD // 128), :] = posit[
            0:PATCHES, j * 128 : (j + 1) * 128
        ]
    put_row(dvec, DV[1], total_row(token))
    back = jnp.concatenate(back, 0)
    put_row(dvec, DV[0], jnp.sum(back, 0, keepdims=True))
    back = back.astype(BF)
    for j in range(DE // 256):
        grads[0].put_band(j, t_dot(latent[:, j * 256 : (j + 1) * 256], back))
        dlatent[:, j * 256 : (j + 1) * 256] = dot_t(back, mats[0].band(j)).astype(BF)
    grads[0].done()
    stores.finish()


def decoder_step(images, layout, out_layout, masked_total, latent, places, pix, vec, weights):
    rows = images * ROWS_D
    vm = pl.BlockSpec(memory_space=pltpu.VMEM)
    hbm = pl.BlockSpec(memory_space=pl.ANY)
    probs = images * HD
    return pl.pallas_call(
        functools.partial(decoder_kernel, images, layout, out_layout, masked_total),
        out_shape=[
            jax.ShapeDtypeStruct((images * ROWS_E, DE), BF),
            jax.ShapeDtypeStruct((8, 128), F32),
            jax.ShapeDtypeStruct(out_layout.shape, BF),
            jax.ShapeDtypeStruct(vec.shape, F32),
        ],
        in_specs=[vm, vm, vm, vm, hbm],
        out_specs=[vm, vm, hbm, vm],
        scratch_shapes=[
            pltpu.VMEM((rows, DD), F32),
            pltpu.VMEM((rows, DD), F32),
            pltpu.VMEM((rows, DD), F32),
            pltpu.VMEM((rows, DD), BF),
            pltpu.VMEM((rows, DD), BF),
            pltpu.VMEM((rows, 3 * DD), BF),
            pltpu.VMEM((probs, ROWS_D, ROWS_D), BF),
            pltpu.VMEM((rows, DD), BF),
            pltpu.VMEM((rows, FD), F32),
            pltpu.VMEM((rows, DD), F32),
            pltpu.VMEM((rows, DD), BF),
            pltpu.VMEM((rows, DD), F32),
            pltpu.VMEM((rows, 3 * DD), BF),
            pltpu.VMEM((DD, rows), BF),
            pltpu.VMEM((DEC_TOTAL, 16, 128), BF),
            pltpu.VMEM((DEC_TOTAL, 16, 128), BF),
            pltpu.VMEM((ROWS_D, DD), F32),
            pltpu.VMEM((rows, PIX), BF),
            pltpu.SemaphoreType.DMA((len(out_layout.moves),)),
        ]
        + load_scratch(layout),
        name="decoder_step",
        compiler_params=pltpu.CompilerParams(vmem_limit_bytes=VMEM_LIMIT),
    )(latent, places, pix, vec, weights)


def natural(flat, shapes):
    pieces, offset = [], 0
    for rows, columns in shapes:
        piece = flat[offset : offset + rows * columns].reshape(rows // 16, 16, columns // 128, 128)
        pieces.append(piece.transpose(0, 2, 1, 3).reshape(-1, 16, 128))
        offset += rows * columns
    return jnp.concatenate(pieces, 0)


def flat_from_natural(tiles, shapes, total):
    pieces, offset = [], 0
    for rows, columns in shapes:
        count = rows * columns // 2048
        piece = tiles[offset : offset + count].reshape(rows // 16, columns // 128, 16, 128)
        pieces.append(piece.transpose(0, 2, 1, 3).reshape(-1))
        offset += count
    flat = jnp.concatenate(pieces)
    return jnp.pad(flat, (0, total - flat.shape[0]))


MESH = pl.DeviceIdType.MESH
DEPTH, WIDTH = 4, 2
SLOT_M, SLOT_V = 264, 5
SLOT = SLOT_M + SLOT_V
PART = ((0, 224), (224, SLOT - 224))
MARGIN = 384
LINES = 3744


def shard_plan(shapes, total, devices):
    lines = total // devices // 128
    plans = []
    for device in range(devices):
        low, high = device * lines, (device + 1) * lines
        first, count, pieces = 0, 0, []
        line, tile = 0, 0
        for rows, columns in shapes:
            blocks = columns // 128
            begin, end = max(low, line), min(high, line + rows * blocks)
            if begin < end:
                top, bottom = (begin - line) // blocks, (end - line) // blocks
                assert top * blocks == begin - line and bottom * blocks == end - line
                up, down = top // 16, -(-bottom // 16)
                if not pieces:
                    first = tile + up * blocks
                pieces.append((blocks, line + up * 16 * blocks - low, down - up, count))
                count += (down - up) * blocks
            line += rows * blocks
            tile += rows * blocks // 16
        plans.append((first, count, pieces))
    return plans


def devices_around(z, y, c, s):
    at = lambda zz, yy, cc: (s, zz * 4 + yy * 2 + cc)
    around = {"side": at(z, 1 - y, c), "core": at(z, y, 1 - c)}
    if z + 1 < DEPTH:
        around["up"] = at(z + 1, y, c)
    if z > 0:
        around["down"] = at(z - 1, y, c)
    return around


def greet(around):
    barrier = pltpu.get_barrier_semaphore()
    for target in around.values():
        pl.semaphore_signal(barrier, inc=1, device_id=target, device_id_type=MESH)
    pl.semaphore_wait(barrier, len(around))


def place():
    d = lax.axis_index("dp")
    return lax.axis_index("section"), d // 4, (d // 2) % 2, d % 2


def for_each_depth(run):
    s, z_now, y, c = place()
    for z in range(DEPTH):
        pl.when(z_now == z)(functools.partial(run, s, z, y, c))


def gather_kernel(own, out, send, recv, local):
    def run(s, z, y, c):
        around = devices_around(z, y, c, s)
        greet(around)
        slot = lambda zz, yy, cc: zz * 4 + yy * 2 + cc
        sent = []

        def at(ref, index, part):
            start, count = PART[part]
            return ref.at[index, pl.ds(start, count)]

        def push(index, part, targets, mine=False):
            start, count = PART[part]
            for name in targets:
                if name not in around:
                    continue
                copy = pltpu.make_async_remote_copy(
                    own.at[pl.ds(start, count)] if mine else at(out, index, part),
                    at(out, index, part),
                    send.at[len(sent)],
                    recv.at[index, part],
                    device_id=around[name],
                    device_id_type=MESH,
                )
                copy.start()
                sent.append(copy)

        def arrive(index, part):
            pltpu.make_async_remote_copy(
                at(out, index, part),
                at(out, index, part),
                send.at[0],
                recv.at[index, part],
                device_id=around["core"],
                device_id_type=MESH,
            ).wait_recv()

        me = slot(z, y, c)
        push(me, 1, ["side"], True)
        push(me, 0, ["up", "down", "side"], True)
        push(me, 1, ["up", "down"], True)
        push(me, 0, ["core"], True)
        push(me, 1, ["core"], True)
        keep = pltpu.make_async_copy(own, out.at[me], local)
        keep.start()
        arrive(slot(z, 1 - y, c), 1)
        push(slot(z, 1 - y, c), 1, ["up", "down", "core"])
        for k in range(1, DEPTH):
            for zz in (z - k, z + k):
                if 0 <= zz < DEPTH:
                    onward = "up" if zz < z else "down"
                    arrive(slot(zz, y, c), 0)
                    push(slot(zz, y, c), 0, [onward, "side", "core"])
                    for yy in (y, 1 - y):
                        arrive(slot(zz, yy, c), 1)
                        push(slot(zz, yy, c), 1, [onward, "core"])
            for zz in sorted({z - k + 1, z + k - 1}):
                if 0 <= zz < DEPTH:
                    arrive(slot(zz, 1 - y, c), 0)
                    push(slot(zz, 1 - y, c), 0, ["core"])
        for zz in (z - DEPTH + 1, z + DEPTH - 1):
            if 0 <= zz < DEPTH:
                arrive(slot(zz, 1 - y, c), 0)
                push(slot(zz, 1 - y, c), 0, ["core"])
        for zz in range(DEPTH):
            for yy in range(WIDTH):
                for part in range(2):
                    arrive(slot(zz, yy, 1 - c), part)
        keep.wait()
        for copy in sent:
            copy.wait_send()

    for_each_depth(run)


def gather_slots(own):
    hbm = pl.BlockSpec(memory_space=pl.ANY)
    return pl.pallas_call(
        gather_kernel,
        out_shape=jax.ShapeDtypeStruct((16, SLOT, 16, 128), BF),
        in_specs=[hbm],
        out_specs=hbm,
        scratch_shapes=[
            pltpu.SemaphoreType.DMA((48,)),
            pltpu.SemaphoreType.DMA((16, 2)),
            pltpu.SemaphoreType.DMA,
        ],
        name="gather_slots",
        compiler_params=pltpu.CompilerParams(collective_id=0, has_side_effects=True),
    )(own)


def send_order(z):
    order = []
    for k in range(DEPTH - 1, -1, -1):
        for zz in (z + k, z - k):
            if 0 <= zz < DEPTH and zz not in order:
                order.append(zz)
    return order


def add_tiles(target, sources, start, count):
    step = 8

    def some(base, size):
        value = sources[0][pl.ds(base, size)].astype(F32)
        for source in sources[1:]:
            value = value + source[pl.ds(base, size)].astype(F32)
        target[pl.ds(base, size)] = value.astype(target.dtype)

    def body(i, carry):
        some(start + i * step, step)
        return carry

    lax.fori_loop(0, count // step, body, 0)
    if count % step:
        some(start + count // step * step, count % step)


class Shifted:
    def __init__(self, ref, start):
        self.ref, self.start = ref, start

    def __getitem__(self, index):
        return self.ref[pl.ds(index.start - self.start, index.size)]


def owned_limits(plans):
    limits = []
    for plan, shapes in zip(plans, (ENC_MATS, DEC_MATS)):
        low = 0
        for _, count, pieces in plan:
            if not pieces:
                limits.append((0, 0, 0, 0, 0))
                continue
            blocks, line, _, _ = pieces[0]
            skip = -line // blocks if line < 0 else 0
            last, line, rows, _ = pieces[-1]
            over = max(0, line + rows * 16 * last - LINES) // last
            limits.append((count, blocks, skip, last, over))
    return limits


def finish_tiles(out, sources, start, count, owned, square):
    tiles, first, skip, last, over = owned
    row = lax.broadcasted_iota(jnp.int32, (1, 16, 1), 1)

    def some(base, size, square):
        value = sources[0][pl.ds(base, size)].astype(F32)
        for source in sources[1:]:
            value = value + source[pl.ds(base, size)].astype(F32)
        out[pl.ds(base, size)] = value
        tile = base - SLOT_V + lax.broadcasted_iota(jnp.int32, (size, 1, 1), 0)
        mine = (tile < tiles) & ((tile >= first) | (row >= skip))
        mine = mine & ((tile < tiles - last) | (row < 16 - over))
        mine = mine | (tile < 0)
        value = jnp.where(mine, value * value, 0.0)
        return square + value.reshape(size * 2, 8, 128).sum(0)

    def body(i, carry):
        return some(start + i * 8, 8, carry)

    square = lax.fori_loop(0, count // 8, body, square)
    if count % 8:
        square = some(start + count // 8 * 8, count % 8, square)
    return square


def scatter_kernel(limits, mats, vecs, loss, out, total, held, core_in, side_a, side_b, z_a, z_b, parts, load, send, r_core, r_side, r_z, r_parts):
    me = lax.axis_index("section") * 16 + lax.axis_index("dp")

    def other(k):
        device = lax.rem(me + k, 32)
        return device, (device // 16, lax.rem(device, 16))

    def run(s, z, y, c):
        around = devices_around(z, y, c, s)
        loads = {}
        order = send_order(z)
        slot = lambda zz, yy, cc: zz * 4 + yy * 2 + cc
        n = 0
        for cc in (1 - c, c):
            for zz in order:
                for yy in (1 - y, y):
                    index = slot(zz, yy, cc)
                    pair = (
                        pltpu.make_async_copy(
                            mats.at[index], held.at[index, pl.ds(SLOT_V, SLOT_M)], load.at[n]
                        ),
                        pltpu.make_async_copy(
                            vecs.at[index], held.at[index, pl.ds(0, SLOT_V)], load.at[16 + n]
                        ),
                    )
                    for copy in pair:
                        copy.start()
                    loads[n] = pair
                    n += 1
        barrier = pltpu.get_barrier_semaphore()
        for k in range(1, 32):
            pl.semaphore_signal(barrier, inc=1, device_id=other(k)[1], device_id_type=MESH)
        pl.semaphore_wait(barrier, 31)
        sent = []

        def remote(source, target, sem, name):
            return pltpu.make_async_remote_copy(
                source,
                target,
                send.at[len(sent)],
                sem,
                device_id=around[name],
                device_id_type=MESH,
            )

        def push(source, target, sem, name):
            copy = remote(source, target, sem, name)
            copy.start()
            sent.append(copy)

        def cut(index, part):
            start, count = PART[part]
            return held.at[index, pl.ds(start, count)]

        def arrive(target, sem):
            pltpu.make_async_remote_copy(
                target, target, send.at[0], sem, device_id=around["core"], device_id_type=MESH
            ).wait_recv()

        n = 0
        for zz in order:
            for yy in (1 - y, y):
                for copy in loads[n]:
                    copy.wait()
                push(
                    held.at[slot(zz, yy, 1 - c)],
                    core_in.at[zz * 2 + yy],
                    r_core.at[zz * 2 + yy],
                    "core",
                )
                n += 1
        ready = set()

        def prepare(zz, flip):
            if (zz, flip) in ready:
                return
            ready.add((zz, flip))
            yy = 1 - y if flip else y
            for copy in loads[8 + order.index(zz) * 2 + (0 if flip else 1)]:
                copy.wait()
            arrive(core_in.at[zz * 2 + yy], r_core.at[zz * 2 + yy])

        def z_in(part, way, zz, yy):
            if part == 0:
                return z_a.at[way, zz], r_z.at[way, zz, 2]
            return z_b.at[way, zz, yy], r_z.at[way, zz, yy]

        def side_sources(zz, yy):
            return [held.at[slot(zz, yy, c)], core_in.at[zz * 2 + yy]]

        for zz in order:
            prepare(zz, True)
            index = slot(zz, 1 - y, c)
            add_tiles(held.at[index], side_sources(zz, 1 - y), *PART[0])
            push(cut(index, 0), side_a.at[zz], r_side.at[zz], "side")

        def along(part, zz, flip):
            yy = 1 - y if flip else y
            prepare(zz, flip)
            index = slot(zz, yy, c)
            way, name, first = (0, "up", 0) if zz > z else (1, "down", DEPTH - 1)
            sources = side_sources(zz, yy)
            if part == 0:
                arrive(side_a.at[zz], r_side.at[zz])
                sources.append(side_a.at[zz])
            if z != first:
                ref, sem = z_in(part, way, zz, yy)
                arrive(ref, sem)
                sources.append(ref if part == 0 else Shifted(ref, PART[1][0]))
            add_tiles(held.at[index], sources, *PART[part])
            ref, sem = z_in(part, way, zz, yy)
            push(cut(index, part), ref, sem, name)

        def gathered(part, yy):
            found = []
            for way, here in ((0, z > 0), (1, z < DEPTH - 1)):
                if here:
                    ref, sem = z_in(part, way, z, yy)
                    arrive(ref, sem)
                    found.append(ref if part == 0 else Shifted(ref, PART[1][0]))
            return found

        for zz in order[:-1]:
            along(1, zz, True)
            along(1, zz, False)
        prepare(z, False)
        index = slot(z, 1 - y, c)
        add_tiles(held.at[index], side_sources(z, 1 - y) + gathered(1, 1 - y), *PART[1])
        push(cut(index, 1), side_b, r_side.at[DEPTH], "side")
        for zz in order[:-1]:
            along(0, zz, False)
        arrive(side_b, r_side.at[DEPTH])
        owned = [sum(jnp.where(me == k, row[n], 0) for k, row in enumerate(limits)) for n in range(5)]
        square = finish_tiles(
            out,
            side_sources(z, y) + gathered(1, y) + [Shifted(side_b, PART[1][0])],
            *PART[1],
            owned,
            jnp.zeros((8, 128), F32),
        )
        arrive(side_a.at[z], r_side.at[z])
        square = finish_tiles(
            out,
            side_sources(z, y) + [side_a.at[z]] + gathered(0, y),
            *PART[0],
            owned,
            square,
        )
        row = lax.broadcasted_iota(jnp.int32, (8, 128), 0)
        parts[me] = jnp.where(row == 0, jnp.sum(square), loss[...])
        for copy in sent:
            copy.wait_send()

    for_each_depth(run)
    copies = []
    for k in range(1, 32):
        copy = pltpu.make_async_remote_copy(
            parts.at[me],
            parts.at[me],
            send.at[k],
            r_parts.at[me],
            device_id=other(k)[1],
            device_id_type=MESH,
        )
        copy.start()
        copies.append(copy)
    for k in range(1, 32):
        device, where = other(k)
        pltpu.make_async_remote_copy(
            parts.at[device],
            parts.at[device],
            send.at[k],
            r_parts.at[device],
            device_id=where,
            device_id_type=MESH,
        ).wait_recv()
    total[...] = jnp.sum(parts[...], 0)
    for copy in copies:
        copy.wait_send()


def scatter_slots(limits, mats, vecs, loss):
    hbm = pl.BlockSpec(memory_space=pl.ANY)
    tail = PART[1][1]
    return pl.pallas_call(
        functools.partial(scatter_kernel, limits),
        out_shape=[
            jax.ShapeDtypeStruct((SLOT, 16, 128), F32),
            jax.ShapeDtypeStruct((8, 128), F32),
        ],
        in_specs=[hbm, hbm, pl.BlockSpec(memory_space=pltpu.VMEM)],
        out_specs=[pl.BlockSpec(memory_space=pltpu.VMEM)] * 2,
        scratch_shapes=[
            pltpu.VMEM((16, SLOT, 16, 128), BF),
            pltpu.VMEM((8, SLOT, 16, 128), BF),
            pltpu.VMEM((DEPTH, PART[0][1], 16, 128), BF),
            pltpu.VMEM((tail, 16, 128), BF),
            pltpu.VMEM((2, DEPTH, PART[0][1], 16, 128), BF),
            pltpu.VMEM((2, DEPTH, 2, tail, 16, 128), BF),
            pltpu.VMEM((32, 8, 128), F32),
            pltpu.SemaphoreType.DMA((32,)),
            pltpu.SemaphoreType.DMA((32,)),
            pltpu.SemaphoreType.DMA((8,)),
            pltpu.SemaphoreType.DMA((DEPTH + 1,)),
            pltpu.SemaphoreType.DMA((2, DEPTH, 3)),
            pltpu.SemaphoreType.DMA((32,)),
        ],
        name="scatter_slots",
        compiler_params=pltpu.CompilerParams(
            collective_id=1, has_side_effects=True, vmem_limit_bytes=VMEM_LIMIT
        ),
    )(mats, vecs, loss)


def piece_table(lines):
    plans = [shard_plan(m, lines * 128 * 16, 16) for m in (ENC_MATS, DEC_MATS)]
    most = max(len(pieces) for plan in plans for _, _, pieces in plan)
    table = [
        [[list(p) for p in pieces] + [[0] * 4] * (most - len(pieces)) for _, _, pieces in plan]
        for plan in plans
    ]
    widths = sorted({p[0] for plan in plans for _, _, pieces in plan for p in pieces})
    return plans, table, widths


def each_tile(table, widths, run):
    for piece in range(table.shape[0]):
        for width in widths:

            @pl.when(table[piece, 0] == width)
            def _(piece=piece, width=width):
                def step(i, carry):
                    for j in range(width):
                        line = MARGIN + table[piece, 1] + i * (16 * width) + j
                        run(line, width, SLOT_V + table[piece, 3] + i * width + j)
                    return carry

                lax.fori_loop(0, table[piece, 2], step, 0)


def pack_kernel(widths, table, mat, vec, out, lines, sem):
    count = mat.shape[0]
    copy = pltpu.make_async_copy(mat, lines.at[pl.ds(MARGIN, count)], sem)
    copy.start()
    lines[0:MARGIN, :] = jnp.zeros((MARGIN, 128), F32)
    lines[MARGIN + count :, :] = jnp.zeros((MARGIN, 128), F32)
    out[0:SLOT_V] = vec[...].astype(BF).reshape(SLOT_V, 16, 128)
    copy.wait()

    def run(line, width, tile):
        out[tile] = lines[pl.ds(line, 16, stride=width), :].astype(BF)

    each_tile(table, widths, run)


def pack(table, widths, mat, vec):
    vm = pl.BlockSpec(memory_space=pltpu.VMEM)
    return pl.pallas_call(
        functools.partial(pack_kernel, widths),
        out_shape=jax.ShapeDtypeStruct((SLOT, 16, 128), BF),
        in_specs=[
            pl.BlockSpec(memory_space=pltpu.SMEM),
            pl.BlockSpec(memory_space=pl.ANY),
            vm,
        ],
        out_specs=vm,
        scratch_shapes=[
            pltpu.VMEM((mat.shape[0] + 2 * MARGIN, 128), F32),
            pltpu.SemaphoreType.DMA,
        ],
        name="pack",
        compiler_params=pltpu.CompilerParams(vmem_limit_bytes=VMEM_LIMIT),
    )(table, mat, vec)


def clip_factor(square):
    return jnp.minimum(1.0, 0.001 / (jnp.sqrt(square) + 1e-06))


def adam_update(master, first, second, grad, rate, decay):
    first = 0.9 * first + 0.1 * grad
    second = 0.95 * second + 0.05 * grad * grad
    step_first = first / (1.0 - 0.9**STEP)
    step_second = second / (1.0 - 0.95**STEP)
    master = master - rate * (step_first / (jnp.sqrt(step_second) + 1e-08) + decay * master)
    return (master, first, second)


STEPS = 6


def update_kernel(widths, table, tiles, total, *refs):
    states, news, news_vec, (lines, held, fresh, sem_in, sem_out) = (
        refs[0:3],
        refs[3:6],
        refs[6],
        refs[7:],
    )
    count = held.shape[1]
    size = count // STEPS

    def part(i):
        return pl.ds(i * size, size)

    loads = [
        [
            pltpu.make_async_copy(state.at[part(i)], held.at[n, part(i)], sem_in.at[n, i])
            for n, state in enumerate(states)
        ]
        for i in range(STEPS)
    ]
    for step in loads:
        for copy in step:
            copy.start()
    lines[...] = jnp.zeros_like(lines)

    def run(line, width, tile):
        lines[pl.ds(line, 16, stride=width), :] = tiles[tile]

    each_tile(table, widths, run)
    news_vec[...] = tiles[0:SLOT_V].reshape(SLOT_V * 16, 128)
    factor = clip_factor(total[0:1, :])
    stores = []
    for i in range(STEPS):
        for copy in loads[i]:
            copy.wait()

        def body(k, carry, i=i):
            base = i * size + k * 104
            rows = pl.ds(pl.multiple_of(base, 8), 104)
            grad = factor * lines[pl.ds(pl.multiple_of(MARGIN + base, 8), 104), :]
            for n, value in enumerate(
                adam_update(held[0, rows, :], held[1, rows, :], held[2, rows, :], grad, 0.05, 0.05)
            ):
                fresh[n, rows, :] = value
            return carry

        lax.fori_loop(0, size // 104, body, 0)
        for n, new in enumerate(news):
            copy = pltpu.make_async_copy(fresh.at[n, part(i)], new.at[part(i)], sem_out.at[n, i])
            copy.start()
            stores.append(copy)
    for copy in stores:
        copy.wait()


def update(table, widths, tiles, total, states):
    count = states[0].shape[0]
    vm = pl.BlockSpec(memory_space=pltpu.VMEM)
    hbm = pl.BlockSpec(memory_space=pl.ANY)
    shape = jax.ShapeDtypeStruct((count, 128), F32)
    return pl.pallas_call(
        functools.partial(update_kernel, widths),
        out_shape=[shape] * 3 + [jax.ShapeDtypeStruct((SLOT_V * 16, 128), F32)],
        in_specs=[pl.BlockSpec(memory_space=pltpu.SMEM), vm, vm] + [hbm] * 3,
        out_specs=[hbm] * 3 + [vm],
        scratch_shapes=[
            pltpu.VMEM((count + 2 * MARGIN, 128), F32),
            pltpu.VMEM((3, count, 128), F32),
            pltpu.VMEM((3, count, 128), F32),
            pltpu.SemaphoreType.DMA((3, STEPS)),
            pltpu.SemaphoreType.DMA((3, STEPS)),
        ],
        name="update",
        compiler_params=pltpu.CompilerParams(vmem_limit_bytes=VMEM_LIMIT),
    )(table, tiles, total, *states)


def shifted(value, axis, steps):
    count = lax.axis_size(axis)
    initial, last = (max(0, -steps), min(count, count - steps))
    return lax.ppermute(value, axis, [(source, source + steps) for source in range(initial, last)])


def train(images, masked_total, enc, dec, enc_out, dec_out, pixels, visible, restore, vecs, weights):
    encoding = lax.axis_index("section") == 0
    pix = jnp.pad(pixels, ((0, 0), (0, ROWS_D - PATCHES), (0, 0)))
    vis = jnp.pad(visible, ((0, 0), (0, ROWS_E - VIS)), constant_values=-1).reshape(-1, 1)
    places = jnp.pad(restore, ((0, 0), (0, ROWS_D - PATCHES)), constant_values=-1).reshape(-1, 1)
    blank_saved = [jnp.zeros(*item) for item in enc_shapes(images).values()]
    blank_latent = jnp.zeros((images * ROWS_E, DE), BF)
    latent, *saved = lax.cond(
        encoding,
        lambda: list(encoder_forward(images, enc, vis, pix, vecs, weights)),
        lambda: [blank_latent] + blank_saved,
    )
    arrived = shifted(latent, "section", 1)
    dlatent, loss, dmats, dvec = lax.cond(
        encoding,
        lambda: [
            blank_latent,
            jnp.zeros((8, 128), F32),
            jnp.zeros(dec_out.shape, BF),
            jnp.zeros(vecs.shape, F32),
        ],
        lambda: list(
            decoder_step(
                images, dec, dec_out, masked_total, arrived, places, pix, vecs, weights
            )
        ),
    )
    returned = shifted(dlatent, "section", -1)
    if dec_out.shape == enc_out.shape:
        other = lambda: [dmats, dvec]
    else:
        more = enc_out.shape[0] - dec_out.shape[0]
        other = lambda: [jnp.pad(dmats, ((0, more), (0, 0), (0, 0))), dvec]
    dmats, dvec = lax.cond(
        encoding,
        lambda: list(
            encoder_backward(images, enc, enc_out, vis, vecs, returned, saved, weights)
        ),
        other,
    )
    return dmats, dvec, loss


def body_block(
    pixels, visible, restore, mat_master, mat_first, mat_second, vec_master, vec_first, vec_second
):
    images = pixels.shape[0]
    masked_total = (PATCHES - VIS) * images * 16
    count, size = mat_master.shape[1] // 128, vec_master.shape[1]
    plans, table, widths = piece_table(count)
    table = jnp.asarray(table, jnp.int32)[lax.axis_index("section"), lax.axis_index("dp")]
    lines = [value.reshape(count, 128) for value in (mat_master, mat_first, mat_second)]
    room = SLOT_V * 2048
    own = pack(
        table, widths, lines[0], jnp.pad(vec_master[0], (0, room - size)).reshape(-1, 128)
    )
    slots = gather_slots(own)
    vecs = slots[:, :SLOT_V].reshape(16, room)[:, :size].reshape(-1, 128).astype(F32)
    inward = [slot_layout(plan, slots.shape, SLOT_V) for plan in plans]
    outward = [whole_slots(plan, (16, SLOT_M, 16, 128)) for plan in plans]
    dmats, dvec, loss = train(
        images, masked_total, *inward, *outward, pixels, visible, restore, vecs, slots
    )
    dvec = jnp.pad(dvec.reshape(16, size), ((0, 0), (0, room - size))).astype(BF)
    tiles, total = scatter_slots(
        owned_limits(plans), dmats, dvec.reshape(16, SLOT_V, 16, 128), loss
    )
    *news, grad_vec = update(table, widths, tiles, total, lines)
    news = [value.reshape(mat_master.shape) for value in news]
    square, loss_sum = total[0, 0], total[1, 0]
    vec_news = adam_update(
        vec_master,
        vec_first,
        vec_second,
        clip_factor(square) * grad_vec.reshape(1, room)[:, :size],
        0.3,
        0.0,
    )
    return (
        (loss_sum, jnp.sqrt(square))
        + tuple(news)
        + (news[0].astype(BF),)
        + tuple(vec_news)
        + (vec_news[0].astype(BF),)
    )


def body(
    pixels, visible, restore, mat_master, mat_first, mat_second, vec_master, vec_first, vec_second
):
    images = pixels.shape[0]
    total = mat_master.shape[1] * lax.axis_size("dp")
    masked_total = (PATCHES - VIS) * images * lax.axis_size("dp")
    encoding = lax.axis_index("section") == 0
    enc, dec = plain_layout(ENC_TOTAL), plain_layout(DEC_TOTAL)
    mats = lax.all_gather(mat_master.astype(BF), "dp", axis=1, tiled=True)[0]
    vecs = lax.all_gather(vec_master.astype(BF), "dp", axis=1, tiled=True)[0]
    vecs = vecs.astype(F32).reshape(-1, 128)
    weights = lax.cond(
        encoding,
        lambda m: natural(m, ENC_MATS),
        lambda m: jnp.pad(natural(m, DEC_MATS), ((0, ENC_TOTAL - DEC_TOTAL), (0, 0), (0, 0))),
        mats,
    )
    dec_in = Layout((ENC_TOTAL, 16, 128), [(lambda ref: ref.at[pl.ds(0, DEC_TOTAL)], 0, DEC_TOTAL)], [])
    dmats, grad_vecs, loss = train(
        images, masked_total, enc, dec_in, enc, dec, pixels, visible, restore, vecs, weights
    )
    grad_mats = lax.cond(
        encoding,
        lambda m: flat_from_natural(m.astype(F32), ENC_MATS, total),
        lambda m: flat_from_natural(m[0:DEC_TOTAL].astype(F32), DEC_MATS, total),
        dmats,
    )
    summed_mats = lax.psum_scatter(grad_mats[None], "dp", scatter_dimension=1, tiled=True)
    summed_vecs = lax.psum_scatter(
        grad_vecs.reshape(1, -1), "dp", scatter_dimension=1, tiled=True
    )
    square = jnp.sum(summed_mats * summed_mats) + jnp.sum(summed_vecs * summed_vecs)
    square, loss_sum = lax.psum((square, loss[0, 0]), ("section", "dp"))
    factor = clip_factor(square)
    mat_news = adam_update(mat_master, mat_first, mat_second, factor * summed_mats, 0.05, 0.05)
    vec_news = adam_update(vec_master, vec_first, vec_second, factor * summed_vecs, 0.3, 0.0)
    return (
        (loss_sum, jnp.sqrt(square))
        + tuple(mat_news)
        + (mat_news[0].astype(BF),)
        + tuple(vec_news)
        + (vec_news[0].astype(BF),)
    )


def solution(mesh):
    split = P("section", "dp")
    fits = mesh.shape["section"] == 2 and mesh.shape["dp"] == 16
    return jax.shard_map(
        body_block if fits else body,
        mesh=mesh,
        in_specs=(P("dp", None, None), P("dp", None), P("dp", None)) + (split,) * 6,
        out_specs=(P(), P()) + (split,) * 8,
        check_vma=False,
    )
```

```python
import functools
import math

import jax
import jax.numpy as jnp
from jax import lax
from jax.experimental import pallas as pl
from jax.experimental.pallas import tpu as pltpu
from jax.sharding import PartitionSpec as P

PIX = 768
DE = 768
HE = 12
FE = 3072
DD = 512
HD = 16
FD = 2048
PATCHES = 196
VIS = 49
STEP = 10
ROWS_E = 64
ROWS_D = 208
EPS = 1e-6
BF = jnp.bfloat16
F32 = jnp.float32
VMEM_LIMIT = 63 * 1024 * 1024

ENC_MATS = [(PIX, DE), (DE, 3 * DE), (DE, DE), (DE, FE), (FE, DE)]
DEC_MATS = [(DE, DD), (DD, 3 * DD), (DD, DD), (DD, FD), (FD, DD), (DD, PIX)]
ENC_VECS = [DE, PATCHES * DE, DE, DE, 2 * DE, DE, DE, DE, FE, DE, DE, DE]
DEC_VECS = [DD, DD, PATCHES * DD, DD, DD, 2 * DD, DD, DD, DD, FD, DD, DD, DD, PIX]


def starts(sizes):
    total, found = 0, []
    for size in sizes:
        found.append(total)
        total += size
    return found, total


ENC_TILES = [k * n // 2048 for k, n in ENC_MATS]
DEC_TILES = [k * n // 2048 for k, n in DEC_MATS]
ENC_BASE, ENC_TOTAL = starts(ENC_TILES)
DEC_BASE, DEC_TOTAL = starts(DEC_TILES)
EV, _ = starts([size // 128 for size in ENC_VECS])
DV, _ = starts([size // 128 for size in DEC_VECS])


class Mat:
    def __init__(self, ref, base, shape, loads=None, stores=None):
        self.base, self.loads, self.stores = base, loads, stores
        self.rows, self.columns = shape
        self.blocks = self.columns // 128
        count = self.rows * self.columns // 2048
        self.ref = ref.at[pl.ds(base, count)].reshape(self.rows // 16, self.blocks, 16, 128)

    def need(self):
        self.loads.need(self.base, self.rows * self.columns // 2048)

    def done(self):
        self.stores.done(self.base, self.rows * self.columns // 2048)

    def cols(self, block):
        parts = [self.ref[:, 2 * block + half].reshape(self.rows, 128) for half in range(2)]
        return jnp.concatenate(parts, 1)

    def band(self, block):
        part = self.ref.at[pl.ds(block * 16, 16)]
        return jnp.concatenate([part[:, j].reshape(256, 128) for j in range(self.blocks)], 1)

    def put_cols(self, block, value):
        for half in range(2):
            piece = value[:, half * 128 : (half + 1) * 128].astype(BF)
            self.ref[:, 2 * block + half] = piece.reshape(self.rows // 16, 16, 128)

    def put_band(self, block, value):
        part = self.ref.at[pl.ds(block * 16, 16)]
        for j in range(self.blocks):
            part[:, j] = value[:, j * 128 : (j + 1) * 128].astype(BF).reshape(16, 16, 128)


def dot(a, b):
    return jnp.dot(a, b, preferred_element_type=F32)


def dot_t(a, b):
    return lax.dot_general(a, b, (((1,), (1,)), ((), ())), preferred_element_type=F32)


def t_dot(a, b):
    return lax.dot_general(a, b, (((0,), (0,)), ((), ())), preferred_element_type=F32)


def loop(count, body, init=0):
    return lax.fori_loop(0, count, body, init)


def lanes(block, width=256):
    return pl.ds(pl.multiple_of(block * width, width), width)


def row_of(vec, start, width):
    return jnp.concatenate([vec[start + j : start + j + 1, :] for j in range(width // 128)], 1)


def row_at(vec, start, block):
    return jnp.concatenate([vec[pl.ds(start + 2 * block + h, 1), :] for h in range(2)], 1)


def put_row(dvec, start, value):
    for j in range(value.shape[1] // 128):
        dvec[start + j : start + j + 1, :] = value[:, j * 128 : (j + 1) * 128]


def put_row_at(dvec, start, block, value):
    for h in range(2):
        dvec[pl.ds(start + 2 * block + h, 1), :] = value[:, h * 128 : (h + 1) * 128]


def fold(value):
    return value.reshape(value.shape[0] // 8, 8, value.shape[1]).sum(0)


def total_row(value):
    return jnp.sum(value, 0, keepdims=True)


def norm_parts(x):
    mean = jnp.mean(x, -1, keepdims=True)
    centred = x - mean
    scale = lax.rsqrt(jnp.mean(centred * centred, -1, keepdims=True) + EPS)
    return centred * scale, scale


CHUNKS = (208, 128, 64, 32)


def chunk_loop(ref, step, init=0):
    count = ref.shape[0]
    size = next(c for c in CHUNKS if count % c == 0)

    def run(i, carry):
        return step(pl.ds(pl.multiple_of(i * size, size), size), carry)

    return lax.fori_loop(0, count // size, run, init)


def norm_rows(x_ref, out_ref, vec, gain_at, shift_at, width, add_ref=None, bias_at=None):
    gain, shift = row_of(vec, gain_at, width), row_of(vec, shift_at, width)
    bias = None if bias_at is None else row_of(vec, bias_at, width)

    def step(rows, carry):
        x = x_ref[rows, :]
        if add_ref is not None:
            x = x + add_ref[rows, :] + bias
            add_ref[rows, :] = x
        unit, _ = norm_parts(x)
        out_ref[rows, :] = (unit * gain + shift).astype(BF)
        return carry

    chunk_loop(x_ref, step)


def norm_back_rows(x_ref, dy_ref, dx_ref, dxb_ref, vec, dvec, gain_at, shift_at, width, bias_at, add):
    gain = row_of(vec, gain_at, width)
    zero = jnp.zeros((8, width), F32)

    def step(rows, carry):
        dgain, dshift, dbias = carry
        unit, scale = norm_parts(x_ref[rows, :])
        dy = dy_ref[rows, :].astype(F32)
        dunit = dy * gain
        dx = scale * (
            dunit
            - jnp.mean(dunit, -1, keepdims=True)
            - unit * jnp.mean(dunit * unit, -1, keepdims=True)
        )
        if add:
            dx = dx + dx_ref[rows, :]
        dx_ref[rows, :] = dx
        dxb_ref[rows, :] = dx.astype(BF)
        return dgain + fold(dy * unit), dshift + fold(dy), dbias + fold(dx)

    dgain, dshift, dbias = chunk_loop(x_ref, step, (zero, zero, zero))
    put_row(dvec, gain_at, total_row(dgain))
    put_row(dvec, shift_at, total_row(dshift))
    if bias_at is not None:
        put_row(dvec, bias_at, total_row(dbias))
    return dbias


GELU_C = math.sqrt(2.0 / math.pi)


def gelu_parts(x):
    square = x * x
    t = jnp.tanh(x * (GELU_C + (GELU_C * 0.044715) * square))
    half = 0.5 * (1.0 + t)
    return x * half, half + (0.5 * x) * (1.0 - t * t) * (
        GELU_C + (3.0 * 0.044715 * GELU_C) * square
    )


def head_mask(size):
    lane = lax.broadcasted_iota(jnp.int32, (1, 128), 1)
    return [(lane >= h * size) & (lane < (h + 1) * size) for h in range(128 // size)]


def attention(qkv, probs, att, bias, group, groups, width, size):
    blocks = width // 128
    masks = head_mask(size)

    def step(i, carry):
        g, b = i // blocks, i % blocks
        rows = pl.ds(pl.multiple_of(g * group, 16), group)
        q = qkv[rows, lanes(b, 128)]
        k = qkv[rows, lanes(blocks + b, 128)]
        v = qkv[rows, lanes(2 * blocks + b, 128)]
        out = jnp.zeros((group, 128), F32)
        for h, mask in enumerate(masks):
            s = dot_t(jnp.where(mask, q, jnp.zeros_like(q)), k) + bias
            e = jnp.exp(s - jnp.max(s, -1, keepdims=True))
            p = (e * (1.0 / jnp.sum(e, -1, keepdims=True))).astype(BF)
            probs[i * len(masks) + h] = p
            out = jnp.where(mask, dot(p, v), out)
        att[rows, lanes(b, 128)] = out.astype(BF)
        return carry

    lax.fori_loop(0, groups * blocks, step, 0, unroll=4 if groups * blocks % 4 == 0 else 2)


def attention_back(qkv, probs, datt, dqkv, dvec, qv_at, group, groups, width, size):
    blocks = width // 128
    masks = head_mask(size)
    scale = size ** (-0.5)
    for j in range(2 * blocks):
        dvec[qv_at + j : qv_at + j + 1, :] = jnp.zeros((1, 128), F32)

    def step(i, carry):
        g, b = i // blocks, i % blocks
        rows = pl.ds(pl.multiple_of(g * group, 16), group)
        q = qkv[rows, lanes(b, 128)]
        k = qkv[rows, lanes(blocks + b, 128)]
        v = qkv[rows, lanes(2 * blocks + b, 128)]
        da = datt[rows, lanes(b, 128)]
        zero = jnp.zeros((group, 128), F32)
        dq, dk, dv = zero, zero, zero
        for h, mask in enumerate(masks):
            p = probs[i * len(masks) + h]
            dp = dot_t(jnp.where(mask, da, jnp.zeros_like(da)), v)
            wide = p.astype(F32)
            prod = wide * dp
            ds = (prod - wide * jnp.sum(prod, -1, keepdims=True)).astype(BF)
            dq = jnp.where(mask, dot(ds, k), dq)
            dk = jnp.where(mask, t_dot(ds, q), dk)
            dv = jnp.where(mask, t_dot(p, da), dv)
        dq = dq * scale
        dqkv[rows, lanes(b, 128)] = dq.astype(BF)
        dqkv[rows, lanes(blocks + b, 128)] = dk.astype(BF)
        dqkv[rows, lanes(2 * blocks + b, 128)] = dv.astype(BF)
        dvec[pl.ds(qv_at + b, 1), :] += total_row(dq)
        dvec[pl.ds(qv_at + blocks + b, 1), :] += total_row(dv)
        return carry

    lax.fori_loop(0, groups * blocks, step, 0, unroll=2)


def block_forward(s, mats, vec, at, width, hidden, size, bias, group, groups):
    w_qkv, w_proj, w_up, w_down = mats
    pairs = width // 256
    scale = size ** (-0.5)
    norm_rows(s.x0, s.n1, vec, at["g1"], at["s1"], width)

    def qkv_step(j, carry):
        part = j // pairs
        row = row_at(vec, at["qv"], jnp.where(part == 0, j, jnp.maximum(j - pairs, 0)))
        value = dot(s.n1[...], w_qkv.cols(j)) + jnp.where(part == 1, 0.0, row)
        s.qkv[:, lanes(j)] = (value * jnp.where(part == 0, scale, 1.0)).astype(BF)
        return carry

    w_qkv.need()
    loop(3 * pairs, qkv_step)
    attention(s.qkv, s.probs, s.att, bias, group, groups, width, size)

    def proj_step(j, carry):
        s.x1[:, lanes(j)] = dot(s.att[...], w_proj.cols(j))
        return carry

    w_proj.need()
    loop(pairs, proj_step)
    norm_rows(s.x0, s.n2, vec, at["g2"], at["s2"], width, s.x1, at["bo"])

    def mlp_step(j, carry):
        h = dot(s.n2[...], w_up.cols(j)) + row_at(vec, at["bu"], j)
        s.h[:, lanes(j)] = h
        u = gelu_parts(h)[0].astype(BF)
        update = dot(u, w_down.band(j))

        @pl.when(j == 0)
        def _():
            s.x2[...] = update

        @pl.when(j > 0)
        def _():
            s.x2[...] += update

        return carry

    w_up.need()
    w_down.need()
    loop(hidden // 256, mlp_step)


def block_backward(s, mats, grads, vec, dvec, at, width, hidden, size, group, groups):
    w_qkv, w_proj, w_up, w_down = mats
    d_qkv, d_proj, d_up, d_down = grads
    pairs = width // 256
    s.flip[...] = s.n2[...].T

    def mlp_step(j, carry):
        dxb = s.dxb[...]
        u, slope = gelu_parts(s.h[:, lanes(j)])
        dh = dot_t(dxb, w_down.band(j)) * slope
        put_row_at(dvec, at["bu"], j, total_row(fold(dh)))
        dh = dh.astype(BF)
        d_down.put_band(j, t_dot(u.astype(BF), dxb))
        d_up.put_cols(j, dot(s.flip[...], dh))
        update = dot_t(dh, w_up.cols(j))

        @pl.when(j == 0)
        def _():
            s.dn[...] = update

        @pl.when(j > 0)
        def _():
            s.dn[...] += update

        return carry

    w_down.need()
    w_up.need()
    loop(hidden // 256, mlp_step)
    d_down.done()
    d_up.done()
    norm_back_rows(s.x1, s.dn, s.dx, s.dxb, vec, dvec, at["g2"], at["s2"], width, at["bo"], True)

    def proj_step(j, carry):
        dxb = s.dxb[...]
        s.datt[:, lanes(j)] = dot_t(dxb, w_proj.band(j)).astype(BF)
        d_proj.put_band(j, t_dot(s.att[:, lanes(j)], dxb))
        return carry

    w_proj.need()
    loop(pairs, proj_step)
    d_proj.done()
    attention_back(s.qkv, s.probs, s.datt, s.dqkv, dvec, at["qv"], group, groups, width, size)
    s.flip[...] = s.n1[...].T

    def weight_step(j, carry):
        d_qkv.put_cols(j, dot(s.flip[...], s.dqkv[:, lanes(j)]))
        return carry

    loop(3 * pairs, weight_step)
    d_qkv.done()

    def input_step(j, carry):
        s.dn[:, lanes(j)] = dot_t(s.dqkv[...], w_qkv.band(j))
        return carry

    w_qkv.need()
    loop(pairs, input_step)
    norm_back_rows(s.x0, s.dn, s.dx, s.dxb, vec, dvec, at["g1"], at["s1"], width, None, True)


ENC_AT = dict(g1=EV[2], s1=EV[3], qv=EV[4], bo=EV[5], g2=EV[6], s2=EV[7], bu=EV[8])
DEC_AT = dict(g1=DV[3], s1=DV[4], qv=DV[5], bo=DV[6], g2=DV[7], s2=DV[8], bu=DV[9])


class Bag:
    def __init__(self, names, refs):
        for name, ref in zip(names, refs):
            setattr(self, name, ref)


class Layout:
    def __init__(self, shape, moves, shared):
        self.shape, self.moves, self.shared = shape, moves, shared


def plain_layout(total):
    return Layout((total, 16, 128), [(lambda ref: ref, 0, total)], [])


def slot_layout(plan, shape, lead):
    moves, shared, done = [], [], 0
    for device, (first, count, _) in enumerate(plan):
        skip = max(0, done - first)
        if skip and count:
            shared.append((lambda ref, d=device, n=skip: ref.at[d, pl.ds(lead, n)], first, skip))
        if count:
            moves.append(
                (
                    lambda ref, d=device, a=skip, n=count - skip: ref.at[d, pl.ds(lead + a, n)],
                    first + skip,
                    count - skip,
                )
            )
        done = first + count
    return Layout(shape, moves, shared)


def whole_slots(plan, shape):
    moves = [
        (lambda ref, d=device, n=count: ref.at[d, pl.ds(0, n)], first, count)
        for device, (first, count, _) in enumerate(plan)
        if count
    ]
    return Layout(shape, moves, [])


SHARED = 24


class Loads:
    def __init__(self, source, kept, side, sem, layout, backward=False):
        self.kept, self.side, self.flying = kept, side, []
        moves = list(enumerate(layout.moves))
        for index, (pick, start, count) in moves[::-1] if backward else moves:
            copy = pltpu.make_async_copy(pick(source), kept.at[pl.ds(start, count)], sem.at[index])
            copy.start()
            self.flying.append((start, count, None, copy))
        for index, (pick, start, count) in enumerate(layout.shared):
            copy = pltpu.make_async_copy(
                pick(source),
                side.at[index, pl.ds(0, count)],
                sem.at[len(layout.moves) + index],
            )
            copy.start()
            self.flying.append((start, count, index, copy))

    def need(self, base, tiles):
        here = [f for f in self.flying if f[0] < base + tiles and f[0] + f[1] > base]
        self.flying = [f for f in self.flying if f not in here]
        for item in here:
            item[3].wait()
        for start, count, index, _ in here:
            if index is not None:
                there = pl.ds(start, count)
                both = self.kept[there].astype(F32) + self.side[index, 0:count].astype(F32)
                self.kept[there] = both.astype(BF)


class Stores:
    def __init__(self, kept, out, sem, layout):
        self.kept, self.out, self.sem = kept, out, sem
        self.left, self.ready, self.flying = list(enumerate(layout.moves)), set(), []

    def done(self, base, tiles):
        self.ready.update(range(base, base + tiles))
        for item in list(self.left):
            index, (pick, start, count) = item
            if self.ready.issuperset(range(start, start + count)):
                copy = pltpu.make_async_copy(
                    self.kept.at[pl.ds(start, count)], pick(self.out), self.sem.at[index]
                )
                copy.start()
                self.flying.append(copy)
                self.left.remove(item)

    def finish(self):
        for copy in self.flying:
            copy.wait()


def load_scratch(layout):
    return [
        pltpu.VMEM((max(1, len(layout.shared)), SHARED, 16, 128), BF),
        pltpu.SemaphoreType.DMA((len(layout.moves) + len(layout.shared),)),
    ]


def visible_rows(column, count):
    lane = lax.broadcasted_iota(jnp.int32, (1, count), 1)
    return jnp.where(column == lane, 1.0, 0.0).astype(BF)


def encoder_bias(rows):
    r = lax.broadcasted_iota(jnp.int32, (rows, rows), 0)
    c = lax.broadcasted_iota(jnp.int32, (rows, rows), 1)
    same = (r // ROWS_E == c // ROWS_E) & (c % ROWS_E < VIS)
    return jnp.where(same, 0.0, -1e30)


ENC_KEEP = ["pick", "x0", "n1", "qkv", "probs", "att", "x1", "n2", "h", "x2"]


def enc_shapes(images):
    rows = images * ROWS_E
    return dict(
        pick=((rows, PIX), BF),
        x0=((rows, DE), F32),
        n1=((rows, DE), BF),
        qkv=((rows, 3 * DE), BF),
        probs=((HE, rows, rows), BF),
        att=((rows, DE), BF),
        x1=((rows, DE), F32),
        n2=((rows, DE), BF),
        h=((rows, FE), F32),
        x2=((rows, DE), F32),
    )


def position_column(vec, start, blocks, j):
    return vec[pl.ds(start + j, PATCHES, stride=blocks), :]


def encoder_forward_kernel(images, layout, vis, pix, vec, weights, *refs):
    latent = refs[0]
    s = Bag(ENC_KEEP, refs[1 : 1 + len(ENC_KEEP)])
    kept, posit, side, sem = refs[1 + len(ENC_KEEP) :]
    loads = Loads(weights, kept, side, sem, layout)
    rows = images * ROWS_E
    mats = [Mat(kept, b, shape, loads) for b, shape in zip(ENC_BASE, ENC_MATS)]
    posit[...] = jnp.zeros_like(posit)
    for j in range(DE // 128):
        posit[0:PATCHES, j * 128 : (j + 1) * 128] = position_column(vec, EV[1], DE // 128, j)
    for i in range(images):
        where = pl.ds(i * ROWS_E, ROWS_E)
        hot = visible_rows(vis[where, :], ROWS_D)
        s.pick[where, :] = dot(hot, pix[i]).astype(BF)
        s.x0[where, :] = dot(hot, posit[...].astype(BF)) + row_of(vec, EV[0], DE)
    mats[0].need()

    def embed_step(j, carry):
        s.x0[:, lanes(j)] += dot(s.pick[...], mats[0].cols(j))
        return carry

    loop(DE // 256, embed_step)
    block_forward(
        s, mats[1:5], vec, ENC_AT, DE, FE, DE // HE, encoder_bias(rows), rows, 1
    )
    norm_rows(s.x1, latent, vec, EV[10], EV[11], DE, s.x2, EV[9])


def encoder_forward(images, layout, vis, pix, vec, weights):
    shapes = enc_shapes(images)
    rows = images * ROWS_E
    vm = pl.BlockSpec(memory_space=pltpu.VMEM)
    return pl.pallas_call(
        functools.partial(encoder_forward_kernel, images, layout),
        out_shape=[jax.ShapeDtypeStruct((rows, DE), BF)]
        + [jax.ShapeDtypeStruct(*shapes[name]) for name in ENC_KEEP],
        in_specs=[vm, vm, vm, pl.BlockSpec(memory_space=pl.ANY)],
        out_specs=[vm] * (1 + len(ENC_KEEP)),
        scratch_shapes=[
            pltpu.VMEM((ENC_TOTAL, 16, 128), BF),
            pltpu.VMEM((ROWS_D, DE), F32),
        ]
        + load_scratch(layout),
        name="encoder_forward",
        compiler_params=pltpu.CompilerParams(vmem_limit_bytes=VMEM_LIMIT),
    )(vis, pix, vec, weights)


def encoder_backward_kernel(images, layout, out_layout, vis, vec, dlatent, *refs):
    s = Bag(ENC_KEEP, refs[: len(ENC_KEEP)])
    weights, dmats, dvec = refs[len(ENC_KEEP) : len(ENC_KEEP) + 3]
    kept, dkept, s.dx, s.dxb, s.dn, s.datt, s.dqkv, s.flip, out_sem, side, sem = refs[
        len(ENC_KEEP) + 3 :
    ]
    loads = Loads(weights, kept, side, sem, layout, True)
    stores = Stores(dkept, dmats, out_sem, out_layout)
    rows = images * ROWS_E
    mats = [Mat(kept, b, shape, loads) for b, shape in zip(ENC_BASE, ENC_MATS)]
    grads = [Mat(dkept, b, shape, None, stores) for b, shape in zip(ENC_BASE, ENC_MATS)]
    dvec[EV[11] + DE // 128 :, :] = jnp.zeros_like(dvec[EV[11] + DE // 128 :, :])
    norm_back_rows(
        s.x2, dlatent, s.dx, s.dxb, vec, dvec, EV[10], EV[11], DE, EV[9], False
    )
    block_backward(
        s, mats[1:5], grads[1:5], vec, dvec, ENC_AT, DE, FE, DE // HE, rows, 1
    )
    put_row(dvec, EV[0], jnp.sum(s.dx[...], 0, keepdims=True))

    def embed_step(j, carry):
        grads[0].put_band(j, t_dot(s.pick[:, lanes(j)], s.dxb[...]))
        return carry

    loop(DE // 256, embed_step)
    grads[0].done()
    mats[0].need()
    hot = visible_rows(vis[...], ROWS_D)
    for j in range(DE // 128):
        value = t_dot(hot, s.dxb[:, j * 128 : (j + 1) * 128])
        dvec[pl.ds(EV[1] + j, PATCHES, stride=DE // 128), :] = value[0:PATCHES]
    stores.finish()


def encoder_backward(images, layout, out_layout, vis, vec, dlatent, saved, weights):
    rows = images * ROWS_E
    vm = pl.BlockSpec(memory_space=pltpu.VMEM)
    hbm = pl.BlockSpec(memory_space=pl.ANY)
    return pl.pallas_call(
        functools.partial(encoder_backward_kernel, images, layout, out_layout),
        out_shape=[
            jax.ShapeDtypeStruct(out_layout.shape, BF),
            jax.ShapeDtypeStruct(vec.shape, F32),
        ],
        in_specs=[vm] * (3 + len(ENC_KEEP)) + [hbm],
        out_specs=[hbm, vm],
        scratch_shapes=[
            pltpu.VMEM((ENC_TOTAL, 16, 128), BF),
            pltpu.VMEM((ENC_TOTAL, 16, 128), BF),
            pltpu.VMEM((rows, DE), F32),
            pltpu.VMEM((rows, DE), BF),
            pltpu.VMEM((rows, DE), F32),
            pltpu.VMEM((rows, DE), BF),
            pltpu.VMEM((rows, 3 * DE), BF),
            pltpu.VMEM((DE, rows), BF),
            pltpu.SemaphoreType.DMA((len(out_layout.moves),)),
        ]
        + load_scratch(layout),
        name="encoder_backward",
        compiler_params=pltpu.CompilerParams(vmem_limit_bytes=VMEM_LIMIT),
    )(vis, vec, dlatent, *saved, weights)


def decoder_kernel(images, layout, out_layout, masked_total, latent, places, pix, vec, weights, *refs):
    dlatent, loss, dmats, dvec = refs[:4]
    s = Bag(
        ["x0", "x1", "x2", "n1", "n2", "qkv", "probs", "att", "h", "dx", "dxb", "dn", "dqkv", "flip"],
        refs[4:18],
    )
    kept, dkept, posit, dguess, out_sem, side, sem = refs[18:]
    s.datt = s.n2
    rows = images * ROWS_D
    loads = Loads(weights, kept, side, sem, layout)
    stores = Stores(dkept, dmats, out_sem, out_layout)
    mats = [Mat(kept, b, shape, loads) for b, shape in zip(DEC_BASE, DEC_MATS)]
    grads = [Mat(dkept, b, shape, None, stores) for b, shape in zip(DEC_BASE, DEC_MATS)]
    posit[...] = jnp.zeros_like(posit)
    for j in range(DD // 128):
        posit[0:PATCHES, j * 128 : (j + 1) * 128] = position_column(vec, DV[2], DD // 128, j)
    dvec[DV[13] + PIX // 128 :, :] = jnp.zeros_like(dvec[DV[13] + PIX // 128 :, :])
    mats[0].need()
    for i in range(images):
        part = pl.ds(i * ROWS_E, ROWS_E)
        where = pl.ds(i * ROWS_D, ROWS_D)
        for j in range(DD // 256):
            cut = slice(j * 256, (j + 1) * 256)
            z = dot(latent[part, :], mats[0].cols(j)) + row_of(vec, DV[0] + 2 * j, 256)
            place = places[where, :]
            hot = visible_rows(jnp.where(place < VIS, place, -1), ROWS_E)
            high = z.astype(BF)
            low = (z - high.astype(F32)).astype(BF)
            token = jnp.where(place >= VIS, 1.0, 0.0) * row_of(vec, DV[1] + 2 * j, 256)
            s.x0[where, cut] = dot(hot, high) + dot(hot, low) + token + posit[:, cut]
    lane = lax.broadcasted_iota(jnp.int32, (1, ROWS_D), 1)
    bias = jnp.where(lane < PATCHES, 0.0, -1e30)
    block_forward(
        s, mats[1:5], vec, DEC_AT, DD, FD, DD // HD, bias, ROWS_D, images
    )
    norm_rows(s.x1, s.dxb, vec, DV[11], DV[12], DD, s.x2, DV[10])
    factor = 2.0 / (PIX * masked_total)

    def head_step(j, total):
        value = dot(s.dxb[...], mats[5].cols(j)) + row_at(vec, DV[13], j)
        count = jnp.zeros((8, 256), F32)
        column = jnp.zeros((8, 256), F32)
        for i in range(images):
            where = slice(i * ROWS_D, (i + 1) * ROWS_D)
            error = value[where] - pix[i, :, lanes(j)].astype(F32)
            error = jnp.where(places[where, :] >= VIS, error, 0.0)
            count = count + fold(error * error)
            error = error * factor
            column = column + fold(error)
            dguess[where, lanes(j)] = error.astype(BF)
        put_row_at(dvec, DV[13], j, total_row(column))
        return total + count

    mats[5].need()
    total = loop(PIX // 256, head_step, jnp.zeros((8, 256), F32))
    loss[...] = jnp.broadcast_to(jnp.sum(total) * (1.0 / PIX), (8, 128))
    s.flip[...] = s.dxb[...].T

    def head_weight_step(j, carry):
        grads[5].put_cols(j, dot(s.flip[...], dguess[:, lanes(j)]))
        return carry

    loop(PIX // 256, head_weight_step)
    grads[5].done()

    def head_input_step(j, carry):
        s.dn[:, lanes(j)] = dot_t(dguess[...], mats[5].band(j))
        return carry

    loop(DD // 256, head_input_step)
    norm_back_rows(s.x2, s.dn, s.dx, s.dxb, vec, dvec, DV[11], DV[12], DD, DV[10], False)
    block_backward(
        s, mats[1:5], grads[1:5], vec, dvec, DEC_AT, DD, FD, DD // HD, ROWS_D, images
    )
    token = jnp.zeros((8, DD), F32)
    spot = jnp.zeros((ROWS_D, DD), F32)
    back = []
    for i in range(images):
        where = pl.ds(i * ROWS_D, ROWS_D)
        place = places[where, :]
        dx = s.dx[where, :]
        spot = spot + dx
        token = token + fold(jnp.where(place >= VIS, dx, 0.0))
        hot = visible_rows(jnp.where(place < VIS, place, -1), ROWS_E)
        back.append(t_dot(hot, s.dxb[where, :]))
    posit[...] = spot
    for j in range(DD // 128):
        dvec[pl.ds(DV[2] + j, PATCHES, stride=DD // 128), :] = posit[
            0:PATCHES, j * 128 : (j + 1) * 128
        ]
    put_row(dvec, DV[1], total_row(token))
    back = jnp.concatenate(back, 0)
    put_row(dvec, DV[0], jnp.sum(back, 0, keepdims=True))
    back = back.astype(BF)
    for j in range(DE // 256):
        grads[0].put_band(j, t_dot(latent[:, j * 256 : (j + 1) * 256], back))
        dlatent[:, j * 256 : (j + 1) * 256] = dot_t(back, mats[0].band(j)).astype(BF)
    grads[0].done()
    stores.finish()


def decoder_step(images, layout, out_layout, masked_total, latent, places, pix, vec, weights):
    rows = images * ROWS_D
    vm = pl.BlockSpec(memory_space=pltpu.VMEM)
    hbm = pl.BlockSpec(memory_space=pl.ANY)
    probs = images * HD
    return pl.pallas_call(
        functools.partial(decoder_kernel, images, layout, out_layout, masked_total),
        out_shape=[
            jax.ShapeDtypeStruct((images * ROWS_E, DE), BF),
            jax.ShapeDtypeStruct((8, 128), F32),
            jax.ShapeDtypeStruct(out_layout.shape, BF),
            jax.ShapeDtypeStruct(vec.shape, F32),
        ],
        in_specs=[vm, vm, vm, vm, hbm],
        out_specs=[vm, vm, hbm, vm],
        scratch_shapes=[
            pltpu.VMEM((rows, DD), F32),
            pltpu.VMEM((rows, DD), F32),
            pltpu.VMEM((rows, DD), F32),
            pltpu.VMEM((rows, DD), BF),
            pltpu.VMEM((rows, DD), BF),
            pltpu.VMEM((rows, 3 * DD), BF),
            pltpu.VMEM((probs, ROWS_D, ROWS_D), BF),
            pltpu.VMEM((rows, DD), BF),
            pltpu.VMEM((rows, FD), F32),
            pltpu.VMEM((rows, DD), F32),
            pltpu.VMEM((rows, DD), BF),
            pltpu.VMEM((rows, DD), F32),
            pltpu.VMEM((rows, 3 * DD), BF),
            pltpu.VMEM((DD, rows), BF),
            pltpu.VMEM((DEC_TOTAL, 16, 128), BF),
            pltpu.VMEM((DEC_TOTAL, 16, 128), BF),
            pltpu.VMEM((ROWS_D, DD), F32),
            pltpu.VMEM((rows, PIX), BF),
            pltpu.SemaphoreType.DMA((len(out_layout.moves),)),
        ]
        + load_scratch(layout),
        name="decoder_step",
        compiler_params=pltpu.CompilerParams(vmem_limit_bytes=VMEM_LIMIT),
    )(latent, places, pix, vec, weights)


def natural(flat, shapes):
    pieces, offset = [], 0
    for rows, columns in shapes:
        piece = flat[offset : offset + rows * columns].reshape(rows // 16, 16, columns // 128, 128)
        pieces.append(piece.transpose(0, 2, 1, 3).reshape(-1, 16, 128))
        offset += rows * columns
    return jnp.concatenate(pieces, 0)


def flat_from_natural(tiles, shapes, total):
    pieces, offset = [], 0
    for rows, columns in shapes:
        count = rows * columns // 2048
        piece = tiles[offset : offset + count].reshape(rows // 16, columns // 128, 16, 128)
        pieces.append(piece.transpose(0, 2, 1, 3).reshape(-1))
        offset += count
    flat = jnp.concatenate(pieces)
    return jnp.pad(flat, (0, total - flat.shape[0]))


MESH = pl.DeviceIdType.MESH
DEPTH, WIDTH = 4, 2
SLOT_M, SLOT_V = 264, 5
SLOT = SLOT_M + SLOT_V
SIZES = (249, 261, 269, 239)
FIRST_Z = 4
PARTS = FIRST_Z + 1


def cut_of(depth, part):
    size = SIZES[depth]
    tail = size // 6
    if part == FIRST_Z:
        return size - tail, tail
    low, high = ((size - tail) * n // FIRST_Z for n in (part, part + 1))
    return low, high - low


MOST = max(SIZES[z] - SIZES[z] // 6 for z in range(DEPTH))
TAIL = max(SIZES[z] // 6 for z in range(DEPTH))
MARGIN = 384
LINES = 3744


def shard_plan(shapes, total, devices):
    lines = total // devices // 128
    plans = []
    for device in range(devices):
        low, high = device * lines, (device + 1) * lines
        first, count, pieces = 0, 0, []
        line, tile = 0, 0
        for rows, columns in shapes:
            blocks = columns // 128
            begin, end = max(low, line), min(high, line + rows * blocks)
            if begin < end:
                top, bottom = (begin - line) // blocks, (end - line) // blocks
                assert top * blocks == begin - line and bottom * blocks == end - line
                up, down = top // 16, -(-bottom // 16)
                if not pieces:
                    first = tile + up * blocks
                pieces.append((blocks, line + up * 16 * blocks - low, down - up, count))
                count += (down - up) * blocks
            line += rows * blocks
            tile += rows * blocks // 16
        plans.append((first, count, pieces))
    return plans


def devices_around(z, y, c, s):
    at = lambda zz, yy, cc: (s, zz * 4 + yy * 2 + cc)
    around = {"side": at(z, 1 - y, c), "core": at(z, y, 1 - c)}
    if z + 1 < DEPTH:
        around["up"] = at(z + 1, y, c)
    if z > 0:
        around["down"] = at(z - 1, y, c)
    return around


def greet(around):
    barrier = pltpu.get_barrier_semaphore()
    for target in around.values():
        pl.semaphore_signal(barrier, inc=1, device_id=target, device_id_type=MESH)
    pl.semaphore_wait(barrier, len(around))


def place():
    d = lax.axis_index("dp")
    return lax.axis_index("section"), d // 4, (d // 2) % 2, d % 2


def for_each_depth(run):
    s, z_now, y, c = place()
    for z in range(DEPTH):
        pl.when(z_now == z)(functools.partial(run, s, z, y, c))


def gather_kernel(own, out, send, recv, local):
    def run(s, z, y, c):
        around = devices_around(z, y, c, s)
        greet(around)
        sent = []

        def slot(zz, yy, cc):
            return zz * 4 + yy * 2 + cc

        def at(zz, yy, cc, part):
            return out.at[slot(zz, yy, cc), pl.ds(*cut_of(zz, part))]

        def push(zz, yy, part, targets, mine=False):
            target = at(zz, yy, c, part)
            for name in targets:
                if name not in around:
                    continue
                copy = pltpu.make_async_remote_copy(
                    own.at[pl.ds(*cut_of(z, part))] if mine else target,
                    target,
                    send.at[len(sent)],
                    recv.at[slot(zz, yy, c), part],
                    device_id=around[name],
                    device_id_type=MESH,
                )
                copy.start()
                sent.append(copy)

        def arrive(zz, yy, cc, part):
            target = at(zz, yy, cc, part)
            pltpu.make_async_remote_copy(
                target,
                target,
                send.at[0],
                recv.at[slot(zz, yy, cc), part],
                device_id=around["core"],
                device_id_type=MESH,
            ).wait_recv()

        tail = FIRST_Z
        push(z, y, tail, ["side"], True)
        for part in range(FIRST_Z):
            push(z, y, part, ["up", "down", "side"], True)
        push(z, y, tail, ["up", "down"], True)
        for part in range(PARTS):
            push(z, y, part, ["core"], True)
        keep = pltpu.make_async_copy(own, out.at[slot(z, y, c)], local)
        keep.start()
        arrive(z, 1 - y, c, tail)
        push(z, 1 - y, tail, ["up", "down", "core"])
        waiting = [z]
        for k in range(1, DEPTH + 1):
            near = [zz for zz in (z - k, z + k) if 0 <= zz < DEPTH]
            for part in range(FIRST_Z):
                for zz in near:
                    arrive(zz, y, c, part)
                    push(zz, y, part, ["up" if zz < z else "down", "side", "core"])
            for zz in near:
                for yy in (y, 1 - y):
                    arrive(zz, yy, c, tail)
                    push(zz, yy, tail, ["up" if zz < z else "down", "core"])
            for part in range(FIRST_Z):
                for zz in waiting:
                    arrive(zz, 1 - y, c, part)
                    push(zz, 1 - y, part, ["core"])
            waiting = near
        for zz in range(DEPTH):
            for yy in range(WIDTH):
                for part in range(PARTS):
                    arrive(zz, yy, 1 - c, part)
        keep.wait()
        for copy in sent:
            copy.wait_send()

    for_each_depth(run)


def gather_slots(own):
    hbm = pl.BlockSpec(memory_space=pl.ANY)
    return pl.pallas_call(
        gather_kernel,
        out_shape=jax.ShapeDtypeStruct((16, SLOT, 16, 128), BF),
        in_specs=[hbm],
        out_specs=hbm,
        scratch_shapes=[
            pltpu.SemaphoreType.DMA((128,)),
            pltpu.SemaphoreType.DMA((16, PARTS)),
            pltpu.SemaphoreType.DMA,
        ],
        name="gather_slots",
        compiler_params=pltpu.CompilerParams(collective_id=0, has_side_effects=True),
    )(own)


def send_order(z):
    order = []
    for k in range(DEPTH - 1, -1, -1):
        for zz in (z + k, z - k):
            if 0 <= zz < DEPTH and zz not in order:
                order.append(zz)
    return order


def add_tiles(target, sources, start, count):
    step = 8

    def some(base, size):
        value = sources[0][pl.ds(base, size)].astype(F32)
        for source in sources[1:]:
            value = value + source[pl.ds(base, size)].astype(F32)
        target[pl.ds(base, size)] = value.astype(target.dtype)

    def body(i, carry):
        some(start + i * step, step)
        return carry

    lax.fori_loop(0, count // step, body, 0)
    if count % step:
        some(start + count // step * step, count % step)


class Shifted:
    def __init__(self, ref, start):
        self.ref, self.start = ref, start

    def __getitem__(self, index):
        return self.ref[pl.ds(index.start - self.start, index.size)]


def owned_limits(plans):
    limits = []
    for plan, shapes in zip(plans, (ENC_MATS, DEC_MATS)):
        low = 0
        for _, count, pieces in plan:
            if not pieces:
                limits.append((0, 0, 0, 0, 0))
                continue
            blocks, line, _, _ = pieces[0]
            skip = -line // blocks if line < 0 else 0
            last, line, rows, _ = pieces[-1]
            over = max(0, line + rows * 16 * last - LINES) // last
            limits.append((count, blocks, skip, last, over))
    return limits


def finish_tiles(out, sources, start, count, owned, square):
    tiles, first, skip, last, over = owned
    row = lax.broadcasted_iota(jnp.int32, (1, 16, 1), 1)

    def some(base, size, square):
        value = sources[0][pl.ds(base, size)].astype(F32)
        for source in sources[1:]:
            value = value + source[pl.ds(base, size)].astype(F32)
        out[pl.ds(base, size)] = value
        tile = base - SLOT_V + lax.broadcasted_iota(jnp.int32, (size, 1, 1), 0)
        mine = (tile < tiles) & ((tile >= first) | (row >= skip))
        mine = mine & ((tile < tiles - last) | (row < 16 - over))
        mine = mine | (tile < 0)
        value = jnp.where(mine, value * value, 0.0)
        return square + value.reshape(size * 2, 8, 128).sum(0)

    def body(i, carry):
        return some(start + i * 8, 8, carry)

    square = lax.fori_loop(0, count // 8, body, square)
    if count % 8:
        square = some(start + count // 8 * 8, count % 8, square)
    return square


def scatter_kernel(limits, mats, vecs, loss, out, total, held, core_in, side_a, side_b, z_a, z_b, parts, load, send, r_core, r_side, r_z, r_parts):
    me = lax.axis_index("section") * 16 + lax.axis_index("dp")

    def other(k):
        device = lax.rem(me + k, 32)
        return device, (device // 16, lax.rem(device, 16))

    def run(s, z, y, c):
        around = devices_around(z, y, c, s)
        loads = {}
        order = send_order(z)
        slot = lambda zz, yy, cc: zz * 4 + yy * 2 + cc
        n = 0
        for cc in (1 - c, c):
            for zz in order:
                for yy in (1 - y, y):
                    index = slot(zz, yy, cc)
                    pair = (
                        pltpu.make_async_copy(
                            mats.at[index], held.at[index, pl.ds(SLOT_V, SLOT_M)], load.at[n]
                        ),
                        pltpu.make_async_copy(
                            vecs.at[index], held.at[index, pl.ds(0, SLOT_V)], load.at[16 + n]
                        ),
                    )
                    for copy in pair:
                        copy.start()
                    loads[n] = pair
                    n += 1
        barrier = pltpu.get_barrier_semaphore()
        for k in range(1, 32):
            pl.semaphore_signal(barrier, inc=1, device_id=other(k)[1], device_id_type=MESH)
        pl.semaphore_wait(barrier, 31)
        sent = []

        def remote(source, target, sem, name):
            return pltpu.make_async_remote_copy(
                source,
                target,
                send.at[len(sent)],
                sem,
                device_id=around[name],
                device_id_type=MESH,
            )

        def push(source, target, sem, name):
            copy = remote(source, target, sem, name)
            copy.start()
            sent.append(copy)

        def cut(zz, yy, part):
            return held.at[slot(zz, yy, c), pl.ds(*cut_of(zz, part))]

        def arrive(target, sem):
            pltpu.make_async_remote_copy(
                target, target, send.at[0], sem, device_id=around["core"], device_id_type=MESH
            ).wait_recv()

        n = 0
        for zz in order:
            for yy in (1 - y, y):
                for copy in loads[n]:
                    copy.wait()
                push(
                    held.at[slot(zz, yy, 1 - c), pl.ds(0, SIZES[zz])],
                    core_in.at[zz * 2 + yy, pl.ds(0, SIZES[zz])],
                    r_core.at[zz * 2 + yy],
                    "core",
                )
                n += 1
        ready = set()

        def prepare(zz, flip):
            if (zz, flip) in ready:
                return
            ready.add((zz, flip))
            yy = 1 - y if flip else y
            for copy in loads[8 + order.index(zz) * 2 + (0 if flip else 1)]:
                copy.wait()
            arrive(core_in.at[zz * 2 + yy, pl.ds(0, SIZES[zz])], r_core.at[zz * 2 + yy])

        tail = FIRST_Z

        def z_in(part, way, zz, yy):
            start, count = cut_of(zz, part)
            if part < tail:
                return z_a.at[way, zz, pl.ds(start, count)], r_z.at[way, zz, part]
            return z_b.at[way, zz, yy, pl.ds(0, count)], r_z.at[way, zz, tail + yy]

        def side_in(zz, part):
            start, count = cut_of(zz, part)
            if part < tail:
                return side_a.at[zz, pl.ds(start, count)], r_side.at[zz, part]
            return side_b.at[pl.ds(0, count)], r_side.at[zz, tail]

        def came(zz, part, pair):
            arrive(*pair)
            return Shifted(pair[0], cut_of(zz, part)[0])

        def core_sources(zz, yy):
            return [held.at[slot(zz, yy, c)], core_in.at[zz * 2 + yy]]

        def along(part, zz, flip):
            yy = 1 - y if flip else y
            prepare(zz, flip)
            way, name, first = (0, "up", 0) if zz > z else (1, "down", DEPTH - 1)
            sources = core_sources(zz, yy)
            if part < tail:
                sources.append(came(zz, part, side_in(zz, part)))
            if z != first:
                sources.append(came(zz, part, z_in(part, way, zz, yy)))
            add_tiles(held.at[slot(zz, yy, c)], sources, *cut_of(zz, part))
            push(cut(zz, yy, part), *z_in(part, way, zz, yy), name)

        def gathered(part, yy):
            return [
                came(z, part, z_in(part, way, z, yy))
                for way, here in ((0, z > 0), (1, z < DEPTH - 1))
                if here
            ]

        for zz in order:
            prepare(zz, True)
            for part in range(tail):
                add_tiles(held.at[slot(zz, 1 - y, c)], core_sources(zz, 1 - y), *cut_of(zz, part))
                push(cut(zz, 1 - y, part), *side_in(zz, part), "side")
            if zz != z:
                along(tail, zz, True)
                along(tail, zz, False)
        prepare(z, False)
        add_tiles(
            held.at[slot(z, 1 - y, c)],
            core_sources(z, 1 - y) + gathered(tail, 1 - y),
            *cut_of(z, tail),
        )
        push(cut(z, 1 - y, tail), *side_in(z, tail), "side")
        for zz in order[:-1]:
            for part in range(tail):
                along(part, zz, False)
        owned = [sum(jnp.where(me == k, row[n], 0) for k, row in enumerate(limits)) for n in range(5)]
        square = jnp.zeros((8, 128), F32)
        for part in (tail,) + tuple(range(tail)):
            sources = core_sources(z, y) + gathered(part, y)
            sources.append(came(z, part, side_in(z, part)))
            square = finish_tiles(out, sources, *cut_of(z, part), owned, square)
        row = lax.broadcasted_iota(jnp.int32, (8, 128), 0)
        parts[me] = jnp.where(row == 0, jnp.sum(square), loss[...])
        for copy in sent:
            copy.wait_send()

    for_each_depth(run)
    copies = []
    for k in range(1, 32):
        copy = pltpu.make_async_remote_copy(
            parts.at[me],
            parts.at[me],
            send.at[k],
            r_parts.at[me],
            device_id=other(k)[1],
            device_id_type=MESH,
        )
        copy.start()
        copies.append(copy)
    for k in range(1, 32):
        device, where = other(k)
        pltpu.make_async_remote_copy(
            parts.at[device],
            parts.at[device],
            send.at[k],
            r_parts.at[device],
            device_id=where,
            device_id_type=MESH,
        ).wait_recv()
    total[...] = jnp.sum(parts[...], 0)
    for copy in copies:
        copy.wait_send()


def scatter_slots(limits, mats, vecs, loss):
    hbm = pl.BlockSpec(memory_space=pl.ANY)
    return pl.pallas_call(
        functools.partial(scatter_kernel, limits),
        out_shape=[
            jax.ShapeDtypeStruct((SLOT, 16, 128), F32),
            jax.ShapeDtypeStruct((8, 128), F32),
        ],
        in_specs=[hbm, hbm, pl.BlockSpec(memory_space=pltpu.VMEM)],
        out_specs=[pl.BlockSpec(memory_space=pltpu.VMEM)] * 2,
        scratch_shapes=[
            pltpu.VMEM((16, SLOT, 16, 128), BF),
            pltpu.VMEM((8, SLOT, 16, 128), BF),
            pltpu.VMEM((DEPTH, MOST, 16, 128), BF),
            pltpu.VMEM((TAIL, 16, 128), BF),
            pltpu.VMEM((2, DEPTH, MOST, 16, 128), BF),
            pltpu.VMEM((2, DEPTH, 2, TAIL, 16, 128), BF),
            pltpu.VMEM((32, 8, 128), F32),
            pltpu.SemaphoreType.DMA((32,)),
            pltpu.SemaphoreType.DMA((64,)),
            pltpu.SemaphoreType.DMA((8,)),
            pltpu.SemaphoreType.DMA((DEPTH, PARTS)),
            pltpu.SemaphoreType.DMA((2, DEPTH, PARTS + 1)),
            pltpu.SemaphoreType.DMA((32,)),
        ],
        name="scatter_slots",
        compiler_params=pltpu.CompilerParams(
            collective_id=1, has_side_effects=True, vmem_limit_bytes=VMEM_LIMIT
        ),
    )(mats, vecs, loss)


def piece_table(lines):
    plans = [shard_plan(m, lines * 128 * 16, 16) for m in (ENC_MATS, DEC_MATS)]
    most = max(len(pieces) for plan in plans for _, _, pieces in plan)
    table = [
        [[list(p) for p in pieces] + [[0] * 4] * (most - len(pieces)) for _, _, pieces in plan]
        for plan in plans
    ]
    widths = sorted({p[0] for plan in plans for _, _, pieces in plan for p in pieces})
    return plans, table, widths


def each_tile(table, widths, run):
    for piece in range(table.shape[0]):
        for width in widths:

            @pl.when(table[piece, 0] == width)
            def _(piece=piece, width=width):
                def step(i, carry):
                    for j in range(width):
                        line = MARGIN + table[piece, 1] + i * (16 * width) + j
                        run(line, width, SLOT_V + table[piece, 3] + i * width + j)
                    return carry

                lax.fori_loop(0, table[piece, 2], step, 0)


def pack_kernel(widths, table, mat, vec, out, lines, sem):
    count = mat.shape[0]
    copy = pltpu.make_async_copy(mat, lines.at[pl.ds(MARGIN, count)], sem)
    copy.start()
    lines[0:MARGIN, :] = jnp.zeros((MARGIN, 128), F32)
    lines[MARGIN + count :, :] = jnp.zeros((MARGIN, 128), F32)
    out[0:SLOT_V] = vec[...].astype(BF).reshape(SLOT_V, 16, 128)
    copy.wait()

    def run(line, width, tile):
        out[tile] = lines[pl.ds(line, 16, stride=width), :].astype(BF)

    each_tile(table, widths, run)


def pack(table, widths, mat, vec):
    vm = pl.BlockSpec(memory_space=pltpu.VMEM)
    return pl.pallas_call(
        functools.partial(pack_kernel, widths),
        out_shape=jax.ShapeDtypeStruct((SLOT, 16, 128), BF),
        in_specs=[
            pl.BlockSpec(memory_space=pltpu.SMEM),
            pl.BlockSpec(memory_space=pl.ANY),
            vm,
        ],
        out_specs=vm,
        scratch_shapes=[
            pltpu.VMEM((mat.shape[0] + 2 * MARGIN, 128), F32),
            pltpu.SemaphoreType.DMA,
        ],
        name="pack",
        compiler_params=pltpu.CompilerParams(vmem_limit_bytes=VMEM_LIMIT),
    )(table, mat, vec)


def clip_factor(square):
    return jnp.minimum(1.0, 0.001 / (jnp.sqrt(square) + 1e-06))


def adam_update(master, first, second, grad, rate, decay):
    first = 0.9 * first + 0.1 * grad
    second = 0.95 * second + 0.05 * grad * grad
    step_first = first / (1.0 - 0.9**STEP)
    step_second = second / (1.0 - 0.95**STEP)
    master = master - rate * (step_first / (jnp.sqrt(step_second) + 1e-08) + decay * master)
    return (master, first, second)


STEPS = 6


def update_kernel(widths, table, tiles, total, *refs):
    states, news, news_vec, (lines, held, fresh, sem_in, sem_out) = (
        refs[0:3],
        refs[3:6],
        refs[6],
        refs[7:],
    )
    count = held.shape[1]
    size = count // STEPS

    def part(i):
        return pl.ds(i * size, size)

    loads = [
        [
            pltpu.make_async_copy(state.at[part(i)], held.at[n, part(i)], sem_in.at[n, i])
            for n, state in enumerate(states)
        ]
        for i in range(STEPS)
    ]
    for step in loads:
        for copy in step:
            copy.start()
    lines[...] = jnp.zeros_like(lines)

    def run(line, width, tile):
        lines[pl.ds(line, 16, stride=width), :] = tiles[tile]

    each_tile(table, widths, run)
    news_vec[...] = tiles[0:SLOT_V].reshape(SLOT_V * 16, 128)
    factor = clip_factor(total[0:1, :])
    stores = []
    for i in range(STEPS):
        for copy in loads[i]:
            copy.wait()

        def body(k, carry, i=i):
            base = i * size + k * 104
            rows = pl.ds(pl.multiple_of(base, 8), 104)
            grad = factor * lines[pl.ds(pl.multiple_of(MARGIN + base, 8), 104), :]
            for n, value in enumerate(
                adam_update(held[0, rows, :], held[1, rows, :], held[2, rows, :], grad, 0.05, 0.05)
            ):
                fresh[n, rows, :] = value
            return carry

        lax.fori_loop(0, size // 104, body, 0)
        for n, new in enumerate(news):
            copy = pltpu.make_async_copy(fresh.at[n, part(i)], new.at[part(i)], sem_out.at[n, i])
            copy.start()
            stores.append(copy)
    for copy in stores:
        copy.wait()


def update(table, widths, tiles, total, states):
    count = states[0].shape[0]
    vm = pl.BlockSpec(memory_space=pltpu.VMEM)
    hbm = pl.BlockSpec(memory_space=pl.ANY)
    shape = jax.ShapeDtypeStruct((count, 128), F32)
    return pl.pallas_call(
        functools.partial(update_kernel, widths),
        out_shape=[shape] * 3 + [jax.ShapeDtypeStruct((SLOT_V * 16, 128), F32)],
        in_specs=[pl.BlockSpec(memory_space=pltpu.SMEM), vm, vm] + [hbm] * 3,
        out_specs=[hbm] * 3 + [vm],
        scratch_shapes=[
            pltpu.VMEM((count + 2 * MARGIN, 128), F32),
            pltpu.VMEM((3, count, 128), F32),
            pltpu.VMEM((3, count, 128), F32),
            pltpu.SemaphoreType.DMA((3, STEPS)),
            pltpu.SemaphoreType.DMA((3, STEPS)),
        ],
        name="update",
        compiler_params=pltpu.CompilerParams(vmem_limit_bytes=VMEM_LIMIT),
    )(table, tiles, total, *states)


def shifted(value, axis, steps):
    count = lax.axis_size(axis)
    initial, last = (max(0, -steps), min(count, count - steps))
    return lax.ppermute(value, axis, [(source, source + steps) for source in range(initial, last)])


def train(images, masked_total, enc, dec, enc_out, dec_out, pixels, visible, restore, vecs, weights):
    encoding = lax.axis_index("section") == 0
    pix = jnp.pad(pixels, ((0, 0), (0, ROWS_D - PATCHES), (0, 0)))
    vis = jnp.pad(visible, ((0, 0), (0, ROWS_E - VIS)), constant_values=-1).reshape(-1, 1)
    places = jnp.pad(restore, ((0, 0), (0, ROWS_D - PATCHES)), constant_values=-1).reshape(-1, 1)
    blank_saved = [jnp.zeros(*item) for item in enc_shapes(images).values()]
    blank_latent = jnp.zeros((images * ROWS_E, DE), BF)
    latent, *saved = lax.cond(
        encoding,
        lambda: list(encoder_forward(images, enc, vis, pix, vecs, weights)),
        lambda: [blank_latent] + blank_saved,
    )
    arrived = shifted(latent, "section", 1)
    dlatent, loss, dmats, dvec = lax.cond(
        encoding,
        lambda: [
            blank_latent,
            jnp.zeros((8, 128), F32),
            jnp.zeros(dec_out.shape, BF),
            jnp.zeros(vecs.shape, F32),
        ],
        lambda: list(
            decoder_step(
                images, dec, dec_out, masked_total, arrived, places, pix, vecs, weights
            )
        ),
    )
    returned = shifted(dlatent, "section", -1)
    if dec_out.shape == enc_out.shape:
        other = lambda: [dmats, dvec]
    else:
        more = enc_out.shape[0] - dec_out.shape[0]
        other = lambda: [jnp.pad(dmats, ((0, more), (0, 0), (0, 0))), dvec]
    dmats, dvec = lax.cond(
        encoding,
        lambda: list(
            encoder_backward(images, enc, enc_out, vis, vecs, returned, saved, weights)
        ),
        other,
    )
    return dmats, dvec, loss


def body_block(
    pixels, visible, restore, mat_master, mat_first, mat_second, vec_master, vec_first, vec_second
):
    images = pixels.shape[0]
    masked_total = (PATCHES - VIS) * images * 16
    count, size = mat_master.shape[1] // 128, vec_master.shape[1]
    plans, table, widths = piece_table(count)
    table = jnp.asarray(table, jnp.int32)[lax.axis_index("section"), lax.axis_index("dp")]
    lines = [value.reshape(count, 128) for value in (mat_master, mat_first, mat_second)]
    room = SLOT_V * 2048
    own = pack(
        table, widths, lines[0], jnp.pad(vec_master[0], (0, room - size)).reshape(-1, 128)
    )
    slots = gather_slots(own)
    vecs = slots[:, :SLOT_V].reshape(16, room)[:, :size].reshape(-1, 128).astype(F32)
    inward = [slot_layout(plan, slots.shape, SLOT_V) for plan in plans]
    outward = [whole_slots(plan, (16, SLOT_M, 16, 128)) for plan in plans]
    dmats, dvec, loss = train(
        images, masked_total, *inward, *outward, pixels, visible, restore, vecs, slots
    )
    dvec = jnp.pad(dvec.reshape(16, size), ((0, 0), (0, room - size))).astype(BF)
    tiles, total = scatter_slots(
        owned_limits(plans), dmats, dvec.reshape(16, SLOT_V, 16, 128), loss
    )
    *news, grad_vec = update(table, widths, tiles, total, lines)
    news = [value.reshape(mat_master.shape) for value in news]
    square, loss_sum = total[0, 0], total[1, 0]
    vec_news = adam_update(
        vec_master,
        vec_first,
        vec_second,
        clip_factor(square) * grad_vec.reshape(1, room)[:, :size],
        0.3,
        0.0,
    )
    return (
        (loss_sum, jnp.sqrt(square))
        + tuple(news)
        + (news[0].astype(BF),)
        + tuple(vec_news)
        + (vec_news[0].astype(BF),)
    )


def body(
    pixels, visible, restore, mat_master, mat_first, mat_second, vec_master, vec_first, vec_second
):
    images = pixels.shape[0]
    total = mat_master.shape[1] * lax.axis_size("dp")
    masked_total = (PATCHES - VIS) * images * lax.axis_size("dp")
    encoding = lax.axis_index("section") == 0
    enc, dec = plain_layout(ENC_TOTAL), plain_layout(DEC_TOTAL)
    mats = lax.all_gather(mat_master.astype(BF), "dp", axis=1, tiled=True)[0]
    vecs = lax.all_gather(vec_master.astype(BF), "dp", axis=1, tiled=True)[0]
    vecs = vecs.astype(F32).reshape(-1, 128)
    weights = lax.cond(
        encoding,
        lambda m: natural(m, ENC_MATS),
        lambda m: jnp.pad(natural(m, DEC_MATS), ((0, ENC_TOTAL - DEC_TOTAL), (0, 0), (0, 0))),
        mats,
    )
    dec_in = Layout((ENC_TOTAL, 16, 128), [(lambda ref: ref.at[pl.ds(0, DEC_TOTAL)], 0, DEC_TOTAL)], [])
    dmats, grad_vecs, loss = train(
        images, masked_total, enc, dec_in, enc, dec, pixels, visible, restore, vecs, weights
    )
    grad_mats = lax.cond(
        encoding,
        lambda m: flat_from_natural(m.astype(F32), ENC_MATS, total),
        lambda m: flat_from_natural(m[0:DEC_TOTAL].astype(F32), DEC_MATS, total),
        dmats,
    )
    summed_mats = lax.psum_scatter(grad_mats[None], "dp", scatter_dimension=1, tiled=True)
    summed_vecs = lax.psum_scatter(
        grad_vecs.reshape(1, -1), "dp", scatter_dimension=1, tiled=True
    )
    square = jnp.sum(summed_mats * summed_mats) + jnp.sum(summed_vecs * summed_vecs)
    square, loss_sum = lax.psum((square, loss[0, 0]), ("section", "dp"))
    factor = clip_factor(square)
    mat_news = adam_update(mat_master, mat_first, mat_second, factor * summed_mats, 0.05, 0.05)
    vec_news = adam_update(vec_master, vec_first, vec_second, factor * summed_vecs, 0.3, 0.0)
    return (
        (loss_sum, jnp.sqrt(square))
        + tuple(mat_news)
        + (mat_news[0].astype(BF),)
        + tuple(vec_news)
        + (vec_news[0].astype(BF),)
    )


def solution(mesh):
    split = P("section", "dp")
    fits = mesh.shape["section"] == 2 and mesh.shape["dp"] == 16
    return jax.shard_map(
        body_block if fits else body,
        mesh=mesh,
        in_specs=(P("dp", None, None), P("dp", None), P("dp", None)) + (split,) * 6,
        out_specs=(P(), P()) + (split,) * 8,
        check_vma=False,
    )
```

```python
import functools
import math

import jax
import jax.numpy as jnp
from jax import lax
from jax.experimental import pallas as pl
from jax.experimental.pallas import tpu as pltpu
from jax.sharding import PartitionSpec as P

PIX = 768
DE = 768
HE = 12
FE = 3072
DD = 512
HD = 16
FD = 2048
PATCHES = 196
VIS = 49
STEP = 10
ROWS_E = 64
ROWS_D = 208
EPS = 1e-6
BF = jnp.bfloat16
F32 = jnp.float32
VMEM_LIMIT = 63 * 1024 * 1024

ENC_MATS = [(PIX, DE), (DE, 3 * DE), (DE, DE), (DE, FE), (FE, DE)]
DEC_MATS = [(DE, DD), (DD, 3 * DD), (DD, DD), (DD, FD), (FD, DD), (DD, PIX)]
ENC_VECS = [DE, PATCHES * DE, DE, DE, 2 * DE, DE, DE, DE, FE, DE, DE, DE]
DEC_VECS = [DD, DD, PATCHES * DD, DD, DD, 2 * DD, DD, DD, DD, FD, DD, DD, DD, PIX]


def starts(sizes):
    total, found = 0, []
    for size in sizes:
        found.append(total)
        total += size
    return found, total


ENC_TILES = [k * n // 2048 for k, n in ENC_MATS]
DEC_TILES = [k * n // 2048 for k, n in DEC_MATS]
ENC_BASE, ENC_TOTAL = starts(ENC_TILES)
DEC_BASE, DEC_TOTAL = starts(DEC_TILES)
EV, _ = starts([size // 128 for size in ENC_VECS])
DV, _ = starts([size // 128 for size in DEC_VECS])


class Mat:
    def __init__(self, ref, base, shape, loads=None, stores=None):
        self.base, self.loads, self.stores = base, loads, stores
        self.rows, self.columns = shape
        self.blocks = self.columns // 128
        count = self.rows * self.columns // 2048
        self.ref = ref.at[pl.ds(base, count)].reshape(self.rows // 16, self.blocks, 16, 128)

    def need(self):
        self.loads.need(self.base, self.rows * self.columns // 2048)

    def done(self):
        self.stores.done(self.base, self.rows * self.columns // 2048)

    def cols(self, block):
        parts = [self.ref[:, 2 * block + half].reshape(self.rows, 128) for half in range(2)]
        return jnp.concatenate(parts, 1)

    def band(self, block):
        part = self.ref.at[pl.ds(block * 16, 16)]
        return jnp.concatenate([part[:, j].reshape(256, 128) for j in range(self.blocks)], 1)

    def put_cols(self, block, value):
        for half in range(2):
            piece = value[:, half * 128 : (half + 1) * 128].astype(BF)
            self.ref[:, 2 * block + half] = piece.reshape(self.rows // 16, 16, 128)

    def put_band(self, block, value):
        part = self.ref.at[pl.ds(block * 16, 16)]
        for j in range(self.blocks):
            part[:, j] = value[:, j * 128 : (j + 1) * 128].astype(BF).reshape(16, 16, 128)


def dot(a, b):
    return jnp.dot(a, b, preferred_element_type=F32)


def dot_t(a, b):
    return lax.dot_general(a, b, (((1,), (1,)), ((), ())), preferred_element_type=F32)


def t_dot(a, b):
    return lax.dot_general(a, b, (((0,), (0,)), ((), ())), preferred_element_type=F32)


def loop(count, body, init=0):
    return lax.fori_loop(0, count, body, init)


def lanes(block, width=256):
    return pl.ds(pl.multiple_of(block * width, width), width)


def row_of(vec, start, width):
    return jnp.concatenate([vec[start + j : start + j + 1, :] for j in range(width // 128)], 1)


def row_at(vec, start, block):
    return jnp.concatenate([vec[pl.ds(start + 2 * block + h, 1), :] for h in range(2)], 1)


def put_row(dvec, start, value):
    for j in range(value.shape[1] // 128):
        dvec[start + j : start + j + 1, :] = value[:, j * 128 : (j + 1) * 128]


def put_row_at(dvec, start, block, value):
    for h in range(2):
        dvec[pl.ds(start + 2 * block + h, 1), :] = value[:, h * 128 : (h + 1) * 128]


def fold(value):
    return value.reshape(value.shape[0] // 8, 8, value.shape[1]).sum(0)


def total_row(value):
    return jnp.sum(value, 0, keepdims=True)


def norm_parts(x):
    mean = jnp.mean(x, -1, keepdims=True)
    centred = x - mean
    scale = lax.rsqrt(jnp.mean(centred * centred, -1, keepdims=True) + EPS)
    return centred * scale, scale


CHUNKS = (208, 128, 64, 32)


def chunk_loop(ref, step, init=0):
    count = ref.shape[0]
    size = next(c for c in CHUNKS if count % c == 0)

    def run(i, carry):
        return step(pl.ds(pl.multiple_of(i * size, size), size), carry)

    return lax.fori_loop(0, count // size, run, init)


def norm_rows(x_ref, out_ref, vec, gain_at, shift_at, width, add_ref=None, bias_at=None):
    gain, shift = row_of(vec, gain_at, width), row_of(vec, shift_at, width)
    bias = None if bias_at is None else row_of(vec, bias_at, width)

    def step(rows, carry):
        x = x_ref[rows, :]
        if add_ref is not None:
            x = x + add_ref[rows, :] + bias
            add_ref[rows, :] = x
        unit, _ = norm_parts(x)
        out_ref[rows, :] = (unit * gain + shift).astype(BF)
        return carry

    chunk_loop(x_ref, step)


def norm_back_rows(x_ref, dy_ref, dx_ref, dxb_ref, vec, dvec, gain_at, shift_at, width, bias_at, add):
    gain = row_of(vec, gain_at, width)
    zero = jnp.zeros((8, width), F32)

    def step(rows, carry):
        dgain, dshift, dbias = carry
        unit, scale = norm_parts(x_ref[rows, :])
        dy = dy_ref[rows, :].astype(F32)
        dunit = dy * gain
        dx = scale * (
            dunit
            - jnp.mean(dunit, -1, keepdims=True)
            - unit * jnp.mean(dunit * unit, -1, keepdims=True)
        )
        if add:
            dx = dx + dx_ref[rows, :]
        dx_ref[rows, :] = dx
        dxb_ref[rows, :] = dx.astype(BF)
        return dgain + fold(dy * unit), dshift + fold(dy), dbias + fold(dx)

    dgain, dshift, dbias = chunk_loop(x_ref, step, (zero, zero, zero))
    put_row(dvec, gain_at, total_row(dgain))
    put_row(dvec, shift_at, total_row(dshift))
    if bias_at is not None:
        put_row(dvec, bias_at, total_row(dbias))
    return dbias


GELU_C = math.sqrt(2.0 / math.pi)


def gelu_parts(x):
    square = x * x
    t = jnp.tanh(x * (GELU_C + (GELU_C * 0.044715) * square))
    half = 0.5 * (1.0 + t)
    return x * half, half + (0.5 * x) * (1.0 - t * t) * (
        GELU_C + (3.0 * 0.044715 * GELU_C) * square
    )


def head_mask(size):
    lane = lax.broadcasted_iota(jnp.int32, (1, 128), 1)
    return [(lane >= h * size) & (lane < (h + 1) * size) for h in range(128 // size)]


def attention(qkv, probs, att, bias, group, groups, width, size):
    blocks = width // 128
    masks = head_mask(size)

    def step(i, carry):
        g, b = i // blocks, i % blocks
        rows = pl.ds(pl.multiple_of(g * group, 16), group)
        q = qkv[rows, lanes(b, 128)]
        k = qkv[rows, lanes(blocks + b, 128)]
        v = qkv[rows, lanes(2 * blocks + b, 128)]
        out = jnp.zeros((group, 128), F32)
        for h, mask in enumerate(masks):
            s = dot_t(jnp.where(mask, q, jnp.zeros_like(q)), k) + bias
            e = jnp.exp(s - jnp.max(s, -1, keepdims=True))
            p = (e * (1.0 / jnp.sum(e, -1, keepdims=True))).astype(BF)
            probs[i * len(masks) + h] = p
            out = jnp.where(mask, dot(p, v), out)
        att[rows, lanes(b, 128)] = out.astype(BF)
        return carry

    lax.fori_loop(0, groups * blocks, step, 0, unroll=4 if groups * blocks % 4 == 0 else 2)


def attention_back(qkv, probs, datt, dqkv, dvec, qv_at, group, groups, width, size):
    blocks = width // 128
    masks = head_mask(size)
    scale = size ** (-0.5)
    for j in range(2 * blocks):
        dvec[qv_at + j : qv_at + j + 1, :] = jnp.zeros((1, 128), F32)

    def step(i, carry):
        g, b = i // blocks, i % blocks
        rows = pl.ds(pl.multiple_of(g * group, 16), group)
        q = qkv[rows, lanes(b, 128)]
        k = qkv[rows, lanes(blocks + b, 128)]
        v = qkv[rows, lanes(2 * blocks + b, 128)]
        da = datt[rows, lanes(b, 128)]
        zero = jnp.zeros((group, 128), F32)
        dq, dk, dv = zero, zero, zero
        for h, mask in enumerate(masks):
            p = probs[i * len(masks) + h]
            dp = dot_t(jnp.where(mask, da, jnp.zeros_like(da)), v)
            wide = p.astype(F32)
            prod = wide * dp
            ds = (prod - wide * jnp.sum(prod, -1, keepdims=True)).astype(BF)
            dq = jnp.where(mask, dot(ds, k), dq)
            dk = jnp.where(mask, t_dot(ds, q), dk)
            dv = jnp.where(mask, t_dot(p, da), dv)
        dq = dq * scale
        dqkv[rows, lanes(b, 128)] = dq.astype(BF)
        dqkv[rows, lanes(blocks + b, 128)] = dk.astype(BF)
        dqkv[rows, lanes(2 * blocks + b, 128)] = dv.astype(BF)
        dvec[pl.ds(qv_at + b, 1), :] += total_row(dq)
        dvec[pl.ds(qv_at + blocks + b, 1), :] += total_row(dv)
        return carry

    lax.fori_loop(0, groups * blocks, step, 0, unroll=2)


def block_forward(s, mats, vec, at, width, hidden, size, bias, group, groups):
    w_qkv, w_proj, w_up, w_down = mats
    pairs = width // 256
    scale = size ** (-0.5)
    norm_rows(s.x0, s.n1, vec, at["g1"], at["s1"], width)

    def qkv_step(j, carry):
        part = j // pairs
        row = row_at(vec, at["qv"], jnp.where(part == 0, j, jnp.maximum(j - pairs, 0)))
        value = dot(s.n1[...], w_qkv.cols(j)) + jnp.where(part == 1, 0.0, row)
        s.qkv[:, lanes(j)] = (value * jnp.where(part == 0, scale, 1.0)).astype(BF)
        return carry

    s.done("n1")
    w_qkv.need()
    loop(3 * pairs, qkv_step)
    s.done("qkv")
    attention(s.qkv, s.probs, s.att, bias, group, groups, width, size)
    s.done("probs", "att")

    def proj_step(j, carry):
        s.x1[:, lanes(j)] = dot(s.att[...], w_proj.cols(j))
        return carry

    w_proj.need()
    loop(pairs, proj_step)
    norm_rows(s.x0, s.n2, vec, at["g2"], at["s2"], width, s.x1, at["bo"])

    def mlp_step(j, carry):
        h = dot(s.n2[...], w_up.cols(j)) + row_at(vec, at["bu"], j)
        s.h[:, lanes(j)] = h
        u = gelu_parts(h)[0].astype(BF)
        update = dot(u, w_down.band(j))

        @pl.when(j == 0)
        def _():
            s.x2[...] = update

        @pl.when(j > 0)
        def _():
            s.x2[...] += update

        return carry

    s.done("x1", "n2")
    w_up.need()
    w_down.need()
    loop(hidden // 256, mlp_step)
    s.done("h")


def block_backward(s, mats, grads, vec, dvec, at, width, hidden, size, group, groups):
    w_qkv, w_proj, w_up, w_down = mats
    d_qkv, d_proj, d_up, d_down = grads
    pairs = width // 256
    s.need("n2")
    s.flip[...] = s.n2[...].T

    def mlp_step(j, carry):
        dxb = s.dxb[...]
        u, slope = gelu_parts(s.h[:, lanes(j)])
        dh = dot_t(dxb, w_down.band(j)) * slope
        put_row_at(dvec, at["bu"], j, total_row(fold(dh)))
        dh = dh.astype(BF)
        d_down.put_band(j, t_dot(u.astype(BF), dxb))
        d_up.put_cols(j, dot(s.flip[...], dh))
        update = dot_t(dh, w_up.cols(j))

        @pl.when(j == 0)
        def _():
            s.dn[...] = update

        @pl.when(j > 0)
        def _():
            s.dn[...] += update

        return carry

    s.need("h")
    w_down.need()
    w_up.need()
    loop(hidden // 256, mlp_step)
    d_down.done()
    d_up.done()
    s.need("x1")
    norm_back_rows(s.x1, s.dn, s.dx, s.dxb, vec, dvec, at["g2"], at["s2"], width, at["bo"], True)

    def proj_step(j, carry):
        dxb = s.dxb[...]
        s.datt[:, lanes(j)] = dot_t(dxb, w_proj.band(j)).astype(BF)
        d_proj.put_band(j, t_dot(s.att[:, lanes(j)], dxb))
        return carry

    s.need("att")
    w_proj.need()
    loop(pairs, proj_step)
    d_proj.done()
    s.need("qkv", "probs")
    attention_back(s.qkv, s.probs, s.datt, s.dqkv, dvec, at["qv"], group, groups, width, size)
    s.need("n1")
    s.flip[...] = s.n1[...].T

    def weight_step(j, carry):
        d_qkv.put_cols(j, dot(s.flip[...], s.dqkv[:, lanes(j)]))
        return carry

    loop(3 * pairs, weight_step)
    d_qkv.done()

    def input_step(j, carry):
        s.dn[:, lanes(j)] = dot_t(s.dqkv[...], w_qkv.band(j))
        return carry

    w_qkv.need()
    loop(pairs, input_step)
    s.need("x0")
    norm_back_rows(s.x0, s.dn, s.dx, s.dxb, vec, dvec, at["g1"], at["s1"], width, None, True)


ENC_AT = dict(g1=EV[2], s1=EV[3], qv=EV[4], bo=EV[5], g2=EV[6], s2=EV[7], bu=EV[8])
DEC_AT = dict(g1=DV[3], s1=DV[4], qv=DV[5], bo=DV[6], g2=DV[7], s2=DV[8], bu=DV[9])


def only(section, run):
    if section is None:
        run()
    else:
        pl.when(lax.axis_index("section") == section)(run)


class Bag:
    def __init__(self, names, refs):
        self.source, self.target, self.flying = {}, {}, {}
        for name, ref in zip(names, refs):
            setattr(self, name, ref)

    def begin(self, name, source, target, sem):
        self.flying[name] = pltpu.make_async_copy(source, target, sem)
        self.flying[name].start()

    def come(self, names, sources, sems):
        for n, (name, source) in enumerate(zip(names, sources)):
            self.begin(name, source, getattr(self, name), sems.at[n])

    def need(self, *names):
        for name in names:
            if name in self.flying:
                self.flying.pop(name).wait()

    def done(self, *names):
        for name in names:
            if name in self.target:
                target, sem = self.target[name]
                self.begin(name, getattr(self, name), target, sem)

    def finish(self):
        self.need(*list(self.flying))


class Layout:
    def __init__(self, shape, moves, shared):
        self.shape, self.moves, self.shared = shape, moves, shared


def plain_layout(total):
    return Layout((total, 16, 128), [(lambda ref: ref, 0, total)], [])


def slot_layout(plan, shape, lead):
    moves, shared, done = [], [], 0
    for device, (first, count, _) in enumerate(plan):
        skip = max(0, done - first)
        if skip and count:
            shared.append((lambda ref, d=device, n=skip: ref.at[d, pl.ds(lead, n)], first, skip))
        if count:
            moves.append(
                (
                    lambda ref, d=device, a=skip, n=count - skip: ref.at[d, pl.ds(lead + a, n)],
                    first + skip,
                    count - skip,
                )
            )
        done = first + count
    return Layout(shape, moves, shared)


def whole_slots(plan, shape):
    moves = [
        (lambda ref, d=device, n=count: ref.at[d, pl.ds(0, n)], first, count)
        for device, (first, count, _) in enumerate(plan)
        if count
    ]
    return Layout(shape, moves, [])


SHARED = 24


class Loads:
    def __init__(self, source, kept, side, sem, layout, backward=False):
        self.kept, self.side, self.flying = kept, side, []
        moves = list(enumerate(layout.moves))
        for index, (pick, start, count) in moves[::-1] if backward else moves:
            copy = pltpu.make_async_copy(pick(source), kept.at[pl.ds(start, count)], sem.at[index])
            copy.start()
            self.flying.append((start, count, None, copy))
        for index, (pick, start, count) in enumerate(layout.shared):
            copy = pltpu.make_async_copy(
                pick(source),
                side.at[index, pl.ds(0, count)],
                sem.at[len(layout.moves) + index],
            )
            copy.start()
            self.flying.append((start, count, index, copy))

    def need(self, base, tiles):
        here = [f for f in self.flying if f[0] < base + tiles and f[0] + f[1] > base]
        self.flying = [f for f in self.flying if f not in here]
        for item in here:
            item[3].wait()
        for start, count, index, _ in here:
            if index is not None:
                there = pl.ds(start, count)
                both = self.kept[there].astype(F32) + self.side[index, 0:count].astype(F32)
                self.kept[there] = both.astype(BF)


class Stores:
    def __init__(self, kept, out, sem, layout):
        self.kept, self.out, self.sem = kept, out, sem
        self.left, self.ready, self.flying = list(enumerate(layout.moves)), set(), []

    def done(self, base, tiles):
        self.ready.update(range(base, base + tiles))
        for item in list(self.left):
            index, (pick, start, count) = item
            if self.ready.issuperset(range(start, start + count)):
                copy = pltpu.make_async_copy(
                    self.kept.at[pl.ds(start, count)], pick(self.out), self.sem.at[index]
                )
                copy.start()
                self.flying.append(copy)
                self.left.remove(item)

    def finish(self):
        for copy in self.flying:
            copy.wait()


def load_scratch(layout):
    return [
        pltpu.VMEM((max(1, len(layout.shared)), SHARED, 16, 128), BF),
        pltpu.SemaphoreType.DMA((len(layout.moves) + len(layout.shared),)),
    ]


def visible_rows(column, count):
    lane = lax.broadcasted_iota(jnp.int32, (1, count), 1)
    return jnp.where(column == lane, 1.0, 0.0).astype(BF)


def encoder_bias(rows):
    r = lax.broadcasted_iota(jnp.int32, (rows, rows), 0)
    c = lax.broadcasted_iota(jnp.int32, (rows, rows), 1)
    same = (r // ROWS_E == c // ROWS_E) & (c % ROWS_E < VIS)
    return jnp.where(same, 0.0, -1e30)


ENC_KEEP = ["pick", "x0", "n1", "qkv", "probs", "att", "x1", "n2", "h", "x2"]


def enc_shapes(images):
    rows = images * ROWS_E
    return dict(
        pick=((rows, PIX), BF),
        x0=((rows, DE), F32),
        n1=((rows, DE), BF),
        qkv=((rows, 3 * DE), BF),
        probs=((HE, rows, rows), BF),
        att=((rows, DE), BF),
        x1=((rows, DE), F32),
        n2=((rows, DE), BF),
        h=((rows, FE), F32),
        x2=((rows, DE), F32),
    )


def position_column(vec, start, blocks, j):
    return vec[pl.ds(start + j, PATCHES, stride=blocks), :]


def encoder_forward_kernel(images, layout, section, vis, pix, vec, weights, *refs):
    latent, outs = refs[0], refs[1 : 1 + len(ENC_KEEP)]
    s = Bag(ENC_KEEP, refs[1 + len(ENC_KEEP) : 1 + 2 * len(ENC_KEEP)])
    keep_sem, kept, posit, side, sem = refs[1 + 2 * len(ENC_KEEP) :]
    s.target = {name: (out, keep_sem.at[n]) for n, (name, out) in enumerate(zip(ENC_KEEP, outs))}
    def run():
        loads = Loads(weights, kept, side, sem, layout)
        rows = images * ROWS_E
        mats = [Mat(kept, b, shape, loads) for b, shape in zip(ENC_BASE, ENC_MATS)]
        posit[...] = jnp.zeros_like(posit)
        for j in range(DE // 128):
            posit[0:PATCHES, j * 128 : (j + 1) * 128] = position_column(vec, EV[1], DE // 128, j)
        for i in range(images):
            where = pl.ds(i * ROWS_E, ROWS_E)
            hot = visible_rows(vis[where, :], ROWS_D)
            s.pick[where, :] = dot(hot, pix[i]).astype(BF)
            s.x0[where, :] = dot(hot, posit[...].astype(BF)) + row_of(vec, EV[0], DE)
        mats[0].need()

        def embed_step(j, carry):
            s.x0[:, lanes(j)] += dot(s.pick[...], mats[0].cols(j))
            return carry

        loop(DE // 256, embed_step)
        s.done("pick", "x0")
        block_forward(
            s, mats[1:5], vec, ENC_AT, DE, FE, DE // HE, encoder_bias(rows), rows, 1
        )
        norm_rows(s.x1, latent, vec, EV[10], EV[11], DE, s.x2, EV[9])
        s.done("x2")
        s.finish()

    only(section, run)


def encoder_forward(images, layout, vis, pix, vec, weights, section=None):
    shapes = enc_shapes(images)
    rows = images * ROWS_E
    vm = pl.BlockSpec(memory_space=pltpu.VMEM)
    return pl.pallas_call(
        functools.partial(encoder_forward_kernel, images, layout, section),
        out_shape=[jax.ShapeDtypeStruct((rows, DE), BF)]
        + [jax.ShapeDtypeStruct(*shapes[name]) for name in ENC_KEEP],
        in_specs=[vm, vm, vm, pl.BlockSpec(memory_space=pl.ANY)],
        out_specs=[vm] + [pl.BlockSpec(memory_space=pl.ANY)] * len(ENC_KEEP),
        scratch_shapes=[pltpu.VMEM(*shapes[name]) for name in ENC_KEEP]
        + [
            pltpu.SemaphoreType.DMA((len(ENC_KEEP),)),
            pltpu.VMEM((ENC_TOTAL, 16, 128), BF),
            pltpu.VMEM((ROWS_D, DE), F32),
        ]
        + load_scratch(layout),
        name="encoder_forward",
        compiler_params=pltpu.CompilerParams(vmem_limit_bytes=VMEM_LIMIT),
    )(vis, pix, vec, weights)


def encoder_backward_kernel(images, layout, out_layout, section, vis, vec, dlatent, *refs):
    n = len(ENC_KEEP)
    saved, (weights, dmats, dvec) = refs[:n], refs[n : n + 3]
    s = Bag(ENC_KEEP, refs[n + 3 : 2 * n + 3])
    keep_sem, kept, dkept, s.dx, s.dxb, s.dn, s.datt, s.dqkv, s.flip, out_sem, side, sem = refs[
        2 * n + 3 :
    ]
    def run():
        s.come(ENC_KEEP[::-1], saved[::-1], keep_sem)
        loads = Loads(weights, kept, side, sem, layout, True)
        stores = Stores(dkept, dmats, out_sem, out_layout)
        rows = images * ROWS_E
        mats = [Mat(kept, b, shape, loads) for b, shape in zip(ENC_BASE, ENC_MATS)]
        grads = [Mat(dkept, b, shape, None, stores) for b, shape in zip(ENC_BASE, ENC_MATS)]
        dvec[EV[11] + DE // 128 :, :] = jnp.zeros_like(dvec[EV[11] + DE // 128 :, :])
        s.need("x2")
        norm_back_rows(
            s.x2, dlatent, s.dx, s.dxb, vec, dvec, EV[10], EV[11], DE, EV[9], False
        )
        block_backward(
            s, mats[1:5], grads[1:5], vec, dvec, ENC_AT, DE, FE, DE // HE, rows, 1
        )
        put_row(dvec, EV[0], jnp.sum(s.dx[...], 0, keepdims=True))

        s.need("pick")

        def embed_step(j, carry):
            grads[0].put_band(j, t_dot(s.pick[:, lanes(j)], s.dxb[...]))
            return carry

        loop(DE // 256, embed_step)
        grads[0].done()
        mats[0].need()
        hot = visible_rows(vis[...], ROWS_D)
        for j in range(DE // 128):
            value = t_dot(hot, s.dxb[:, j * 128 : (j + 1) * 128])
            dvec[pl.ds(EV[1] + j, PATCHES, stride=DE // 128), :] = value[0:PATCHES]
        stores.finish()

    only(section, run)


def encoder_backward(images, layout, out_layout, vis, vec, dlatent, saved, weights, section=None):
    rows = images * ROWS_E
    shapes = enc_shapes(images)
    vm = pl.BlockSpec(memory_space=pltpu.VMEM)
    hbm = pl.BlockSpec(memory_space=pl.ANY)
    return pl.pallas_call(
        functools.partial(encoder_backward_kernel, images, layout, out_layout, section),
        out_shape=[
            jax.ShapeDtypeStruct(out_layout.shape, BF),
            jax.ShapeDtypeStruct(vec.shape, F32),
        ],
        in_specs=[vm] * 3 + [hbm] * (len(ENC_KEEP) + 1),
        out_specs=[hbm, vm],
        scratch_shapes=[pltpu.VMEM(*shapes[name]) for name in ENC_KEEP]
        + [
            pltpu.SemaphoreType.DMA((len(ENC_KEEP),)),
            pltpu.VMEM((ENC_TOTAL, 16, 128), BF),
            pltpu.VMEM((ENC_TOTAL, 16, 128), BF),
            pltpu.VMEM((rows, DE), F32),
            pltpu.VMEM((rows, DE), BF),
            pltpu.VMEM((rows, DE), F32),
            pltpu.VMEM((rows, DE), BF),
            pltpu.VMEM((rows, 3 * DE), BF),
            pltpu.VMEM((DE, rows), BF),
            pltpu.SemaphoreType.DMA((len(out_layout.moves),)),
        ]
        + load_scratch(layout),
        name="encoder_backward",
        compiler_params=pltpu.CompilerParams(vmem_limit_bytes=VMEM_LIMIT),
    )(vis, vec, dlatent, *saved, weights)


def decoder_kernel(images, layout, out_layout, section, masked_total, latent, places, pix, vec, weights, *refs):
    dlatent, loss, dmats, dvec = refs[:4]
    s = Bag(
        ["x0", "x1", "x2", "n1", "n2", "qkv", "probs", "att", "h", "dx", "dxb", "dn", "dqkv", "flip"],
        refs[4:18],
    )
    kept, dkept, posit, dguess, out_sem, side, sem = refs[18:]
    s.datt = s.n2
    loss[...] = jnp.zeros((8, 128), F32)

    def run():
        rows = images * ROWS_D
        loads = Loads(weights, kept, side, sem, layout)
        stores = Stores(dkept, dmats, out_sem, out_layout)
        mats = [Mat(kept, b, shape, loads) for b, shape in zip(DEC_BASE, DEC_MATS)]
        grads = [Mat(dkept, b, shape, None, stores) for b, shape in zip(DEC_BASE, DEC_MATS)]
        posit[...] = jnp.zeros_like(posit)
        for j in range(DD // 128):
            posit[0:PATCHES, j * 128 : (j + 1) * 128] = position_column(vec, DV[2], DD // 128, j)
        dvec[DV[13] + PIX // 128 :, :] = jnp.zeros_like(dvec[DV[13] + PIX // 128 :, :])
        mats[0].need()
        for i in range(images):
            part = pl.ds(i * ROWS_E, ROWS_E)
            where = pl.ds(i * ROWS_D, ROWS_D)
            for j in range(DD // 256):
                cut = slice(j * 256, (j + 1) * 256)
                z = dot(latent[part, :], mats[0].cols(j)) + row_of(vec, DV[0] + 2 * j, 256)
                place = places[where, :]
                hot = visible_rows(jnp.where(place < VIS, place, -1), ROWS_E)
                high = z.astype(BF)
                low = (z - high.astype(F32)).astype(BF)
                token = jnp.where(place >= VIS, 1.0, 0.0) * row_of(vec, DV[1] + 2 * j, 256)
                s.x0[where, cut] = dot(hot, high) + dot(hot, low) + token + posit[:, cut]
        lane = lax.broadcasted_iota(jnp.int32, (1, ROWS_D), 1)
        bias = jnp.where(lane < PATCHES, 0.0, -1e30)
        block_forward(
            s, mats[1:5], vec, DEC_AT, DD, FD, DD // HD, bias, ROWS_D, images
        )
        norm_rows(s.x1, s.dxb, vec, DV[11], DV[12], DD, s.x2, DV[10])
        factor = 2.0 / (PIX * masked_total)

        def head_step(j, total):
            value = dot(s.dxb[...], mats[5].cols(j)) + row_at(vec, DV[13], j)
            count = jnp.zeros((8, 256), F32)
            column = jnp.zeros((8, 256), F32)
            for i in range(images):
                where = slice(i * ROWS_D, (i + 1) * ROWS_D)
                error = value[where] - pix[i, :, lanes(j)].astype(F32)
                error = jnp.where(places[where, :] >= VIS, error, 0.0)
                count = count + fold(error * error)
                error = error * factor
                column = column + fold(error)
                dguess[where, lanes(j)] = error.astype(BF)
            put_row_at(dvec, DV[13], j, total_row(column))
            return total + count

        mats[5].need()
        total = loop(PIX // 256, head_step, jnp.zeros((8, 256), F32))
        loss[...] = jnp.broadcast_to(jnp.sum(total) * (1.0 / PIX), (8, 128))
        s.flip[...] = s.dxb[...].T

        def head_weight_step(j, carry):
            grads[5].put_cols(j, dot(s.flip[...], dguess[:, lanes(j)]))
            return carry

        loop(PIX // 256, head_weight_step)
        grads[5].done()

        def head_input_step(j, carry):
            s.dn[:, lanes(j)] = dot_t(dguess[...], mats[5].band(j))
            return carry

        loop(DD // 256, head_input_step)
        norm_back_rows(s.x2, s.dn, s.dx, s.dxb, vec, dvec, DV[11], DV[12], DD, DV[10], False)
        block_backward(
            s, mats[1:5], grads[1:5], vec, dvec, DEC_AT, DD, FD, DD // HD, ROWS_D, images
        )
        token = jnp.zeros((8, DD), F32)
        spot = jnp.zeros((ROWS_D, DD), F32)
        back = []
        for i in range(images):
            where = pl.ds(i * ROWS_D, ROWS_D)
            place = places[where, :]
            dx = s.dx[where, :]
            spot = spot + dx
            token = token + fold(jnp.where(place >= VIS, dx, 0.0))
            hot = visible_rows(jnp.where(place < VIS, place, -1), ROWS_E)
            back.append(t_dot(hot, s.dxb[where, :]))
        posit[...] = spot
        for j in range(DD // 128):
            dvec[pl.ds(DV[2] + j, PATCHES, stride=DD // 128), :] = posit[
                0:PATCHES, j * 128 : (j + 1) * 128
            ]
        put_row(dvec, DV[1], total_row(token))
        back = jnp.concatenate(back, 0)
        put_row(dvec, DV[0], jnp.sum(back, 0, keepdims=True))
        back = back.astype(BF)
        for j in range(DE // 256):
            grads[0].put_band(j, t_dot(latent[:, j * 256 : (j + 1) * 256], back))
            dlatent[:, j * 256 : (j + 1) * 256] = dot_t(back, mats[0].band(j)).astype(BF)
        grads[0].done()
        stores.finish()

    only(section, run)


def decoder_step(
    images, layout, out_layout, masked_total, latent, places, pix, vec, weights, section=None
):
    rows = images * ROWS_D
    vm = pl.BlockSpec(memory_space=pltpu.VMEM)
    hbm = pl.BlockSpec(memory_space=pl.ANY)
    probs = images * HD
    return pl.pallas_call(
        functools.partial(decoder_kernel, images, layout, out_layout, section, masked_total),
        out_shape=[
            jax.ShapeDtypeStruct((images * ROWS_E, DE), BF),
            jax.ShapeDtypeStruct((8, 128), F32),
            jax.ShapeDtypeStruct(out_layout.shape, BF),
            jax.ShapeDtypeStruct(vec.shape, F32),
        ],
        in_specs=[vm, vm, vm, vm, hbm],
        out_specs=[vm, vm, hbm, vm],
        scratch_shapes=[
            pltpu.VMEM((rows, DD), F32),
            pltpu.VMEM((rows, DD), F32),
            pltpu.VMEM((rows, DD), F32),
            pltpu.VMEM((rows, DD), BF),
            pltpu.VMEM((rows, DD), BF),
            pltpu.VMEM((rows, 3 * DD), BF),
            pltpu.VMEM((probs, ROWS_D, ROWS_D), BF),
            pltpu.VMEM((rows, DD), BF),
            pltpu.VMEM((rows, FD), F32),
            pltpu.VMEM((rows, DD), F32),
            pltpu.VMEM((rows, DD), BF),
            pltpu.VMEM((rows, DD), F32),
            pltpu.VMEM((rows, 3 * DD), BF),
            pltpu.VMEM((DD, rows), BF),
            pltpu.VMEM((DEC_TOTAL, 16, 128), BF),
            pltpu.VMEM((DEC_TOTAL, 16, 128), BF),
            pltpu.VMEM((ROWS_D, DD), F32),
            pltpu.VMEM((rows, PIX), BF),
            pltpu.SemaphoreType.DMA((len(out_layout.moves),)),
        ]
        + load_scratch(layout),
        name="decoder_step",
        compiler_params=pltpu.CompilerParams(vmem_limit_bytes=VMEM_LIMIT),
    )(latent, places, pix, vec, weights)


def natural(flat, shapes):
    pieces, offset = [], 0
    for rows, columns in shapes:
        piece = flat[offset : offset + rows * columns].reshape(rows // 16, 16, columns // 128, 128)
        pieces.append(piece.transpose(0, 2, 1, 3).reshape(-1, 16, 128))
        offset += rows * columns
    return jnp.concatenate(pieces, 0)


def flat_from_natural(tiles, shapes, total):
    pieces, offset = [], 0
    for rows, columns in shapes:
        count = rows * columns // 2048
        piece = tiles[offset : offset + count].reshape(rows // 16, columns // 128, 16, 128)
        pieces.append(piece.transpose(0, 2, 1, 3).reshape(-1))
        offset += count
    flat = jnp.concatenate(pieces)
    return jnp.pad(flat, (0, total - flat.shape[0]))


MESH = pl.DeviceIdType.MESH
DEPTH, WIDTH = 4, 2
SLOT_M, SLOT_V = 264, 5
SLOT = SLOT_M + SLOT_V
FIRST_Z = 8
RELAY = 3
LENGTHS = (
    ((18, 29, 22), (19, 36, 23), (20, 34, 25), (18, 29, 22)),
    ((32, 0, 0), (33, 0, 0), (7, 0, 0), (1, 0, 0)),
)
PARTS = FIRST_Z + 1 + RELAY
EARLY = 5
MARGIN = 384
LINES = 3744


def cut_z(section, depth, part):
    length = LENGTHS[section][depth][0]
    return part * length, length


def cut_y(section, depth):
    first, tail, _ = LENGTHS[section][depth]
    return FIRST_Z * first, tail


def cut_relay(depth, part):
    first, tail, length = LENGTHS[0][depth]
    return FIRST_Z * first + tail + part * length, length


def size_of(section, depth):
    first, tail, length = LENGTHS[section][depth]
    return FIRST_Z * first + tail + RELAY * length


def each(count, run):
    def step(i, carry):
        run(i)
        return carry

    lax.fori_loop(0, count, step, 0)


def shard_plan(shapes, total, devices):
    lines = total // devices // 128
    plans = []
    for device in range(devices):
        low, high = device * lines, (device + 1) * lines
        first, count, pieces = 0, 0, []
        line, tile = 0, 0
        for rows, columns in shapes:
            blocks = columns // 128
            begin, end = max(low, line), min(high, line + rows * blocks)
            if begin < end:
                top, bottom = (begin - line) // blocks, (end - line) // blocks
                assert top * blocks == begin - line and bottom * blocks == end - line
                up, down = top // 16, -(-bottom // 16)
                if not pieces:
                    first = tile + up * blocks
                pieces.append((blocks, line + up * 16 * blocks - low, down - up, count))
                count += (down - up) * blocks
            line += rows * blocks
            tile += rows * blocks // 16
        plans.append((first, count, pieces))
    return plans


def devices_around(z, y, c, s):
    at = lambda zz, yy, cc: (s, zz * 4 + yy * 2 + cc)
    around = {"side": at(z, 1 - y, c), "core": at(z, y, 1 - c)}
    around["cross"] = (1 - s, z * 4 + y * 2 + c)
    if z + 1 < DEPTH:
        around["up"] = at(z + 1, y, c)
    if z > 0:
        around["down"] = at(z - 1, y, c)
    return around


def greet(around):
    barrier = pltpu.get_barrier_semaphore()
    for target in around.values():
        pl.semaphore_signal(barrier, inc=1, device_id=target, device_id_type=MESH)
    pl.semaphore_wait(barrier, len(around))


def place():
    d = lax.axis_index("dp")
    return lax.axis_index("section"), d // 4, (d // 2) % 2, d % 2


def for_each_depth(run):
    s_now, z_now, y, c = place()
    for s in range(2):
        for z in range(DEPTH):
            pl.when((s_now == s) & (z_now == z))(functools.partial(run, s, z, y, c))


class Sender:
    def __init__(self, around, send):
        self.around, self.send, self.used, self.sent = around, send, 0, []

    def many(self, count, make, names):
        groups = []
        for name in names:
            if name in self.around:

                def copy(n, base=self.used, name=name):
                    source, target, sem = make(n)
                    return pltpu.make_async_remote_copy(
                        source,
                        target,
                        self.send.at[base + n],
                        sem,
                        device_id=self.around[name],
                        device_id_type=MESH,
                    )

                self.used += count
                self.sent.append((count, copy))
                groups.append(copy)

        def start(n):
            for copy in groups:
                copy(n).start()

        return start

    def push(self, source, target, sem, *names):
        self.many(1, lambda n: (source, target, sem), names)(0)

    def arrive(self, target, sem):
        pltpu.make_async_remote_copy(
            target,
            target,
            self.send.at[0],
            sem,
            device_id=self.around["core"],
            device_id_type=MESH,
        ).wait_recv()

    def finish(self):
        for count, copy in self.sent:
            each(count, lambda n: copy(n).wait_send())


def gather_kernel(own, out, passing, send, recv, r_pass, local):
    def run(s, z, y, c):
        around = devices_around(z, y, c, s)
        greet(around)
        io = Sender(around, send)

        def slot(zz, yy, cc):
            return zz * 4 + yy * 2 + cc

        def part_z(zz, yy, cc, n, mine=False):
            target = out.at[slot(zz, yy, cc), pl.ds(*cut_z(s, zz, n))]
            source = own.at[pl.ds(*cut_z(s, zz, n))] if mine else target
            return source, target, recv.at[slot(zz, yy, cc), n]

        def part_y(zz, yy, cc, mine=False):
            target = out.at[slot(zz, yy, cc), pl.ds(*cut_y(s, zz))]
            source = own.at[pl.ds(*cut_y(s, zz))] if mine else target
            return source, target, recv.at[slot(zz, yy, cc), FIRST_Z]

        def part_r(zz, yy, cc, n, mine=False):
            target = out.at[slot(zz, yy, cc), pl.ds(*cut_relay(zz, n))]
            source = own.at[pl.ds(*cut_relay(zz, n))] if mine else target
            return source, target, recv.at[slot(zz, yy, cc), FIRST_Z + 1 + n]

        def passed(zz, yy, n):
            length = LENGTHS[0][zz][2]
            target = passing.at[zz * 2 + yy, pl.ds(n * length, length)]
            return target, target, r_pass.at[zz * 2 + yy, n]

        def forward(count, make, names):
            start = io.many(count, make, names)

            def step(n):
                io.arrive(*make(n)[1:])
                start(n)

            each(count, step)

        def relay(zz, yy, names):
            start = io.many(RELAY, lambda n: passed(zz, yy, n), names)
            back = None
            if not (zz == z and yy is y):
                back = io.many(
                    RELAY,
                    lambda n: (passed(zz, yy, n)[0],) + part_r_there(zz, yy, n),
                    ["cross"],
                )

            def step(n):
                io.arrive(*passed(zz, yy, n)[1:])
                start(n)
                if back:
                    back(n)

            each(RELAY, step)

        def part_r_there(zz, yy, n):
            return part_r(zz, yy, c, n)[1:]

        keep = pltpu.make_async_copy(own, out.at[slot(z, y, c)], local)
        if s == 0:
            each(
                RELAY,
                io.many(
                    RELAY,
                    lambda n: (part_r(z, y, c, n, True)[0],) + passed(z, y, n)[1:],
                    ["cross"],
                ),
            )
            io.push(*part_y(z, y, c, True), "side")
            each(
                FIRST_Z,
                io.many(
                    FIRST_Z, lambda n: part_z(z, y, c, n, True), ["up", "down", "side"]
                ),
            )
            io.push(*part_y(z, y, c, True), "up", "down", "core")
            each(RELAY, io.many(RELAY, lambda n: part_r(z, y, c, n, True), ["core"]))
        else:
            relay(z, y, ["up", "down", "side"])
            mine = io.many(FIRST_Z, lambda n: part_z(z, y, c, n, True), ["up", "down", "side"])
            waiting = [z]
            for k in range(1, DEPTH + 1):
                each(FIRST_Z // DEPTH, lambda n, k=k: mine((k - 1) * (FIRST_Z // DEPTH) + n))
                near = [zz for zz in (z - k, z + k) if 0 <= zz < DEPTH]
                for zz in near:
                    relay(zz, y, ["up" if zz < z else "down", "side"])
                for zz in waiting:
                    relay(zz, 1 - y, [])
                waiting = near
        each(FIRST_Z, io.many(FIRST_Z, lambda n: part_z(z, y, c, n, True), ["core"]))
        keep.start()
        if s == 0:
            io.arrive(*part_y(z, 1 - y, c)[1:])
            io.push(*part_y(z, 1 - y, c), "up", "down", "core")
        waiting = [z]
        for k in range(1, DEPTH + 1):
            near = [zz for zz in (z - k, z + k) if 0 <= zz < DEPTH]
            starts = [
                io.many(
                    FIRST_Z,
                    lambda n, zz=zz: part_z(zz, y, c, n),
                    ["up" if zz < z else "down", "side", "core"],
                )
                for zz in near
            ]

            def step(n):
                for zz, start in zip(near, starts):
                    io.arrive(*part_z(zz, y, c, n)[1:])
                    start(n)

            if near:
                each(FIRST_Z, step)
            if s == 0:
                for zz in near:
                    for yy in (y, 1 - y):
                        io.arrive(*part_y(zz, yy, c)[1:])
                        io.push(*part_y(zz, yy, c), "up" if zz < z else "down", "core")
            for zz in waiting:
                forward(FIRST_Z, lambda n, zz=zz: part_z(zz, 1 - y, c, n), ["core"])
            if s == 0:
                for zz, yy in [(zz, 1 - y) for zz in waiting] + [(zz, y) for zz in near]:
                    forward(RELAY, lambda n, zz=zz, yy=yy: part_r(zz, yy, c, n), ["core"])
            waiting = near
        for zz in range(DEPTH):

            def last(yy, zz=zz):
                each(FIRST_Z, lambda n: io.arrive(*part_z(zz, yy, 1 - c, n)[1:]))
                if s == 0:
                    io.arrive(*part_y(zz, yy, 1 - c)[1:])
                    each(RELAY, lambda n: io.arrive(*part_r(zz, yy, 1 - c, n)[1:]))

            each(WIDTH, last)
        keep.wait()
        io.finish()

    for_each_depth(run)


def gather_slots(own):
    hbm = pl.BlockSpec(memory_space=pl.ANY)
    return pl.pallas_call(
        gather_kernel,
        out_shape=[
            jax.ShapeDtypeStruct((16, SLOT, 16, 128), BF),
            jax.ShapeDtypeStruct((8, RELAY * max(n[2] for n in LENGTHS[0]), 16, 128), BF),
        ],
        in_specs=[hbm],
        out_specs=[hbm, hbm],
        scratch_shapes=[
            pltpu.SemaphoreType.DMA((256,)),
            pltpu.SemaphoreType.DMA((16, PARTS)),
            pltpu.SemaphoreType.DMA((8, RELAY)),
            pltpu.SemaphoreType.DMA,
        ],
        name="gather_slots",
        compiler_params=pltpu.CompilerParams(
            collective_id=0, has_side_effects=True, vmem_limit_bytes=VMEM_LIMIT
        ),
    )(own)[0]


def send_order(z):
    order = []
    for k in range(DEPTH - 1, -1, -1):
        for zz in (z + k, z - k):
            if 0 <= zz < DEPTH and zz not in order:
                order.append(zz)
    return order


STEP_TILES = 4


def in_steps(start, count, some, carry=0):
    whole = count // STEP_TILES

    def body(i, carry):
        return some(start + i * STEP_TILES, STEP_TILES, carry)

    carry = lax.fori_loop(0, whole, body, carry)
    if count % STEP_TILES:
        carry = some(start + whole * STEP_TILES, count % STEP_TILES, carry)
    return carry


def total_of(sources, base, size):
    value = sources[0][pl.ds(base, size)].astype(F32)
    for source in sources[1:]:
        value = value + source[pl.ds(base, size)].astype(F32)
    return value


def add_tiles(target, sources, start, count):
    def some(base, size, carry):
        target[pl.ds(base, size)] = total_of(sources, base, size).astype(target.dtype)
        return carry

    in_steps(start, count, some)


class Shifted:
    def __init__(self, ref, start):
        self.ref, self.start = ref, start

    def __getitem__(self, index):
        return self.ref[pl.ds(index.start - self.start, index.size)]


class Section:
    def __init__(self, section, z, y, c, io, refs, sems, low=0, high=FIRST_Z):
        self.section, self.z, self.y, self.c, self.io = section, z, y, c, io
        self.low, self.count = low, high - low
        self.mats, self.vecs, self.held, self.core_in = refs[:4]
        self.side_a, self.side_b, self.z_a, self.z_b = refs[4:]
        self.load, self.r_core, self.r_side, self.r_z = sems
        self.order = send_order(z)
        self.tail = LENGTHS[section][z][1] > 0
        self.loads, self.ready = {}, set()

    def pieces(self, zz, yy, cc):
        slot = zz * 4 + yy * 2 + cc
        low = self.low * LENGTHS[self.section][zz][0]
        high = (self.low + self.count) * LENGTHS[self.section][zz][0]
        if self.low + self.count == FIRST_Z:
            high = size_of(self.section, zz)
        found = []
        if low < SLOT_V:
            count = min(high, SLOT_V) - low
            found.append((self.vecs.at[slot, pl.ds(low, count)], pl.ds(low, count)))
        low = max(low, SLOT_V)
        if high > low:
            source = self.mats.at[slot, pl.ds(low - SLOT_V, high - low)]
            found.append((source, pl.ds(low, high - low)))
        return found

    def begin_loads(self):
        for zz in self.order:
            for yy, flip in ((1 - self.y, True), (self.y, False)):
                where = zz * 2 + yy
                copies = [
                    pltpu.make_async_copy(source, self.held.at[where, there], self.load.at[where, n])
                    for n, (source, there) in enumerate(self.pieces(zz, yy, self.c))
                ]
                for copy in copies:
                    copy.start()
                self.loads[zz, flip] = copies

    def exchange_cores(self):
        for zz in self.order:
            for yy in (1 - self.y, self.y):
                where = zz * 2 + yy
                for n, (source, there) in enumerate(self.pieces(zz, yy, 1 - self.c)):
                    self.io.push(
                        source, self.core_in.at[where, there], self.r_core.at[where, n], "core"
                    )

    def prepare(self, zz, flip):
        if (zz, flip) in self.ready:
            return
        self.ready.add((zz, flip))
        yy = 1 - self.y if flip else self.y
        where = zz * 2 + yy
        for copy in self.loads[zz, flip]:
            copy.wait()
        for n, (_, there) in enumerate(self.pieces(zz, yy, self.c)):
            self.io.arrive(self.core_in.at[where, there], self.r_core.at[where, n])

    def z_cut(self, zz, n):
        return cut_z(self.section, zz, self.low + n)

    def y_cut(self, zz):
        return cut_y(self.section, zz)

    def cut(self, zz, yy, cut):
        return self.held.at[zz * 2 + yy, pl.ds(*cut)]

    def side_in(self, zz, n):
        return self.side_a.at[zz, pl.ds(*self.z_cut(zz, n))], self.r_side.at[zz, self.low + n]

    def side_tail(self, zz):
        return self.side_b.at[pl.ds(0, self.y_cut(zz)[1])], self.r_side.at[zz, FIRST_Z]

    def z_in(self, way, zz, n):
        return self.z_a.at[way, zz, pl.ds(*self.z_cut(zz, n))], self.r_z.at[way, zz, self.low + n]

    def z_tail(self, way, zz, yy):
        ref = self.z_b.at[way, zz, yy, pl.ds(0, self.y_cut(zz)[1])]
        return ref, self.r_z.at[way, zz, FIRST_Z + yy]

    def came(self, cut, pair):
        self.io.arrive(*pair)
        return Shifted(pair[0], cut[0])

    def core_sources(self, zz, yy):
        return [self.held.at[zz * 2 + yy], self.core_in.at[zz * 2 + yy]]

    def add(self, zz, yy, cut, sources):
        add_tiles(self.held.at[zz * 2 + yy], sources, *cut)

    def to_side(self, zz):
        self.prepare(zz, True)
        flip = 1 - self.y
        start = self.io.many(
            self.count,
            lambda n: (self.cut(zz, flip, self.z_cut(zz, n)),) + self.side_in(zz, n),
            ["side"],
        )

        def step(n):
            self.add(zz, flip, self.z_cut(zz, n), self.core_sources(zz, flip))
            start(n)

        each(self.count, step)

    def way(self, zz):
        return (0, "up", 0) if zz > self.z else (1, "down", DEPTH - 1)

    def along(self, zz):
        self.prepare(zz, False)
        way, name, first = self.way(zz)
        start = self.io.many(
            self.count,
            lambda n: (self.cut(zz, self.y, self.z_cut(zz, n)),) + self.z_in(way, zz, n),
            [name],
        )

        def step(n):
            cut = self.z_cut(zz, n)
            sources = self.core_sources(zz, self.y) + [self.came(cut, self.side_in(zz, n))]
            if self.z != first:
                sources.append(self.came(cut, self.z_in(way, zz, n)))
            self.add(zz, self.y, cut, sources)
            start(n)

        each(self.count, step)

    def along_tail(self, zz, flip):
        yy = 1 - self.y if flip else self.y
        self.prepare(zz, flip)
        way, name, first = self.way(zz)
        cut = self.y_cut(zz)
        sources = self.core_sources(zz, yy)
        if self.z != first:
            sources.append(self.came(cut, self.z_tail(way, zz, yy)))
        self.add(zz, yy, cut, sources)
        self.io.push(self.cut(zz, yy, cut), *self.z_tail(way, zz, yy), name)

    def here(self):
        return [way for way, there in ((0, self.z > 0), (1, self.z < DEPTH - 1)) if there]

    def tails(self, yy):
        cut = self.y_cut(self.z)
        return self.core_sources(self.z, yy) + [
            self.came(cut, self.z_tail(way, self.z, yy)) for way in self.here()
        ]

    def tail_to_side(self):
        z, flip = self.z, 1 - self.y
        self.prepare(z, False)
        self.add(z, flip, self.y_cut(z), self.tails(flip))
        self.io.push(self.cut(z, flip, self.y_cut(z)), *self.side_tail(z), "side")

    def end(self, total, carry):
        z, y = self.z, self.y
        self.prepare(z, False)
        if self.tail:
            cut = self.y_cut(z)
            carry = total(cut, self.tails(y) + [self.came(cut, self.side_tail(z))], carry)

        def step(n, carry):
            cut = self.z_cut(z, n)
            sources = self.core_sources(z, y) + [
                self.came(cut, self.z_in(way, z, n)) for way in self.here()
            ]
            return total(cut, sources + [self.came(cut, self.side_in(z, n))], carry)

        return lax.fori_loop(0, self.count, step, carry)


def owned_limits(plans):
    limits = []
    for plan, shapes in zip(plans, (ENC_MATS, DEC_MATS)):
        low = 0
        for _, count, pieces in plan:
            if not pieces:
                limits.append((0, 0, 0, 0, 0))
                continue
            blocks, line, _, _ = pieces[0]
            skip = -line // blocks if line < 0 else 0
            last, line, rows, _ = pieces[-1]
            over = max(0, line + rows * 16 * last - LINES) // last
            limits.append((count, blocks, skip, last, over))
    return limits


def finish_tiles(out, sources, start, count, owned, square):
    tiles, first, skip, last, over = owned
    row = lax.broadcasted_iota(jnp.int32, (1, 16, 1), 1)

    def some(base, size, square):
        value = total_of(sources, base, size)
        out[pl.ds(base, size)] = value
        tile = base - SLOT_V + lax.broadcasted_iota(jnp.int32, (size, 1, 1), 0)
        mine = (tile < tiles) & ((tile >= first) | (row >= skip))
        mine = mine & ((tile < tiles - last) | (row < 16 - over))
        mine = mine | (tile < 0)
        value = jnp.where(mine, value * value, 0.0)
        return square + value.reshape(size * 2, 8, 128).sum(0)

    return in_steps(start, count, some, square)


def section_scratch(section):
    most = FIRST_Z * max(n[0] for n in LENGTHS[0] + LENGTHS[1])
    tail = max(1, max(n[1] for n in LENGTHS[section]))
    size = max(size_of(s, z) for s in range(2) for z in range(DEPTH))
    buffers = [
        pltpu.VMEM((8, size, 16, 128), BF),
        pltpu.VMEM((8, size, 16, 128), BF),
        pltpu.VMEM((DEPTH, most, 16, 128), BF),
        pltpu.VMEM((tail, 16, 128), BF),
        pltpu.VMEM((2, DEPTH, most, 16, 128), BF),
        pltpu.VMEM((2, DEPTH, 2, tail, 16, 128), BF),
    ]
    sems = [
        pltpu.SemaphoreType.DMA((8, 2)),
        pltpu.SemaphoreType.DMA((8, 2)),
        pltpu.SemaphoreType.DMA((DEPTH, FIRST_Z + 1)),
        pltpu.SemaphoreType.DMA((2, DEPTH, FIRST_Z + 2)),
    ]
    return buffers, sems


def scatter_second_kernel(mats, vecs, out, *refs):
    buffers, sems, send = refs[:6], refs[6:10], refs[10]

    def run(s, z, y, c):
        if s == 0:
            return
        around = devices_around(z, y, c, s)
        del around["cross"]
        io = Sender(around, send)
        part = Section(1, z, y, c, io, (mats, vecs) + buffers, sems, 0, EARLY)
        part.begin_loads()
        greet(around)
        part.exchange_cores()
        for zz in part.order:
            part.to_side(zz)
        for zz in part.order[:-1]:
            part.along(zz)

        def total(cut, sources, carry):
            add_tiles(out, sources, *cut)
            return carry

        part.end(total, 0)
        io.finish()

    for_each_depth(run)


def scatter_second(mats, vecs):
    hbm = pl.BlockSpec(memory_space=pl.ANY)
    buffers, sems = section_scratch(1)
    return pl.pallas_call(
        scatter_second_kernel,
        out_shape=jax.ShapeDtypeStruct((SLOT, 16, 128), F32),
        in_specs=[hbm, hbm],
        out_specs=pl.BlockSpec(memory_space=pltpu.VMEM),
        scratch_shapes=buffers + sems + [pltpu.SemaphoreType.DMA((112,))],
        name="scatter_second",
        compiler_params=pltpu.CompilerParams(
            collective_id=3, has_side_effects=True, vmem_limit_bytes=VMEM_LIMIT
        ),
    )(mats, vecs)


def scatter_first_kernel(limits, mats, vecs, second, second_vecs, other_sum, loss, out, total, *refs):
    buffers, sems = refs[:6], refs[6:10]
    r_in, r_side, r_z, r_back, parts, send, s_in, s_side, s_z, s_back, s_parts = refs[10:]
    me = lax.axis_index("section") * 16 + lax.axis_index("dp")
    owned = [sum(jnp.where(me == k, row[n], 0) for k, row in enumerate(limits)) for n in range(5)]

    def other(k):
        device = lax.rem(me + k, 32)
        return device, (device // 16, lax.rem(device, 16))

    def greet_all():
        barrier = pltpu.get_barrier_semaphore()
        for k in range(1, 32):
            pl.semaphore_signal(barrier, inc=1, device_id=other(k)[1], device_id_type=MESH)
        pl.semaphore_wait(barrier, 31)

    def relay(ref, zz, n):
        length = LENGTHS[0][zz][2]
        return ref.at[pl.ds(n * length, length)]

    def keep(square):
        row = lax.broadcasted_iota(jnp.int32, (8, 128), 0)
        parts[me] = jnp.where(row == 0, jnp.sum(square), loss[...])

    def run_first(z, y, c, io):
        part = Section(0, z, y, c, io, (mats, vecs) + buffers, sems)
        part.begin_loads()
        greet_all()
        part.exchange_cores()

        def cross(zz, yy):
            where = zz * 2 + yy
            start = io.many(
                RELAY,
                lambda n: (
                    part.cut(zz, yy, cut_relay(zz, n)),
                    relay(r_in.at[where], zz, n),
                    s_in.at[where, n],
                ),
                ["cross"],
            )

            def step(n):
                part.add(zz, yy, cut_relay(zz, n), part.core_sources(zz, yy))
                start(n)

            each(RELAY, step)

        for zz in part.order:
            part.to_side(zz)
            cross(zz, 1 - y)
            if zz != z:
                part.prepare(zz, False)
                cross(zz, y)
                part.along_tail(zz, True)
                part.along_tail(zz, False)
        part.tail_to_side()
        for zz in part.order[:-1]:
            part.along(zz)

        def total(cut, sources, square):
            return finish_tiles(out, sources, *cut, owned, square)

        square = part.end(total, jnp.zeros((8, 128), F32))

        def last(n, square):
            io.arrive(relay(r_back, z, n), s_back.at[n])
            sources = part.core_sources(z, y) + [Shifted(r_back, cut_relay(z, 0)[0])]
            return total(cut_relay(z, n), sources, square)

        keep(lax.fori_loop(0, RELAY, last, square))

    def run_second(z, y, c, io):
        part = Section(1, z, y, c, io, (second, second_vecs) + buffers, sems, EARLY)
        part.begin_loads()
        greet_all()
        part.exchange_cores()

        def came(ref, zz, n, sem):
            there = relay(ref, zz, n)
            io.arrive(there, sem)
            return there

        def small_add(target, sources):
            add_tiles(target, sources, 0, target.shape[0])

        for zz in part.order:
            flip, same = zz * 2 + 1 - y, zz * 2 + y
            start = io.many(
                RELAY,
                lambda n, zz=zz, flip=flip: (
                    relay(r_in.at[flip], zz, n),
                    relay(r_side.at[zz], zz, n),
                    s_side.at[zz, n],
                ),
                ["side"],
            )

            def to_side(n):
                came(r_in.at[flip], zz, n, s_in.at[flip, n])
                start(n)

            each(RELAY, to_side)
            part.to_side(zz)
            if zz == z:
                continue
            way, name, first = part.way(zz)
            onward = io.many(
                RELAY,
                lambda n, zz=zz, same=same, way=way: (
                    relay(r_in.at[same], zz, n),
                    relay(r_z.at[way, zz], zz, n),
                    s_z.at[way, zz, n],
                ),
                [name],
            )

            def along(n):
                mine = came(r_in.at[same], zz, n, s_in.at[same, n])
                sources = [mine, came(r_side.at[zz], zz, n, s_side.at[zz, n])]
                if z != first:
                    sources.append(came(r_z.at[way, zz], zz, n, s_z.at[way, zz, n]))
                small_add(mine, sources)
                onward(n)

            each(RELAY, along)
            part.along(zz)
        mine = r_in.at[z * 2 + y]
        back = io.many(
            RELAY,
            lambda n: (relay(mine, z, n), relay(r_back, z, n), s_back.at[n]),
            ["cross"],
        )

        def last(n):
            sources = [came(r_side.at[z], z, n, s_side.at[z, n])]
            for way in part.here():
                sources.append(came(r_z.at[way, z], z, n, s_z.at[way, z, n]))
            small_add(relay(mine, z, n), sources)
            back(n)

        each(RELAY, last)
        square = jnp.zeros((8, 128), F32)
        high = EARLY * LENGTHS[1][z][0]
        square = finish_tiles(out, [other_sum], 0, high, owned, square)

        def total(cut, sources, square):
            return finish_tiles(out, sources, *cut, owned, square)

        keep(part.end(total, square))

    def run(s, z, y, c):
        io = Sender(devices_around(z, y, c, s), send)
        (run_second if s else run_first)(z, y, c, io)
        io.finish()

    for_each_depth(run)
    copies = []
    for k in range(1, 32):
        copy = pltpu.make_async_remote_copy(
            parts.at[me],
            parts.at[me],
            send.at[k],
            s_parts.at[me],
            device_id=other(k)[1],
            device_id_type=MESH,
        )
        copy.start()
        copies.append(copy)
    for k in range(1, 32):
        device, where = other(k)
        pltpu.make_async_remote_copy(
            parts.at[device],
            parts.at[device],
            send.at[k],
            s_parts.at[device],
            device_id=where,
            device_id_type=MESH,
        ).wait_recv()
    total[...] = jnp.sum(parts[...], 0)
    for copy in copies:
        copy.wait_send()


def scatter_first(limits, mats, vecs, second, second_vecs, other_sum, loss):
    hbm = pl.BlockSpec(memory_space=pl.ANY)
    vm = pl.BlockSpec(memory_space=pltpu.VMEM)
    buffers, sems = section_scratch(0)
    most, count = RELAY * max(n[2] for n in LENGTHS[0]), RELAY
    return pl.pallas_call(
        functools.partial(scatter_first_kernel, limits),
        out_shape=[
            jax.ShapeDtypeStruct((SLOT, 16, 128), F32),
            jax.ShapeDtypeStruct((8, 128), F32),
        ],
        in_specs=[hbm] * 4 + [vm, vm],
        out_specs=[vm] * 2,
        scratch_shapes=buffers
        + sems
        + [
            pltpu.VMEM((8, most, 16, 128), BF),
            pltpu.VMEM((DEPTH, most, 16, 128), BF),
            pltpu.VMEM((2, DEPTH, most, 16, 128), BF),
            pltpu.VMEM((most, 16, 128), BF),
            pltpu.VMEM((32, 8, 128), F32),
            pltpu.SemaphoreType.DMA((160,)),
            pltpu.SemaphoreType.DMA((8, count)),
            pltpu.SemaphoreType.DMA((DEPTH, count)),
            pltpu.SemaphoreType.DMA((2, DEPTH, count)),
            pltpu.SemaphoreType.DMA((count,)),
            pltpu.SemaphoreType.DMA((32,)),
        ],
        name="scatter_first",
        compiler_params=pltpu.CompilerParams(
            collective_id=1, has_side_effects=True, vmem_limit_bytes=VMEM_LIMIT
        ),
    )(mats, vecs, second, second_vecs, other_sum, loss)


def piece_table(lines):
    plans = [shard_plan(m, lines * 128 * 16, 16) for m in (ENC_MATS, DEC_MATS)]
    most = max(len(pieces) for plan in plans for _, _, pieces in plan)
    table = [
        [[list(p) for p in pieces] + [[0] * 4] * (most - len(pieces)) for _, _, pieces in plan]
        for plan in plans
    ]
    widths = sorted({p[0] for plan in plans for _, _, pieces in plan for p in pieces})
    return plans, table, widths


def each_tile(table, widths, run):
    for piece in range(table.shape[0]):
        for width in widths:

            @pl.when(table[piece, 0] == width)
            def _(piece=piece, width=width):
                def step(i, carry):
                    for j in range(width):
                        line = MARGIN + table[piece, 1] + i * (16 * width) + j
                        run(line, width, SLOT_V + table[piece, 3] + i * width + j)
                    return carry

                lax.fori_loop(0, table[piece, 2], step, 0)


def pack_kernel(widths, table, mat, vec, out, lines, sem):
    count = mat.shape[0]
    copy = pltpu.make_async_copy(mat, lines.at[pl.ds(MARGIN, count)], sem)
    copy.start()
    lines[0:MARGIN, :] = jnp.zeros((MARGIN, 128), F32)
    lines[MARGIN + count :, :] = jnp.zeros((MARGIN, 128), F32)
    out[0:SLOT_V] = vec[...].astype(BF).reshape(SLOT_V, 16, 128)
    copy.wait()

    def run(line, width, tile):
        out[tile] = lines[pl.ds(line, 16, stride=width), :].astype(BF)

    each_tile(table, widths, run)


def pack(table, widths, mat, vec):
    vm = pl.BlockSpec(memory_space=pltpu.VMEM)
    return pl.pallas_call(
        functools.partial(pack_kernel, widths),
        out_shape=jax.ShapeDtypeStruct((SLOT, 16, 128), BF),
        in_specs=[
            pl.BlockSpec(memory_space=pltpu.SMEM),
            pl.BlockSpec(memory_space=pl.ANY),
            vm,
        ],
        out_specs=vm,
        scratch_shapes=[
            pltpu.VMEM((mat.shape[0] + 2 * MARGIN, 128), F32),
            pltpu.SemaphoreType.DMA,
        ],
        name="pack",
        compiler_params=pltpu.CompilerParams(vmem_limit_bytes=VMEM_LIMIT),
    )(table, mat, vec)


def clip_factor(square):
    return jnp.minimum(1.0, 0.001 / (jnp.sqrt(square) + 1e-06))


def adam_update(master, first, second, grad, rate, decay):
    first = 0.9 * first + 0.1 * grad
    second = 0.95 * second + 0.05 * grad * grad
    step_first = first / (1.0 - 0.9**STEP)
    step_second = second / (1.0 - 0.95**STEP)
    master = master - rate * (step_first / (jnp.sqrt(step_second) + 1e-08) + decay * master)
    return (master, first, second)


STEPS = 6


def update_kernel(widths, table, tiles, total, *refs):
    states, news, news_vec, (lines, held, fresh, sem_in, sem_out) = (
        refs[0:3],
        refs[3:6],
        refs[6],
        refs[7:],
    )
    count = held.shape[1]
    size = count // STEPS

    def part(i):
        return pl.ds(i * size, size)

    loads = [
        [
            pltpu.make_async_copy(state.at[part(i)], held.at[n, part(i)], sem_in.at[n, i])
            for n, state in enumerate(states)
        ]
        for i in range(STEPS)
    ]
    for step in loads:
        for copy in step:
            copy.start()
    lines[...] = jnp.zeros_like(lines)

    def run(line, width, tile):
        lines[pl.ds(line, 16, stride=width), :] = tiles[tile]

    each_tile(table, widths, run)
    news_vec[...] = tiles[0:SLOT_V].reshape(SLOT_V * 16, 128)
    factor = clip_factor(total[0:1, :])
    stores = []
    for i in range(STEPS):
        for copy in loads[i]:
            copy.wait()

        def body(k, carry, i=i):
            base = i * size + k * 104
            rows = pl.ds(pl.multiple_of(base, 8), 104)
            grad = factor * lines[pl.ds(pl.multiple_of(MARGIN + base, 8), 104), :]
            for n, value in enumerate(
                adam_update(held[0, rows, :], held[1, rows, :], held[2, rows, :], grad, 0.05, 0.05)
            ):
                fresh[n, rows, :] = value
            return carry

        lax.fori_loop(0, size // 104, body, 0)
        for n, new in enumerate(news):
            copy = pltpu.make_async_copy(fresh.at[n, part(i)], new.at[part(i)], sem_out.at[n, i])
            copy.start()
            stores.append(copy)
    for copy in stores:
        copy.wait()


def update(table, widths, tiles, total, states):
    count = states[0].shape[0]
    vm = pl.BlockSpec(memory_space=pltpu.VMEM)
    hbm = pl.BlockSpec(memory_space=pl.ANY)
    shape = jax.ShapeDtypeStruct((count, 128), F32)
    return pl.pallas_call(
        functools.partial(update_kernel, widths),
        out_shape=[shape] * 3 + [jax.ShapeDtypeStruct((SLOT_V * 16, 128), F32)],
        in_specs=[pl.BlockSpec(memory_space=pltpu.SMEM), vm, vm] + [hbm] * 3,
        out_specs=[hbm] * 3 + [vm],
        scratch_shapes=[
            pltpu.VMEM((count + 2 * MARGIN, 128), F32),
            pltpu.VMEM((3, count, 128), F32),
            pltpu.VMEM((3, count, 128), F32),
            pltpu.SemaphoreType.DMA((3, STEPS)),
            pltpu.SemaphoreType.DMA((3, STEPS)),
        ],
        name="update",
        compiler_params=pltpu.CompilerParams(vmem_limit_bytes=VMEM_LIMIT),
    )(table, tiles, total, *states)


def shifted(value, axis, steps):
    count = lax.axis_size(axis)
    initial, last = (max(0, -steps), min(count, count - steps))
    return lax.ppermute(value, axis, [(source, source + steps) for source in range(initial, last)])


def train(images, masked_total, enc, dec, enc_out, dec_out, pixels, visible, restore, vecs, weights):
    pix = jnp.pad(pixels, ((0, 0), (0, ROWS_D - PATCHES), (0, 0)))
    vis = jnp.pad(visible, ((0, 0), (0, ROWS_E - VIS)), constant_values=-1).reshape(-1, 1)
    places = jnp.pad(restore, ((0, 0), (0, ROWS_D - PATCHES)), constant_values=-1).reshape(-1, 1)
    latent, *saved = encoder_forward(images, enc, vis, pix, vecs, weights, 0)
    arrived = shifted(latent, "section", 1)
    dlatent, loss, dmats_dec, dvec_dec = decoder_step(
        images, dec, dec_out, masked_total, arrived, places, pix, vecs, weights, 1
    )
    returned = shifted(dlatent, "section", -1)
    dmats, dvec = encoder_backward(images, enc, enc_out, vis, vecs, returned, saved, weights, 0)
    return dmats, dvec, dmats_dec, dvec_dec, loss


def body_block(
    pixels, visible, restore, mat_master, mat_first, mat_second, vec_master, vec_first, vec_second
):
    images = pixels.shape[0]
    masked_total = (PATCHES - VIS) * images * 16
    count, size = mat_master.shape[1] // 128, vec_master.shape[1]
    plans, table, widths = piece_table(count)
    table = jnp.asarray(table, jnp.int32)[lax.axis_index("section"), lax.axis_index("dp")]
    lines = [value.reshape(count, 128) for value in (mat_master, mat_first, mat_second)]
    room = SLOT_V * 2048
    own = pack(
        table, widths, lines[0], jnp.pad(vec_master[0], (0, room - size)).reshape(-1, 128)
    )
    slots = gather_slots(own)
    vecs = slots[:, :SLOT_V].reshape(16, room)[:, :size].reshape(-1, 128).astype(F32)
    inward = [slot_layout(plan, slots.shape, SLOT_V) for plan in plans]
    outward = [whole_slots(plan, (16, SLOT_M, 16, 128)) for plan in plans]
    dmats, dvec, dmats_dec, dvec_dec, loss = train(
        images, masked_total, *inward, *outward, pixels, visible, restore, vecs, slots
    )
    dvec, dvec_dec = (
        jnp.pad(value.reshape(16, size), ((0, 0), (0, room - size)))
        .astype(BF)
        .reshape(16, SLOT_V, 16, 128)
        for value in (dvec, dvec_dec)
    )
    second = scatter_second(dmats_dec, dvec_dec)
    tiles, total = scatter_first(
        owned_limits(plans), dmats, dvec, dmats_dec, dvec_dec, second, loss
    )
    *news, grad_vec = update(table, widths, tiles, total, lines)
    news = [value.reshape(mat_master.shape) for value in news]
    square, loss_sum = total[0, 0], total[1, 0]
    vec_news = adam_update(
        vec_master,
        vec_first,
        vec_second,
        clip_factor(square) * grad_vec.reshape(1, room)[:, :size],
        0.3,
        0.0,
    )
    return (
        (loss_sum, jnp.sqrt(square))
        + tuple(news)
        + (news[0].astype(BF),)
        + tuple(vec_news)
        + (vec_news[0].astype(BF),)
    )


def body(
    pixels, visible, restore, mat_master, mat_first, mat_second, vec_master, vec_first, vec_second
):
    images = pixels.shape[0]
    total = mat_master.shape[1] * lax.axis_size("dp")
    masked_total = (PATCHES - VIS) * images * lax.axis_size("dp")
    encoding = lax.axis_index("section") == 0
    enc, dec = plain_layout(ENC_TOTAL), plain_layout(DEC_TOTAL)
    mats = lax.all_gather(mat_master.astype(BF), "dp", axis=1, tiled=True)[0]
    vecs = lax.all_gather(vec_master.astype(BF), "dp", axis=1, tiled=True)[0]
    vecs = vecs.astype(F32).reshape(-1, 128)
    weights = lax.cond(
        encoding,
        lambda m: natural(m, ENC_MATS),
        lambda m: jnp.pad(natural(m, DEC_MATS), ((0, ENC_TOTAL - DEC_TOTAL), (0, 0), (0, 0))),
        mats,
    )
    dec_in = Layout((ENC_TOTAL, 16, 128), [(lambda ref: ref.at[pl.ds(0, DEC_TOTAL)], 0, DEC_TOTAL)], [])
    dmats, dvec, dmats_dec, dvec_dec, loss = train(
        images, masked_total, enc, dec_in, enc, dec, pixels, visible, restore, vecs, weights
    )
    grad_mats, grad_vecs = lax.cond(
        encoding,
        lambda: (flat_from_natural(dmats.astype(F32), ENC_MATS, total), dvec),
        lambda: (flat_from_natural(dmats_dec.astype(F32), DEC_MATS, total), dvec_dec),
    )
    summed_mats = lax.psum_scatter(grad_mats[None], "dp", scatter_dimension=1, tiled=True)
    summed_vecs = lax.psum_scatter(
        grad_vecs.reshape(1, -1), "dp", scatter_dimension=1, tiled=True
    )
    square = jnp.sum(summed_mats * summed_mats) + jnp.sum(summed_vecs * summed_vecs)
    square, loss_sum = lax.psum((square, loss[0, 0]), ("section", "dp"))
    factor = clip_factor(square)
    mat_news = adam_update(mat_master, mat_first, mat_second, factor * summed_mats, 0.05, 0.05)
    vec_news = adam_update(vec_master, vec_first, vec_second, factor * summed_vecs, 0.3, 0.0)
    return (
        (loss_sum, jnp.sqrt(square))
        + tuple(mat_news)
        + (mat_news[0].astype(BF),)
        + tuple(vec_news)
        + (vec_news[0].astype(BF),)
    )


def solution(mesh):
    split = P("section", "dp")
    fits = mesh.shape["section"] == 2 and mesh.shape["dp"] == 16
    return jax.shard_map(
        body_block if fits else body,
        mesh=mesh,
        in_specs=(P("dp", None, None), P("dp", None), P("dp", None)) + (split,) * 6,
        out_specs=(P(), P()) + (split,) * 8,
        check_vma=False,
    )
```

```python
import functools
import math

import jax
import jax.numpy as jnp
from jax import lax
from jax.experimental import pallas as pl
from jax.experimental.pallas import tpu as pltpu
from jax.sharding import PartitionSpec as P

PIX = 768
DE = 768
HE = 12
FE = 3072
DD = 512
HD = 16
FD = 2048
PATCHES = 196
VIS = 49
STEP = 10
ROWS_E = 64
ROWS_D = 208
EPS = 1e-6
BF = jnp.bfloat16
F32 = jnp.float32
VMEM_LIMIT = 63 * 1024 * 1024

ENC_MATS = [(PIX, DE), (DE, 3 * DE), (DE, DE), (DE, FE), (FE, DE)]
DEC_MATS = [(DE, DD), (DD, 3 * DD), (DD, DD), (DD, FD), (FD, DD), (DD, PIX)]
ENC_VECS = [DE, PATCHES * DE, DE, DE, 2 * DE, DE, DE, DE, FE, DE, DE, DE]
DEC_VECS = [DD, DD, PATCHES * DD, DD, DD, 2 * DD, DD, DD, DD, FD, DD, DD, DD, PIX]


def starts(sizes):
    total, found = 0, []
    for size in sizes:
        found.append(total)
        total += size
    return found, total


ENC_TILES = [k * n // 2048 for k, n in ENC_MATS]
DEC_TILES = [k * n // 2048 for k, n in DEC_MATS]
ENC_BASE, ENC_TOTAL = starts(ENC_TILES)
DEC_BASE, DEC_TOTAL = starts(DEC_TILES)
EV, _ = starts([size // 128 for size in ENC_VECS])
DV, _ = starts([size // 128 for size in DEC_VECS])


class Mat:
    def __init__(self, ref, base, shape, loads=None, stores=None):
        self.base, self.loads, self.stores = base, loads, stores
        self.rows, self.columns = shape
        self.blocks = self.columns // 128
        count = self.rows * self.columns // 2048
        self.ref = ref.at[pl.ds(base, count)].reshape(self.rows // 16, self.blocks, 16, 128)

    def need(self):
        self.loads.need(self.base, self.rows * self.columns // 2048)

    def done(self):
        self.stores.done(self.base, self.rows * self.columns // 2048)

    def cols(self, block):
        parts = [self.ref[:, 2 * block + half].reshape(self.rows, 128) for half in range(2)]
        return jnp.concatenate(parts, 1)

    def band(self, block):
        part = self.ref.at[pl.ds(block * 16, 16)]
        return jnp.concatenate([part[:, j].reshape(256, 128) for j in range(self.blocks)], 1)

    def put_cols(self, block, value):
        for half in range(2):
            piece = value[:, half * 128 : (half + 1) * 128].astype(BF)
            self.ref[:, 2 * block + half] = piece.reshape(self.rows // 16, 16, 128)

    def put_band(self, block, value):
        part = self.ref.at[pl.ds(block * 16, 16)]
        for j in range(self.blocks):
            part[:, j] = value[:, j * 128 : (j + 1) * 128].astype(BF).reshape(16, 16, 128)


def dot(a, b):
    return jnp.dot(a, b, preferred_element_type=F32)


def dot_t(a, b):
    return lax.dot_general(a, b, (((1,), (1,)), ((), ())), preferred_element_type=F32)


def t_dot(a, b):
    return lax.dot_general(a, b, (((0,), (0,)), ((), ())), preferred_element_type=F32)


def loop(count, body, init=0):
    return lax.fori_loop(0, count, body, init)


def lanes(block, width=256):
    return pl.ds(pl.multiple_of(block * width, width), width)


def row_of(vec, start, width):
    return jnp.concatenate([vec[start + j : start + j + 1, :] for j in range(width // 128)], 1)


def row_at(vec, start, block):
    return jnp.concatenate([vec[pl.ds(start + 2 * block + h, 1), :] for h in range(2)], 1)


def put_row(dvec, start, value):
    for j in range(value.shape[1] // 128):
        dvec[start + j : start + j + 1, :] = value[:, j * 128 : (j + 1) * 128]


def put_row_at(dvec, start, block, value):
    for h in range(2):
        dvec[pl.ds(start + 2 * block + h, 1), :] = value[:, h * 128 : (h + 1) * 128]


def fold(value):
    return value.reshape(value.shape[0] // 8, 8, value.shape[1]).sum(0)


def total_row(value):
    return jnp.sum(value, 0, keepdims=True)


def norm_parts(x):
    mean = jnp.mean(x, -1, keepdims=True)
    centred = x - mean
    scale = lax.rsqrt(jnp.mean(centred * centred, -1, keepdims=True) + EPS)
    return centred * scale, scale


CHUNKS = (208, 128, 64, 32)


def chunk_loop(ref, step, init=0):
    count = ref.shape[0]
    size = next(c for c in CHUNKS if count % c == 0)

    def run(i, carry):
        return step(pl.ds(pl.multiple_of(i * size, size), size), carry)

    return lax.fori_loop(0, count // size, run, init)


def norm_rows(x_ref, out_ref, vec, gain_at, shift_at, width, add_ref=None, bias_at=None):
    gain, shift = row_of(vec, gain_at, width), row_of(vec, shift_at, width)
    bias = None if bias_at is None else row_of(vec, bias_at, width)

    def step(rows, carry):
        x = x_ref[rows, :]
        if add_ref is not None:
            x = x + add_ref[rows, :] + bias
            add_ref[rows, :] = x
        unit, _ = norm_parts(x)
        out_ref[rows, :] = (unit * gain + shift).astype(BF)
        return carry

    chunk_loop(x_ref, step)


def norm_back_rows(x_ref, dy_ref, dx_ref, dxb_ref, vec, dvec, gain_at, shift_at, width, bias_at, add):
    gain = row_of(vec, gain_at, width)
    zero = jnp.zeros((8, width), F32)

    def step(rows, carry):
        dgain, dshift, dbias = carry
        unit, scale = norm_parts(x_ref[rows, :])
        dy = dy_ref[rows, :].astype(F32)
        dunit = dy * gain
        dx = scale * (
            dunit
            - jnp.mean(dunit, -1, keepdims=True)
            - unit * jnp.mean(dunit * unit, -1, keepdims=True)
        )
        if add:
            dx = dx + dx_ref[rows, :]
        dx_ref[rows, :] = dx
        dxb_ref[rows, :] = dx.astype(BF)
        return dgain + fold(dy * unit), dshift + fold(dy), dbias + fold(dx)

    dgain, dshift, dbias = chunk_loop(x_ref, step, (zero, zero, zero))
    put_row(dvec, gain_at, total_row(dgain))
    put_row(dvec, shift_at, total_row(dshift))
    if bias_at is not None:
        put_row(dvec, bias_at, total_row(dbias))
    return dbias


GELU_C = math.sqrt(2.0 / math.pi)


def gelu_parts(x):
    square = x * x
    t = jnp.tanh(x * (GELU_C + (GELU_C * 0.044715) * square))
    half = 0.5 * (1.0 + t)
    return x * half, half + (0.5 * x) * (1.0 - t * t) * (
        GELU_C + (3.0 * 0.044715 * GELU_C) * square
    )


def head_mask(size):
    lane = lax.broadcasted_iota(jnp.int32, (1, 128), 1)
    return [(lane >= h * size) & (lane < (h + 1) * size) for h in range(128 // size)]


def heads_apart(value, masks):
    return jnp.concatenate([jnp.where(mask, value, jnp.zeros_like(value)) for mask in masks], 0)


def heads_joined(stacked, masks, group):
    value = stacked[0:group]
    for h, mask in list(enumerate(masks))[1:]:
        value = jnp.where(mask, stacked[h * group : (h + 1) * group], value)
    return value


def attention(qkv, probs, att, bias, group, groups, width, size):
    blocks = width // 128
    masks = head_mask(size)
    heads = len(masks)

    def step(i, carry):
        g, b = i // blocks, i % blocks
        rows = pl.ds(pl.multiple_of(g * group, 16), group)
        q = qkv[rows, lanes(b, 128)]
        k = qkv[rows, lanes(blocks + b, 128)]
        v = qkv[rows, lanes(2 * blocks + b, 128)]
        s = dot_t(heads_apart(k, masks), q).reshape(heads, group, group) + bias
        e = jnp.exp(s - jnp.max(s, 1, keepdims=True))
        p = (e * (1.0 / jnp.sum(e, 1, keepdims=True))).astype(BF)
        probs[pl.ds(i * heads, heads)] = p
        turned = v.T
        out = [dot(turned[h * size : (h + 1) * size], p[h]) for h in range(heads)]
        att[rows, lanes(b, 128)] = jnp.concatenate(out, 0).astype(BF).T
        return carry

    lax.fori_loop(0, groups * blocks, step, 0, unroll=UNROLL)


UNROLL = 2


def attention_back(qkv, probs, datt, dqkv, dvec, qv_at, group, groups, width, size):
    blocks = width // 128
    masks = head_mask(size)
    heads = len(masks)
    scale = size ** (-0.5)
    for j in range(2 * blocks):
        dvec[qv_at + j : qv_at + j + 1, :] = jnp.zeros((1, 128), F32)

    def step(i, carry):
        g, b = i // blocks, i % blocks
        rows = pl.ds(pl.multiple_of(g * group, 16), group)
        q = qkv[rows, lanes(b, 128)]
        k = qkv[rows, lanes(blocks + b, 128)]
        v = qkv[rows, lanes(2 * blocks + b, 128)]
        da = datt[rows, lanes(b, 128)]
        p = probs[pl.ds(i * heads, heads)]
        dp = dot_t(heads_apart(v, masks), da).reshape(heads, group, group)
        wide = p.astype(F32)
        prod = wide * dp
        ds = (prod - wide * jnp.sum(prod, 1, keepdims=True)).astype(BF)
        turned = k.T
        dq = [dot(turned[h * size : (h + 1) * size], ds[h]) for h in range(heads)]
        dq = jnp.concatenate(dq, 0).T * scale
        dk = heads_joined(dot(ds.reshape(heads * group, group), q), masks, group)
        dv = heads_joined(dot(p.reshape(heads * group, group), da), masks, group)
        dqkv[rows, lanes(b, 128)] = dq.astype(BF)
        dqkv[rows, lanes(blocks + b, 128)] = dk.astype(BF)
        dqkv[rows, lanes(2 * blocks + b, 128)] = dv.astype(BF)
        dvec[pl.ds(qv_at + b, 1), :] += total_row(dq)
        dvec[pl.ds(qv_at + blocks + b, 1), :] += total_row(dv)
        return carry

    lax.fori_loop(0, groups * blocks, step, 0, unroll=UNROLL)


def block_forward(s, mats, vec, at, width, hidden, size, bias, group, groups):
    w_qkv, w_proj, w_up, w_down = mats
    pairs = width // 256
    scale = size ** (-0.5)
    norm_rows(s.x0, s.n1, vec, at["g1"], at["s1"], width)

    def qkv_step(j, carry):
        part = j // pairs
        row = row_at(vec, at["qv"], jnp.where(part == 0, j, jnp.maximum(j - pairs, 0)))
        value = dot(s.n1[...], w_qkv.cols(j)) + jnp.where(part == 1, 0.0, row)
        s.qkv[:, lanes(j)] = (value * jnp.where(part == 0, scale, 1.0)).astype(BF)
        return carry

    s.done("n1")
    w_qkv.need()
    loop(3 * pairs, qkv_step)
    s.done("qkv")
    attention(s.qkv, s.probs, s.att, bias, group, groups, width, size)
    s.done("probs", "att")

    def proj_step(j, carry):
        s.x1[:, lanes(j)] = dot(s.att[...], w_proj.cols(j))
        return carry

    w_proj.need()
    loop(pairs, proj_step)
    norm_rows(s.x0, s.n2, vec, at["g2"], at["s2"], width, s.x1, at["bo"])

    def mlp_step(j, carry):
        h = dot(s.n2[...], w_up.cols(j)) + row_at(vec, at["bu"], j)
        s.h[:, lanes(j)] = h
        u = gelu_parts(h)[0].astype(BF)
        update = dot(u, w_down.band(j))

        @pl.when(j == 0)
        def _():
            s.x2[...] = update

        @pl.when(j > 0)
        def _():
            s.x2[...] += update

        return carry

    s.done("x1", "n2")
    w_up.need()
    w_down.need()
    loop(hidden // 256, mlp_step)
    s.done("h")


def block_backward(s, mats, grads, vec, dvec, at, width, hidden, size, group, groups):
    w_qkv, w_proj, w_up, w_down = mats
    d_qkv, d_proj, d_up, d_down = grads
    pairs = width // 256
    s.need("n2")
    s.flip[...] = s.n2[...].T

    def mlp_step(j, carry):
        dxb = s.dxb[...]
        u, slope = gelu_parts(s.h[:, lanes(j)])
        dh = dot_t(dxb, w_down.band(j)) * slope
        put_row_at(dvec, at["bu"], j, total_row(fold(dh)))
        dh = dh.astype(BF)
        d_down.put_band(j, t_dot(u.astype(BF), dxb))
        d_up.put_cols(j, dot(s.flip[...], dh))
        update = dot_t(dh, w_up.cols(j))

        @pl.when(j == 0)
        def _():
            s.dn[...] = update

        @pl.when(j > 0)
        def _():
            s.dn[...] += update

        return carry

    s.need("h")
    w_down.need()
    w_up.need()
    loop(hidden // 256, mlp_step)
    d_down.done()
    d_up.done()
    s.need("x1")
    norm_back_rows(s.x1, s.dn, s.dx, s.dxb, vec, dvec, at["g2"], at["s2"], width, at["bo"], True)

    def proj_step(j, carry):
        dxb = s.dxb[...]
        s.datt[:, lanes(j)] = dot_t(dxb, w_proj.band(j)).astype(BF)
        d_proj.put_band(j, t_dot(s.att[:, lanes(j)], dxb))
        return carry

    s.need("att")
    w_proj.need()
    loop(pairs, proj_step)
    d_proj.done()
    s.need("qkv", "probs")
    attention_back(s.qkv, s.probs, s.datt, s.dqkv, dvec, at["qv"], group, groups, width, size)
    s.need("n1")
    s.flip[...] = s.n1[...].T

    def weight_step(j, carry):
        d_qkv.put_cols(j, dot(s.flip[...], s.dqkv[:, lanes(j)]))
        return carry

    loop(3 * pairs, weight_step)
    d_qkv.done()

    def input_step(j, carry):
        s.dn[:, lanes(j)] = dot_t(s.dqkv[...], w_qkv.band(j))
        return carry

    w_qkv.need()
    loop(pairs, input_step)
    s.need("x0")
    norm_back_rows(s.x0, s.dn, s.dx, s.dxb, vec, dvec, at["g1"], at["s1"], width, None, True)


ENC_AT = dict(g1=EV[2], s1=EV[3], qv=EV[4], bo=EV[5], g2=EV[6], s2=EV[7], bu=EV[8])
DEC_AT = dict(g1=DV[3], s1=DV[4], qv=DV[5], bo=DV[6], g2=DV[7], s2=DV[8], bu=DV[9])


def only(section, run):
    if section is None:
        run()
    else:
        pl.when(lax.axis_index("section") == section)(run)


class Bag:
    def __init__(self, names, refs):
        self.source, self.target, self.flying = {}, {}, {}
        for name, ref in zip(names, refs):
            setattr(self, name, ref)

    def begin(self, name, source, target, sem):
        self.flying[name] = pltpu.make_async_copy(source, target, sem)
        self.flying[name].start()

    def come(self, names, sources, sems):
        for n, (name, source) in enumerate(zip(names, sources)):
            self.begin(name, source, getattr(self, name), sems.at[n])

    def need(self, *names):
        for name in names:
            if name in self.flying:
                self.flying.pop(name).wait()

    def done(self, *names):
        for name in names:
            if name in self.target:
                target, sem = self.target[name]
                self.begin(name, getattr(self, name), target, sem)

    def finish(self):
        self.need(*list(self.flying))


class Layout:
    def __init__(self, shape, moves, shared):
        self.shape, self.moves, self.shared = shape, moves, shared


def plain_layout(total):
    return Layout((total, 16, 128), [(lambda ref: ref, 0, total)], [])


def slot_layout(plan, shape, lead):
    moves, shared, done = [], [], 0
    for device, (first, count, _) in enumerate(plan):
        skip = max(0, done - first)
        if skip and count:
            shared.append((lambda ref, d=device, n=skip: ref.at[d, pl.ds(lead, n)], first, skip))
        if count:
            moves.append(
                (
                    lambda ref, d=device, a=skip, n=count - skip: ref.at[d, pl.ds(lead + a, n)],
                    first + skip,
                    count - skip,
                )
            )
        done = first + count
    return Layout(shape, moves, shared)


def whole_slots(plan, shape):
    moves = [
        (lambda ref, d=device, n=count: ref.at[d, pl.ds(0, n)], first, count)
        for device, (first, count, _) in enumerate(plan)
        if count
    ]
    return Layout(shape, moves, [])


SHARED = 24


class Loads:
    def __init__(self, source, kept, side, sem, layout, backward=False):
        self.kept, self.side, self.flying = kept, side, []
        moves = list(enumerate(layout.moves))
        for index, (pick, start, count) in moves[::-1] if backward else moves:
            copy = pltpu.make_async_copy(pick(source), kept.at[pl.ds(start, count)], sem.at[index])
            copy.start()
            self.flying.append((start, count, None, copy))
        for index, (pick, start, count) in enumerate(layout.shared):
            copy = pltpu.make_async_copy(
                pick(source),
                side.at[index, pl.ds(0, count)],
                sem.at[len(layout.moves) + index],
            )
            copy.start()
            self.flying.append((start, count, index, copy))

    def need(self, base, tiles):
        here = [f for f in self.flying if f[0] < base + tiles and f[0] + f[1] > base]
        self.flying = [f for f in self.flying if f not in here]
        for item in here:
            item[3].wait()
        for start, count, index, _ in here:
            if index is not None:
                there = pl.ds(start, count)
                both = self.kept[there].astype(F32) + self.side[index, 0:count].astype(F32)
                self.kept[there] = both.astype(BF)


class Stores:
    def __init__(self, kept, out, sem, layout):
        self.kept, self.out, self.sem = kept, out, sem
        self.left, self.ready, self.flying = list(enumerate(layout.moves)), set(), []

    def done(self, base, tiles):
        self.ready.update(range(base, base + tiles))
        for item in list(self.left):
            index, (pick, start, count) = item
            if self.ready.issuperset(range(start, start + count)):
                copy = pltpu.make_async_copy(
                    self.kept.at[pl.ds(start, count)], pick(self.out), self.sem.at[index]
                )
                copy.start()
                self.flying.append(copy)
                self.left.remove(item)

    def finish(self):
        for copy in self.flying:
            copy.wait()


def load_scratch(layout):
    return [
        pltpu.VMEM((max(1, len(layout.shared)), SHARED, 16, 128), BF),
        pltpu.SemaphoreType.DMA((len(layout.moves) + len(layout.shared),)),
    ]


def visible_rows(column, count):
    lane = lax.broadcasted_iota(jnp.int32, (1, count), 1)
    return jnp.where(column == lane, 1.0, 0.0).astype(BF)


def encoder_bias(rows):
    r = lax.broadcasted_iota(jnp.int32, (rows, rows), 0)
    c = lax.broadcasted_iota(jnp.int32, (rows, rows), 1)
    same = (r // ROWS_E == c // ROWS_E) & (r % ROWS_E < VIS)
    return jnp.where(same, 0.0, -1e30)


ENC_KEEP = ["pick", "x0", "n1", "qkv", "probs", "att", "x1", "n2", "h", "x2"]


def enc_shapes(images):
    rows = images * ROWS_E
    return dict(
        pick=((rows, PIX), BF),
        x0=((rows, DE), F32),
        n1=((rows, DE), BF),
        qkv=((rows, 3 * DE), BF),
        probs=((HE, rows, rows), BF),
        att=((rows, DE), BF),
        x1=((rows, DE), F32),
        n2=((rows, DE), BF),
        h=((rows, FE), F32),
        x2=((rows, DE), F32),
    )


def position_column(vec, start, blocks, j):
    return vec[pl.ds(start + j, PATCHES, stride=blocks), :]


def encoder_forward_kernel(images, layout, section, vis, pix, vec, weights, *refs):
    latent, outs = refs[0], refs[1 : 1 + len(ENC_KEEP)]
    s = Bag(ENC_KEEP, refs[1 + len(ENC_KEEP) : 1 + 2 * len(ENC_KEEP)])
    keep_sem, kept, posit, side, sem = refs[1 + 2 * len(ENC_KEEP) :]
    s.target = {name: (out, keep_sem.at[n]) for n, (name, out) in enumerate(zip(ENC_KEEP, outs))}
    def run():
        loads = Loads(weights, kept, side, sem, layout)
        rows = images * ROWS_E
        mats = [Mat(kept, b, shape, loads) for b, shape in zip(ENC_BASE, ENC_MATS)]
        posit[...] = jnp.zeros_like(posit)
        for j in range(DE // 128):
            posit[0:PATCHES, j * 128 : (j + 1) * 128] = position_column(vec, EV[1], DE // 128, j)
        for i in range(images):
            where = pl.ds(i * ROWS_E, ROWS_E)
            hot = visible_rows(vis[where, :], ROWS_D)
            s.pick[where, :] = dot(hot, pix[i]).astype(BF)
            s.x0[where, :] = dot(hot, posit[...].astype(BF)) + row_of(vec, EV[0], DE)
        mats[0].need()

        def embed_step(j, carry):
            s.x0[:, lanes(j)] += dot(s.pick[...], mats[0].cols(j))
            return carry

        loop(DE // 256, embed_step)
        s.done("pick", "x0")
        block_forward(
            s, mats[1:5], vec, ENC_AT, DE, FE, DE // HE, encoder_bias(rows), rows, 1
        )
        norm_rows(s.x1, latent, vec, EV[10], EV[11], DE, s.x2, EV[9])
        s.done("x2")
        s.finish()

    only(section, run)


def encoder_forward(images, layout, vis, pix, vec, weights, section=None):
    shapes = enc_shapes(images)
    rows = images * ROWS_E
    vm = pl.BlockSpec(memory_space=pltpu.VMEM)
    return pl.pallas_call(
        functools.partial(encoder_forward_kernel, images, layout, section),
        out_shape=[jax.ShapeDtypeStruct((rows, DE), BF)]
        + [jax.ShapeDtypeStruct(*shapes[name]) for name in ENC_KEEP],
        in_specs=[vm, vm, vm, pl.BlockSpec(memory_space=pl.ANY)],
        out_specs=[vm] + [pl.BlockSpec(memory_space=pl.ANY)] * len(ENC_KEEP),
        scratch_shapes=[pltpu.VMEM(*shapes[name]) for name in ENC_KEEP]
        + [
            pltpu.SemaphoreType.DMA((len(ENC_KEEP),)),
            pltpu.VMEM((ENC_TOTAL, 16, 128), BF),
            pltpu.VMEM((ROWS_D, DE), F32),
        ]
        + load_scratch(layout),
        name="encoder_forward",
        compiler_params=pltpu.CompilerParams(vmem_limit_bytes=VMEM_LIMIT),
    )(vis, pix, vec, weights)


def encoder_backward_kernel(images, layout, out_layout, section, vis, vec, dlatent, *refs):
    n = len(ENC_KEEP)
    saved, (weights, dmats, dvec) = refs[:n], refs[n : n + 3]
    s = Bag(ENC_KEEP, refs[n + 3 : 2 * n + 3])
    keep_sem, kept, dkept, s.dx, s.dxb, s.dn, s.datt, s.dqkv, s.flip, out_sem, side, sem = refs[
        2 * n + 3 :
    ]
    def run():
        s.come(ENC_KEEP[::-1], saved[::-1], keep_sem)
        loads = Loads(weights, kept, side, sem, layout, True)
        stores = Stores(dkept, dmats, out_sem, out_layout)
        rows = images * ROWS_E
        mats = [Mat(kept, b, shape, loads) for b, shape in zip(ENC_BASE, ENC_MATS)]
        grads = [Mat(dkept, b, shape, None, stores) for b, shape in zip(ENC_BASE, ENC_MATS)]
        dvec[EV[11] + DE // 128 :, :] = jnp.zeros_like(dvec[EV[11] + DE // 128 :, :])
        s.need("x2")
        norm_back_rows(
            s.x2, dlatent, s.dx, s.dxb, vec, dvec, EV[10], EV[11], DE, EV[9], False
        )
        block_backward(
            s, mats[1:5], grads[1:5], vec, dvec, ENC_AT, DE, FE, DE // HE, rows, 1
        )
        put_row(dvec, EV[0], jnp.sum(s.dx[...], 0, keepdims=True))

        s.need("pick")

        def embed_step(j, carry):
            grads[0].put_band(j, t_dot(s.pick[:, lanes(j)], s.dxb[...]))
            return carry

        loop(DE // 256, embed_step)
        grads[0].done()
        mats[0].need()
        hot = visible_rows(vis[...], ROWS_D)
        for j in range(DE // 128):
            value = t_dot(hot, s.dxb[:, j * 128 : (j + 1) * 128])
            dvec[pl.ds(EV[1] + j, PATCHES, stride=DE // 128), :] = value[0:PATCHES]
        stores.finish()

    only(section, run)


def encoder_backward(images, layout, out_layout, vis, vec, dlatent, saved, weights, section=None):
    rows = images * ROWS_E
    shapes = enc_shapes(images)
    vm = pl.BlockSpec(memory_space=pltpu.VMEM)
    hbm = pl.BlockSpec(memory_space=pl.ANY)
    return pl.pallas_call(
        functools.partial(encoder_backward_kernel, images, layout, out_layout, section),
        out_shape=[
            jax.ShapeDtypeStruct(out_layout.shape, BF),
            jax.ShapeDtypeStruct(vec.shape, F32),
        ],
        in_specs=[vm] * 3 + [hbm] * (len(ENC_KEEP) + 1),
        out_specs=[hbm, vm],
        scratch_shapes=[pltpu.VMEM(*shapes[name]) for name in ENC_KEEP]
        + [
            pltpu.SemaphoreType.DMA((len(ENC_KEEP),)),
            pltpu.VMEM((ENC_TOTAL, 16, 128), BF),
            pltpu.VMEM((ENC_TOTAL, 16, 128), BF),
            pltpu.VMEM((rows, DE), F32),
            pltpu.VMEM((rows, DE), BF),
            pltpu.VMEM((rows, DE), F32),
            pltpu.VMEM((rows, DE), BF),
            pltpu.VMEM((rows, 3 * DE), BF),
            pltpu.VMEM((DE, rows), BF),
            pltpu.SemaphoreType.DMA((len(out_layout.moves),)),
        ]
        + load_scratch(layout),
        name="encoder_backward",
        compiler_params=pltpu.CompilerParams(vmem_limit_bytes=VMEM_LIMIT),
    )(vis, vec, dlatent, *saved, weights)


def decoder_kernel(images, layout, out_layout, section, masked_total, latent, places, pix, vec, weights, *refs):
    dlatent, loss, dmats, dvec = refs[:4]
    s = Bag(
        ["x0", "x1", "x2", "n1", "n2", "qkv", "probs", "att", "h", "dx", "dxb", "dn", "dqkv", "flip"],
        refs[4:18],
    )
    kept, dkept, posit, dguess, out_sem, side, sem = refs[18:]
    s.datt = s.n2
    loss[...] = jnp.zeros((8, 128), F32)

    def run():
        rows = images * ROWS_D
        loads = Loads(weights, kept, side, sem, layout)
        stores = Stores(dkept, dmats, out_sem, out_layout)
        mats = [Mat(kept, b, shape, loads) for b, shape in zip(DEC_BASE, DEC_MATS)]
        grads = [Mat(dkept, b, shape, None, stores) for b, shape in zip(DEC_BASE, DEC_MATS)]
        posit[...] = jnp.zeros_like(posit)
        for j in range(DD // 128):
            posit[0:PATCHES, j * 128 : (j + 1) * 128] = position_column(vec, DV[2], DD // 128, j)
        dvec[DV[13] + PIX // 128 :, :] = jnp.zeros_like(dvec[DV[13] + PIX // 128 :, :])
        mats[0].need()
        for i in range(images):
            part = pl.ds(i * ROWS_E, ROWS_E)
            where = pl.ds(i * ROWS_D, ROWS_D)
            for j in range(DD // 256):
                cut = slice(j * 256, (j + 1) * 256)
                z = dot(latent[part, :], mats[0].cols(j)) + row_of(vec, DV[0] + 2 * j, 256)
                place = places[where, :]
                hot = visible_rows(jnp.where(place < VIS, place, -1), ROWS_E)
                high = z.astype(BF)
                low = (z - high.astype(F32)).astype(BF)
                token = jnp.where(place >= VIS, 1.0, 0.0) * row_of(vec, DV[1] + 2 * j, 256)
                s.x0[where, cut] = dot(hot, high) + dot(hot, low) + token + posit[:, cut]
        key = lax.broadcasted_iota(jnp.int32, (ROWS_D, 1), 0)
        bias = jnp.where(key < PATCHES, 0.0, -1e30)
        block_forward(
            s, mats[1:5], vec, DEC_AT, DD, FD, DD // HD, bias, ROWS_D, images
        )
        norm_rows(s.x1, s.dxb, vec, DV[11], DV[12], DD, s.x2, DV[10])
        factor = 2.0 / (PIX * masked_total)

        def head_step(j, total):
            value = dot(s.dxb[...], mats[5].cols(j)) + row_at(vec, DV[13], j)
            count = jnp.zeros((8, 256), F32)
            column = jnp.zeros((8, 256), F32)
            for i in range(images):
                where = slice(i * ROWS_D, (i + 1) * ROWS_D)
                error = value[where] - pix[i, :, lanes(j)].astype(F32)
                error = jnp.where(places[where, :] >= VIS, error, 0.0)
                count = count + fold(error * error)
                error = error * factor
                column = column + fold(error)
                dguess[where, lanes(j)] = error.astype(BF)
            put_row_at(dvec, DV[13], j, total_row(column))
            return total + count

        mats[5].need()
        total = loop(PIX // 256, head_step, jnp.zeros((8, 256), F32))
        loss[...] = jnp.broadcast_to(jnp.sum(total) * (1.0 / PIX), (8, 128))
        s.flip[...] = s.dxb[...].T

        def head_weight_step(j, carry):
            grads[5].put_cols(j, dot(s.flip[...], dguess[:, lanes(j)]))
            return carry

        loop(PIX // 256, head_weight_step)
        grads[5].done()

        def head_input_step(j, carry):
            s.dn[:, lanes(j)] = dot_t(dguess[...], mats[5].band(j))
            return carry

        loop(DD // 256, head_input_step)
        norm_back_rows(s.x2, s.dn, s.dx, s.dxb, vec, dvec, DV[11], DV[12], DD, DV[10], False)
        block_backward(
            s, mats[1:5], grads[1:5], vec, dvec, DEC_AT, DD, FD, DD // HD, ROWS_D, images
        )
        token = jnp.zeros((8, DD), F32)
        spot = jnp.zeros((ROWS_D, DD), F32)
        back = []
        for i in range(images):
            where = pl.ds(i * ROWS_D, ROWS_D)
            place = places[where, :]
            dx = s.dx[where, :]
            spot = spot + dx
            token = token + fold(jnp.where(place >= VIS, dx, 0.0))
            hot = visible_rows(jnp.where(place < VIS, place, -1), ROWS_E)
            back.append(t_dot(hot, s.dxb[where, :]))
        posit[...] = spot
        for j in range(DD // 128):
            dvec[pl.ds(DV[2] + j, PATCHES, stride=DD // 128), :] = posit[
                0:PATCHES, j * 128 : (j + 1) * 128
            ]
        put_row(dvec, DV[1], total_row(token))
        back = jnp.concatenate(back, 0)
        put_row(dvec, DV[0], jnp.sum(back, 0, keepdims=True))
        back = back.astype(BF)
        for j in range(DE // 256):
            grads[0].put_band(j, t_dot(latent[:, j * 256 : (j + 1) * 256], back))
            dlatent[:, j * 256 : (j + 1) * 256] = dot_t(back, mats[0].band(j)).astype(BF)
        grads[0].done()
        stores.finish()

    only(section, run)


def decoder_step(
    images, layout, out_layout, masked_total, latent, places, pix, vec, weights, section=None
):
    rows = images * ROWS_D
    vm = pl.BlockSpec(memory_space=pltpu.VMEM)
    hbm = pl.BlockSpec(memory_space=pl.ANY)
    probs = images * HD
    return pl.pallas_call(
        functools.partial(decoder_kernel, images, layout, out_layout, section, masked_total),
        out_shape=[
            jax.ShapeDtypeStruct((images * ROWS_E, DE), BF),
            jax.ShapeDtypeStruct((8, 128), F32),
            jax.ShapeDtypeStruct(out_layout.shape, BF),
            jax.ShapeDtypeStruct(vec.shape, F32),
        ],
        in_specs=[vm, vm, vm, vm, hbm],
        out_specs=[vm, vm, hbm, vm],
        scratch_shapes=[
            pltpu.VMEM((rows, DD), F32),
            pltpu.VMEM((rows, DD), F32),
            pltpu.VMEM((rows, DD), F32),
            pltpu.VMEM((rows, DD), BF),
            pltpu.VMEM((rows, DD), BF),
            pltpu.VMEM((rows, 3 * DD), BF),
            pltpu.VMEM((probs, ROWS_D, ROWS_D), BF),
            pltpu.VMEM((rows, DD), BF),
            pltpu.VMEM((rows, FD), F32),
            pltpu.VMEM((rows, DD), F32),
            pltpu.VMEM((rows, DD), BF),
            pltpu.VMEM((rows, DD), F32),
            pltpu.VMEM((rows, 3 * DD), BF),
            pltpu.VMEM((DD, rows), BF),
            pltpu.VMEM((DEC_TOTAL, 16, 128), BF),
            pltpu.VMEM((DEC_TOTAL, 16, 128), BF),
            pltpu.VMEM((ROWS_D, DD), F32),
            pltpu.VMEM((rows, PIX), BF),
            pltpu.SemaphoreType.DMA((len(out_layout.moves),)),
        ]
        + load_scratch(layout),
        name="decoder_step",
        compiler_params=pltpu.CompilerParams(vmem_limit_bytes=VMEM_LIMIT),
    )(latent, places, pix, vec, weights)


def natural(flat, shapes):
    pieces, offset = [], 0
    for rows, columns in shapes:
        piece = flat[offset : offset + rows * columns].reshape(rows // 16, 16, columns // 128, 128)
        pieces.append(piece.transpose(0, 2, 1, 3).reshape(-1, 16, 128))
        offset += rows * columns
    return jnp.concatenate(pieces, 0)


def flat_from_natural(tiles, shapes, total):
    pieces, offset = [], 0
    for rows, columns in shapes:
        count = rows * columns // 2048
        piece = tiles[offset : offset + count].reshape(rows // 16, columns // 128, 16, 128)
        pieces.append(piece.transpose(0, 2, 1, 3).reshape(-1))
        offset += count
    flat = jnp.concatenate(pieces)
    return jnp.pad(flat, (0, total - flat.shape[0]))


MESH = pl.DeviceIdType.MESH
DEPTH, WIDTH = 4, 2
SLOT_M, SLOT_V = 264, 5
SLOT = SLOT_M + SLOT_V
FIRST_Z = 8
RELAY = 3
LENGTHS = (
    ((18, 29, 22), (19, 36, 23), (20, 34, 25), (18, 29, 22)),
    ((32, 0, 0), (33, 0, 0), (7, 0, 0), (1, 0, 0)),
)
PARTS = FIRST_Z + 1 + RELAY
EARLY = 5
MARGIN = 384
LINES = 3744


def cut_z(section, depth, part):
    length = LENGTHS[section][depth][0]
    return part * length, length


def cut_y(section, depth):
    first, tail, _ = LENGTHS[section][depth]
    return FIRST_Z * first, tail


def cut_relay(depth, part):
    first, tail, length = LENGTHS[0][depth]
    return FIRST_Z * first + tail + part * length, length


def size_of(section, depth):
    first, tail, length = LENGTHS[section][depth]
    return FIRST_Z * first + tail + RELAY * length


def each(count, run):
    def step(i, carry):
        run(i)
        return carry

    lax.fori_loop(0, count, step, 0)


def shard_plan(shapes, total, devices):
    lines = total // devices // 128
    plans = []
    for device in range(devices):
        low, high = device * lines, (device + 1) * lines
        first, count, pieces = 0, 0, []
        line, tile = 0, 0
        for rows, columns in shapes:
            blocks = columns // 128
            begin, end = max(low, line), min(high, line + rows * blocks)
            if begin < end:
                top, bottom = (begin - line) // blocks, (end - line) // blocks
                assert top * blocks == begin - line and bottom * blocks == end - line
                up, down = top // 16, -(-bottom // 16)
                if not pieces:
                    first = tile + up * blocks
                pieces.append((blocks, line + up * 16 * blocks - low, down - up, count))
                count += (down - up) * blocks
            line += rows * blocks
            tile += rows * blocks // 16
        plans.append((first, count, pieces))
    return plans


def devices_around(z, y, c, s):
    at = lambda zz, yy, cc: (s, zz * 4 + yy * 2 + cc)
    around = {"side": at(z, 1 - y, c), "core": at(z, y, 1 - c)}
    around["cross"] = (1 - s, z * 4 + y * 2 + c)
    if z + 1 < DEPTH:
        around["up"] = at(z + 1, y, c)
    if z > 0:
        around["down"] = at(z - 1, y, c)
    return around


def greet(around):
    barrier = pltpu.get_barrier_semaphore()
    for target in around.values():
        pl.semaphore_signal(barrier, inc=1, device_id=target, device_id_type=MESH)
    pl.semaphore_wait(barrier, len(around))


def place():
    d = lax.axis_index("dp")
    return lax.axis_index("section"), d // 4, (d // 2) % 2, d % 2


def for_each_depth(run):
    s_now, z_now, y, c = place()
    for s in range(2):
        for z in range(DEPTH):
            pl.when((s_now == s) & (z_now == z))(functools.partial(run, s, z, y, c))


class Sender:
    def __init__(self, around, send):
        self.around, self.send, self.used, self.sent = around, send, 0, []

    def many(self, count, make, names):
        groups = []
        for name in names:
            if name in self.around:

                def copy(n, base=self.used, name=name):
                    source, target, sem = make(n)
                    return pltpu.make_async_remote_copy(
                        source,
                        target,
                        self.send.at[base + n],
                        sem,
                        device_id=self.around[name],
                        device_id_type=MESH,
                    )

                self.used += count
                self.sent.append((count, copy))
                groups.append(copy)

        def start(n):
            for copy in groups:
                copy(n).start()

        return start

    def push(self, source, target, sem, *names):
        self.many(1, lambda n: (source, target, sem), names)(0)

    def arrive(self, target, sem):
        pltpu.make_async_remote_copy(
            target,
            target,
            self.send.at[0],
            sem,
            device_id=self.around["core"],
            device_id_type=MESH,
        ).wait_recv()

    def finish(self):
        for count, copy in self.sent:
            each(count, lambda n: copy(n).wait_send())


def gather_kernel(own, out, passing, send, recv, r_pass, local):
    def run(s, z, y, c):
        around = devices_around(z, y, c, s)
        greet(around)
        io = Sender(around, send)

        def slot(zz, yy, cc):
            return zz * 4 + yy * 2 + cc

        def part_z(zz, yy, cc, n, mine=False):
            target = out.at[slot(zz, yy, cc), pl.ds(*cut_z(s, zz, n))]
            source = own.at[pl.ds(*cut_z(s, zz, n))] if mine else target
            return source, target, recv.at[slot(zz, yy, cc), n]

        def part_y(zz, yy, cc, mine=False):
            target = out.at[slot(zz, yy, cc), pl.ds(*cut_y(s, zz))]
            source = own.at[pl.ds(*cut_y(s, zz))] if mine else target
            return source, target, recv.at[slot(zz, yy, cc), FIRST_Z]

        def part_r(zz, yy, cc, n, mine=False):
            target = out.at[slot(zz, yy, cc), pl.ds(*cut_relay(zz, n))]
            source = own.at[pl.ds(*cut_relay(zz, n))] if mine else target
            return source, target, recv.at[slot(zz, yy, cc), FIRST_Z + 1 + n]

        def passed(zz, yy, n):
            length = LENGTHS[0][zz][2]
            target = passing.at[zz * 2 + yy, pl.ds(n * length, length)]
            return target, target, r_pass.at[zz * 2 + yy, n]

        def forward(count, make, names):
            start = io.many(count, make, names)

            def step(n):
                io.arrive(*make(n)[1:])
                start(n)

            each(count, step)

        def relay(zz, yy, names):
            start = io.many(RELAY, lambda n: passed(zz, yy, n), names)
            back = None
            if not (zz == z and yy is y):
                back = io.many(
                    RELAY,
                    lambda n: (passed(zz, yy, n)[0],) + part_r_there(zz, yy, n),
                    ["cross"],
                )

            def step(n):
                io.arrive(*passed(zz, yy, n)[1:])
                start(n)
                if back:
                    back(n)

            each(RELAY, step)

        def part_r_there(zz, yy, n):
            return part_r(zz, yy, c, n)[1:]

        keep = pltpu.make_async_copy(own, out.at[slot(z, y, c)], local)
        if s == 0:
            each(
                RELAY,
                io.many(
                    RELAY,
                    lambda n: (part_r(z, y, c, n, True)[0],) + passed(z, y, n)[1:],
                    ["cross"],
                ),
            )
            io.push(*part_y(z, y, c, True), "side")
            each(
                FIRST_Z,
                io.many(
                    FIRST_Z, lambda n: part_z(z, y, c, n, True), ["up", "down", "side"]
                ),
            )
            io.push(*part_y(z, y, c, True), "up", "down", "core")
            each(RELAY, io.many(RELAY, lambda n: part_r(z, y, c, n, True), ["core"]))
        else:
            relay(z, y, ["up", "down", "side"])
            mine = io.many(FIRST_Z, lambda n: part_z(z, y, c, n, True), ["up", "down", "side"])
            waiting = [z]
            for k in range(1, DEPTH + 1):
                each(FIRST_Z // DEPTH, lambda n, k=k: mine((k - 1) * (FIRST_Z // DEPTH) + n))
                near = [zz for zz in (z - k, z + k) if 0 <= zz < DEPTH]
                for zz in near:
                    relay(zz, y, ["up" if zz < z else "down", "side"])
                for zz in waiting:
                    relay(zz, 1 - y, [])
                waiting = near
        each(FIRST_Z, io.many(FIRST_Z, lambda n: part_z(z, y, c, n, True), ["core"]))
        keep.start()
        if s == 0:
            io.arrive(*part_y(z, 1 - y, c)[1:])
            io.push(*part_y(z, 1 - y, c), "up", "down", "core")
        waiting = [z]
        for k in range(1, DEPTH + 1):
            near = [zz for zz in (z - k, z + k) if 0 <= zz < DEPTH]
            starts = [
                io.many(
                    FIRST_Z,
                    lambda n, zz=zz: part_z(zz, y, c, n),
                    ["up" if zz < z else "down", "side", "core"],
                )
                for zz in near
            ]

            def step(n):
                for zz, start in zip(near, starts):
                    io.arrive(*part_z(zz, y, c, n)[1:])
                    start(n)

            if near:
                each(FIRST_Z, step)
            if s == 0:
                for zz in near:
                    for yy in (y, 1 - y):
                        io.arrive(*part_y(zz, yy, c)[1:])
                        io.push(*part_y(zz, yy, c), "up" if zz < z else "down", "core")
            for zz in waiting:
                forward(FIRST_Z, lambda n, zz=zz: part_z(zz, 1 - y, c, n), ["core"])
            if s == 0:
                for zz, yy in [(zz, 1 - y) for zz in waiting] + [(zz, y) for zz in near]:
                    forward(RELAY, lambda n, zz=zz, yy=yy: part_r(zz, yy, c, n), ["core"])
            waiting = near
        for zz in range(DEPTH):

            def last(yy, zz=zz):
                each(FIRST_Z, lambda n: io.arrive(*part_z(zz, yy, 1 - c, n)[1:]))
                if s == 0:
                    io.arrive(*part_y(zz, yy, 1 - c)[1:])
                    each(RELAY, lambda n: io.arrive(*part_r(zz, yy, 1 - c, n)[1:]))

            each(WIDTH, last)
        keep.wait()
        io.finish()

    for_each_depth(run)


def gather_slots(own):
    hbm = pl.BlockSpec(memory_space=pl.ANY)
    return pl.pallas_call(
        gather_kernel,
        out_shape=[
            jax.ShapeDtypeStruct((16, SLOT, 16, 128), BF),
            jax.ShapeDtypeStruct((8, RELAY * max(n[2] for n in LENGTHS[0]), 16, 128), BF),
        ],
        in_specs=[hbm],
        out_specs=[hbm, hbm],
        scratch_shapes=[
            pltpu.SemaphoreType.DMA((256,)),
            pltpu.SemaphoreType.DMA((16, PARTS)),
            pltpu.SemaphoreType.DMA((8, RELAY)),
            pltpu.SemaphoreType.DMA,
        ],
        name="gather_slots",
        compiler_params=pltpu.CompilerParams(
            collective_id=0, has_side_effects=True, vmem_limit_bytes=VMEM_LIMIT
        ),
    )(own)[0]


def send_order(z):
    order = []
    for k in range(DEPTH - 1, -1, -1):
        for zz in (z + k, z - k):
            if 0 <= zz < DEPTH and zz not in order:
                order.append(zz)
    return order


STEP_TILES = 4


def in_steps(start, count, some, carry=0):
    whole = count // STEP_TILES

    def body(i, carry):
        return some(start + i * STEP_TILES, STEP_TILES, carry)

    carry = lax.fori_loop(0, whole, body, carry)
    if count % STEP_TILES:
        carry = some(start + whole * STEP_TILES, count % STEP_TILES, carry)
    return carry


def total_of(sources, base, size):
    value = sources[0][pl.ds(base, size)].astype(F32)
    for source in sources[1:]:
        value = value + source[pl.ds(base, size)].astype(F32)
    return value


def add_tiles(target, sources, start, count):
    def some(base, size, carry):
        target[pl.ds(base, size)] = total_of(sources, base, size).astype(target.dtype)
        return carry

    in_steps(start, count, some)


class Shifted:
    def __init__(self, ref, start):
        self.ref, self.start = ref, start

    def __getitem__(self, index):
        return self.ref[pl.ds(index.start - self.start, index.size)]


class Section:
    def __init__(self, section, z, y, c, io, refs, sems, low=0, high=FIRST_Z):
        self.section, self.z, self.y, self.c, self.io = section, z, y, c, io
        self.low, self.count = low, high - low
        self.mats, self.vecs, self.held, self.core_in = refs[:4]
        self.side_a, self.side_b, self.z_a, self.z_b = refs[4:]
        self.load, self.r_core, self.r_side, self.r_z = sems
        self.order = send_order(z)
        self.tail = LENGTHS[section][z][1] > 0
        self.loads, self.ready = {}, set()

    def pieces(self, zz, yy, cc):
        slot = zz * 4 + yy * 2 + cc
        low = self.low * LENGTHS[self.section][zz][0]
        high = (self.low + self.count) * LENGTHS[self.section][zz][0]
        if self.low + self.count == FIRST_Z:
            high = size_of(self.section, zz)
        found = []
        if low < SLOT_V:
            count = min(high, SLOT_V) - low
            found.append((self.vecs.at[slot, pl.ds(low, count)], pl.ds(low, count)))
        low = max(low, SLOT_V)
        if high > low:
            source = self.mats.at[slot, pl.ds(low - SLOT_V, high - low)]
            found.append((source, pl.ds(low, high - low)))
        return found

    def begin_loads(self):
        for zz in self.order:
            for yy, flip in ((1 - self.y, True), (self.y, False)):
                where = zz * 2 + yy
                copies = [
                    pltpu.make_async_copy(source, self.held.at[where, there], self.load.at[where, n])
                    for n, (source, there) in enumerate(self.pieces(zz, yy, self.c))
                ]
                for copy in copies:
                    copy.start()
                self.loads[zz, flip] = copies

    def exchange_cores(self):
        for zz in self.order:
            for yy in (1 - self.y, self.y):
                where = zz * 2 + yy
                for n, (source, there) in enumerate(self.pieces(zz, yy, 1 - self.c)):
                    self.io.push(
                        source, self.core_in.at[where, there], self.r_core.at[where, n], "core"
                    )

    def prepare(self, zz, flip):
        if (zz, flip) in self.ready:
            return
        self.ready.add((zz, flip))
        yy = 1 - self.y if flip else self.y
        where = zz * 2 + yy
        for copy in self.loads[zz, flip]:
            copy.wait()
        for n, (_, there) in enumerate(self.pieces(zz, yy, self.c)):
            self.io.arrive(self.core_in.at[where, there], self.r_core.at[where, n])

    def z_cut(self, zz, n):
        return cut_z(self.section, zz, self.low + n)

    def y_cut(self, zz):
        return cut_y(self.section, zz)

    def cut(self, zz, yy, cut):
        return self.held.at[zz * 2 + yy, pl.ds(*cut)]

    def side_in(self, zz, n):
        return self.side_a.at[zz, pl.ds(*self.z_cut(zz, n))], self.r_side.at[zz, self.low + n]

    def side_tail(self, zz):
        return self.side_b.at[pl.ds(0, self.y_cut(zz)[1])], self.r_side.at[zz, FIRST_Z]

    def z_in(self, way, zz, n):
        return self.z_a.at[way, zz, pl.ds(*self.z_cut(zz, n))], self.r_z.at[way, zz, self.low + n]

    def z_tail(self, way, zz, yy):
        ref = self.z_b.at[way, zz, yy, pl.ds(0, self.y_cut(zz)[1])]
        return ref, self.r_z.at[way, zz, FIRST_Z + yy]

    def came(self, cut, pair):
        self.io.arrive(*pair)
        return Shifted(pair[0], cut[0])

    def core_sources(self, zz, yy):
        return [self.held.at[zz * 2 + yy], self.core_in.at[zz * 2 + yy]]

    def add(self, zz, yy, cut, sources):
        add_tiles(self.held.at[zz * 2 + yy], sources, *cut)

    def to_side(self, zz):
        self.prepare(zz, True)
        flip = 1 - self.y
        start = self.io.many(
            self.count,
            lambda n: (self.cut(zz, flip, self.z_cut(zz, n)),) + self.side_in(zz, n),
            ["side"],
        )

        def step(n):
            self.add(zz, flip, self.z_cut(zz, n), self.core_sources(zz, flip))
            start(n)

        each(self.count, step)

    def way(self, zz):
        return (0, "up", 0) if zz > self.z else (1, "down", DEPTH - 1)

    def along(self, zz):
        self.prepare(zz, False)
        way, name, first = self.way(zz)
        start = self.io.many(
            self.count,
            lambda n: (self.cut(zz, self.y, self.z_cut(zz, n)),) + self.z_in(way, zz, n),
            [name],
        )

        def step(n):
            cut = self.z_cut(zz, n)
            sources = self.core_sources(zz, self.y) + [self.came(cut, self.side_in(zz, n))]
            if self.z != first:
                sources.append(self.came(cut, self.z_in(way, zz, n)))
            self.add(zz, self.y, cut, sources)
            start(n)

        each(self.count, step)

    def along_tail(self, zz, flip):
        yy = 1 - self.y if flip else self.y
        self.prepare(zz, flip)
        way, name, first = self.way(zz)
        cut = self.y_cut(zz)
        sources = self.core_sources(zz, yy)
        if self.z != first:
            sources.append(self.came(cut, self.z_tail(way, zz, yy)))
        self.add(zz, yy, cut, sources)
        self.io.push(self.cut(zz, yy, cut), *self.z_tail(way, zz, yy), name)

    def here(self):
        return [way for way, there in ((0, self.z > 0), (1, self.z < DEPTH - 1)) if there]

    def tails(self, yy):
        cut = self.y_cut(self.z)
        return self.core_sources(self.z, yy) + [
            self.came(cut, self.z_tail(way, self.z, yy)) for way in self.here()
        ]

    def tail_to_side(self):
        z, flip = self.z, 1 - self.y
        self.prepare(z, False)
        self.add(z, flip, self.y_cut(z), self.tails(flip))
        self.io.push(self.cut(z, flip, self.y_cut(z)), *self.side_tail(z), "side")

    def end(self, total, carry):
        z, y = self.z, self.y
        self.prepare(z, False)
        if self.tail:
            cut = self.y_cut(z)
            carry = total(cut, self.tails(y) + [self.came(cut, self.side_tail(z))], carry)

        def step(n, carry):
            cut = self.z_cut(z, n)
            sources = self.core_sources(z, y) + [
                self.came(cut, self.z_in(way, z, n)) for way in self.here()
            ]
            return total(cut, sources + [self.came(cut, self.side_in(z, n))], carry)

        return lax.fori_loop(0, self.count, step, carry)


def owned_limits(plans):
    limits = []
    for plan, shapes in zip(plans, (ENC_MATS, DEC_MATS)):
        low = 0
        for _, count, pieces in plan:
            if not pieces:
                limits.append((0, 0, 0, 0, 0))
                continue
            blocks, line, _, _ = pieces[0]
            skip = -line // blocks if line < 0 else 0
            last, line, rows, _ = pieces[-1]
            over = max(0, line + rows * 16 * last - LINES) // last
            limits.append((count, blocks, skip, last, over))
    return limits


def finish_tiles(out, sources, start, count, owned, square):
    tiles, first, skip, last, over = owned
    row = lax.broadcasted_iota(jnp.int32, (1, 16, 1), 1)

    def some(base, size, square):
        value = total_of(sources, base, size)
        out[pl.ds(base, size)] = value
        tile = base - SLOT_V + lax.broadcasted_iota(jnp.int32, (size, 1, 1), 0)
        mine = (tile < tiles) & ((tile >= first) | (row >= skip))
        mine = mine & ((tile < tiles - last) | (row < 16 - over))
        mine = mine | (tile < 0)
        value = jnp.where(mine, value * value, 0.0)
        return square + value.reshape(size * 2, 8, 128).sum(0)

    return in_steps(start, count, some, square)


def section_scratch(section):
    most = FIRST_Z * max(n[0] for n in LENGTHS[0] + LENGTHS[1])
    tail = max(1, max(n[1] for n in LENGTHS[section]))
    size = max(size_of(s, z) for s in range(2) for z in range(DEPTH))
    buffers = [
        pltpu.VMEM((8, size, 16, 128), BF),
        pltpu.VMEM((8, size, 16, 128), BF),
        pltpu.VMEM((DEPTH, most, 16, 128), BF),
        pltpu.VMEM((tail, 16, 128), BF),
        pltpu.VMEM((2, DEPTH, most, 16, 128), BF),
        pltpu.VMEM((2, DEPTH, 2, tail, 16, 128), BF),
    ]
    sems = [
        pltpu.SemaphoreType.DMA((8, 2)),
        pltpu.SemaphoreType.DMA((8, 2)),
        pltpu.SemaphoreType.DMA((DEPTH, FIRST_Z + 1)),
        pltpu.SemaphoreType.DMA((2, DEPTH, FIRST_Z + 2)),
    ]
    return buffers, sems


def scatter_second_kernel(mats, vecs, out, *refs):
    buffers, sems, send = refs[:6], refs[6:10], refs[10]

    def run(s, z, y, c):
        if s == 0:
            return
        around = devices_around(z, y, c, s)
        del around["cross"]
        io = Sender(around, send)
        part = Section(1, z, y, c, io, (mats, vecs) + buffers, sems, 0, EARLY)
        part.begin_loads()
        greet(around)
        part.exchange_cores()
        for zz in part.order:
            part.to_side(zz)
        for zz in part.order[:-1]:
            part.along(zz)

        def total(cut, sources, carry):
            add_tiles(out, sources, *cut)
            return carry

        part.end(total, 0)
        io.finish()

    for_each_depth(run)


def scatter_second(mats, vecs):
    hbm = pl.BlockSpec(memory_space=pl.ANY)
    buffers, sems = section_scratch(1)
    return pl.pallas_call(
        scatter_second_kernel,
        out_shape=jax.ShapeDtypeStruct((SLOT, 16, 128), F32),
        in_specs=[hbm, hbm],
        out_specs=pl.BlockSpec(memory_space=pltpu.VMEM),
        scratch_shapes=buffers + sems + [pltpu.SemaphoreType.DMA((112,))],
        name="scatter_second",
        compiler_params=pltpu.CompilerParams(
            collective_id=3, has_side_effects=True, vmem_limit_bytes=VMEM_LIMIT
        ),
    )(mats, vecs)


def scatter_first_kernel(limits, mats, vecs, second, second_vecs, other_sum, loss, out, total, *refs):
    buffers, sems = refs[:6], refs[6:10]
    r_in, r_side, r_z, r_back, parts, send, s_in, s_side, s_z, s_back, s_parts = refs[10:]
    me = lax.axis_index("section") * 16 + lax.axis_index("dp")
    owned = [sum(jnp.where(me == k, row[n], 0) for k, row in enumerate(limits)) for n in range(5)]

    def other(k):
        device = lax.rem(me + k, 32)
        return device, (device // 16, lax.rem(device, 16))

    def greet_all():
        barrier = pltpu.get_barrier_semaphore()
        for k in range(1, 32):
            pl.semaphore_signal(barrier, inc=1, device_id=other(k)[1], device_id_type=MESH)
        pl.semaphore_wait(barrier, 31)

    def relay(ref, zz, n):
        length = LENGTHS[0][zz][2]
        return ref.at[pl.ds(n * length, length)]

    def keep(square):
        row = lax.broadcasted_iota(jnp.int32, (8, 128), 0)
        parts[me] = jnp.where(row == 0, jnp.sum(square), loss[...])

    def run_first(z, y, c, io):
        part = Section(0, z, y, c, io, (mats, vecs) + buffers, sems)
        part.begin_loads()
        greet_all()
        part.exchange_cores()

        def cross(zz, yy):
            where = zz * 2 + yy
            start = io.many(
                RELAY,
                lambda n: (
                    part.cut(zz, yy, cut_relay(zz, n)),
                    relay(r_in.at[where], zz, n),
                    s_in.at[where, n],
                ),
                ["cross"],
            )

            def step(n):
                part.add(zz, yy, cut_relay(zz, n), part.core_sources(zz, yy))
                start(n)

            each(RELAY, step)

        for zz in part.order:
            part.to_side(zz)
            cross(zz, 1 - y)
            if zz != z:
                part.prepare(zz, False)
                cross(zz, y)
                part.along_tail(zz, True)
                part.along_tail(zz, False)
        part.tail_to_side()
        for zz in part.order[:-1]:
            part.along(zz)

        def total(cut, sources, square):
            return finish_tiles(out, sources, *cut, owned, square)

        square = part.end(total, jnp.zeros((8, 128), F32))

        def last(n, square):
            io.arrive(relay(r_back, z, n), s_back.at[n])
            sources = part.core_sources(z, y) + [Shifted(r_back, cut_relay(z, 0)[0])]
            return total(cut_relay(z, n), sources, square)

        keep(lax.fori_loop(0, RELAY, last, square))

    def run_second(z, y, c, io):
        part = Section(1, z, y, c, io, (second, second_vecs) + buffers, sems, EARLY)
        part.begin_loads()
        greet_all()
        part.exchange_cores()

        def came(ref, zz, n, sem):
            there = relay(ref, zz, n)
            io.arrive(there, sem)
            return there

        def small_add(target, sources):
            add_tiles(target, sources, 0, target.shape[0])

        for zz in part.order:
            flip, same = zz * 2 + 1 - y, zz * 2 + y
            start = io.many(
                RELAY,
                lambda n, zz=zz, flip=flip: (
                    relay(r_in.at[flip], zz, n),
                    relay(r_side.at[zz], zz, n),
                    s_side.at[zz, n],
                ),
                ["side"],
            )

            def to_side(n):
                came(r_in.at[flip], zz, n, s_in.at[flip, n])
                start(n)

            each(RELAY, to_side)
            part.to_side(zz)
            if zz == z:
                continue
            way, name, first = part.way(zz)
            onward = io.many(
                RELAY,
                lambda n, zz=zz, same=same, way=way: (
                    relay(r_in.at[same], zz, n),
                    relay(r_z.at[way, zz], zz, n),
                    s_z.at[way, zz, n],
                ),
                [name],
            )

            def along(n):
                mine = came(r_in.at[same], zz, n, s_in.at[same, n])
                sources = [mine, came(r_side.at[zz], zz, n, s_side.at[zz, n])]
                if z != first:
                    sources.append(came(r_z.at[way, zz], zz, n, s_z.at[way, zz, n]))
                small_add(mine, sources)
                onward(n)

            each(RELAY, along)
            part.along(zz)
        mine = r_in.at[z * 2 + y]
        back = io.many(
            RELAY,
            lambda n: (relay(mine, z, n), relay(r_back, z, n), s_back.at[n]),
            ["cross"],
        )

        def last(n):
            sources = [came(r_side.at[z], z, n, s_side.at[z, n])]
            for way in part.here():
                sources.append(came(r_z.at[way, z], z, n, s_z.at[way, z, n]))
            small_add(relay(mine, z, n), sources)
            back(n)

        each(RELAY, last)
        square = jnp.zeros((8, 128), F32)
        high = EARLY * LENGTHS[1][z][0]
        square = finish_tiles(out, [other_sum], 0, high, owned, square)

        def total(cut, sources, square):
            return finish_tiles(out, sources, *cut, owned, square)

        keep(part.end(total, square))

    def run(s, z, y, c):
        io = Sender(devices_around(z, y, c, s), send)
        (run_second if s else run_first)(z, y, c, io)
        io.finish()

    for_each_depth(run)
    copies = []
    for k in range(1, 32):
        copy = pltpu.make_async_remote_copy(
            parts.at[me],
            parts.at[me],
            send.at[k],
            s_parts.at[me],
            device_id=other(k)[1],
            device_id_type=MESH,
        )
        copy.start()
        copies.append(copy)
    for k in range(1, 32):
        device, where = other(k)
        pltpu.make_async_remote_copy(
            parts.at[device],
            parts.at[device],
            send.at[k],
            s_parts.at[device],
            device_id=where,
            device_id_type=MESH,
        ).wait_recv()
    total[...] = jnp.sum(parts[...], 0)
    for copy in copies:
        copy.wait_send()


def scatter_first(limits, mats, vecs, second, second_vecs, other_sum, loss):
    hbm = pl.BlockSpec(memory_space=pl.ANY)
    vm = pl.BlockSpec(memory_space=pltpu.VMEM)
    buffers, sems = section_scratch(0)
    most, count = RELAY * max(n[2] for n in LENGTHS[0]), RELAY
    return pl.pallas_call(
        functools.partial(scatter_first_kernel, limits),
        out_shape=[
            jax.ShapeDtypeStruct((SLOT, 16, 128), F32),
            jax.ShapeDtypeStruct((8, 128), F32),
        ],
        in_specs=[hbm] * 4 + [vm, vm],
        out_specs=[vm] * 2,
        scratch_shapes=buffers
        + sems
        + [
            pltpu.VMEM((8, most, 16, 128), BF),
            pltpu.VMEM((DEPTH, most, 16, 128), BF),
            pltpu.VMEM((2, DEPTH, most, 16, 128), BF),
            pltpu.VMEM((most, 16, 128), BF),
            pltpu.VMEM((32, 8, 128), F32),
            pltpu.SemaphoreType.DMA((160,)),
            pltpu.SemaphoreType.DMA((8, count)),
            pltpu.SemaphoreType.DMA((DEPTH, count)),
            pltpu.SemaphoreType.DMA((2, DEPTH, count)),
            pltpu.SemaphoreType.DMA((count,)),
            pltpu.SemaphoreType.DMA((32,)),
        ],
        name="scatter_first",
        compiler_params=pltpu.CompilerParams(
            collective_id=1, has_side_effects=True, vmem_limit_bytes=VMEM_LIMIT
        ),
    )(mats, vecs, second, second_vecs, other_sum, loss)


def piece_table(lines):
    plans = [shard_plan(m, lines * 128 * 16, 16) for m in (ENC_MATS, DEC_MATS)]
    most = max(len(pieces) for plan in plans for _, _, pieces in plan)
    table = [
        [[list(p) for p in pieces] + [[0] * 4] * (most - len(pieces)) for _, _, pieces in plan]
        for plan in plans
    ]
    widths = sorted({p[0] for plan in plans for _, _, pieces in plan for p in pieces})
    return plans, table, widths


def each_tile(table, widths, run):
    for piece in range(table.shape[0]):
        for width in widths:

            @pl.when(table[piece, 0] == width)
            def _(piece=piece, width=width):
                def step(i, carry):
                    for j in range(width):
                        line = MARGIN + table[piece, 1] + i * (16 * width) + j
                        run(line, width, SLOT_V + table[piece, 3] + i * width + j)
                    return carry

                lax.fori_loop(0, table[piece, 2], step, 0)


def pack_kernel(widths, table, mat, vec, out, lines, sem):
    count = mat.shape[0]
    copy = pltpu.make_async_copy(mat, lines.at[pl.ds(MARGIN, count)], sem)
    copy.start()
    lines[0:MARGIN, :] = jnp.zeros((MARGIN, 128), F32)
    lines[MARGIN + count :, :] = jnp.zeros((MARGIN, 128), F32)
    out[0:SLOT_V] = vec[...].astype(BF).reshape(SLOT_V, 16, 128)
    copy.wait()

    def run(line, width, tile):
        out[tile] = lines[pl.ds(line, 16, stride=width), :].astype(BF)

    each_tile(table, widths, run)


def pack(table, widths, mat, vec):
    vm = pl.BlockSpec(memory_space=pltpu.VMEM)
    return pl.pallas_call(
        functools.partial(pack_kernel, widths),
        out_shape=jax.ShapeDtypeStruct((SLOT, 16, 128), BF),
        in_specs=[
            pl.BlockSpec(memory_space=pltpu.SMEM),
            pl.BlockSpec(memory_space=pl.ANY),
            vm,
        ],
        out_specs=vm,
        scratch_shapes=[
            pltpu.VMEM((mat.shape[0] + 2 * MARGIN, 128), F32),
            pltpu.SemaphoreType.DMA,
        ],
        name="pack",
        compiler_params=pltpu.CompilerParams(vmem_limit_bytes=VMEM_LIMIT),
    )(table, mat, vec)


def clip_factor(square):
    return jnp.minimum(1.0, 0.001 / (jnp.sqrt(square) + 1e-06))


def adam_update(master, first, second, grad, rate, decay):
    first = 0.9 * first + 0.1 * grad
    second = 0.95 * second + 0.05 * grad * grad
    step_first = first / (1.0 - 0.9**STEP)
    step_second = second / (1.0 - 0.95**STEP)
    master = master - rate * (step_first / (jnp.sqrt(step_second) + 1e-08) + decay * master)
    return (master, first, second)


STEPS = 6


def update_kernel(widths, table, tiles, total, *refs):
    states, news, news_vec, (lines, held, fresh, sem_in, sem_out) = (
        refs[0:3],
        refs[3:6],
        refs[6],
        refs[7:],
    )
    count = held.shape[1]
    size = count // STEPS

    def part(i):
        return pl.ds(i * size, size)

    loads = [
        [
            pltpu.make_async_copy(state.at[part(i)], held.at[n, part(i)], sem_in.at[n, i])
            for n, state in enumerate(states)
        ]
        for i in range(STEPS)
    ]
    for step in loads:
        for copy in step:
            copy.start()
    lines[...] = jnp.zeros_like(lines)

    def run(line, width, tile):
        lines[pl.ds(line, 16, stride=width), :] = tiles[tile]

    each_tile(table, widths, run)
    news_vec[...] = tiles[0:SLOT_V].reshape(SLOT_V * 16, 128)
    factor = clip_factor(total[0:1, :])
    stores = []
    for i in range(STEPS):
        for copy in loads[i]:
            copy.wait()

        def body(k, carry, i=i):
            base = i * size + k * 104
            rows = pl.ds(pl.multiple_of(base, 8), 104)
            grad = factor * lines[pl.ds(pl.multiple_of(MARGIN + base, 8), 104), :]
            for n, value in enumerate(
                adam_update(held[0, rows, :], held[1, rows, :], held[2, rows, :], grad, 0.05, 0.05)
            ):
                fresh[n, rows, :] = value
            return carry

        lax.fori_loop(0, size // 104, body, 0)
        for n, new in enumerate(news):
            copy = pltpu.make_async_copy(fresh.at[n, part(i)], new.at[part(i)], sem_out.at[n, i])
            copy.start()
            stores.append(copy)
    for copy in stores:
        copy.wait()


def update(table, widths, tiles, total, states):
    count = states[0].shape[0]
    vm = pl.BlockSpec(memory_space=pltpu.VMEM)
    hbm = pl.BlockSpec(memory_space=pl.ANY)
    shape = jax.ShapeDtypeStruct((count, 128), F32)
    return pl.pallas_call(
        functools.partial(update_kernel, widths),
        out_shape=[shape] * 3 + [jax.ShapeDtypeStruct((SLOT_V * 16, 128), F32)],
        in_specs=[pl.BlockSpec(memory_space=pltpu.SMEM), vm, vm] + [hbm] * 3,
        out_specs=[hbm] * 3 + [vm],
        scratch_shapes=[
            pltpu.VMEM((count + 2 * MARGIN, 128), F32),
            pltpu.VMEM((3, count, 128), F32),
            pltpu.VMEM((3, count, 128), F32),
            pltpu.SemaphoreType.DMA((3, STEPS)),
            pltpu.SemaphoreType.DMA((3, STEPS)),
        ],
        name="update",
        compiler_params=pltpu.CompilerParams(vmem_limit_bytes=VMEM_LIMIT),
    )(table, tiles, total, *states)


def shifted(value, axis, steps):
    count = lax.axis_size(axis)
    initial, last = (max(0, -steps), min(count, count - steps))
    return lax.ppermute(value, axis, [(source, source + steps) for source in range(initial, last)])


def train(images, masked_total, enc, dec, enc_out, dec_out, pixels, visible, restore, vecs, weights):
    pix = jnp.pad(pixels, ((0, 0), (0, ROWS_D - PATCHES), (0, 0)))
    vis = jnp.pad(visible, ((0, 0), (0, ROWS_E - VIS)), constant_values=-1).reshape(-1, 1)
    places = jnp.pad(restore, ((0, 0), (0, ROWS_D - PATCHES)), constant_values=-1).reshape(-1, 1)
    latent, *saved = encoder_forward(images, enc, vis, pix, vecs, weights, 0)
    arrived = shifted(latent, "section", 1)
    dlatent, loss, dmats_dec, dvec_dec = decoder_step(
        images, dec, dec_out, masked_total, arrived, places, pix, vecs, weights, 1
    )
    returned = shifted(dlatent, "section", -1)
    dmats, dvec = encoder_backward(images, enc, enc_out, vis, vecs, returned, saved, weights, 0)
    return dmats, dvec, dmats_dec, dvec_dec, loss


def body_block(
    pixels, visible, restore, mat_master, mat_first, mat_second, vec_master, vec_first, vec_second
):
    images = pixels.shape[0]
    masked_total = (PATCHES - VIS) * images * 16
    count, size = mat_master.shape[1] // 128, vec_master.shape[1]
    plans, table, widths = piece_table(count)
    table = jnp.asarray(table, jnp.int32)[lax.axis_index("section"), lax.axis_index("dp")]
    lines = [value.reshape(count, 128) for value in (mat_master, mat_first, mat_second)]
    room = SLOT_V * 2048
    own = pack(
        table, widths, lines[0], jnp.pad(vec_master[0], (0, room - size)).reshape(-1, 128)
    )
    slots = gather_slots(own)
    vecs = slots[:, :SLOT_V].reshape(16, room)[:, :size].reshape(-1, 128).astype(F32)
    inward = [slot_layout(plan, slots.shape, SLOT_V) for plan in plans]
    outward = [whole_slots(plan, (16, SLOT_M, 16, 128)) for plan in plans]
    dmats, dvec, dmats_dec, dvec_dec, loss = train(
        images, masked_total, *inward, *outward, pixels, visible, restore, vecs, slots
    )
    dvec, dvec_dec = (
        jnp.pad(value.reshape(16, size), ((0, 0), (0, room - size)))
        .astype(BF)
        .reshape(16, SLOT_V, 16, 128)
        for value in (dvec, dvec_dec)
    )
    second = scatter_second(dmats_dec, dvec_dec)
    tiles, total = scatter_first(
        owned_limits(plans), dmats, dvec, dmats_dec, dvec_dec, second, loss
    )
    *news, grad_vec = update(table, widths, tiles, total, lines)
    news = [value.reshape(mat_master.shape) for value in news]
    square, loss_sum = total[0, 0], total[1, 0]
    vec_news = adam_update(
        vec_master,
        vec_first,
        vec_second,
        clip_factor(square) * grad_vec.reshape(1, room)[:, :size],
        0.3,
        0.0,
    )
    return (
        (loss_sum, jnp.sqrt(square))
        + tuple(news)
        + (news[0].astype(BF),)
        + tuple(vec_news)
        + (vec_news[0].astype(BF),)
    )


def body(
    pixels, visible, restore, mat_master, mat_first, mat_second, vec_master, vec_first, vec_second
):
    images = pixels.shape[0]
    total = mat_master.shape[1] * lax.axis_size("dp")
    masked_total = (PATCHES - VIS) * images * lax.axis_size("dp")
    encoding = lax.axis_index("section") == 0
    enc, dec = plain_layout(ENC_TOTAL), plain_layout(DEC_TOTAL)
    mats = lax.all_gather(mat_master.astype(BF), "dp", axis=1, tiled=True)[0]
    vecs = lax.all_gather(vec_master.astype(BF), "dp", axis=1, tiled=True)[0]
    vecs = vecs.astype(F32).reshape(-1, 128)
    weights = lax.cond(
        encoding,
        lambda m: natural(m, ENC_MATS),
        lambda m: jnp.pad(natural(m, DEC_MATS), ((0, ENC_TOTAL - DEC_TOTAL), (0, 0), (0, 0))),
        mats,
    )
    dec_in = Layout((ENC_TOTAL, 16, 128), [(lambda ref: ref.at[pl.ds(0, DEC_TOTAL)], 0, DEC_TOTAL)], [])
    dmats, dvec, dmats_dec, dvec_dec, loss = train(
        images, masked_total, enc, dec_in, enc, dec, pixels, visible, restore, vecs, weights
    )
    grad_mats, grad_vecs = lax.cond(
        encoding,
        lambda: (flat_from_natural(dmats.astype(F32), ENC_MATS, total), dvec),
        lambda: (flat_from_natural(dmats_dec.astype(F32), DEC_MATS, total), dvec_dec),
    )
    summed_mats = lax.psum_scatter(grad_mats[None], "dp", scatter_dimension=1, tiled=True)
    summed_vecs = lax.psum_scatter(
        grad_vecs.reshape(1, -1), "dp", scatter_dimension=1, tiled=True
    )
    square = jnp.sum(summed_mats * summed_mats) + jnp.sum(summed_vecs * summed_vecs)
    square, loss_sum = lax.psum((square, loss[0, 0]), ("section", "dp"))
    factor = clip_factor(square)
    mat_news = adam_update(mat_master, mat_first, mat_second, factor * summed_mats, 0.05, 0.05)
    vec_news = adam_update(vec_master, vec_first, vec_second, factor * summed_vecs, 0.3, 0.0)
    return (
        (loss_sum, jnp.sqrt(square))
        + tuple(mat_news)
        + (mat_news[0].astype(BF),)
        + tuple(vec_news)
        + (vec_news[0].astype(BF),)
    )


def solution(mesh):
    split = P("section", "dp")
    fits = mesh.shape["section"] == 2 and mesh.shape["dp"] == 16
    return jax.shard_map(
        body_block if fits else body,
        mesh=mesh,
        in_specs=(P("dp", None, None), P("dp", None), P("dp", None)) + (split,) * 6,
        out_specs=(P(), P()) + (split,) * 8,
        check_vma=False,
    )
```

```python
import functools
import math

import jax
import jax.numpy as jnp
from jax import lax
from jax.experimental import pallas as pl
from jax.experimental.pallas import tpu as pltpu
from jax.sharding import PartitionSpec as P

PIX = 768
DE = 768
HE = 12
FE = 3072
DD = 512
HD = 16
FD = 2048
PATCHES = 196
VIS = 49
STEP = 10
ROWS_E = 64
ROWS_D = 208
EPS = 1e-6
BF = jnp.bfloat16
F32 = jnp.float32
VMEM_LIMIT = 63 * 1024 * 1024

ENC_MATS = [(PIX, DE), (DE, 3 * DE), (DE, DE), (DE, FE), (FE, DE)]
DEC_MATS = [(DE, DD), (DD, 3 * DD), (DD, DD), (DD, FD), (FD, DD), (DD, PIX)]
ENC_VECS = [DE, PATCHES * DE, DE, DE, 2 * DE, DE, DE, DE, FE, DE, DE, DE]
DEC_VECS = [DD, DD, PATCHES * DD, DD, DD, 2 * DD, DD, DD, DD, FD, DD, DD, DD, PIX]


def starts(sizes):
    total, found = 0, []
    for size in sizes:
        found.append(total)
        total += size
    return found, total


ENC_TILES = [k * n // 2048 for k, n in ENC_MATS]
DEC_TILES = [k * n // 2048 for k, n in DEC_MATS]
ENC_BASE, ENC_TOTAL = starts(ENC_TILES)
DEC_BASE, DEC_TOTAL = starts(DEC_TILES)
EV, _ = starts([size // 128 for size in ENC_VECS])
DV, _ = starts([size // 128 for size in DEC_VECS])


class Mat:
    def __init__(self, ref, base, shape, loads=None, stores=None):
        self.base, self.loads, self.stores = base, loads, stores
        self.rows, self.columns = shape
        self.blocks = self.columns // 128
        count = self.rows * self.columns // 2048
        self.ref = ref.at[pl.ds(base, count)].reshape(self.rows // 16, self.blocks, 16, 128)

    def need(self):
        self.loads.need(self.base, self.rows * self.columns // 2048)

    def done(self):
        self.stores.done(self.base, self.rows * self.columns // 2048)

    def cols(self, block):
        parts = [self.ref[:, 2 * block + half].reshape(self.rows, 128) for half in range(2)]
        return jnp.concatenate(parts, 1)

    def band(self, block):
        part = self.ref.at[pl.ds(block * 16, 16)]
        return jnp.concatenate([part[:, j].reshape(256, 128) for j in range(self.blocks)], 1)

    def put_cols(self, block, value):
        for half in range(2):
            piece = value[:, half * 128 : (half + 1) * 128].astype(BF)
            self.ref[:, 2 * block + half] = piece.reshape(self.rows // 16, 16, 128)

    def put_band(self, block, value):
        part = self.ref.at[pl.ds(block * 16, 16)]
        for j in range(self.blocks):
            part[:, j] = value[:, j * 128 : (j + 1) * 128].astype(BF).reshape(16, 16, 128)


def dot(a, b):
    return jnp.dot(a, b, preferred_element_type=F32)


def dot_t(a, b):
    return lax.dot_general(a, b, (((1,), (1,)), ((), ())), preferred_element_type=F32)


def t_dot(a, b):
    return lax.dot_general(a, b, (((0,), (0,)), ((), ())), preferred_element_type=F32)


def loop(count, body, init=0):
    return lax.fori_loop(0, count, body, init)


def lanes(block, width=256):
    return pl.ds(pl.multiple_of(block * width, width), width)


def row_of(vec, start, width):
    return jnp.concatenate([vec[start + j : start + j + 1, :] for j in range(width // 128)], 1)


def row_at(vec, start, block):
    return jnp.concatenate([vec[pl.ds(start + 2 * block + h, 1), :] for h in range(2)], 1)


def put_row(dvec, start, value):
    for j in range(value.shape[1] // 128):
        dvec[start + j : start + j + 1, :] = value[:, j * 128 : (j + 1) * 128]


def put_row_at(dvec, start, block, value):
    for h in range(2):
        dvec[pl.ds(start + 2 * block + h, 1), :] = value[:, h * 128 : (h + 1) * 128]


def fold(value):
    return value.reshape(value.shape[0] // 8, 8, value.shape[1]).sum(0)


def total_row(value):
    return jnp.sum(value, 0, keepdims=True)


def norm_parts(x):
    mean = jnp.mean(x, -1, keepdims=True)
    centred = x - mean
    scale = lax.rsqrt(jnp.mean(centred * centred, -1, keepdims=True) + EPS)
    return centred * scale, scale


CHUNKS = (208, 128, 64, 32)


def chunk_loop(ref, step, init=0):
    count = ref.shape[0]
    size = next(c for c in CHUNKS if count % c == 0)

    def run(i, carry):
        return step(pl.ds(pl.multiple_of(i * size, size), size), carry)

    return lax.fori_loop(0, count // size, run, init)


def norm_rows(x_ref, out_ref, vec, gain_at, shift_at, width, add_ref=None, bias_at=None):
    gain, shift = row_of(vec, gain_at, width), row_of(vec, shift_at, width)
    bias = None if bias_at is None else row_of(vec, bias_at, width)

    def step(rows, carry):
        x = x_ref[rows, :]
        if add_ref is not None:
            x = x + add_ref[rows, :] + bias
            add_ref[rows, :] = x
        unit, _ = norm_parts(x)
        out_ref[rows, :] = (unit * gain + shift).astype(BF)
        return carry

    chunk_loop(x_ref, step)


def norm_back_rows(x_ref, dy_ref, dx_ref, dxb_ref, vec, dvec, gain_at, shift_at, width, bias_at, add):
    gain = row_of(vec, gain_at, width)
    zero = jnp.zeros((8, width), F32)

    def step(rows, carry):
        dgain, dshift, dbias = carry
        unit, scale = norm_parts(x_ref[rows, :])
        dy = dy_ref[rows, :].astype(F32)
        dunit = dy * gain
        dx = scale * (
            dunit
            - jnp.mean(dunit, -1, keepdims=True)
            - unit * jnp.mean(dunit * unit, -1, keepdims=True)
        )
        if add:
            dx = dx + dx_ref[rows, :]
        dx_ref[rows, :] = dx
        dxb_ref[rows, :] = dx.astype(BF)
        return dgain + fold(dy * unit), dshift + fold(dy), dbias + fold(dx)

    dgain, dshift, dbias = chunk_loop(x_ref, step, (zero, zero, zero))
    put_row(dvec, gain_at, total_row(dgain))
    put_row(dvec, shift_at, total_row(dshift))
    if bias_at is not None:
        put_row(dvec, bias_at, total_row(dbias))
    return dbias


GELU_C = math.sqrt(2.0 / math.pi)


def gelu_parts(x):
    square = x * x
    t = jnp.tanh(x * (GELU_C + (GELU_C * 0.044715) * square))
    half = 0.5 * (1.0 + t)
    return x * half, half + (0.5 * x) * (1.0 - t * t) * (
        GELU_C + (3.0 * 0.044715 * GELU_C) * square
    )


def head_mask(size):
    lane = lax.broadcasted_iota(jnp.int32, (1, 128), 1)
    return [(lane >= h * size) & (lane < (h + 1) * size) for h in range(128 // size)]


def heads_apart(value, masks):
    return jnp.concatenate([jnp.where(mask, value, jnp.zeros_like(value)) for mask in masks], 0)


def heads_joined(stacked, masks, group):
    value = stacked[0:group]
    for h, mask in list(enumerate(masks))[1:]:
        value = jnp.where(mask, stacked[h * group : (h + 1) * group], value)
    return value


def attention(qkv, probs, att, bias, group, groups, width, size):
    blocks = width // 128
    masks = head_mask(size)
    heads = len(masks)

    def step(i, carry):
        g, b = i // blocks, i % blocks
        rows = pl.ds(pl.multiple_of(g * group, 16), group)
        q = qkv[rows, lanes(b, 128)]
        k = qkv[rows, lanes(blocks + b, 128)]
        v = qkv[rows, lanes(2 * blocks + b, 128)]
        s = dot_t(heads_apart(k, masks), q).reshape(heads, group, group) + bias
        e = jnp.exp(s - jnp.max(s, 1, keepdims=True))
        p = (e * (1.0 / jnp.sum(e, 1, keepdims=True))).astype(BF)
        probs[pl.ds(i * heads, heads)] = p
        turned = v.T
        out = [dot(turned[h * size : (h + 1) * size], p[h]) for h in range(heads)]
        att[rows, lanes(b, 128)] = jnp.concatenate(out, 0).astype(BF).T
        return carry

    lax.fori_loop(0, groups * blocks, step, 0, unroll=UNROLL)


UNROLL = 2


def attention_back(qkv, probs, datt, dqkv, dvec, qv_at, group, groups, width, size):
    blocks = width // 128
    masks = head_mask(size)
    heads = len(masks)
    scale = size ** (-0.5)
    for j in range(2 * blocks):
        dvec[qv_at + j : qv_at + j + 1, :] = jnp.zeros((1, 128), F32)

    def step(i, carry):
        g, b = i // blocks, i % blocks
        rows = pl.ds(pl.multiple_of(g * group, 16), group)
        q = qkv[rows, lanes(b, 128)]
        k = qkv[rows, lanes(blocks + b, 128)]
        v = qkv[rows, lanes(2 * blocks + b, 128)]
        da = datt[rows, lanes(b, 128)]
        p = probs[pl.ds(i * heads, heads)]
        dp = dot_t(heads_apart(v, masks), da).reshape(heads, group, group)
        wide = p.astype(F32)
        prod = wide * dp
        ds = (prod - wide * jnp.sum(prod, 1, keepdims=True)).astype(BF)
        turned = k.T
        dq = [dot(turned[h * size : (h + 1) * size], ds[h]) for h in range(heads)]
        dq = jnp.concatenate(dq, 0).T * scale
        dk = heads_joined(dot(ds.reshape(heads * group, group), q), masks, group)
        dv = heads_joined(dot(p.reshape(heads * group, group), da), masks, group)
        dqkv[rows, lanes(b, 128)] = dq.astype(BF)
        dqkv[rows, lanes(blocks + b, 128)] = dk.astype(BF)
        dqkv[rows, lanes(2 * blocks + b, 128)] = dv.astype(BF)
        dvec[pl.ds(qv_at + b, 1), :] += total_row(dq)
        dvec[pl.ds(qv_at + blocks + b, 1), :] += total_row(dv)
        return carry

    lax.fori_loop(0, groups * blocks, step, 0, unroll=UNROLL)


def block_forward(s, mats, vec, at, width, hidden, size, bias, group, groups):
    w_qkv, w_proj, w_up, w_down = mats
    pairs = width // 256
    scale = size ** (-0.5)
    norm_rows(s.x0, s.n1, vec, at["g1"], at["s1"], width)

    def qkv_step(j, carry):
        part = j // pairs
        row = row_at(vec, at["qv"], jnp.where(part == 0, j, jnp.maximum(j - pairs, 0)))
        value = dot(s.n1[...], w_qkv.cols(j)) + jnp.where(part == 1, 0.0, row)
        s.qkv[:, lanes(j)] = (value * jnp.where(part == 0, scale, 1.0)).astype(BF)
        return carry

    s.done("n1")
    w_qkv.need()
    loop(3 * pairs, qkv_step)
    s.done("qkv")
    attention(s.qkv, s.probs, s.att, bias, group, groups, width, size)
    s.done("probs", "att")

    def proj_step(j, carry):
        s.x1[:, lanes(j)] = dot(s.att[...], w_proj.cols(j))
        return carry

    w_proj.need()
    loop(pairs, proj_step)
    norm_rows(s.x0, s.n2, vec, at["g2"], at["s2"], width, s.x1, at["bo"])

    def mlp_step(j, carry):
        h = dot(s.n2[...], w_up.cols(j)) + row_at(vec, at["bu"], j)
        s.h[:, lanes(j)] = h
        u = gelu_parts(h)[0].astype(BF)
        update = dot(u, w_down.band(j))

        @pl.when(j == 0)
        def _():
            s.x2[...] = update

        @pl.when(j > 0)
        def _():
            s.x2[...] += update

        return carry

    s.done("x1", "n2")
    w_up.need()
    w_down.need()
    loop(hidden // 256, mlp_step)
    s.done("h")


def block_backward(s, mats, grads, vec, dvec, at, width, hidden, size, group, groups):
    w_qkv, w_proj, w_up, w_down = mats
    d_qkv, d_proj, d_up, d_down = grads
    pairs = width // 256
    s.need("n2")
    s.flip[...] = s.n2[...].T

    def mlp_step(j, carry):
        dxb = s.dxb[...]
        u, slope = gelu_parts(s.h[:, lanes(j)])
        dh = dot_t(dxb, w_down.band(j)) * slope
        put_row_at(dvec, at["bu"], j, total_row(fold(dh)))
        dh = dh.astype(BF)
        d_down.put_band(j, t_dot(u.astype(BF), dxb))
        d_up.put_cols(j, dot(s.flip[...], dh))
        update = dot_t(dh, w_up.cols(j))

        @pl.when(j == 0)
        def _():
            s.dn[...] = update

        @pl.when(j > 0)
        def _():
            s.dn[...] += update

        return carry

    s.need("h")
    w_down.need()
    w_up.need()
    loop(hidden // 256, mlp_step)
    d_down.done()
    d_up.done()
    s.need("x1")
    norm_back_rows(s.x1, s.dn, s.dx, s.dxb, vec, dvec, at["g2"], at["s2"], width, at["bo"], True)

    def proj_step(j, carry):
        dxb = s.dxb[...]
        s.datt[:, lanes(j)] = dot_t(dxb, w_proj.band(j)).astype(BF)
        d_proj.put_band(j, t_dot(s.att[:, lanes(j)], dxb))
        return carry

    s.need("att")
    w_proj.need()
    loop(pairs, proj_step)
    d_proj.done()
    s.need("qkv", "probs")
    attention_back(s.qkv, s.probs, s.datt, s.dqkv, dvec, at["qv"], group, groups, width, size)
    s.need("n1")
    s.flip[...] = s.n1[...].T

    def weight_step(j, carry):
        d_qkv.put_cols(j, dot(s.flip[...], s.dqkv[:, lanes(j)]))
        return carry

    loop(3 * pairs, weight_step)
    d_qkv.done()

    def input_step(j, carry):
        s.dn[:, lanes(j)] = dot_t(s.dqkv[...], w_qkv.band(j))
        return carry

    w_qkv.need()
    loop(pairs, input_step)
    s.need("x0")
    norm_back_rows(s.x0, s.dn, s.dx, s.dxb, vec, dvec, at["g1"], at["s1"], width, None, True)


ENC_AT = dict(g1=EV[2], s1=EV[3], qv=EV[4], bo=EV[5], g2=EV[6], s2=EV[7], bu=EV[8])
DEC_AT = dict(g1=DV[3], s1=DV[4], qv=DV[5], bo=DV[6], g2=DV[7], s2=DV[8], bu=DV[9])


def only(section, run):
    if section is None:
        run()
    else:
        pl.when(lax.axis_index("section") == section)(run)


class Bag:
    def __init__(self, names, refs):
        self.source, self.target, self.flying = {}, {}, {}
        for name, ref in zip(names, refs):
            setattr(self, name, ref)

    def begin(self, name, source, target, sem):
        self.flying[name] = pltpu.make_async_copy(source, target, sem)
        self.flying[name].start()

    def come(self, names, sources, sems):
        for n, (name, source) in enumerate(zip(names, sources)):
            self.begin(name, source, getattr(self, name), sems.at[n])

    def need(self, *names):
        for name in names:
            if name in self.flying:
                self.flying.pop(name).wait()

    def done(self, *names):
        for name in names:
            if name in self.target:
                target, sem = self.target[name]
                self.begin(name, getattr(self, name), target, sem)

    def finish(self):
        self.need(*list(self.flying))


class Layout:
    def __init__(self, shape, moves, shared, sums=None):
        self.shape, self.moves, self.shared, self.sums = shape, moves, shared, sums


def plain_layout(total):
    return Layout((total, 16, 128), [(lambda ref: ref, 0, total)], [])


def slot_layout(plan, shape, lead):
    moves, shared, done = [], [], 0
    for device, (first, count, _) in enumerate(plan):
        skip = max(0, done - first)
        if skip and count:
            shared.append((lambda ref, d=device, n=skip: ref.at[d, pl.ds(lead, n)], first, skip))
        if count:
            moves.append(
                (
                    lambda ref, d=device, a=skip, n=count - skip: ref.at[d, pl.ds(lead + a, n)],
                    first + skip,
                    count - skip,
                )
            )
        done = first + count
    return Layout(shape, moves, shared)


def put_sums(dvec, out):
    if out.shape == dvec.shape:
        out[...] = dvec[...]
        return
    rows = out.shape[1] * 16
    for device in range(out.shape[0]):
        first = device * dvec.shape[0] // out.shape[0]
        out[device] = dvec[first : first + rows, :].astype(BF).reshape(out.shape[1:])


def whole_slots(plan, shape, sums):
    moves = [
        (lambda ref, d=device, n=count: ref.at[d, pl.ds(0, n)], first, count)
        for device, (first, count, _) in enumerate(plan)
        if count
    ]
    return Layout(shape, moves, [], jax.ShapeDtypeStruct(sums, BF))


SHARED = 24


class Loads:
    def __init__(self, source, kept, side, sem, layout, backward=False):
        self.kept, self.side, self.flying = kept, side, []
        moves = list(enumerate(layout.moves))
        for index, (pick, start, count) in moves[::-1] if backward else moves:
            copy = pltpu.make_async_copy(pick(source), kept.at[pl.ds(start, count)], sem.at[index])
            copy.start()
            self.flying.append((start, count, None, copy))
        for index, (pick, start, count) in enumerate(layout.shared):
            copy = pltpu.make_async_copy(
                pick(source),
                side.at[index, pl.ds(0, count)],
                sem.at[len(layout.moves) + index],
            )
            copy.start()
            self.flying.append((start, count, index, copy))

    def need(self, base, tiles):
        here = [f for f in self.flying if f[0] < base + tiles and f[0] + f[1] > base]
        self.flying = [f for f in self.flying if f not in here]
        for item in here:
            item[3].wait()
        for start, count, index, _ in here:
            if index is not None:
                there = pl.ds(start, count)
                both = self.kept[there].astype(F32) + self.side[index, 0:count].astype(F32)
                self.kept[there] = both.astype(BF)


class Stores:
    def __init__(self, kept, out, sem, layout):
        self.kept, self.out, self.sem = kept, out, sem
        self.left, self.ready, self.flying = list(enumerate(layout.moves)), set(), []

    def done(self, base, tiles):
        self.ready.update(range(base, base + tiles))
        for item in list(self.left):
            index, (pick, start, count) = item
            if self.ready.issuperset(range(start, start + count)):
                copy = pltpu.make_async_copy(
                    self.kept.at[pl.ds(start, count)], pick(self.out), self.sem.at[index]
                )
                copy.start()
                self.flying.append(copy)
                self.left.remove(item)

    def finish(self):
        for copy in self.flying:
            copy.wait()


def load_scratch(layout):
    return [
        pltpu.VMEM((max(1, len(layout.shared)), SHARED, 16, 128), BF),
        pltpu.SemaphoreType.DMA((len(layout.moves) + len(layout.shared),)),
    ]


def visible_rows(column, count):
    lane = lax.broadcasted_iota(jnp.int32, (1, count), 1)
    return jnp.where(column == lane, 1.0, 0.0).astype(BF)


def encoder_bias(rows):
    r = lax.broadcasted_iota(jnp.int32, (rows, rows), 0)
    c = lax.broadcasted_iota(jnp.int32, (rows, rows), 1)
    same = (r // ROWS_E == c // ROWS_E) & (r % ROWS_E < VIS)
    return jnp.where(same, 0.0, -1e30)


ENC_KEEP = ["pick", "x0", "n1", "qkv", "probs", "att", "x1", "n2", "h", "x2"]


def enc_shapes(images):
    rows = images * ROWS_E
    return dict(
        pick=((rows, PIX), BF),
        x0=((rows, DE), F32),
        n1=((rows, DE), BF),
        qkv=((rows, 3 * DE), BF),
        probs=((HE, rows, rows), BF),
        att=((rows, DE), BF),
        x1=((rows, DE), F32),
        n2=((rows, DE), BF),
        h=((rows, FE), F32),
        x2=((rows, DE), F32),
    )


def position_column(vec, start, blocks, j):
    return vec[pl.ds(start + j, PATCHES, stride=blocks), :]


def encoder_forward_kernel(images, layout, section, vis, pix, vec, weights, *refs):
    latent, outs = refs[0], refs[1 : 1 + len(ENC_KEEP)]
    s = Bag(ENC_KEEP, refs[1 + len(ENC_KEEP) : 1 + 2 * len(ENC_KEEP)])
    keep_sem, kept, posit, side, sem = refs[1 + 2 * len(ENC_KEEP) :]
    s.target = {name: (out, keep_sem.at[n]) for n, (name, out) in enumerate(zip(ENC_KEEP, outs))}
    def run():
        loads = Loads(weights, kept, side, sem, layout)
        rows = images * ROWS_E
        mats = [Mat(kept, b, shape, loads) for b, shape in zip(ENC_BASE, ENC_MATS)]
        posit[...] = jnp.zeros_like(posit)
        for j in range(DE // 128):
            posit[0:PATCHES, j * 128 : (j + 1) * 128] = position_column(vec, EV[1], DE // 128, j)
        for i in range(images):
            where = pl.ds(i * ROWS_E, ROWS_E)
            hot = visible_rows(vis[where, :], ROWS_D)
            s.pick[where, :] = dot(hot, pix[i]).astype(BF)
            s.x0[where, :] = dot(hot, posit[...].astype(BF)) + row_of(vec, EV[0], DE)
        mats[0].need()

        def embed_step(j, carry):
            s.x0[:, lanes(j)] += dot(s.pick[...], mats[0].cols(j))
            return carry

        loop(DE // 256, embed_step)
        s.done("pick", "x0")
        block_forward(
            s, mats[1:5], vec, ENC_AT, DE, FE, DE // HE, encoder_bias(rows), rows, 1
        )
        norm_rows(s.x1, latent, vec, EV[10], EV[11], DE, s.x2, EV[9])
        s.done("x2")
        s.finish()

    only(section, run)


def encoder_forward(images, layout, vis, pix, vec, weights, section=None):
    shapes = enc_shapes(images)
    rows = images * ROWS_E
    vm = pl.BlockSpec(memory_space=pltpu.VMEM)
    return pl.pallas_call(
        functools.partial(encoder_forward_kernel, images, layout, section),
        out_shape=[jax.ShapeDtypeStruct((rows, DE), BF)]
        + [jax.ShapeDtypeStruct(*shapes[name]) for name in ENC_KEEP],
        in_specs=[vm, vm, vm, pl.BlockSpec(memory_space=pl.ANY)],
        out_specs=[vm] + [pl.BlockSpec(memory_space=pl.ANY)] * len(ENC_KEEP),
        scratch_shapes=[pltpu.VMEM(*shapes[name]) for name in ENC_KEEP]
        + [
            pltpu.SemaphoreType.DMA((len(ENC_KEEP),)),
            pltpu.VMEM((ENC_TOTAL, 16, 128), BF),
            pltpu.VMEM((ROWS_D, DE), F32),
        ]
        + load_scratch(layout),
        name="encoder_forward",
        compiler_params=pltpu.CompilerParams(vmem_limit_bytes=VMEM_LIMIT),
    )(vis, pix, vec, weights)


def encoder_backward_kernel(images, layout, out_layout, section, vis, vec, dlatent, *refs):
    n = len(ENC_KEEP)
    saved, (weights, dmats, sums) = refs[:n], refs[n : n + 3]
    s = Bag(ENC_KEEP, refs[n + 3 : 2 * n + 3])
    keep_sem, kept, dkept, s.dx, s.dxb, s.dn, s.datt, s.dqkv, s.flip, dvec, out_sem, side, sem = refs[
        2 * n + 3 :
    ]
    def run():
        s.come(ENC_KEEP[::-1], saved[::-1], keep_sem)
        loads = Loads(weights, kept, side, sem, layout, True)
        stores = Stores(dkept, dmats, out_sem, out_layout)
        rows = images * ROWS_E
        mats = [Mat(kept, b, shape, loads) for b, shape in zip(ENC_BASE, ENC_MATS)]
        grads = [Mat(dkept, b, shape, None, stores) for b, shape in zip(ENC_BASE, ENC_MATS)]
        dvec[EV[11] + DE // 128 :, :] = jnp.zeros_like(dvec[EV[11] + DE // 128 :, :])
        s.need("x2")
        norm_back_rows(
            s.x2, dlatent, s.dx, s.dxb, vec, dvec, EV[10], EV[11], DE, EV[9], False
        )
        block_backward(
            s, mats[1:5], grads[1:5], vec, dvec, ENC_AT, DE, FE, DE // HE, rows, 1
        )
        put_row(dvec, EV[0], jnp.sum(s.dx[...], 0, keepdims=True))

        s.need("pick")

        def embed_step(j, carry):
            grads[0].put_band(j, t_dot(s.pick[:, lanes(j)], s.dxb[...]))
            return carry

        loop(DE // 256, embed_step)
        grads[0].done()
        mats[0].need()
        hot = visible_rows(vis[...], ROWS_D)
        for j in range(DE // 128):
            value = t_dot(hot, s.dxb[:, j * 128 : (j + 1) * 128])
            dvec[pl.ds(EV[1] + j, PATCHES, stride=DE // 128), :] = value[0:PATCHES]
        put_sums(dvec, sums)
        stores.finish()

    only(section, run)


def encoder_backward(images, layout, out_layout, vis, vec, dlatent, saved, weights, section=None):
    rows = images * ROWS_E
    shapes = enc_shapes(images)
    vm = pl.BlockSpec(memory_space=pltpu.VMEM)
    hbm = pl.BlockSpec(memory_space=pl.ANY)
    return pl.pallas_call(
        functools.partial(encoder_backward_kernel, images, layout, out_layout, section),
        out_shape=[
            jax.ShapeDtypeStruct(out_layout.shape, BF),
            out_layout.sums or jax.ShapeDtypeStruct(vec.shape, F32),
        ],
        in_specs=[vm] * 3 + [hbm] * (len(ENC_KEEP) + 1),
        out_specs=[hbm, vm],
        scratch_shapes=[pltpu.VMEM(*shapes[name]) for name in ENC_KEEP]
        + [
            pltpu.SemaphoreType.DMA((len(ENC_KEEP),)),
            pltpu.VMEM((ENC_TOTAL, 16, 128), BF),
            pltpu.VMEM((ENC_TOTAL, 16, 128), BF),
            pltpu.VMEM((rows, DE), F32),
            pltpu.VMEM((rows, DE), BF),
            pltpu.VMEM((rows, DE), F32),
            pltpu.VMEM((rows, DE), BF),
            pltpu.VMEM((rows, 3 * DE), BF),
            pltpu.VMEM((DE, rows), BF),
            pltpu.VMEM(vec.shape, F32),
            pltpu.SemaphoreType.DMA((len(out_layout.moves),)),
        ]
        + load_scratch(layout),
        name="encoder_backward",
        compiler_params=pltpu.CompilerParams(vmem_limit_bytes=VMEM_LIMIT),
    )(vis, vec, dlatent, *saved, weights)


def decoder_kernel(images, layout, out_layout, section, masked_total, latent, places, pix, vec, weights, *refs):
    dlatent, loss, dmats, sums = refs[:4]
    s = Bag(
        ["x0", "x1", "x2", "n1", "n2", "qkv", "probs", "att", "h", "dx", "dxb", "dn", "dqkv", "flip"],
        refs[4:18],
    )
    kept, dkept, posit, dguess, dvec, out_sem, side, sem = refs[18:]
    s.datt = s.n2
    loss[...] = jnp.zeros((8, 128), F32)

    def run():
        rows = images * ROWS_D
        loads = Loads(weights, kept, side, sem, layout)
        stores = Stores(dkept, dmats, out_sem, out_layout)
        mats = [Mat(kept, b, shape, loads) for b, shape in zip(DEC_BASE, DEC_MATS)]
        grads = [Mat(dkept, b, shape, None, stores) for b, shape in zip(DEC_BASE, DEC_MATS)]
        posit[...] = jnp.zeros_like(posit)
        for j in range(DD // 128):
            posit[0:PATCHES, j * 128 : (j + 1) * 128] = position_column(vec, DV[2], DD // 128, j)
        dvec[DV[13] + PIX // 128 :, :] = jnp.zeros_like(dvec[DV[13] + PIX // 128 :, :])
        mats[0].need()
        for i in range(images):
            part = pl.ds(i * ROWS_E, ROWS_E)
            where = pl.ds(i * ROWS_D, ROWS_D)
            for j in range(DD // 256):
                cut = slice(j * 256, (j + 1) * 256)
                z = dot(latent[part, :], mats[0].cols(j)) + row_of(vec, DV[0] + 2 * j, 256)
                place = places[where, :]
                hot = visible_rows(jnp.where(place < VIS, place, -1), ROWS_E)
                high = z.astype(BF)
                low = (z - high.astype(F32)).astype(BF)
                token = jnp.where(place >= VIS, 1.0, 0.0) * row_of(vec, DV[1] + 2 * j, 256)
                s.x0[where, cut] = dot(hot, high) + dot(hot, low) + token + posit[:, cut]
        key = lax.broadcasted_iota(jnp.int32, (ROWS_D, 1), 0)
        bias = jnp.where(key < PATCHES, 0.0, -1e30)
        block_forward(
            s, mats[1:5], vec, DEC_AT, DD, FD, DD // HD, bias, ROWS_D, images
        )
        norm_rows(s.x1, s.dxb, vec, DV[11], DV[12], DD, s.x2, DV[10])
        factor = 2.0 / (PIX * masked_total)

        def head_step(j, total):
            value = dot(s.dxb[...], mats[5].cols(j)) + row_at(vec, DV[13], j)
            count = jnp.zeros((8, 256), F32)
            column = jnp.zeros((8, 256), F32)
            for i in range(images):
                where = slice(i * ROWS_D, (i + 1) * ROWS_D)
                error = value[where] - pix[i, :, lanes(j)].astype(F32)
                error = jnp.where(places[where, :] >= VIS, error, 0.0)
                count = count + fold(error * error)
                error = error * factor
                column = column + fold(error)
                dguess[where, lanes(j)] = error.astype(BF)
            put_row_at(dvec, DV[13], j, total_row(column))
            return total + count

        mats[5].need()
        total = loop(PIX // 256, head_step, jnp.zeros((8, 256), F32))
        loss[...] = jnp.broadcast_to(jnp.sum(total) * (1.0 / PIX), (8, 128))
        s.flip[...] = s.dxb[...].T

        def head_weight_step(j, carry):
            grads[5].put_cols(j, dot(s.flip[...], dguess[:, lanes(j)]))
            return carry

        loop(PIX // 256, head_weight_step)
        grads[5].done()

        def head_input_step(j, carry):
            s.dn[:, lanes(j)] = dot_t(dguess[...], mats[5].band(j))
            return carry

        loop(DD // 256, head_input_step)
        norm_back_rows(s.x2, s.dn, s.dx, s.dxb, vec, dvec, DV[11], DV[12], DD, DV[10], False)
        block_backward(
            s, mats[1:5], grads[1:5], vec, dvec, DEC_AT, DD, FD, DD // HD, ROWS_D, images
        )
        token = jnp.zeros((8, DD), F32)
        spot = jnp.zeros((ROWS_D, DD), F32)
        back = []
        for i in range(images):
            where = pl.ds(i * ROWS_D, ROWS_D)
            place = places[where, :]
            dx = s.dx[where, :]
            spot = spot + dx
            token = token + fold(jnp.where(place >= VIS, dx, 0.0))
            hot = visible_rows(jnp.where(place < VIS, place, -1), ROWS_E)
            back.append(t_dot(hot, s.dxb[where, :]))
        posit[...] = spot
        for j in range(DD // 128):
            dvec[pl.ds(DV[2] + j, PATCHES, stride=DD // 128), :] = posit[
                0:PATCHES, j * 128 : (j + 1) * 128
            ]
        put_row(dvec, DV[1], total_row(token))
        back = jnp.concatenate(back, 0)
        put_row(dvec, DV[0], jnp.sum(back, 0, keepdims=True))
        back = back.astype(BF)
        for j in range(DE // 256):
            grads[0].put_band(j, t_dot(latent[:, j * 256 : (j + 1) * 256], back))
            dlatent[:, j * 256 : (j + 1) * 256] = dot_t(back, mats[0].band(j)).astype(BF)
        grads[0].done()
        put_sums(dvec, sums)
        stores.finish()

    only(section, run)


def decoder_step(
    images, layout, out_layout, masked_total, latent, places, pix, vec, weights, section=None
):
    rows = images * ROWS_D
    vm = pl.BlockSpec(memory_space=pltpu.VMEM)
    hbm = pl.BlockSpec(memory_space=pl.ANY)
    probs = images * HD
    return pl.pallas_call(
        functools.partial(decoder_kernel, images, layout, out_layout, section, masked_total),
        out_shape=[
            jax.ShapeDtypeStruct((images * ROWS_E, DE), BF),
            jax.ShapeDtypeStruct((8, 128), F32),
            jax.ShapeDtypeStruct(out_layout.shape, BF),
            out_layout.sums or jax.ShapeDtypeStruct(vec.shape, F32),
        ],
        in_specs=[vm, vm, vm, vm, hbm],
        out_specs=[vm, vm, hbm, vm],
        scratch_shapes=[
            pltpu.VMEM((rows, DD), F32),
            pltpu.VMEM((rows, DD), F32),
            pltpu.VMEM((rows, DD), F32),
            pltpu.VMEM((rows, DD), BF),
            pltpu.VMEM((rows, DD), BF),
            pltpu.VMEM((rows, 3 * DD), BF),
            pltpu.VMEM((probs, ROWS_D, ROWS_D), BF),
            pltpu.VMEM((rows, DD), BF),
            pltpu.VMEM((rows, FD), F32),
            pltpu.VMEM((rows, DD), F32),
            pltpu.VMEM((rows, DD), BF),
            pltpu.VMEM((rows, DD), F32),
            pltpu.VMEM((rows, 3 * DD), BF),
            pltpu.VMEM((DD, rows), BF),
            pltpu.VMEM((DEC_TOTAL, 16, 128), BF),
            pltpu.VMEM((DEC_TOTAL, 16, 128), BF),
            pltpu.VMEM((ROWS_D, DD), F32),
            pltpu.VMEM((rows, PIX), BF),
            pltpu.VMEM(vec.shape, F32),
            pltpu.SemaphoreType.DMA((len(out_layout.moves),)),
        ]
        + load_scratch(layout),
        name="decoder_step",
        compiler_params=pltpu.CompilerParams(vmem_limit_bytes=VMEM_LIMIT),
    )(latent, places, pix, vec, weights)


def natural(flat, shapes):
    pieces, offset = [], 0
    for rows, columns in shapes:
        piece = flat[offset : offset + rows * columns].reshape(rows // 16, 16, columns // 128, 128)
        pieces.append(piece.transpose(0, 2, 1, 3).reshape(-1, 16, 128))
        offset += rows * columns
    return jnp.concatenate(pieces, 0)


def flat_from_natural(tiles, shapes, total):
    pieces, offset = [], 0
    for rows, columns in shapes:
        count = rows * columns // 2048
        piece = tiles[offset : offset + count].reshape(rows // 16, columns // 128, 16, 128)
        pieces.append(piece.transpose(0, 2, 1, 3).reshape(-1))
        offset += count
    flat = jnp.concatenate(pieces)
    return jnp.pad(flat, (0, total - flat.shape[0]))


MESH = pl.DeviceIdType.MESH
DEPTH, WIDTH = 4, 2
SLOT_M, SLOT_V = 264, 5
SLOT = SLOT_M + SLOT_V
FIRST_Z = 8
RELAY = 3
LENGTHS = (
    ((18, 29, 22), (19, 36, 23), (20, 34, 25), (18, 29, 22)),
    ((32, 0, 0), (33, 0, 0), (7, 0, 0), (1, 0, 0)),
)
PARTS = FIRST_Z + 1 + RELAY
EARLY = 5
MARGIN = 384
LINES = 3744


def cut_z(section, depth, part):
    length = LENGTHS[section][depth][0]
    return part * length, length


def cut_y(section, depth):
    first, tail, _ = LENGTHS[section][depth]
    return FIRST_Z * first, tail


def cut_relay(depth, part):
    first, tail, length = LENGTHS[0][depth]
    return FIRST_Z * first + tail + part * length, length


def size_of(section, depth):
    first, tail, length = LENGTHS[section][depth]
    return FIRST_Z * first + tail + RELAY * length


def each(count, run):
    def step(i, carry):
        run(i)
        return carry

    lax.fori_loop(0, count, step, 0)


def shard_plan(shapes, total, devices):
    lines = total // devices // 128
    plans = []
    for device in range(devices):
        low, high = device * lines, (device + 1) * lines
        first, count, pieces = 0, 0, []
        line, tile = 0, 0
        for rows, columns in shapes:
            blocks = columns // 128
            begin, end = max(low, line), min(high, line + rows * blocks)
            if begin < end:
                top, bottom = (begin - line) // blocks, (end - line) // blocks
                assert top * blocks == begin - line and bottom * blocks == end - line
                up, down = top // 16, -(-bottom // 16)
                if not pieces:
                    first = tile + up * blocks
                pieces.append((blocks, line + up * 16 * blocks - low, down - up, count))
                count += (down - up) * blocks
            line += rows * blocks
            tile += rows * blocks // 16
        plans.append((first, count, pieces))
    return plans


def devices_around(z, y, c, s):
    at = lambda zz, yy, cc: (s, zz * 4 + yy * 2 + cc)
    around = {"side": at(z, 1 - y, c), "core": at(z, y, 1 - c)}
    around["cross"] = (1 - s, z * 4 + y * 2 + c)
    if z + 1 < DEPTH:
        around["up"] = at(z + 1, y, c)
    if z > 0:
        around["down"] = at(z - 1, y, c)
    return around


def greet(around):
    barrier = pltpu.get_barrier_semaphore()
    for target in around.values():
        pl.semaphore_signal(barrier, inc=1, device_id=target, device_id_type=MESH)
    pl.semaphore_wait(barrier, len(around))


def place():
    d = lax.axis_index("dp")
    return lax.axis_index("section"), d // 4, (d // 2) % 2, d % 2


def for_each_depth(run):
    s_now, z_now, y, c = place()
    for s in range(2):
        for z in range(DEPTH):
            pl.when((s_now == s) & (z_now == z))(functools.partial(run, s, z, y, c))


class Sender:
    def __init__(self, around, send):
        self.around, self.send, self.used, self.sent = around, send, 0, []

    def many(self, count, make, names):
        groups = []
        for name in names:
            if name in self.around:

                def copy(n, base=self.used, name=name):
                    source, target, sem = make(n)
                    return pltpu.make_async_remote_copy(
                        source,
                        target,
                        self.send.at[base + n],
                        sem,
                        device_id=self.around[name],
                        device_id_type=MESH,
                    )

                self.used += count
                self.sent.append((count, copy))
                groups.append(copy)

        def start(n):
            for copy in groups:
                copy(n).start()

        return start

    def push(self, source, target, sem, *names):
        self.many(1, lambda n: (source, target, sem), names)(0)

    def arrive(self, target, sem):
        pltpu.make_async_remote_copy(
            target,
            target,
            self.send.at[0],
            sem,
            device_id=self.around["core"],
            device_id_type=MESH,
        ).wait_recv()

    def finish(self):
        for count, copy in self.sent:
            each(count, lambda n: copy(n).wait_send())


def gather_kernel(own, out, passing, send, recv, r_pass, local):
    def run(s, z, y, c):
        around = devices_around(z, y, c, s)
        greet(around)
        io = Sender(around, send)

        def slot(zz, yy, cc):
            return zz * 4 + yy * 2 + cc

        def part_z(zz, yy, cc, n, mine=False):
            target = out.at[slot(zz, yy, cc), pl.ds(*cut_z(s, zz, n))]
            source = own.at[pl.ds(*cut_z(s, zz, n))] if mine else target
            return source, target, recv.at[slot(zz, yy, cc), n]

        def part_y(zz, yy, cc, mine=False):
            target = out.at[slot(zz, yy, cc), pl.ds(*cut_y(s, zz))]
            source = own.at[pl.ds(*cut_y(s, zz))] if mine else target
            return source, target, recv.at[slot(zz, yy, cc), FIRST_Z]

        def part_r(zz, yy, cc, n, mine=False):
            target = out.at[slot(zz, yy, cc), pl.ds(*cut_relay(zz, n))]
            source = own.at[pl.ds(*cut_relay(zz, n))] if mine else target
            return source, target, recv.at[slot(zz, yy, cc), FIRST_Z + 1 + n]

        def passed(zz, yy, n):
            length = LENGTHS[0][zz][2]
            target = passing.at[zz * 2 + yy, pl.ds(n * length, length)]
            return target, target, r_pass.at[zz * 2 + yy, n]

        def forward(count, make, names):
            start = io.many(count, make, names)

            def step(n):
                io.arrive(*make(n)[1:])
                start(n)

            each(count, step)

        def relay(zz, yy, names):
            start = io.many(RELAY, lambda n: passed(zz, yy, n), names)
            back = None
            if not (zz == z and yy is y):
                back = io.many(
                    RELAY,
                    lambda n: (passed(zz, yy, n)[0],) + part_r_there(zz, yy, n),
                    ["cross"],
                )

            def step(n):
                io.arrive(*passed(zz, yy, n)[1:])
                start(n)
                if back:
                    back(n)

            each(RELAY, step)

        def part_r_there(zz, yy, n):
            return part_r(zz, yy, c, n)[1:]

        keep = pltpu.make_async_copy(own, out.at[slot(z, y, c)], local)
        if s == 0:
            each(
                RELAY,
                io.many(
                    RELAY,
                    lambda n: (part_r(z, y, c, n, True)[0],) + passed(z, y, n)[1:],
                    ["cross"],
                ),
            )
            io.push(*part_y(z, y, c, True), "side")
            each(
                FIRST_Z,
                io.many(
                    FIRST_Z, lambda n: part_z(z, y, c, n, True), ["up", "down", "side"]
                ),
            )
            io.push(*part_y(z, y, c, True), "up", "down", "core")
            each(RELAY, io.many(RELAY, lambda n: part_r(z, y, c, n, True), ["core"]))
        else:
            relay(z, y, ["up", "down", "side"])
            mine = io.many(FIRST_Z, lambda n: part_z(z, y, c, n, True), ["up", "down", "side"])
            waiting = [z]
            for k in range(1, DEPTH + 1):
                each(FIRST_Z // DEPTH, lambda n, k=k: mine((k - 1) * (FIRST_Z // DEPTH) + n))
                near = [zz for zz in (z - k, z + k) if 0 <= zz < DEPTH]
                for zz in near:
                    relay(zz, y, ["up" if zz < z else "down", "side"])
                for zz in waiting:
                    relay(zz, 1 - y, [])
                waiting = near
        each(FIRST_Z, io.many(FIRST_Z, lambda n: part_z(z, y, c, n, True), ["core"]))
        keep.start()
        if s == 0:
            io.arrive(*part_y(z, 1 - y, c)[1:])
            io.push(*part_y(z, 1 - y, c), "up", "down", "core")
        waiting = [z]
        for k in range(1, DEPTH + 1):
            near = [zz for zz in (z - k, z + k) if 0 <= zz < DEPTH]
            starts = [
                io.many(
                    FIRST_Z,
                    lambda n, zz=zz: part_z(zz, y, c, n),
                    ["up" if zz < z else "down", "side", "core"],
                )
                for zz in near
            ]

            def step(n):
                for zz, start in zip(near, starts):
                    io.arrive(*part_z(zz, y, c, n)[1:])
                    start(n)

            if near:
                each(FIRST_Z, step)
            if s == 0:
                for zz in near:
                    for yy in (y, 1 - y):
                        io.arrive(*part_y(zz, yy, c)[1:])
                        io.push(*part_y(zz, yy, c), "up" if zz < z else "down", "core")
            for zz in waiting:
                forward(FIRST_Z, lambda n, zz=zz: part_z(zz, 1 - y, c, n), ["core"])
            if s == 0:
                for zz, yy in [(zz, 1 - y) for zz in waiting] + [(zz, y) for zz in near]:
                    forward(RELAY, lambda n, zz=zz, yy=yy: part_r(zz, yy, c, n), ["core"])
            waiting = near
        for zz in range(DEPTH):

            def last(yy, zz=zz):
                each(FIRST_Z, lambda n: io.arrive(*part_z(zz, yy, 1 - c, n)[1:]))
                if s == 0:
                    io.arrive(*part_y(zz, yy, 1 - c)[1:])
                    each(RELAY, lambda n: io.arrive(*part_r(zz, yy, 1 - c, n)[1:]))

            each(WIDTH, last)
        keep.wait()
        io.finish()

    for_each_depth(run)


def gather_slots(own):
    hbm = pl.BlockSpec(memory_space=pl.ANY)
    return pl.pallas_call(
        gather_kernel,
        out_shape=[
            jax.ShapeDtypeStruct((16, SLOT, 16, 128), BF),
            jax.ShapeDtypeStruct((8, RELAY * max(n[2] for n in LENGTHS[0]), 16, 128), BF),
        ],
        in_specs=[hbm],
        out_specs=[hbm, hbm],
        scratch_shapes=[
            pltpu.SemaphoreType.DMA((256,)),
            pltpu.SemaphoreType.DMA((16, PARTS)),
            pltpu.SemaphoreType.DMA((8, RELAY)),
            pltpu.SemaphoreType.DMA,
        ],
        name="gather_slots",
        compiler_params=pltpu.CompilerParams(
            collective_id=0, has_side_effects=True, vmem_limit_bytes=VMEM_LIMIT
        ),
    )(own)[0]


def send_order(z):
    order = []
    for k in range(DEPTH - 1, -1, -1):
        for zz in (z + k, z - k):
            if 0 <= zz < DEPTH and zz not in order:
                order.append(zz)
    return order


STEP_TILES = 4


def in_steps(start, count, some, carry=0):
    whole = count // STEP_TILES

    def body(i, carry):
        return some(start + i * STEP_TILES, STEP_TILES, carry)

    carry = lax.fori_loop(0, whole, body, carry)
    if count % STEP_TILES:
        carry = some(start + whole * STEP_TILES, count % STEP_TILES, carry)
    return carry


def total_of(sources, base, size):
    value = sources[0][pl.ds(base, size)].astype(F32)
    for source in sources[1:]:
        value = value + source[pl.ds(base, size)].astype(F32)
    return value


def add_tiles(target, sources, start, count):
    def some(base, size, carry):
        target[pl.ds(base, size)] = total_of(sources, base, size).astype(target.dtype)
        return carry

    in_steps(start, count, some)


class Shifted:
    def __init__(self, ref, start):
        self.ref, self.start = ref, start

    def __getitem__(self, index):
        return self.ref[pl.ds(index.start - self.start, index.size)]


class Section:
    def __init__(self, section, z, y, c, io, refs, sems, low=0, high=FIRST_Z):
        self.section, self.z, self.y, self.c, self.io = section, z, y, c, io
        self.low, self.count = low, high - low
        self.mats, self.vecs, self.held, self.core_in = refs[:4]
        self.side_a, self.side_b, self.z_a, self.z_b = refs[4:]
        self.load, self.r_core, self.r_side, self.r_z = sems
        self.order = send_order(z)
        self.tail = LENGTHS[section][z][1] > 0
        self.loads, self.ready = {}, set()

    def pieces(self, zz, yy, cc):
        slot = zz * 4 + yy * 2 + cc
        low = self.low * LENGTHS[self.section][zz][0]
        high = (self.low + self.count) * LENGTHS[self.section][zz][0]
        if self.low + self.count == FIRST_Z:
            high = size_of(self.section, zz)
        found = []
        if low < SLOT_V:
            count = min(high, SLOT_V) - low
            found.append((self.vecs.at[slot, pl.ds(low, count)], pl.ds(low, count)))
        low = max(low, SLOT_V)
        if high > low:
            source = self.mats.at[slot, pl.ds(low - SLOT_V, high - low)]
            found.append((source, pl.ds(low, high - low)))
        return found

    def begin_loads(self):
        for zz in self.order:
            for yy, flip in ((1 - self.y, True), (self.y, False)):
                where = zz * 2 + yy
                copies = [
                    pltpu.make_async_copy(source, self.held.at[where, there], self.load.at[where, n])
                    for n, (source, there) in enumerate(self.pieces(zz, yy, self.c))
                ]
                for copy in copies:
                    copy.start()
                self.loads[zz, flip] = copies

    def exchange_cores(self):
        for zz in self.order:
            for yy in (1 - self.y, self.y):
                where = zz * 2 + yy
                for n, (source, there) in enumerate(self.pieces(zz, yy, 1 - self.c)):
                    self.io.push(
                        source, self.core_in.at[where, there], self.r_core.at[where, n], "core"
                    )

    def prepare(self, zz, flip):
        if (zz, flip) in self.ready:
            return
        self.ready.add((zz, flip))
        yy = 1 - self.y if flip else self.y
        where = zz * 2 + yy
        for copy in self.loads[zz, flip]:
            copy.wait()
        for n, (_, there) in enumerate(self.pieces(zz, yy, self.c)):
            self.io.arrive(self.core_in.at[where, there], self.r_core.at[where, n])

    def z_cut(self, zz, n):
        return cut_z(self.section, zz, self.low + n)

    def y_cut(self, zz):
        return cut_y(self.section, zz)

    def cut(self, zz, yy, cut):
        return self.held.at[zz * 2 + yy, pl.ds(*cut)]

    def side_in(self, zz, n):
        return self.side_a.at[zz, pl.ds(*self.z_cut(zz, n))], self.r_side.at[zz, self.low + n]

    def side_tail(self, zz):
        return self.side_b.at[pl.ds(0, self.y_cut(zz)[1])], self.r_side.at[zz, FIRST_Z]

    def z_in(self, way, zz, n):
        return self.z_a.at[way, zz, pl.ds(*self.z_cut(zz, n))], self.r_z.at[way, zz, self.low + n]

    def z_tail(self, way, zz, yy):
        ref = self.z_b.at[way, zz, yy, pl.ds(0, self.y_cut(zz)[1])]
        return ref, self.r_z.at[way, zz, FIRST_Z + yy]

    def came(self, cut, pair):
        self.io.arrive(*pair)
        return Shifted(pair[0], cut[0])

    def core_sources(self, zz, yy):
        return [self.held.at[zz * 2 + yy], self.core_in.at[zz * 2 + yy]]

    def add(self, zz, yy, cut, sources):
        add_tiles(self.held.at[zz * 2 + yy], sources, *cut)

    def to_side(self, zz):
        self.prepare(zz, True)
        flip = 1 - self.y
        start = self.io.many(
            self.count,
            lambda n: (self.cut(zz, flip, self.z_cut(zz, n)),) + self.side_in(zz, n),
            ["side"],
        )

        def step(n):
            self.add(zz, flip, self.z_cut(zz, n), self.core_sources(zz, flip))
            start(n)

        each(self.count, step)

    def way(self, zz):
        return (0, "up", 0) if zz > self.z else (1, "down", DEPTH - 1)

    def along(self, zz):
        self.prepare(zz, False)
        way, name, first = self.way(zz)
        start = self.io.many(
            self.count,
            lambda n: (self.cut(zz, self.y, self.z_cut(zz, n)),) + self.z_in(way, zz, n),
            [name],
        )

        def step(n):
            cut = self.z_cut(zz, n)
            sources = self.core_sources(zz, self.y) + [self.came(cut, self.side_in(zz, n))]
            if self.z != first:
                sources.append(self.came(cut, self.z_in(way, zz, n)))
            self.add(zz, self.y, cut, sources)
            start(n)

        each(self.count, step)

    def along_tail(self, zz, flip):
        yy = 1 - self.y if flip else self.y
        self.prepare(zz, flip)
        way, name, first = self.way(zz)
        cut = self.y_cut(zz)
        sources = self.core_sources(zz, yy)
        if self.z != first:
            sources.append(self.came(cut, self.z_tail(way, zz, yy)))
        self.add(zz, yy, cut, sources)
        self.io.push(self.cut(zz, yy, cut), *self.z_tail(way, zz, yy), name)

    def here(self):
        return [way for way, there in ((0, self.z > 0), (1, self.z < DEPTH - 1)) if there]

    def tails(self, yy):
        cut = self.y_cut(self.z)
        return self.core_sources(self.z, yy) + [
            self.came(cut, self.z_tail(way, self.z, yy)) for way in self.here()
        ]

    def tail_to_side(self):
        z, flip = self.z, 1 - self.y
        self.prepare(z, False)
        self.add(z, flip, self.y_cut(z), self.tails(flip))
        self.io.push(self.cut(z, flip, self.y_cut(z)), *self.side_tail(z), "side")

    def end(self, total, carry):
        z, y = self.z, self.y
        self.prepare(z, False)
        if self.tail:
            cut = self.y_cut(z)
            carry = total(cut, self.tails(y) + [self.came(cut, self.side_tail(z))], carry)

        def step(n, carry):
            cut = self.z_cut(z, n)
            sources = self.core_sources(z, y) + [
                self.came(cut, self.z_in(way, z, n)) for way in self.here()
            ]
            return total(cut, sources + [self.came(cut, self.side_in(z, n))], carry)

        return lax.fori_loop(0, self.count, step, carry)


def owned_limits(plans):
    limits = []
    for plan, shapes in zip(plans, (ENC_MATS, DEC_MATS)):
        low = 0
        for _, count, pieces in plan:
            if not pieces:
                limits.append((0, 0, 0, 0, 0))
                continue
            blocks, line, _, _ = pieces[0]
            skip = -line // blocks if line < 0 else 0
            last, line, rows, _ = pieces[-1]
            over = max(0, line + rows * 16 * last - LINES) // last
            limits.append((count, blocks, skip, last, over))
    return limits


def finish_tiles(out, sources, start, count, owned, square):
    tiles, first, skip, last, over, odd = owned
    row = lax.broadcasted_iota(jnp.int32, (1, 16, 1), 1)
    lane = lax.broadcasted_iota(jnp.int32, (1, 1, 128), 2)

    def some(base, size, square):
        value = total_of(sources, base, size)
        out[pl.ds(base, size)] = value
        tile = base - SLOT_V + lax.broadcasted_iota(jnp.int32, (size, 1, 1), 0)
        mine = (tile >= 0) & (tile < tiles) & ((tile >= first) | (row >= skip))
        mine = mine & ((tile < tiles - last) | (row < 16 - over))
        end, edge = odd * -SLOT_V - (1 - odd), (1 - odd) * 15
        theirs = (tile == end) & (row == edge) & (jnp.where(lane < 64, 1, 0) == odd)
        mine = mine | ((tile < 0) & jnp.logical_not(theirs))
        value = jnp.where(mine, value * value, 0.0)
        return square + value.reshape(size * 2, 8, 128).sum(0)

    return in_steps(start, count, some, square)


def section_scratch(section):
    most = FIRST_Z * max(n[0] for n in LENGTHS[0] + LENGTHS[1])
    tail = max(1, max(n[1] for n in LENGTHS[section]))
    size = max(size_of(s, z) for s in range(2) for z in range(DEPTH))
    buffers = [
        pltpu.VMEM((8, size, 16, 128), BF),
        pltpu.VMEM((8, size, 16, 128), BF),
        pltpu.VMEM((DEPTH, most, 16, 128), BF),
        pltpu.VMEM((tail, 16, 128), BF),
        pltpu.VMEM((2, DEPTH, most, 16, 128), BF),
        pltpu.VMEM((2, DEPTH, 2, tail, 16, 128), BF),
    ]
    sems = [
        pltpu.SemaphoreType.DMA((8, 2)),
        pltpu.SemaphoreType.DMA((8, 2)),
        pltpu.SemaphoreType.DMA((DEPTH, FIRST_Z + 1)),
        pltpu.SemaphoreType.DMA((2, DEPTH, FIRST_Z + 2)),
    ]
    return buffers, sems


def scatter_second_kernel(mats, vecs, out, *refs):
    buffers, sems, send = refs[:6], refs[6:10], refs[10]

    def run(s, z, y, c):
        if s == 0:
            return
        around = devices_around(z, y, c, s)
        del around["cross"]
        io = Sender(around, send)
        part = Section(1, z, y, c, io, (mats, vecs) + buffers, sems, 0, EARLY)
        part.begin_loads()
        greet(around)
        part.exchange_cores()
        for zz in part.order:
            part.to_side(zz)
        for zz in part.order[:-1]:
            part.along(zz)

        def total(cut, sources, carry):
            add_tiles(out, sources, *cut)
            return carry

        part.end(total, 0)
        io.finish()

    for_each_depth(run)


def scatter_second(mats, vecs):
    hbm = pl.BlockSpec(memory_space=pl.ANY)
    buffers, sems = section_scratch(1)
    return pl.pallas_call(
        scatter_second_kernel,
        out_shape=jax.ShapeDtypeStruct((SLOT, 16, 128), F32),
        in_specs=[hbm, hbm],
        out_specs=pl.BlockSpec(memory_space=pltpu.VMEM),
        scratch_shapes=buffers + sems + [pltpu.SemaphoreType.DMA((112,))],
        name="scatter_second",
        compiler_params=pltpu.CompilerParams(
            collective_id=3, has_side_effects=True, vmem_limit_bytes=VMEM_LIMIT
        ),
    )(mats, vecs)


def scatter_first_kernel(limits, mats, vecs, second, second_vecs, other_sum, loss, out, total, *refs):
    buffers, sems = refs[:6], refs[6:10]
    r_in, r_side, r_z, r_back, parts, send, s_in, s_side, s_z, s_back, s_parts = refs[10:]
    me = lax.axis_index("section") * 16 + lax.axis_index("dp")
    owned = [sum(jnp.where(me == k, row[n], 0) for k, row in enumerate(limits)) for n in range(5)]
    owned.append(lax.rem(me, 2))

    def other(k):
        device = lax.rem(me + k, 32)
        return device, (device // 16, lax.rem(device, 16))

    def greet_all():
        barrier = pltpu.get_barrier_semaphore()
        for k in range(1, 32):
            pl.semaphore_signal(barrier, inc=1, device_id=other(k)[1], device_id_type=MESH)
        pl.semaphore_wait(barrier, 31)

    def relay(ref, zz, n):
        length = LENGTHS[0][zz][2]
        return ref.at[pl.ds(n * length, length)]

    def keep(square):
        row = lax.broadcasted_iota(jnp.int32, (8, 128), 0)
        parts[me] = jnp.where(row == 0, jnp.sum(square), loss[...])

    def run_first(z, y, c, io):
        part = Section(0, z, y, c, io, (mats, vecs) + buffers, sems)
        part.begin_loads()
        greet_all()
        part.exchange_cores()

        def cross(zz, yy):
            where = zz * 2 + yy
            start = io.many(
                RELAY,
                lambda n: (
                    part.cut(zz, yy, cut_relay(zz, n)),
                    relay(r_in.at[where], zz, n),
                    s_in.at[where, n],
                ),
                ["cross"],
            )

            def step(n):
                part.add(zz, yy, cut_relay(zz, n), part.core_sources(zz, yy))
                start(n)

            each(RELAY, step)

        for zz in part.order:
            part.to_side(zz)
            cross(zz, 1 - y)
            if zz != z:
                part.prepare(zz, False)
                cross(zz, y)
                part.along_tail(zz, True)
                part.along_tail(zz, False)
        part.tail_to_side()
        for zz in part.order[:-1]:
            part.along(zz)

        def total(cut, sources, square):
            return finish_tiles(out, sources, *cut, owned, square)

        square = part.end(total, jnp.zeros((8, 128), F32))

        def last(n, square):
            io.arrive(relay(r_back, z, n), s_back.at[n])
            sources = part.core_sources(z, y) + [Shifted(r_back, cut_relay(z, 0)[0])]
            return total(cut_relay(z, n), sources, square)

        keep(lax.fori_loop(0, RELAY, last, square))

    def run_second(z, y, c, io):
        part = Section(1, z, y, c, io, (second, second_vecs) + buffers, sems, EARLY)
        part.begin_loads()
        greet_all()
        part.exchange_cores()

        def came(ref, zz, n, sem):
            there = relay(ref, zz, n)
            io.arrive(there, sem)
            return there

        def small_add(target, sources):
            add_tiles(target, sources, 0, target.shape[0])

        for zz in part.order:
            flip, same = zz * 2 + 1 - y, zz * 2 + y
            start = io.many(
                RELAY,
                lambda n, zz=zz, flip=flip: (
                    relay(r_in.at[flip], zz, n),
                    relay(r_side.at[zz], zz, n),
                    s_side.at[zz, n],
                ),
                ["side"],
            )

            def to_side(n):
                came(r_in.at[flip], zz, n, s_in.at[flip, n])
                start(n)

            each(RELAY, to_side)
            part.to_side(zz)
            if zz == z:
                continue
            way, name, first = part.way(zz)
            onward = io.many(
                RELAY,
                lambda n, zz=zz, same=same, way=way: (
                    relay(r_in.at[same], zz, n),
                    relay(r_z.at[way, zz], zz, n),
                    s_z.at[way, zz, n],
                ),
                [name],
            )

            def along(n):
                mine = came(r_in.at[same], zz, n, s_in.at[same, n])
                sources = [mine, came(r_side.at[zz], zz, n, s_side.at[zz, n])]
                if z != first:
                    sources.append(came(r_z.at[way, zz], zz, n, s_z.at[way, zz, n]))
                small_add(mine, sources)
                onward(n)

            each(RELAY, along)
            part.along(zz)
        mine = r_in.at[z * 2 + y]
        back = io.many(
            RELAY,
            lambda n: (relay(mine, z, n), relay(r_back, z, n), s_back.at[n]),
            ["cross"],
        )

        def last(n):
            sources = [came(r_side.at[z], z, n, s_side.at[z, n])]
            for way in part.here():
                sources.append(came(r_z.at[way, z], z, n, s_z.at[way, z, n]))
            small_add(relay(mine, z, n), sources)
            back(n)

        each(RELAY, last)
        square = jnp.zeros((8, 128), F32)
        high = EARLY * LENGTHS[1][z][0]
        square = finish_tiles(out, [other_sum], 0, high, owned, square)

        def total(cut, sources, square):
            return finish_tiles(out, sources, *cut, owned, square)

        keep(part.end(total, square))

    def run(s, z, y, c):
        io = Sender(devices_around(z, y, c, s), send)
        (run_second if s else run_first)(z, y, c, io)
        io.finish()

    for_each_depth(run)
    copies = []
    for k in range(1, 32):
        copy = pltpu.make_async_remote_copy(
            parts.at[me],
            parts.at[me],
            send.at[k],
            s_parts.at[me],
            device_id=other(k)[1],
            device_id_type=MESH,
        )
        copy.start()
        copies.append(copy)
    for k in range(1, 32):
        device, where = other(k)
        pltpu.make_async_remote_copy(
            parts.at[device],
            parts.at[device],
            send.at[k],
            s_parts.at[device],
            device_id=where,
            device_id_type=MESH,
        ).wait_recv()
    total[...] = jnp.sum(parts[...], 0)
    for copy in copies:
        copy.wait_send()


def scatter_first(limits, mats, vecs, second, second_vecs, other_sum, loss):
    hbm = pl.BlockSpec(memory_space=pl.ANY)
    vm = pl.BlockSpec(memory_space=pltpu.VMEM)
    buffers, sems = section_scratch(0)
    most, count = RELAY * max(n[2] for n in LENGTHS[0]), RELAY
    return pl.pallas_call(
        functools.partial(scatter_first_kernel, limits),
        out_shape=[
            jax.ShapeDtypeStruct((SLOT, 16, 128), F32),
            jax.ShapeDtypeStruct((8, 128), F32),
        ],
        in_specs=[hbm] * 4 + [vm, vm],
        out_specs=[vm] * 2,
        scratch_shapes=buffers
        + sems
        + [
            pltpu.VMEM((8, most, 16, 128), BF),
            pltpu.VMEM((DEPTH, most, 16, 128), BF),
            pltpu.VMEM((2, DEPTH, most, 16, 128), BF),
            pltpu.VMEM((most, 16, 128), BF),
            pltpu.VMEM((32, 8, 128), F32),
            pltpu.SemaphoreType.DMA((160,)),
            pltpu.SemaphoreType.DMA((8, count)),
            pltpu.SemaphoreType.DMA((DEPTH, count)),
            pltpu.SemaphoreType.DMA((2, DEPTH, count)),
            pltpu.SemaphoreType.DMA((count,)),
            pltpu.SemaphoreType.DMA((32,)),
        ],
        name="scatter_first",
        compiler_params=pltpu.CompilerParams(
            collective_id=1, has_side_effects=True, vmem_limit_bytes=VMEM_LIMIT
        ),
    )(mats, vecs, second, second_vecs, other_sum, loss)


def piece_table(lines):
    plans = [shard_plan(m, lines * 128 * 16, 16) for m in (ENC_MATS, DEC_MATS)]
    most = max(len(pieces) for plan in plans for _, _, pieces in plan)
    table = [
        [[list(p) for p in pieces] + [[0] * 4] * (most - len(pieces)) for _, _, pieces in plan]
        for plan in plans
    ]
    widths = sorted({p[0] for plan in plans for _, _, pieces in plan for p in pieces})
    return plans, table, widths


def each_tile(table, widths, run):
    most = table.shape[0] // 128
    mine = (lax.axis_index("section") * 16 + lax.axis_index("dp")) * most
    for piece in range(most):
        at = (mine + piece) * 4
        for width in widths:

            @pl.when(table[at] == width)
            def _(at=at, width=width):
                def step(i, carry):
                    for j in range(width):
                        line = MARGIN + table[at + 1] + i * (16 * width) + j
                        run(line, width, SLOT_V + table[at + 3] + i * width + j)
                    return carry

                lax.fori_loop(0, table[at + 2], step, 0)


def pack_kernel(widths, table, mat, vec, out, lines, sem):
    count = mat.shape[0]
    copy = pltpu.make_async_copy(mat, lines.at[pl.ds(MARGIN, count)], sem)
    copy.start()
    lines[0:MARGIN, :] = jnp.zeros((MARGIN, 128), F32)
    lines[MARGIN + count :, :] = jnp.zeros((MARGIN, 128), F32)
    out[0:SLOT_V] = vec[...].astype(BF).reshape(SLOT_V, 16, 128)
    copy.wait()

    def run(line, width, tile):
        out[tile] = lines[pl.ds(line, 16, stride=width), :].astype(BF)

    each_tile(table, widths, run)


def pack(table, widths, mat, vec):
    vm = pl.BlockSpec(memory_space=pltpu.VMEM)
    return pl.pallas_call(
        functools.partial(pack_kernel, widths),
        out_shape=jax.ShapeDtypeStruct((SLOT, 16, 128), BF),
        in_specs=[
            pl.BlockSpec(memory_space=pltpu.SMEM),
            pl.BlockSpec(memory_space=pl.ANY),
            vm,
        ],
        out_specs=vm,
        scratch_shapes=[
            pltpu.VMEM((mat.shape[0] + 2 * MARGIN, 128), F32),
            pltpu.SemaphoreType.DMA,
        ],
        name="pack",
        compiler_params=pltpu.CompilerParams(vmem_limit_bytes=VMEM_LIMIT),
    )(table, mat, vec)


def clip_factor(square):
    return jnp.minimum(1.0, 0.001 / (jnp.sqrt(square) + 1e-06))


def adam_update(master, first, second, grad, rate, decay):
    first = 0.9 * first + 0.1 * grad
    second = 0.95 * second + 0.05 * grad * grad
    step_first = first / (1.0 - 0.9**STEP)
    step_second = second / (1.0 - 0.95**STEP)
    master = master - rate * (step_first / (jnp.sqrt(step_second) + 1e-08) + decay * master)
    return (master, first, second)


STEPS = 6


def update_kernel(widths, table, tiles, total, *refs):
    states, news, news_vec, (lines, held, fresh, sem_in, sem_out) = (
        refs[0:3],
        refs[3:6],
        refs[6],
        refs[7:],
    )
    count = held.shape[1]
    size = count // STEPS

    def part(i):
        return pl.ds(i * size, size)

    loads = [
        [
            pltpu.make_async_copy(state.at[part(i)], held.at[n, part(i)], sem_in.at[n, i])
            for n, state in enumerate(states)
        ]
        for i in range(STEPS)
    ]
    for step in loads:
        for copy in step:
            copy.start()
    lines[...] = jnp.zeros_like(lines)

    def run(line, width, tile):
        lines[pl.ds(line, 16, stride=width), :] = tiles[tile]

    each_tile(table, widths, run)
    news_vec[...] = tiles[0:SLOT_V].reshape(SLOT_V * 16, 128)
    factor = clip_factor(total[0:1, :])
    stores = []
    for i in range(STEPS):
        for copy in loads[i]:
            copy.wait()

        def body(k, carry, i=i):
            base = i * size + k * 104
            rows = pl.ds(pl.multiple_of(base, 8), 104)
            grad = factor * lines[pl.ds(pl.multiple_of(MARGIN + base, 8), 104), :]
            for n, value in enumerate(
                adam_update(held[0, rows, :], held[1, rows, :], held[2, rows, :], grad, 0.05, 0.05)
            ):
                fresh[n, rows, :] = value
            return carry

        lax.fori_loop(0, size // 104, body, 0)
        for n, new in enumerate(news):
            copy = pltpu.make_async_copy(fresh.at[n, part(i)], new.at[part(i)], sem_out.at[n, i])
            copy.start()
            stores.append(copy)
    for copy in stores:
        copy.wait()


def update(table, widths, tiles, total, states):
    count = states[0].shape[0]
    vm = pl.BlockSpec(memory_space=pltpu.VMEM)
    hbm = pl.BlockSpec(memory_space=pl.ANY)
    shape = jax.ShapeDtypeStruct((count, 128), F32)
    return pl.pallas_call(
        functools.partial(update_kernel, widths),
        out_shape=[shape] * 3 + [jax.ShapeDtypeStruct((SLOT_V * 16, 128), F32)],
        in_specs=[pl.BlockSpec(memory_space=pltpu.SMEM), vm, vm] + [hbm] * 3,
        out_specs=[hbm] * 3 + [vm],
        scratch_shapes=[
            pltpu.VMEM((count + 2 * MARGIN, 128), F32),
            pltpu.VMEM((3, count, 128), F32),
            pltpu.VMEM((3, count, 128), F32),
            pltpu.SemaphoreType.DMA((3, STEPS)),
            pltpu.SemaphoreType.DMA((3, STEPS)),
        ],
        name="update",
        compiler_params=pltpu.CompilerParams(vmem_limit_bytes=VMEM_LIMIT),
    )(table, tiles, total, *states)


def shifted(value, axis, steps):
    count = lax.axis_size(axis)
    initial, last = (max(0, -steps), min(count, count - steps))
    return lax.ppermute(value, axis, [(source, source + steps) for source in range(initial, last)])


def train(images, masked_total, enc, dec, enc_out, dec_out, pixels, visible, restore, vecs, weights):
    pix = jnp.pad(pixels, ((0, 0), (0, ROWS_D - PATCHES), (0, 0)))
    vis = jnp.pad(visible, ((0, 0), (0, ROWS_E - VIS)), constant_values=-1).reshape(-1, 1)
    places = jnp.pad(restore, ((0, 0), (0, ROWS_D - PATCHES)), constant_values=-1).reshape(-1, 1)
    latent, *saved = encoder_forward(images, enc, vis, pix, vecs, weights, 0)
    arrived = shifted(latent, "section", 1)
    dlatent, loss, dmats_dec, dvec_dec = decoder_step(
        images, dec, dec_out, masked_total, arrived, places, pix, vecs, weights, 1
    )
    returned = shifted(dlatent, "section", -1)
    dmats, dvec = encoder_backward(images, enc, enc_out, vis, vecs, returned, saved, weights, 0)
    return dmats, dvec, dmats_dec, dvec_dec, loss


def body_block(
    pixels, visible, restore, mat_master, mat_first, mat_second, vec_master, vec_first, vec_second
):
    images = pixels.shape[0]
    masked_total = (PATCHES - VIS) * images * 16
    count, size = mat_master.shape[1] // 128, vec_master.shape[1]
    plans, table, widths = piece_table(count)
    table = jnp.asarray(table, jnp.int32).reshape(-1)
    lines = [value.reshape(count, 128) for value in (mat_master, mat_first, mat_second)]
    room = SLOT_V * 2048
    own = pack(
        table, widths, lines[0], jnp.pad(vec_master[0], (0, room - size)).reshape(-1, 128)
    )
    odd = lax.axis_index("dp") % 2 == 1
    slots = gather_slots(own)
    vecs = slots[:, :SLOT_V].reshape(16, room)[:, :size].reshape(-1, 128).astype(F32)
    inward = [slot_layout(plan, slots.shape, SLOT_V) for plan in plans]
    sums = (16, SLOT_V, 16, 128)
    outward = [whole_slots(plan, (16, SLOT_M, 16, 128), sums) for plan in plans]
    dmats, dvec, dmats_dec, dvec_dec, loss = train(
        images, masked_total, *inward, *outward, pixels, visible, restore, vecs, slots
    )
    second = scatter_second(dmats_dec, dvec_dec)
    tiles, total = scatter_first(
        owned_limits(plans), dmats, dvec, dmats_dec, dvec_dec, second, loss
    )
    *news, grad_vec = update(table, widths, tiles, total, lines)
    news = [value.reshape(mat_master.shape) for value in news]
    square, loss_sum = total[0, 0], total[1, 0]
    grad_vec = grad_vec.reshape(1, room)
    grad_vec = jnp.where(odd, grad_vec[:, room - size :], grad_vec[:, :size])
    vec_news = adam_update(
        vec_master,
        vec_first,
        vec_second,
        clip_factor(square) * grad_vec,
        0.3,
        0.0,
    )
    return (
        (loss_sum, jnp.sqrt(square))
        + tuple(news)
        + (news[0].astype(BF),)
        + tuple(vec_news)
        + (vec_news[0].astype(BF),)
    )


def body(
    pixels, visible, restore, mat_master, mat_first, mat_second, vec_master, vec_first, vec_second
):
    images = pixels.shape[0]
    total = mat_master.shape[1] * lax.axis_size("dp")
    masked_total = (PATCHES - VIS) * images * lax.axis_size("dp")
    encoding = lax.axis_index("section") == 0
    enc, dec = plain_layout(ENC_TOTAL), plain_layout(DEC_TOTAL)
    mats = lax.all_gather(mat_master.astype(BF), "dp", axis=1, tiled=True)[0]
    vecs = lax.all_gather(vec_master.astype(BF), "dp", axis=1, tiled=True)[0]
    vecs = vecs.astype(F32).reshape(-1, 128)
    weights = lax.cond(
        encoding,
        lambda m: natural(m, ENC_MATS),
        lambda m: jnp.pad(natural(m, DEC_MATS), ((0, ENC_TOTAL - DEC_TOTAL), (0, 0), (0, 0))),
        mats,
    )
    dec_in = Layout((ENC_TOTAL, 16, 128), [(lambda ref: ref.at[pl.ds(0, DEC_TOTAL)], 0, DEC_TOTAL)], [])
    dmats, dvec, dmats_dec, dvec_dec, loss = train(
        images, masked_total, enc, dec_in, enc, dec, pixels, visible, restore, vecs, weights
    )
    grad_mats, grad_vecs = lax.cond(
        encoding,
        lambda: (flat_from_natural(dmats.astype(F32), ENC_MATS, total), dvec),
        lambda: (flat_from_natural(dmats_dec.astype(F32), DEC_MATS, total), dvec_dec),
    )
    summed_mats = lax.psum_scatter(grad_mats[None], "dp", scatter_dimension=1, tiled=True)
    summed_vecs = lax.psum_scatter(
        grad_vecs.reshape(1, -1), "dp", scatter_dimension=1, tiled=True
    )
    square = jnp.sum(summed_mats * summed_mats) + jnp.sum(summed_vecs * summed_vecs)
    square, loss_sum = lax.psum((square, loss[0, 0]), ("section", "dp"))
    factor = clip_factor(square)
    mat_news = adam_update(mat_master, mat_first, mat_second, factor * summed_mats, 0.05, 0.05)
    vec_news = adam_update(vec_master, vec_first, vec_second, factor * summed_vecs, 0.3, 0.0)
    return (
        (loss_sum, jnp.sqrt(square))
        + tuple(mat_news)
        + (mat_news[0].astype(BF),)
        + tuple(vec_news)
        + (vec_news[0].astype(BF),)
    )


def solution(mesh):
    split = P("section", "dp")
    fits = mesh.shape["section"] == 2 and mesh.shape["dp"] == 16
    return jax.shard_map(
        body_block if fits else body,
        mesh=mesh,
        in_specs=(P("dp", None, None), P("dp", None), P("dp", None)) + (split,) * 6,
        out_specs=(P(), P()) + (split,) * 8,
        check_vma=False,
    )
```
